32 devices in a mesh: gx: 4 (over y, x), gy: 2 (over core), gz: 4 (over z).
Axes of the slice: x: 2, y: 2, z: 4, core: 2. Of those that a mesh axis runs over, the one named last changes fastest.
Arguments:
- volume: bfloat16 [48, 64, 16384], P(None, 'gz', ('gx', 'gy')), may hold values from -6 to 6
- tissue: int32 [32, 8, 4], replicated, may hold values 0 or 1
- w_down1: bfloat16 [8, 64, 48], replicated, may hold values from -0.4375 to 0.4375
- b_down1: float32 [64], replicated, may hold values from -1.5 to 1.5
- w_conv1a: bfloat16 [27, 64, 64], replicated, may hold values from -0.21875 to 0.21875
- b_conv1a: float32 [64], replicated, may hold values from -1.5 to 1.5
- w_conv1b: bfloat16 [27, 64, 64], replicated, may hold values from -0.21875 to 0.21875
- b_conv1b: float32 [64], replicated, may hold values from -1.5 to 1.5
- w_down2: bfloat16 [8, 96, 64], replicated, may hold values from -0.375 to 0.375
- b_down2: float32 [96], replicated, may hold values from -1.5 to 1.5
- w_conv2a: bfloat16 [27, 96, 96], replicated, may hold values from -0.15625 to 0.15625
- b_conv2a: float32 [96], replicated, may hold values from -1.5 to 1.5
- w_conv2b: bfloat16 [27, 96, 96], replicated, may hold values from -0.15625 to 0.15625
- b_conv2b: float32 [96], replicated, may hold values from -1.5 to 1.5
Outputs:
- level_one: bfloat16 [64, 32, 4096], P(None, 'gz', ('gx', 'gy'))
- level_two: bfloat16 [96, 16, 1024], P(None, 'gz', ('gx', 'gy'))
The draws below stay inside these ranges and needn't reach their ends.
All inputs are finite; a program needn't handle non-finite values.
Results may differ from the reference program's by a relative error of at most 0.012.
Values may be sent and summed in bfloat16 or wider, within the bound.
No kernel may reach another device: no remote copies, remote signals or barrier semaphores. Data moves between devices by JAX's collectives and lax.ppermute only.
A program may use at most 128 MiB of HBM per device.

```python
import jax
import jax.numpy as jnp
from jax import lax

C0 = 48
C1 = 64
C2 = 96
CX = 64
CY = 32
NX = 256
NY = 64
NZ = 64
N_GX = 4
N_GY = 2


def with_ends(values, key, low, largest):
    longest = values.shape.index(max(values.shape))
    spots = []
    for shift in (0, 1):
        where = [jax.random.randint(jax.random.fold_in(key, axis), (), 0, length) for axis, length in enumerate(values.shape)]
        where[longest] = (where[longest] + shift) % values.shape[longest]
        spots.append(tuple(where))
    return values.at[spots[0]].set(low).at[spots[1]].set(largest)


def block_levels(stream_key, shape, shards, low, top_value):
    def one(position, blocks):
        draws = jax.random.uniform(jax.random.fold_in(jax.random.fold_in(stream_key, 6), position), (blocks,), jnp.float32, low / len(shards), top_value / len(shards))
        return jnp.repeat(jnp.exp(draws), shape[position] // blocks).reshape((-1,) + (1,) * (len(shape) - position - 1))

    level = one(*shards[0])
    for cut in shards[1:]:
        level = level * one(*cut)
    return level


def normal_values(stream_key, dims, deviation, reach, cuts=(), kind=jnp.bfloat16):
    factor_of = block_levels(stream_key, dims, cuts, -0.22, 0.18) if cuts else 1.0
    array = jax.random.normal(stream_key, dims, jnp.float32) * deviation * factor_of
    return jnp.minimum(jnp.maximum(array, -reach), reach).astype(kind)


def setup_inputs(seed: int = 0) -> dict:
    keys = jax.random.split(jax.random.key(seed), 15)
    volume = normal_values(keys[0], (C0, NZ, NX * NY), 1.0, 6.0, ((1, 4), (2, 8)))
    tissue = with_ends((jax.random.randint(keys[1], (NX // 8, NY // 8, NZ // 16), 0, 3) < 2).astype(jnp.int32), jax.random.fold_in(keys[1], 1), 0, 1)
    w_down1 = normal_values(keys[2], (8, C1, C0), (C0 * 4) ** -0.5, 0.4375)
    b_down1 = normal_values(keys[3], (C1,), 0.3, 1.5, (), jnp.float32)
    w_conv1a = normal_values(keys[4], (27, C1, C1), (C1 * 27 // 2) ** -0.5, 0.21875)
    b_conv1a = normal_values(keys[5], (C1,), 0.3, 1.5, (), jnp.float32)
    w_conv1b = normal_values(keys[6], (27, C1, C1), (C1 * 27 // 2) ** -0.5, 0.21875)
    b_conv1b = normal_values(keys[7], (C1,), 0.3, 1.5, (), jnp.float32)
    w_down2 = normal_values(keys[8], (8, C2, C1), (C1 * 4) ** -0.5, 0.375)
    b_down2 = normal_values(keys[9], (C2,), 0.3, 1.5, (), jnp.float32)
    w_conv2a = normal_values(keys[10], (27, C2, C2), (C2 * 27 // 2) ** -0.5, 0.15625)
    b_conv2a = normal_values(keys[11], (C2,), 0.3, 1.5, (), jnp.float32)
    w_conv2b = normal_values(keys[12], (27, C2, C2), (C2 * 27 // 2) ** -0.5, 0.15625)
    b_conv2b = normal_values(keys[13], (C2,), 0.3, 1.5, (), jnp.float32)
    return dict(volume=volume, tissue=tissue, w_down1=w_down1, b_down1=b_down1, w_conv1a=w_conv1a, b_conv1a=b_conv1a, w_conv1b=w_conv1b, b_conv1b=b_conv1b, w_down2=w_down2, b_down2=b_down2, w_conv2a=w_conv2a, b_conv2a=b_conv2a, w_conv2b=w_conv2b, b_conv2b=b_conv2b)


def upsample(tissue, fx, fy, fz):
    grown = jnp.repeat(tissue.astype(jnp.float32), fx, axis=0)
    grown = jnp.repeat(grown, fy, axis=1)
    return jnp.repeat(grown, fz, axis=2)


def activate(summed, offsets, tissue_mask):
    return (jnp.maximum(summed + offsets[:, None, None, None], 0.0) * tissue_mask).astype(jnp.bfloat16)


def conv_same(field, weights):
    kernel = weights.astype(jnp.float32).reshape(3, 3, 3, weights.shape[1], weights.shape[2]).transpose(3, 4, 0, 1, 2)
    result = lax.conv_general_dilated(field.astype(jnp.float32)[None], kernel, (1, 1, 1), ((1, 1), (1, 1), (1, 1)),
                                      dimension_numbers=("NCDHW", "OIDHW", "NCDHW"), precision=lax.Precision.HIGHEST)
    return result[0]


def conv_down(field, weights):
    kernel = weights.astype(jnp.float32).reshape(2, 2, 2, weights.shape[1], weights.shape[2]).transpose(3, 4, 0, 1, 2)
    result = lax.conv_general_dilated(field.astype(jnp.float32)[None], kernel, (2, 2, 2), "VALID",
                                      dimension_numbers=("NCDHW", "OIDHW", "NCDHW"), precision=lax.Precision.HIGHEST)
    return result[0]


def unpack(packed, block_x, block_y):
    chans, depth = packed.shape[0], packed.shape[1]
    split = packed.reshape(chans, depth, N_GX, N_GY, block_y, block_x)
    return split.transpose(0, 2, 5, 3, 4, 1).reshape(chans, N_GX * block_x, N_GY * block_y, depth)


def pack(grid, block_x, block_y):
    chans, depth = grid.shape[0], grid.shape[3]
    split = grid.reshape(chans, N_GX, block_x, N_GY, block_y, depth)
    return split.transpose(0, 5, 1, 3, 4, 2).reshape(chans, depth, -1)


def reference(volume, tissue, w_down1, b_down1, w_conv1a, b_conv1a, w_conv1b, b_conv1b,
              w_down2, b_down2, w_conv2a, b_conv2a, w_conv2b, b_conv2b):
    grid_zero = unpack(volume, CX, CY)
    mask_one = upsample(tissue, 4, 4, 8)
    mask_two = upsample(tissue, 2, 2, 4)
    slab_count = 8
    slab_width = grid_zero.shape[1] // slab_count

    def one_slab(number):
        piece = lax.dynamic_slice_in_dim(grid_zero, number * slab_width, slab_width, 1)
        return conv_down(piece, w_down1)

    slab_terms = lax.map(one_slab, jnp.arange(slab_count, dtype=jnp.int32))
    summed = jnp.moveaxis(slab_terms, 0, 1).reshape(w_down1.shape[1], -1, slab_terms.shape[3], slab_terms.shape[4])
    down_one = activate(summed, b_down1, mask_one)
    inner_one = activate(conv_same(down_one, w_conv1a), b_conv1a, mask_one)
    feat_one = activate(conv_same(inner_one, w_conv1b), b_conv1b, mask_one)
    down_two = activate(conv_down(feat_one, w_down2), b_down2, mask_two)
    inner_two = activate(conv_same(down_two, w_conv2a), b_conv2a, mask_two)
    feat_two = activate(conv_same(inner_two, w_conv2b), b_conv2b, mask_two)
    return (pack(feat_one, CX // 2, CY // 2), pack(feat_two, CX // 4, CY // 4))
```

```python
import functools

import jax
import jax.numpy as jnp
from jax import lax
from jax.experimental import pallas as pl
from jax.experimental.pallas import tpu as pltpu
from jax.sharding import PartitionSpec as P

CX = 64
CY = 32
X1 = CX // 2
Y1 = CY // 2
X2 = X1 // 2
Y2 = Y1 // 2
Z1 = 8
Z2 = 4
C0 = 48
C1 = 64
C2 = 96
CP = 128
HALO = 6
XB = 10
PITCH1 = 48
PITCH2 = 32
BF = jnp.bfloat16
F32 = jnp.float32
NN = (((1,), (0,)), ((), ()))
NT = (((1,), (1,)), ((), ()))
VMEM_BYTES = 40 * 1024 * 1024


def mm(a, b, dims=NN):
    return lax.dot_general(a, b, dims, preferred_element_type=F32)


def iota(shape, dim):
    return lax.broadcasted_iota(jnp.int32, shape, dim)


def one_hot(flag):
    return jnp.where(flag, 1.0, 0.0).astype(BF)


class Window:
    def __init__(self, n_gy):
        self.one_sided = n_gy == 2
        sides = 1 if self.one_sided else 2
        self.sides = sides
        self.rows = Y1 + HALO * sides
        self.rows_a = self.rows - sides
        self.rows_b = self.rows - 2 * sides
        self.rows_2 = self.rows_b // 2
        self.blocks = 6 if self.one_sided else 8

    def index(self):
        return lax.axis_index("gy") if self.one_sided else 1

    def start_a(self):
        return self.index()

    def start_b(self):
        return 2 * self.index()

    def own(self):
        return HALO * self.index()

    def own_b(self):
        return 4 * self.index()

    def own_2(self):
        return 2 * self.index()

    def shift(self):
        return 2 * self.index()


def mask_rows(tab, y_start, rows, pitch, x_start, x_cells, y_cells, y_shift, window):
    shape = (rows, pitch, 128)
    y_block = lax.div(iota(shape, 0) + (y_start + y_shift), y_cells)
    x_block = lax.div(iota(shape, 1) + (x_start + x_cells), x_cells)
    x_block = jnp.minimum(x_block, XB - 1)
    hit = one_hot(y_block * XB + x_block == iota(shape, 2)).reshape(rows * pitch, 128)
    return mm(hit, tab)


def split_cells(v, dest, first):
    kz = v.shape[0]
    shape = (4 * CX, 4 * CX)
    r = iota(shape, 0)
    a, b, y, x = r // 128, (r // 64) % 2, (r // 32) % 2, r % 32
    select = one_hot((2 * y + b) * CX + 2 * x + a == iota(shape, 1))
    cells = mm(select, v, NT).astype(BF)
    for ab in range(4):
        dest[pl.ds(first, 64), ab * kz : (ab + 1) * kz] = cells[64 * ab : 64 * ab + 64]


def down1_own_kernel(v_ref, w_ref, b_ref, out_ref, wd_ref, cells_ref):
    step = pl.program_id(0)
    steps = pl.num_programs(0)
    z0 = v_ref.shape[1]
    kz = C0 * z0
    lanes = Z1 * C1

    @pl.when(step == 0)
    def _():
        r = iota((kz, 2 * C0), 0)
        l = iota((kz, 2 * C0), 1)
        spread = one_hot((r // z0 == l % C0) & (r % 2 == l // C0))
        keep = (iota((kz, lanes), 0) % z0) // 2 == iota((kz, lanes), 1) // C1
        for ab in range(4):
            pair = w_ref[2 * ab : 2 * ab + 2].reshape(2 * C0, C1)
            wide = jnp.concatenate([pair] * Z1, axis=1)
            wd_ref[ab * kz : (ab + 1) * kz, :] = jnp.where(keep, mm(spread, wide), 0.0).astype(BF)

    for part in range(2):
        v = v_ref[:, :, part * 256 : part * 256 + 256].reshape(kz, 256)
        split_cells(v, cells_ref, pl.multiple_of(step * 128 + part * 64, 64))

    @pl.when(step == steps - 1)
    def _():
        acc = mm(cells_ref[...], wd_ref[...])
        out_ref[...] = jnp.maximum(acc + b_ref[...], 0.0).astype(BF)


def down1_window_kernel(window, v_ref, own_ref, wd_ref, b_ref, tab_ref, out_ref, lo_ref, hi_ref, cells_ref):
    z0 = v_ref.shape[1]
    kz = C0 * z0
    parts = v_ref.shape[2] // 256
    for part in range(parts):
        split_cells(v_ref[:, :, part * 256 : part * 256 + 256].reshape(kz, 256), cells_ref, part * 64)
    acc = mm(cells_ref[...], wd_ref[...])
    halo = jnp.maximum(acc + b_ref[...], 0.0).astype(BF)
    tab = tab_ref[:, 128:256]

    def put(value, start, rows):
        mask = mask_rows(tab, start, rows, X1, 0, 4, 4, window.shift(), window).astype(BF)
        for q in range(4):
            piece = (value[:, q * 128 : q * 128 + 128] * mask).reshape(rows, X1, 128)
            out_ref[pl.ds(start, rows), :, q * 128 : q * 128 + 128] = piece
            if q == 0:
                lo_ref[pl.ds(start, rows)] = piece
            if q == 3:
                hi_ref[pl.ds(start, rows)] = piece

    put(own_ref[...], window.own(), Y1)
    if window.one_sided:
        put(halo, Y1 * (1 - window.index()), HALO)
    else:
        put(halo[: HALO * X1], 0, HALO)
        put(halo[HALO * X1 :], HALO + Y1, HALO)


def banded_kernel(group, chan, pad, w_refs, t_refs):
    for w_ref, t_ref in zip(w_refs, t_refs):
        t_ref[...] = jnp.zeros_like(t_ref)
        for j in range(3):
            for i in range(3):
                for zo in range(group):
                    for k in range(3):
                        lane = i * (group + 2) * pad + (zo + k) * pad
                        t_ref[j, zo * pad : zo * pad + chan, lane : lane + chan] = w_ref[9 * i + 3 * j + k]


def banded(w_first, w_second, group, chan, pad):
    shape = jax.ShapeDtypeStruct((3, group * pad, 3 * (group + 2) * pad), BF)

    def kernel(w1, w2, t1, t2):
        banded_kernel(group, chan, pad, (w1, w2), (t1, t2))

    return pl.pallas_call(
        kernel,
        out_shape=(shape, shape),
        compiler_params=pltpu.CompilerParams(vmem_limit_bytes=VMEM_BYTES),
    )(w_first, w_second)


def conv_group(copies, t_ref, y_first, rows, pitch, lane, group_in, group_out, group_full):
    total = None
    for j in range(3):
        parts = [c[pl.ds(y_first + j, rows), 0:pitch, lane : lane + group_in] for c in copies]
        left = jnp.concatenate([p.reshape(rows * pitch, group_in) for p in parts], axis=1)
        if group_in == group_full:
            right = t_ref[j, 0:group_out, :]
        else:
            right = jnp.concatenate([t_ref[j, 0:group_out, i * group_full : i * group_full + group_in] for i in range(3)], axis=1)
        term = mm(left, right, NT)
        total = term if total is None else total + term
    return total


def fill_copies(copies, pieces, xl_ref, xr_ref, rows, pitch):
    lane = 0
    for ref, first, width in pieces:
        inner = ref[:, :, first : first + width]
        left = xl_ref[:, :, lane : lane + width]
        right = xr_ref[:, :, lane : lane + width]
        cells = inner.shape[1]
        for s in range(3):
            spare = jnp.zeros((rows, pitch - cells - 4 + s, width), BF)
            line = [inner, right, spare] if s == 2 else [left[:, s:], inner, right, spare]
            copies[s][1 : rows + 1, :, lane : lane + width] = jnp.concatenate(line, axis=1)
        lane += width
    for s in range(3):
        edge = jnp.zeros((1, pitch, lane), BF)
        copies[s][0:1] = edge
        copies[s][rows + 1 : rows + 2] = edge


def shift_copies(base, copies, rows, cells):
    for s, copy in enumerate(copies, 1):
        copy[...] = base[:, s : s + cells, :]


def level_one_kernel(
    window, win_ref, zl_ref, zr_ref, xl_ref, xr_ref, ta_ref, tb_ref, ba_ref, bb_ref, wd_ref, bd_ref, tab_ref, tab2_ref,
    one_ref, lo_ref, hi_ref, a0, a1, a2, i0, i1, i2, feat_ref, d_ref,
):
    rows = window.rows
    pieces = [(zl_ref, 0, 128)] + [(win_ref, 128 * q, 128) for q in range(4)] + [(zr_ref, 0, 128)]
    fill_copies((a0, a1, a2), pieces, xl_ref, xr_ref, rows, PITCH1)

    ya, na = window.start_a(), window.rows_a
    mask = mask_rows(tab_ref[...], ya, na, PITCH1, -1, 4, 4, window.shift(), window)
    i0[0:1] = jnp.zeros((1,) + i0.shape[1:], BF)
    i0[rows + 1 : rows + 2] = jnp.zeros((1,) + i0.shape[1:], BF)
    for g, (lane, width, out) in enumerate(((0, 384, 256), (256, 384, 256), (512, 256, 128))):
        acc = conv_group((a0, a1, a2), ta_ref, ya, na, PITCH1, lane, width, out, 384)
        for q in range(out // 128):
            chunk = 2 * g + q
            which = 0 if chunk == 0 else (2 if chunk == 4 else 1)
            value = jnp.maximum(acc[:, q * 128 : q * 128 + 128] + ba_ref[...], 0.0) * mask[:, which * 128 : which * 128 + 128]
            i0[pl.ds(ya + 1, na), :, chunk * 128 : chunk * 128 + 128] = value.astype(BF).reshape(na, PITCH1, 128)

    shift_copies(i0, (i1, i2), rows, X1)
    yb, nb = window.start_b(), window.rows_b
    mask = mask_rows(tab_ref[:, 128:256], yb, nb, X1, 0, 4, 4, window.shift(), window)
    for g in range(2):
        acc = conv_group((i0, i1, i2), tb_ref, yb, nb, X1, 256 * g, 384, 256, 384)
        for q in range(2):
            value = jnp.maximum(acc[:, q * 128 : q * 128 + 128] + bb_ref[...], 0.0) * mask
            feat_ref[:, (2 * g + q) * 128 : (2 * g + q + 1) * 128] = value.astype(BF)

    lanes = Z1 * C1
    r = iota((lanes, lanes), 0)
    order = one_hot((r % Z1) * C1 + r // Z1 == iota((lanes, lanes), 1))
    own = feat_ref[pl.ds(pl.multiple_of(window.own_b() * X1, 128), Y1 * X1), :]
    one_ref[...] = mm(order, own, NT).astype(BF)

    done = 0
    while done < nb:
        n = min(8, nb - done)
        size = n * X1
        quarter = size // 4
        r = iota((size, size), 0)
        ab = r // quarter
        y = (r % quarter) // X2
        select = one_hot((2 * y + ab % 2) * X1 + 2 * (r % X2) + ab // 2 == iota((size, size), 1))
        cells = mm(select, feat_ref[done * X1 : done * X1 + size, :]).astype(BF)
        for q in range(4):
            d_ref[q, done // 2 * X2 : done // 2 * X2 + quarter, :] = cells[q * quarter : (q + 1) * quarter]
        done += n
    n2 = window.rows_2
    mask = mask_rows(tab2_ref[:, 128:256], 0, n2, X2, 0, 2, 2, window.shift(), window)
    for z in range(Z2):
        left = jnp.concatenate([d_ref[q, :, z * 128 : z * 128 + 128] for q in range(4)], axis=1)
        value = (jnp.maximum(mm(left, wd_ref[...]) + bd_ref[...], 0.0) * mask).astype(BF).reshape(n2, X2, CP)
        (lo_ref, hi_ref)[z // 2][:, :, z % 2 * CP : (z % 2 + 1) * CP] = value


def level_two_kernel(
    window, zl_ref, lo_ref, hi_ref, zr_ref, xl_ref, xr_ref, ta_ref, tb_ref, ba_ref, bb_ref, tab_ref,
    out_ref, a0, a1, a2, i0, i1, i2,
):
    rows = window.rows_2
    pieces = [(ref, 128 * q, 128) for ref in (zl_ref, lo_ref, hi_ref, zr_ref) for q in range(2)]
    fill_copies((a0, a1, a2), pieces, xl_ref, xr_ref, rows, PITCH2)
    mask = mask_rows(tab_ref[...], 0, rows, PITCH2, -1, 2, 2, window.shift(), window)
    i0[0:1] = jnp.zeros((1,) + i0.shape[1:], BF)
    i0[rows + 1 : rows + 2] = jnp.zeros((1,) + i0.shape[1:], BF)
    for g in range(3):
        acc = conv_group((a0, a1, a2), ta_ref, 0, rows, PITCH2, 256 * g, 512, 256, 512)
        for q in range(2):
            chunk = 2 * g + q
            which = 0 if chunk == 0 else (2 if chunk == 5 else 1)
            value = jnp.maximum(acc[:, q * 128 : q * 128 + 128] + ba_ref[...], 0.0) * mask[:, which * 128 : which * 128 + 128]
            i0[1 : rows + 1, :, chunk * 128 : chunk * 128 + 128] = value.astype(BF).reshape(rows, PITCH2, 128)
    shift_copies(i0, (i1, i2), rows, X2)
    first = window.own_2()
    mask = mask_rows(tab_ref[:, 128:256], first, Y2, X2, 0, 2, 2, window.shift(), window)
    feat = []
    for g in range(2):
        acc = conv_group((i0, i1, i2), tb_ref, first, Y2, X2, 256 * g, 512, 256, 512)
        for q in range(2):
            feat.append((jnp.maximum(acc[:, q * 128 : q * 128 + 128] + bb_ref[...], 0.0) * mask).astype(BF))
    shape = (C2 * Z2, Z2 * CP)
    r = iota(shape, 0)
    order = one_hot((r % Z2) * CP + r // Z2 == iota(shape, 1))
    out_ref[...] = mm(order, jnp.concatenate(feat, axis=1), NT).astype(BF)


def shift_along(low_edge, high_edge, axis):
    count = lax.axis_size(axis)
    below = lax.ppermute(high_edge, axis, [(i, i + 1) for i in range(count - 1)])
    above = lax.ppermute(low_edge, axis, [(i + 1, i) for i in range(count - 1)])
    return below, above


def params():
    return pltpu.CompilerParams(vmem_limit_bytes=VMEM_BYTES)


def local(
    window, volume, tissue, w_down1, b_down1, w_conv1a, b_conv1a, w_conv1b, b_conv1b,
    w_down2, b_down2, w_conv2a, b_conv2a, w_conv2b, b_conv2b,
):
    index_x = lax.axis_index("gx")
    index_y = lax.axis_index("gy")
    index_z = lax.axis_index("gz")
    depth = volume.shape[1]
    kz = C0 * depth
    send_lanes = 2 * HALO * CX
    last = volume.shape[2] - send_lanes

    if window.one_sided:
        edge = lax.dynamic_slice_in_dim(volume, (1 - index_y) * last, send_lanes, 2)
        halo = lax.ppermute(edge, "gy", [(0, 1), (1, 0)])
    else:
        halo = jnp.concatenate(shift_along(volume[:, :, :send_lanes], volume[:, :, last:], "gy"), axis=2)

    def pad_lanes(value):
        return jnp.pad(value, [(0, 0)] * (value.ndim - 1) + [(0, CP - value.shape[-1])])

    flags = jnp.pad(tissue, ((1, 1), (2, 2), (1, 1)))
    y_first = 2 * index_y if window.one_sided else 4 * index_y
    y_first = y_first + (2 if window.one_sided else 0)
    flags = lax.dynamic_slice(flags, (8 * index_x, y_first, index_z), (XB, window.blocks, 3))
    flags = flags.transpose(1, 0, 2).reshape(window.blocks * XB, 3).astype(BF)
    flags = jnp.pad(flags, ((0, 128 - window.blocks * XB), (0, 0)))
    tab2 = jnp.repeat(flags, 128, axis=1)
    tab1 = jnp.repeat(flags[:, jnp.array([0, 1, 1, 1, 1, 2])], 64, axis=1)

    lanes1 = Z1 * C1
    bias1 = jnp.tile(b_down1, Z1)[None]
    own, wd1 = pl.pallas_call(
        down1_own_kernel,
        grid=(volume.shape[2] // 512,),
        in_specs=[
            pl.BlockSpec((C0, depth, 512), lambda i: (0, 0, i)),
            pl.BlockSpec((8, C0, C1), lambda i: (0, 0, 0)),
            pl.BlockSpec((1, lanes1), lambda i: (0, 0)),
        ],
        out_specs=[
            pl.BlockSpec((Y1 * X1, lanes1), lambda i: (0, 0)),
            pl.BlockSpec((4 * kz, lanes1), lambda i: (0, 0)),
        ],
        out_shape=[
            jax.ShapeDtypeStruct((Y1 * X1, lanes1), BF),
            jax.ShapeDtypeStruct((4 * kz, lanes1), BF),
        ],
        scratch_shapes=[pltpu.VMEM((Y1 * X1, 4 * kz), BF)],
        compiler_params=params(),
    )(volume, jnp.swapaxes(w_down1, 1, 2), bias1)

    rows = window.rows
    win, z_lo, z_hi = pl.pallas_call(
        functools.partial(down1_window_kernel, window),
        out_shape=[
            jax.ShapeDtypeStruct((rows, X1, lanes1), BF),
            jax.ShapeDtypeStruct((rows, X1, 2 * C1), BF),
            jax.ShapeDtypeStruct((rows, X1, 2 * C1), BF),
        ],
        scratch_shapes=[pltpu.VMEM((window.sides * HALO * X1, 4 * kz), BF)],
        compiler_params=params(),
    )(halo, own, wd1, bias1, tab1)

    t1a, t1b = banded(w_conv1a, w_conv1b, 4, C1, C1)
    t2a, t2b = banded(w_conv2a, w_conv2b, 2, C2, CP)

    z_below, z_above = shift_along(z_lo, z_hi, "gz")
    low = jnp.concatenate([z_below[:, :2], win[:, :2], z_above[:, :2]], axis=2)
    high = jnp.concatenate([z_below[:, X1 - 2 :], win[:, X1 - 2 :], z_above[:, X1 - 2 :]], axis=2)
    x_below, x_above = shift_along(low, high, "gx")

    n2 = window.rows_2
    one, d_lo, d_hi = pl.pallas_call(
        functools.partial(level_one_kernel, window),
        out_shape=[
            jax.ShapeDtypeStruct((C1 * Z1, Y1 * X1), BF),
            jax.ShapeDtypeStruct((n2, X2, 2 * CP), BF),
            jax.ShapeDtypeStruct((n2, X2, 2 * CP), BF),
        ],
        scratch_shapes=[pltpu.VMEM((rows + 2, PITCH1, (Z1 + 4) * C1), BF)] * 3
        + [pltpu.VMEM((rows + 2, PITCH1, (Z1 + 2) * C1), BF)]
        + [pltpu.VMEM((rows + 2, X1, (Z1 + 2) * C1), BF)] * 2
        + [pltpu.VMEM((window.rows_b * X1, lanes1), BF), pltpu.VMEM((4, n2 * X2, lanes1), BF)],
        compiler_params=params(),
    )(
        win, z_below, z_above, x_below, x_above, t1a, t1b, jnp.tile(b_conv1a, 2)[None], jnp.tile(b_conv1b, 2)[None],
        pad_lanes(jnp.swapaxes(w_down2, 1, 2).reshape(8 * C1, C2)), pad_lanes(b_down2[None]), tab1, tab2,
    )

    z_below, z_above = shift_along(d_lo, d_hi, "gz")
    line = [z_below, d_lo, d_hi, z_above]
    low = jnp.concatenate([p[:, :2] for p in line], axis=2)
    high = jnp.concatenate([p[:, X2 - 2 :] for p in line], axis=2)
    x_below, x_above = shift_along(low, high, "gx")
    two = pl.pallas_call(
        functools.partial(level_two_kernel, window),
        out_shape=jax.ShapeDtypeStruct((C2 * Z2, Y2 * X2), BF),
        scratch_shapes=[pltpu.VMEM((n2 + 2, PITCH2, (Z2 + 4) * CP), BF)] * 3
        + [pltpu.VMEM((n2 + 2, PITCH2, (Z2 + 2) * CP), BF)]
        + [pltpu.VMEM((n2 + 2, X2, (Z2 + 2) * CP), BF)] * 2,
        compiler_params=params(),
    )(
        z_below, d_lo, d_hi, z_above, x_below, x_above, t2a, t2b, pad_lanes(b_conv2a[None]), pad_lanes(b_conv2b[None]), tab2
    )
    return one.reshape(C1, Z1, Y1 * X1), two.reshape(C2, Z2, Y2 * X2)


def solution(mesh):
    block = P(None, "gz", ("gx", "gy"))
    return jax.shard_map(
        functools.partial(local, Window(mesh.shape["gy"])),
        mesh=mesh,
        in_specs=(block,) + (P(),) * 13,
        out_specs=(block, block),
        check_vma=False,
    )
```

```python
import functools

import jax
import jax.numpy as jnp
from jax import lax
from jax.experimental import pallas as pl
from jax.experimental.pallas import tpu as pltpu
from jax.sharding import PartitionSpec as P

CX = 64
CY = 32
X1 = CX // 2
Y1 = CY // 2
X2 = X1 // 2
Y2 = Y1 // 2
Z1 = 8
Z2 = 4
C0 = 48
C1 = 64
C2 = 96
CP = 128
HALO = 6
XB = 10
PITCH1 = 48
PITCH2 = 32
BF = jnp.bfloat16
F32 = jnp.float32
NN = (((1,), (0,)), ((), ()))
NT = (((1,), (1,)), ((), ()))
VMEM_BYTES = 40 * 1024 * 1024


def mm(a, b, dims=NN):
    return lax.dot_general(a, b, dims, preferred_element_type=F32)


def iota(shape, dim):
    return lax.broadcasted_iota(jnp.int32, shape, dim)


def one_hot(flag):
    return jnp.where(flag, 1.0, 0.0).astype(BF)


class Window:
    def __init__(self, n_gy):
        self.one_sided = n_gy == 2
        sides = 1 if self.one_sided else 2
        self.sides = sides
        self.rows = Y1 + HALO * sides
        self.rows_a = self.rows - sides
        self.rows_b = self.rows - 2 * sides
        self.rows_2 = self.rows_b // 2
        self.blocks = 6 if self.one_sided else 8

    def index(self):
        return lax.axis_index("gy") if self.one_sided else 1

    def start_a(self):
        return self.index()

    def start_b(self):
        return 2 * self.index()

    def own(self):
        return HALO * self.index()

    def own_b(self):
        return 4 * self.index()

    def own_2(self):
        return 2 * self.index()

    def shift(self):
        return 2 * self.index()


def mask_rows(tab, y_start, rows, pitch, x_start, x_cells, y_cells, y_shift, window):
    shape = (rows, pitch, 128)
    y_block = lax.div(iota(shape, 0) + (y_start + y_shift), y_cells)
    x_block = lax.div(iota(shape, 1) + (x_start + x_cells), x_cells)
    x_block = jnp.minimum(x_block, XB - 1)
    hit = one_hot(y_block * XB + x_block == iota(shape, 2)).reshape(rows * pitch, 128)
    return mm(hit, tab)


def split_cells(v, dest, first):
    kz = v.shape[0]
    shape = (4 * CX, 4 * CX)
    r = iota(shape, 0)
    a, b, y, x = r // 128, (r // 64) % 2, (r // 32) % 2, r % 32
    select = one_hot((2 * y + b) * CX + 2 * x + a == iota(shape, 1))
    cells = mm(select, v, NT).astype(BF)
    for ab in range(4):
        dest[pl.ds(first, 64), ab * kz : (ab + 1) * kz] = cells[64 * ab : 64 * ab + 64]


def edge_kernel(last, v_ref, out_ref, sem):
    start = pl.multiple_of((1 - lax.axis_index("gy")) * last, 128)
    copy = pltpu.make_async_copy(v_ref.at[:, :, pl.ds(start, out_ref.shape[2])], out_ref, sem)
    copy.start()
    copy.wait()


def down1_own_kernel(v_ref, w_ref, b_ref, out_ref, wd_ref, field_ref, cells_ref, sems):
    z0 = v_ref.shape[1]
    kz = C0 * z0
    lanes = Z1 * C1
    copies = []
    for n in range(sems.shape[0]):
        cut = (slice(None), slice(None), slice(n * 512, n * 512 + 512))
        copies.append(pltpu.make_async_copy(v_ref.at[cut], field_ref.at[cut], sems.at[n]))
        copies[-1].start()

    r = iota((kz, 2 * C0), 0)
    l = iota((kz, 2 * C0), 1)
    spread = one_hot((r // z0 == l % C0) & (r % 2 == l // C0))
    keep = (iota((kz, lanes), 0) % z0) // 2 == iota((kz, lanes), 1) // C1
    for ab in range(4):
        pair = w_ref[2 * ab : 2 * ab + 2].reshape(2 * C0, C1)
        wide = jnp.concatenate([pair] * Z1, axis=1)
        wd_ref[ab * kz : (ab + 1) * kz, :] = jnp.where(keep, mm(spread, wide), 0.0).astype(BF)

    for n, copy in enumerate(copies):
        copy.wait()
        for part in range(2 * n, 2 * n + 2):
            v = field_ref[:, :, part * 256 : part * 256 + 256].reshape(kz, 256)
            split_cells(v, cells_ref, part * 64)
    acc = mm(cells_ref[...], wd_ref[...])
    out_ref[...] = jnp.maximum(acc + b_ref[...], 0.0).astype(BF)


def down1_window_kernel(window, v_ref, own_ref, wd_ref, b_ref, tab_ref, out_ref, lo_ref, hi_ref, cells_ref):
    z0 = v_ref.shape[1]
    kz = C0 * z0
    parts = v_ref.shape[2] // 256
    for part in range(parts):
        split_cells(v_ref[:, :, part * 256 : part * 256 + 256].reshape(kz, 256), cells_ref, part * 64)
    acc = mm(cells_ref[...], wd_ref[...])
    halo = jnp.maximum(acc + b_ref[...], 0.0).astype(BF)
    tab = tab_ref[:, 128:256]

    def put(value, start, rows):
        mask = mask_rows(tab, start, rows, X1, 0, 4, 4, window.shift(), window).astype(BF)
        for q in range(4):
            piece = (value[:, q * 128 : q * 128 + 128] * mask).reshape(rows, X1, 128)
            out_ref[pl.ds(start, rows), :, q * 128 : q * 128 + 128] = piece
            if q == 0:
                lo_ref[pl.ds(start, rows)] = piece
            if q == 3:
                hi_ref[pl.ds(start, rows)] = piece

    put(own_ref[...], window.own(), Y1)
    if window.one_sided:
        put(halo, Y1 * (1 - window.index()), HALO)
    else:
        put(halo[: HALO * X1], 0, HALO)
        put(halo[HALO * X1 :], HALO + Y1, HALO)


def banded_kernel(group, chan, pad, w_refs, t_refs):
    for w_ref, t_ref in zip(w_refs, t_refs):
        t_ref[...] = jnp.zeros_like(t_ref)
        for j in range(3):
            for i in range(3):
                for zo in range(group):
                    for k in range(3):
                        lane = i * (group + 2) * pad + (zo + k) * pad
                        t_ref[j, zo * pad : zo * pad + chan, lane : lane + chan] = w_ref[9 * i + 3 * j + k]


def banded(w_first, w_second, group, chan, pad):
    shape = jax.ShapeDtypeStruct((3, group * pad, 3 * (group + 2) * pad), BF)

    def kernel(w1, w2, t1, t2):
        banded_kernel(group, chan, pad, (w1, w2), (t1, t2))

    return pl.pallas_call(
        kernel,
        out_shape=(shape, shape),
        compiler_params=pltpu.CompilerParams(vmem_limit_bytes=VMEM_BYTES),
    )(w_first, w_second)


def conv_group(copies, t_ref, y_first, rows, pitch, lane, group_in, group_out, group_full):
    total = None
    for j in range(3):
        parts = [c[pl.ds(y_first + j, rows), 0:pitch, lane : lane + group_in] for c in copies]
        left = jnp.concatenate([p.reshape(rows * pitch, group_in) for p in parts], axis=1)
        if group_in == group_full:
            right = t_ref[j, 0:group_out, :]
        else:
            right = jnp.concatenate([t_ref[j, 0:group_out, i * group_full : i * group_full + group_in] for i in range(3)], axis=1)
        term = mm(left, right, NT)
        total = term if total is None else total + term
    return total


def fill_copies(copies, pieces, xl_ref, xr_ref, rows, pitch):
    lane = 0
    for ref, first, width in pieces:
        inner = ref[:, :, first : first + width]
        left = xl_ref[:, :, lane : lane + width]
        right = xr_ref[:, :, lane : lane + width]
        cells = inner.shape[1]
        for s in range(3):
            spare = jnp.zeros((rows, pitch - cells - 4 + s, width), BF)
            line = [inner, right, spare] if s == 2 else [left[:, s:], inner, right, spare]
            copies[s][1 : rows + 1, :, lane : lane + width] = jnp.concatenate(line, axis=1)
        lane += width
    for s in range(3):
        edge = jnp.zeros((1, pitch, lane), BF)
        copies[s][0:1] = edge
        copies[s][rows + 1 : rows + 2] = edge


def shift_copies(base, copies, rows, cells):
    for s, copy in enumerate(copies, 1):
        copy[...] = base[:, s : s + cells, :]


def level_one_kernel(
    window, win_ref, zl_ref, zr_ref, xl_ref, xr_ref, ta_ref, tb_ref, ba_ref, bb_ref, wd_ref, bd_ref, tab_ref, tab2_ref,
    one_ref, lo_ref, hi_ref, a0, a1, a2, i0, i1, i2, feat_ref, d_ref,
):
    rows = window.rows
    pieces = [(zl_ref, 0, 128)] + [(win_ref, 128 * q, 128) for q in range(4)] + [(zr_ref, 0, 128)]
    fill_copies((a0, a1, a2), pieces, xl_ref, xr_ref, rows, PITCH1)

    ya, na = window.start_a(), window.rows_a
    mask = mask_rows(tab_ref[...], ya, na, PITCH1, -1, 4, 4, window.shift(), window)
    i0[0:1] = jnp.zeros((1,) + i0.shape[1:], BF)
    i0[rows + 1 : rows + 2] = jnp.zeros((1,) + i0.shape[1:], BF)
    for g, (lane, width, out) in enumerate(((0, 384, 256), (256, 384, 256), (512, 256, 128))):
        acc = conv_group((a0, a1, a2), ta_ref, ya, na, PITCH1, lane, width, out, 384)
        for q in range(out // 128):
            chunk = 2 * g + q
            which = 0 if chunk == 0 else (2 if chunk == 4 else 1)
            value = jnp.maximum(acc[:, q * 128 : q * 128 + 128] + ba_ref[...], 0.0) * mask[:, which * 128 : which * 128 + 128]
            i0[pl.ds(ya + 1, na), :, chunk * 128 : chunk * 128 + 128] = value.astype(BF).reshape(na, PITCH1, 128)

    shift_copies(i0, (i1, i2), rows, X1)
    yb, nb = window.start_b(), window.rows_b
    mask = mask_rows(tab_ref[:, 128:256], yb, nb, X1, 0, 4, 4, window.shift(), window)
    for g in range(2):
        acc = conv_group((i0, i1, i2), tb_ref, yb, nb, X1, 256 * g, 384, 256, 384)
        for q in range(2):
            value = jnp.maximum(acc[:, q * 128 : q * 128 + 128] + bb_ref[...], 0.0) * mask
            feat_ref[:, (2 * g + q) * 128 : (2 * g + q + 1) * 128] = value.astype(BF)

    lanes = Z1 * C1
    r = iota((lanes, lanes), 0)
    order = one_hot((r % Z1) * C1 + r // Z1 == iota((lanes, lanes), 1))
    own = feat_ref[pl.ds(pl.multiple_of(window.own_b() * X1, 128), Y1 * X1), :]
    one_ref[...] = mm(order, own, NT).astype(BF)

    done = 0
    while done < nb:
        n = min(8, nb - done)
        size = n * X1
        quarter = size // 4
        r = iota((size, size), 0)
        ab = r // quarter
        y = (r % quarter) // X2
        select = one_hot((2 * y + ab % 2) * X1 + 2 * (r % X2) + ab // 2 == iota((size, size), 1))
        cells = mm(select, feat_ref[done * X1 : done * X1 + size, :]).astype(BF)
        for q in range(4):
            d_ref[q, done // 2 * X2 : done // 2 * X2 + quarter, :] = cells[q * quarter : (q + 1) * quarter]
        done += n
    n2 = window.rows_2
    mask = mask_rows(tab2_ref[:, 128:256], 0, n2, X2, 0, 2, 2, window.shift(), window)
    for z in range(Z2):
        left = jnp.concatenate([d_ref[q, :, z * 128 : z * 128 + 128] for q in range(4)], axis=1)
        value = (jnp.maximum(mm(left, wd_ref[...]) + bd_ref[...], 0.0) * mask).astype(BF).reshape(n2, X2, CP)
        (lo_ref, hi_ref)[z // 2][:, :, z % 2 * CP : (z % 2 + 1) * CP] = value


def level_two_kernel(
    window, zl_ref, lo_ref, hi_ref, zr_ref, xl_ref, xr_ref, ta_ref, tb_ref, ba_ref, bb_ref, tab_ref,
    out_ref, a0, a1, a2, i0, i1, i2,
):
    rows = window.rows_2
    pieces = [(ref, 128 * q, 128) for ref in (zl_ref, lo_ref, hi_ref, zr_ref) for q in range(2)]
    fill_copies((a0, a1, a2), pieces, xl_ref, xr_ref, rows, PITCH2)
    mask = mask_rows(tab_ref[...], 0, rows, PITCH2, -1, 2, 2, window.shift(), window)
    i0[0:1] = jnp.zeros((1,) + i0.shape[1:], BF)
    i0[rows + 1 : rows + 2] = jnp.zeros((1,) + i0.shape[1:], BF)
    for g in range(3):
        acc = conv_group((a0, a1, a2), ta_ref, 0, rows, PITCH2, 256 * g, 512, 256, 512)
        for q in range(2):
            chunk = 2 * g + q
            which = 0 if chunk == 0 else (2 if chunk == 5 else 1)
            value = jnp.maximum(acc[:, q * 128 : q * 128 + 128] + ba_ref[...], 0.0) * mask[:, which * 128 : which * 128 + 128]
            i0[1 : rows + 1, :, chunk * 128 : chunk * 128 + 128] = value.astype(BF).reshape(rows, PITCH2, 128)
    shift_copies(i0, (i1, i2), rows, X2)
    first = window.own_2()
    mask = mask_rows(tab_ref[:, 128:256], first, Y2, X2, 0, 2, 2, window.shift(), window)
    feat = []
    for g in range(2):
        acc = conv_group((i0, i1, i2), tb_ref, first, Y2, X2, 256 * g, 512, 256, 512)
        for q in range(2):
            feat.append((jnp.maximum(acc[:, q * 128 : q * 128 + 128] + bb_ref[...], 0.0) * mask).astype(BF))
    shape = (C2 * Z2, Z2 * CP)
    r = iota(shape, 0)
    order = one_hot((r % Z2) * CP + r // Z2 == iota(shape, 1))
    out_ref[...] = mm(order, jnp.concatenate(feat, axis=1), NT).astype(BF)


def swap_pairs(count, first):
    pairs = [(i, i) for i in range(first)]
    for i in range(first, count, 2):
        pairs += [(i, i + 1), (i + 1, i)] if i + 1 < count else [(i, i)]
    return pairs


def shift_along(low_edge, high_edge, axis):
    count = lax.axis_size(axis)
    index = lax.axis_index(axis)
    even = index % 2 == 0
    one = lax.ppermute(jnp.where(even, high_edge, low_edge), axis, swap_pairs(count, 0))
    two = lax.ppermute(jnp.where(even, low_edge, high_edge), axis, swap_pairs(count, 1))
    below = jnp.where(index > 0, jnp.where(even, two, one), jnp.zeros_like(one))
    above = jnp.where(index < count - 1, jnp.where(even, one, two), jnp.zeros_like(one))
    return below, above


def params():
    return pltpu.CompilerParams(vmem_limit_bytes=VMEM_BYTES)


def local(
    window, volume, tissue, w_down1, b_down1, w_conv1a, b_conv1a, w_conv1b, b_conv1b,
    w_down2, b_down2, w_conv2a, b_conv2a, w_conv2b, b_conv2b,
):
    index_x = lax.axis_index("gx")
    index_y = lax.axis_index("gy")
    index_z = lax.axis_index("gz")
    depth = volume.shape[1]
    kz = C0 * depth
    send_lanes = 2 * HALO * CX
    last = volume.shape[2] - send_lanes

    if window.one_sided:
        edge = pl.pallas_call(
            functools.partial(edge_kernel, last),
            in_specs=[pl.BlockSpec(memory_space=pltpu.HBM)],
            out_shape=jax.ShapeDtypeStruct((C0, depth, send_lanes), BF),
            scratch_shapes=[pltpu.SemaphoreType.DMA],
        )(volume)
        halo = lax.ppermute(edge, "gy", [(0, 1), (1, 0)])
    else:
        halo = jnp.concatenate(shift_along(volume[:, :, :send_lanes], volume[:, :, last:], "gy"), axis=2)

    def pad_lanes(value):
        return jnp.pad(value, [(0, 0)] * (value.ndim - 1) + [(0, CP - value.shape[-1])])

    flags = jnp.pad(tissue, ((1, 1), (2, 2), (1, 1)))
    y_first = 2 * index_y if window.one_sided else 4 * index_y
    y_first = y_first + (2 if window.one_sided else 0)
    flags = lax.dynamic_slice(flags, (8 * index_x, y_first, index_z), (XB, window.blocks, 3))
    flags = flags.transpose(1, 0, 2).reshape(window.blocks * XB, 3).astype(BF)
    flags = jnp.pad(flags, ((0, 128 - window.blocks * XB), (0, 0)))
    tab2 = jnp.repeat(flags, 128, axis=1)
    tab1 = jnp.repeat(flags[:, jnp.array([0, 1, 1, 1, 1, 2])], 64, axis=1)

    lanes1 = Z1 * C1
    bias1 = jnp.tile(b_down1, Z1)[None]
    own, wd1 = pl.pallas_call(
        down1_own_kernel,
        in_specs=[pl.BlockSpec(memory_space=pltpu.HBM)] + [pl.BlockSpec(memory_space=pltpu.VMEM)] * 2,
        out_shape=[
            jax.ShapeDtypeStruct((Y1 * X1, lanes1), BF),
            jax.ShapeDtypeStruct((4 * kz, lanes1), BF),
        ],
        scratch_shapes=[
            pltpu.VMEM(volume.shape, BF),
            pltpu.VMEM((Y1 * X1, 4 * kz), BF),
            pltpu.SemaphoreType.DMA((volume.shape[2] // 512,)),
        ],
        compiler_params=params(),
    )(volume, jnp.swapaxes(w_down1, 1, 2), bias1)

    rows = window.rows
    win, z_lo, z_hi = pl.pallas_call(
        functools.partial(down1_window_kernel, window),
        out_shape=[
            jax.ShapeDtypeStruct((rows, X1, lanes1), BF),
            jax.ShapeDtypeStruct((rows, X1, 2 * C1), BF),
            jax.ShapeDtypeStruct((rows, X1, 2 * C1), BF),
        ],
        scratch_shapes=[pltpu.VMEM((window.sides * HALO * X1, 4 * kz), BF)],
        compiler_params=params(),
    )(halo, own, wd1, bias1, tab1)

    t1a, t1b = banded(w_conv1a, w_conv1b, 4, C1, C1)
    t2a, t2b = banded(w_conv2a, w_conv2b, 2, C2, CP)

    z_below, z_above = shift_along(z_lo, z_hi, "gz")
    low = jnp.concatenate([z_below[:, :2], win[:, :2], z_above[:, :2]], axis=2)
    high = jnp.concatenate([z_below[:, X1 - 2 :], win[:, X1 - 2 :], z_above[:, X1 - 2 :]], axis=2)
    x_below, x_above = shift_along(low, high, "gx")

    n2 = window.rows_2
    one, d_lo, d_hi = pl.pallas_call(
        functools.partial(level_one_kernel, window),
        out_shape=[
            jax.ShapeDtypeStruct((C1 * Z1, Y1 * X1), BF),
            jax.ShapeDtypeStruct((n2, X2, 2 * CP), BF),
            jax.ShapeDtypeStruct((n2, X2, 2 * CP), BF),
        ],
        scratch_shapes=[pltpu.VMEM((rows + 2, PITCH1, (Z1 + 4) * C1), BF)] * 3
        + [pltpu.VMEM((rows + 2, PITCH1, (Z1 + 2) * C1), BF)]
        + [pltpu.VMEM((rows + 2, X1, (Z1 + 2) * C1), BF)] * 2
        + [pltpu.VMEM((window.rows_b * X1, lanes1), BF), pltpu.VMEM((4, n2 * X2, lanes1), BF)],
        compiler_params=params(),
    )(
        win, z_below, z_above, x_below, x_above, t1a, t1b, jnp.tile(b_conv1a, 2)[None], jnp.tile(b_conv1b, 2)[None],
        pad_lanes(jnp.swapaxes(w_down2, 1, 2).reshape(8 * C1, C2)), pad_lanes(b_down2[None]), tab1, tab2,
    )

    z_below, z_above = shift_along(d_lo, d_hi, "gz")
    line = [z_below, d_lo, d_hi, z_above]
    low = jnp.concatenate([p[:, :2] for p in line], axis=2)
    high = jnp.concatenate([p[:, X2 - 2 :] for p in line], axis=2)
    x_below, x_above = shift_along(low, high, "gx")
    two = pl.pallas_call(
        functools.partial(level_two_kernel, window),
        out_shape=jax.ShapeDtypeStruct((C2 * Z2, Y2 * X2), BF),
        scratch_shapes=[pltpu.VMEM((n2 + 2, PITCH2, (Z2 + 4) * CP), BF)] * 3
        + [pltpu.VMEM((n2 + 2, PITCH2, (Z2 + 2) * CP), BF)]
        + [pltpu.VMEM((n2 + 2, X2, (Z2 + 2) * CP), BF)] * 2,
        compiler_params=params(),
    )(
        z_below, d_lo, d_hi, z_above, x_below, x_above, t2a, t2b, pad_lanes(b_conv2a[None]), pad_lanes(b_conv2b[None]), tab2
    )
    return one.reshape(C1, Z1, Y1 * X1), two.reshape(C2, Z2, Y2 * X2)


def solution(mesh):
    block = P(None, "gz", ("gx", "gy"))
    return jax.shard_map(
        functools.partial(local, Window(mesh.shape["gy"])),
        mesh=mesh,
        in_specs=(block,) + (P(),) * 13,
        out_specs=(block, block),
        check_vma=False,
    )
```

```python
import jax
import jax.numpy as jnp
from jax import lax
from jax.experimental import pallas as pl
from jax.experimental.pallas import tpu as pltpu
from jax.sharding import PartitionSpec as P

CX = 64
CY = 32
X1 = CX // 2
Y1 = CY // 2
X2 = X1 // 2
Y2 = Y1 // 2
Z1 = 8
Z2 = 4
C0 = 48
C1 = 64
C2 = 96
CP = 128
HALO = 2
XB = 10
YB = 6
ROWS1 = Y1 + 2 * HALO
ROWS2 = Y2 + 2 * HALO
EDGE = 16
PITCH2 = 32
BF = jnp.bfloat16
F32 = jnp.float32
NN = (((1,), (0,)), ((), ()))
NT = (((1,), (1,)), ((), ()))
VMEM_BYTES = 40 * 1024 * 1024


def mm(a, b, dims=NN):
    return lax.dot_general(a, b, dims, preferred_element_type=F32)


def iota(shape, dim):
    return lax.broadcasted_iota(jnp.int32, shape, dim)


def one_hot(flag):
    return jnp.where(flag, 1.0, 0.0).astype(BF)


def mask_rows(tab, y_start, rows, pitch, x_of, cell):
    shape = (rows, pitch, 128)
    y_block = lax.div(iota(shape, 0) + (y_start + cell), cell)
    x_block = jnp.minimum(lax.div(x_of(iota(shape, 1)) + cell, cell), XB - 1)
    hit = one_hot(y_block * XB + x_block == iota(shape, 2)).reshape(rows * pitch, 128)
    return mm(hit, tab)


def down1_kernel(v_ref, w_ref, b_ref, tab_ref, out_ref, wd_ref, field_ref, cells_ref, sems):
    z0 = v_ref.shape[1]
    kz = C0 * z0
    lanes = Z1 * C1
    copies = []
    for n in range(sems.shape[0]):
        cut = (slice(None), slice(None), slice(n * 256, n * 256 + 256))
        copies.append(pltpu.make_async_copy(v_ref.at[cut], field_ref.at[cut], sems.at[n]))
        copies[-1].start()

    r = iota((kz, 2 * C0), 0)
    l = iota((kz, 2 * C0), 1)
    spread = one_hot((r // z0 == l % C0) & (r % 2 == l // C0))
    keep = (iota((kz, lanes), 0) % z0) // 2 == iota((kz, lanes), 1) // C1
    for ab in range(4):
        pair = w_ref[2 * ab : 2 * ab + 2].reshape(2 * C0, C1)
        wide = jnp.concatenate([pair] * Z1, axis=1)
        wd_ref[ab * kz : (ab + 1) * kz, :] = jnp.where(keep, mm(spread, wide), 0.0).astype(BF)

    shape = (4 * CX, 4 * CX)
    r = iota(shape, 0)
    a, b, y, x = r // 128, (r // 64) % 2, (r // 32) % 2, r % 32
    select = one_hot((2 * y + b) * CX + 2 * x + a == iota(shape, 1))
    for n, copy in enumerate(copies):
        copy.wait()
        v = field_ref[:, :, n * 256 : n * 256 + 256].reshape(kz, 256)
        cells = mm(select, v, NT).astype(BF)
        for ab in range(4):
            cells_ref[n * 64 : n * 64 + 64, ab * kz : (ab + 1) * kz] = cells[64 * ab : 64 * ab + 64]
    mask = mask_rows(tab_ref[:, 128:256], 0, Y1, X1, lambda x: x, 4)
    acc = mm(cells_ref[...], wd_ref[...])
    for q in range(4):
        cut = slice(q * 128, q * 128 + 128)
        value = jnp.maximum(acc[:, cut] + b_ref[...], 0.0) * mask
        out_ref[:, :, cut] = value.astype(BF).reshape(Y1, X1, 128)


def banded(weights, group, pad):
    chan = weights.shape[1]

    def kernel(w_ref, t_ref):
        t_ref[...] = jnp.zeros_like(t_ref)
        for j in range(3):
            for i in range(3):
                for zo in range(group):
                    for k in range(3):
                        lane = i * (group + 2) * pad + (zo + k) * pad
                        t_ref[j, zo * pad : zo * pad + chan, lane : lane + chan] = w_ref[9 * i + 3 * j + k]

    return pl.pallas_call(
        kernel,
        out_shape=jax.ShapeDtypeStruct((3, group * pad, 3 * (group + 2) * pad), BF),
        compiler_params=params(),
        cost_estimate=cost(1e-6),
    )(weights)


def conv_group(taps, t_ref, y_first, rows, group_out, group_full):
    pitch = taps[0][0][0].shape[1]
    width = sum(piece[2] for piece in taps[0])
    total = None
    for j in range(3):
        parts = [ref[y_first + j : y_first + j + rows, :, lane : lane + n] for tap in taps for ref, lane, n in tap]
        left = jnp.concatenate([p.reshape(rows * pitch, p.shape[2]) for p in parts], axis=1)
        if width == group_full:
            right = t_ref[j, 0:group_out, :]
        else:
            right = jnp.concatenate([t_ref[j, 0:group_out, i * group_full : i * group_full + width] for i in range(3)], axis=1)
        term = mm(left, right, NT)
        total = term if total is None else total + term
    return total


def finish(acc, bias, mask, rows):
    value = jnp.maximum(acc + bias, 0.0) * mask
    return value.astype(BF).reshape(rows, value.shape[0] // rows, value.shape[1])


def fill_sides(left, right, lane, inner):
    cut = slice(lane, lane + inner.shape[2])
    none = jnp.zeros_like(inner[:, :1])
    left[:, :, cut] = jnp.concatenate([none, inner[:, :-1]], axis=1)
    right[:, :, cut] = jnp.concatenate([inner[:, 1:], none], axis=1)


def middle_kernel(win_ref, t_ref, b_ref, tab_ref, left_ref, right_ref, out_ref):
    for q in range(4):
        fill_sides(left_ref, right_ref, q * 128, win_ref[:, :, q * 128 : q * 128 + 128])
    rows = Y1 + 2
    mask = mask_rows(tab_ref[:, 128:256], -1, rows, X1, lambda x: x, 4)
    acc = conv_group([[(ref, 128, 384)] for ref in (left_ref, win_ref, right_ref)], t_ref, 0, rows, 256, 384)
    for q in range(2):
        cut = slice(q * 128, q * 128 + 128)
        out_ref[:, :, cut] = finish(acc[:, cut], b_ref[...], mask, rows)


def outer_kernel(win_ref, left_ref, right_ref, zl_ref, zr_ref, t_ref, b_ref, tab_ref, low_ref, high_ref, ll, lr, hl, hr):
    fill_sides(ll, lr, 0, zl_ref[...])
    fill_sides(hl, hr, 0, zr_ref[...])
    own = (left_ref, win_ref, right_ref)
    rows = Y1 + 2
    mask = mask_rows(tab_ref[...], -1, rows, X1, lambda x: x, 4)
    taps = [[(z, 0, 128), (ref, 0, 256)] for z, ref in zip((ll, zl_ref, lr), own)]
    acc = conv_group(taps, t_ref, 0, rows, 256, 384)
    for q in range(2):
        cut = slice(q * 128, q * 128 + 128)
        low_ref[:, :, cut] = finish(acc[:, cut], b_ref[...], mask[:, cut], rows)
    taps = [[(ref, 384, 128), (z, 0, 128)] for z, ref in zip((hl, zr_ref, hr), own)]
    acc = conv_group(taps, t_ref, 0, rows, 128, 384)
    high_ref[...] = finish(acc, b_ref[...], mask[:, 256:384], rows)


def fill_edges(copies, pieces):
    rows, pitch, lanes = copies[0].shape
    for lane in range(0, lanes, 128):
        line = [p[:, :, lane : lane + 128] for p in pieces]
        used = sum(p.shape[1] for p in line)
        for i, copy in enumerate(copies):
            moved = [line[0][:, i:]] + line[1:] if i < line[0].shape[1] else line[1:]
            spare = jnp.zeros((rows, pitch - used + i, 128), BF)
            copy[:, :, lane : lane + 128] = jnp.concatenate(moved + [spare], axis=1)


def level_one_kernel(
    xl_ref, low_ref, high_ref, xr_ref, g1_ref, g2_ref, g3_ref, ta_ref, tb_ref, ba_ref, bb_ref, wd_ref, bd_ref, tab_ref, tab2_ref,
    one_ref, down_ref, e0, e1, e2, i0, i1, i2, feat_ref, d_ref,
):
    fill_edges((e0, e1, e2), (xl_ref, low_ref, high_ref, xr_ref))
    rows = Y1 + 2
    mask = mask_rows(tab_ref[...], -1, rows, EDGE, lambda r: jnp.where(r < 4, r - 1, r + X1 - 5), 4)
    for g, (lane, width, out) in enumerate(((0, 384, 256), (256, 384, 256), (512, 256, 128))):
        acc = conv_group([[(e, lane, width)] for e in (e0, e1, e2)], ta_ref, 0, rows, out, 384)
        for q in range(out // 128):
            chunk = 2 * g + q
            which = 0 if chunk == 0 else (2 if chunk == 4 else 1)
            edge = finish(acc[:, q * 128 : q * 128 + 128], ba_ref[...], mask[:, which * 128 : which * 128 + 128], rows)
            inner = (g1_ref, g2_ref, g3_ref)[g][:, :, q * 128 : q * 128 + 128][:, 1:-1]
            cut = slice(chunk * 128, chunk * 128 + 128)
            i0[:, :, cut] = jnp.concatenate([edge[:, 0:2], inner], axis=1)
            i1[:, :, cut] = jnp.concatenate([edge[:, 1:2], inner, edge[:, 4:5]], axis=1)
            i2[:, :, cut] = jnp.concatenate([inner, edge[:, 4:6]], axis=1)

    mask = mask_rows(tab_ref[:, 128:256], 0, Y1, X1, lambda x: x, 4)
    for g in range(2):
        acc = conv_group([[(ref, 256 * g, 384)] for ref in (i0, i1, i2)], tb_ref, 0, Y1, 256, 384)
        for q in range(2):
            value = jnp.maximum(acc[:, q * 128 : q * 128 + 128] + bb_ref[...], 0.0) * mask
            feat_ref[:, (2 * g + q) * 128 : (2 * g + q + 1) * 128] = value.astype(BF)

    lanes = Z1 * C1
    size = 8 * X1
    quarter = size // 4
    r = iota((size, size), 0)
    ab = r // quarter
    y = (r % quarter) // X2
    select = one_hot((2 * y + ab % 2) * X1 + 2 * (r % X2) + ab // 2 == iota((size, size), 1))
    for n in range(Y1 // 8):
        cells = mm(select, feat_ref[n * size : n * size + size, :]).astype(BF)
        for q in range(4):
            d_ref[q, n * quarter : n * quarter + quarter, :] = cells[q * quarter : (q + 1) * quarter]
    mask = mask_rows(tab2_ref[:, 128:256], 0, Y2, X2, lambda x: x, 2)
    for z in range(Z2):
        left = jnp.concatenate([d_ref[q, :, z * 128 : z * 128 + 128] for q in range(4)], axis=1)
        down_ref[:, :, z * CP : z * CP + CP] = finish(mm(left, wd_ref[...]), bd_ref[...], mask, Y2)

    r = iota((lanes, lanes), 0)
    order = one_hot((r % Z1) * C1 + r // Z1 == iota((lanes, lanes), 1))
    one_ref[...] = mm(order, feat_ref[...], NT).astype(BF)


def level_two_kernel(
    win_ref, zl_ref, zr_ref, xl_ref, xr_ref, ta_ref, tb_ref, ba_ref, bb_ref, tab_ref, out_ref, a0, a1, a2, i0, i1, i2
):
    for chunk in range(8):
        ref, lane = (zl_ref, chunk) if chunk < 2 else ((win_ref, chunk - 2) if chunk < 6 else (zr_ref, chunk - 6))
        inner = ref[:, :, lane * 128 : lane * 128 + 128]
        cut = slice(chunk * 128, chunk * 128 + 128)
        left, right = xl_ref[:, :, cut], xr_ref[:, :, cut]
        for i, copy in enumerate((a0, a1, a2)):
            spare = jnp.zeros((ROWS2, PITCH2 - X2 - 4 + i, 128), BF)
            line = [inner, right, spare] if i == 2 else [left[:, i:], inner, right, spare]
            copy[:, :, cut] = jnp.concatenate(line, axis=1)
    rows = Y2 + 2
    mask = mask_rows(tab_ref[...], -1, rows, PITCH2, lambda x: x - 1, 2)
    for g in range(3):
        acc = conv_group([[(ref, 256 * g, 512)] for ref in (a0, a1, a2)], ta_ref, 0, rows, 256, 512)
        for q in range(2):
            chunk = 2 * g + q
            which = 0 if chunk == 0 else (2 if chunk == 5 else 1)
            value = finish(acc[:, q * 128 : q * 128 + 128], ba_ref[...], mask[:, which * 128 : which * 128 + 128], rows)
            cut = slice(chunk * 128, chunk * 128 + 128)
            for s, copy in enumerate((i0, i1, i2)):
                copy[:, :, cut] = value[:, s : s + X2]
    mask = mask_rows(tab_ref[:, 128:256], 0, Y2, X2, lambda x: x, 2)
    feat = []
    for g in range(2):
        acc = conv_group([[(ref, 256 * g, 512)] for ref in (i0, i1, i2)], tb_ref, 0, Y2, 256, 512)
        for q in range(2):
            feat.append((jnp.maximum(acc[:, q * 128 : q * 128 + 128] + bb_ref[...], 0.0) * mask).astype(BF))
    shape = (C2 * Z2, Z2 * CP)
    r = iota(shape, 0)
    order = one_hot((r % Z2) * CP + r // Z2 == iota(shape, 1))
    out_ref[...] = mm(order, jnp.concatenate(feat, axis=1), NT).astype(BF)


def swap_pairs(count, first):
    pairs = [(i, i) for i in range(first)]
    for i in range(first, count, 2):
        pairs += [(i, i + 1), (i + 1, i)] if i + 1 < count else [(i, i)]
    return pairs


def shift_along(low_edge, high_edge, axis):
    count = lax.axis_size(axis)
    index = lax.axis_index(axis)
    even = index % 2 == 0
    one = lax.ppermute(jnp.where(even, high_edge, low_edge), axis, swap_pairs(count, 0))
    two = one
    if count > 2:
        two = lax.ppermute(jnp.where(even, low_edge, high_edge), axis, swap_pairs(count, 1))
    below = jnp.where(index > 0, jnp.where(even, two, one), jnp.zeros_like(one))
    above = jnp.where(index < count - 1, jnp.where(even, one, two), jnp.zeros_like(one))
    return below, above


def params():
    return pltpu.CompilerParams(vmem_limit_bytes=VMEM_BYTES)


def cost(seconds):
    return pl.CostEstimate(flops=int(1e15 * seconds), bytes_accessed=0, transcendentals=0)


def shaped(*shape):
    return jax.ShapeDtypeStruct(shape, BF)


def pad_lanes(value):
    return jnp.pad(value, [(0, 0)] * (value.ndim - 1) + [(0, CP - value.shape[-1])])


def tissue_tables(tissue):
    flags = jnp.pad(tissue, 1)
    start = (8 * lax.axis_index("gx"), 4 * lax.axis_index("gy"), lax.axis_index("gz"))
    flags = lax.dynamic_slice(flags, start, (XB, YB, 3))
    flags = flags.transpose(1, 0, 2).reshape(YB * XB, 3).astype(F32)
    flags = jnp.pad(flags, ((0, 128 - YB * XB), (0, 0)))
    lane = iota((128, 384), 1)

    def spread(first, last):
        return jnp.where(lane < first, flags[:, 0:1], jnp.where(lane < last, flags[:, 1:2], flags[:, 2:3])).astype(BF)

    return spread(64, 320), spread(128, 256)


def local(
    volume, tissue, w_down1, b_down1, w_conv1a, b_conv1a, w_conv1b, b_conv1b,
    w_down2, b_down2, w_conv2a, b_conv2a, w_conv2b, b_conv2b,
):
    depth = volume.shape[1]
    kz = C0 * depth
    lanes1 = Z1 * C1
    tab1, tab2 = tissue_tables(tissue)
    own = pl.pallas_call(
        down1_kernel,
        in_specs=[pl.BlockSpec(memory_space=pltpu.HBM)] + [pl.BlockSpec(memory_space=pltpu.VMEM)] * 3,
        out_shape=shaped(Y1, X1, lanes1),
        scratch_shapes=[
            pltpu.VMEM((4 * kz, lanes1), BF),
            pltpu.VMEM(volume.shape, BF),
            pltpu.VMEM((Y1 * X1, 4 * kz), BF),
            pltpu.SemaphoreType.DMA((volume.shape[2] // 256,)),
        ],
        compiler_params=params(),
        cost_estimate=cost(4e-6),
    )(volume, jnp.swapaxes(w_down1, 1, 2), jnp.tile(b_down1, 2)[None], tab1)

    t1a = banded(w_conv1a, 4, C1)
    t1b = banded(w_conv1b, 4, C1)
    t2a = banded(w_conv2a, 2, CP)
    t2b = banded(w_conv2b, 2, CP)
    bias1a = jnp.tile(b_conv1a, 2)[None]

    y_below, y_above = shift_along(own[:HALO], own[Y1 - HALO :], "gy")
    win = jnp.concatenate([y_below, own, y_above], axis=0)
    z_below, z_above = shift_along(win[:, :, :128], win[:, :, lanes1 - 128 :], "gz")
    rows = Y1 + 2
    left, right, g2 = pl.pallas_call(
        middle_kernel,
        out_shape=[shaped(ROWS1, X1, lanes1), shaped(ROWS1, X1, lanes1), shaped(rows, X1, 256)],
        compiler_params=params(),
        cost_estimate=cost(3e-6),
    )(win, t1a, bias1a, tab1)

    low = jnp.concatenate([z_below[:, :2], win[:, :2], z_above[:, :2]], axis=2)
    high = jnp.concatenate([z_below[:, X1 - 2 :], win[:, X1 - 2 :], z_above[:, X1 - 2 :]], axis=2)
    x_below, x_above = shift_along(low, high, "gx")
    g1, g3 = pl.pallas_call(
        outer_kernel,
        out_shape=[shaped(rows, X1, 256), shaped(rows, X1, 128)],
        scratch_shapes=[pltpu.VMEM((ROWS1, X1, 128), BF)] * 4,
        compiler_params=params(),
        cost_estimate=cost(4e-6),
    )(win, left, right, z_below, z_above, t1a, bias1a, tab1)

    one, down = pl.pallas_call(
        level_one_kernel,
        out_shape=[shaped(lanes1, Y1 * X1), shaped(Y2, X2, Z2 * CP)],
        scratch_shapes=[pltpu.VMEM((ROWS1, EDGE, (Z1 + 4) * C1), BF)] * 3
        + [pltpu.VMEM((rows, X1, (Z1 + 2) * C1), BF)] * 3
        + [pltpu.VMEM((Y1 * X1, lanes1), BF), pltpu.VMEM((4, Y2 * X2, lanes1), BF)],
        compiler_params=params(),
        cost_estimate=cost(6e-6),
    )(
        x_below, low, high, x_above, g1, g2, g3, t1a, t1b, bias1a, jnp.tile(b_conv1b, 2)[None],
        pad_lanes(jnp.swapaxes(w_down2, 1, 2).reshape(8 * C1, C2)), pad_lanes(b_down2[None]), tab1, tab2,
    )

    y_below, y_above = shift_along(down[:HALO], down[Y2 - HALO :], "gy")
    win = jnp.concatenate([y_below, down, y_above], axis=0)
    z_below, z_above = shift_along(win[:, :, : 2 * CP], win[:, :, 2 * CP :], "gz")
    low = jnp.concatenate([z_below[:, :2], win[:, :2], z_above[:, :2]], axis=2)
    high = jnp.concatenate([z_below[:, X2 - 2 :], win[:, X2 - 2 :], z_above[:, X2 - 2 :]], axis=2)
    x_below, x_above = shift_along(low, high, "gx")
    two = pl.pallas_call(
        level_two_kernel,
        out_shape=shaped(C2 * Z2, Y2 * X2),
        scratch_shapes=[pltpu.VMEM((ROWS2, PITCH2, (Z2 + 4) * CP), BF)] * 3
        + [pltpu.VMEM((Y2 + 2, X2, (Z2 + 2) * CP), BF)] * 3,
        compiler_params=params(),
        cost_estimate=cost(5e-6),
    )(win, z_below, z_above, x_below, x_above, t2a, t2b, pad_lanes(b_conv2a[None]), pad_lanes(b_conv2b[None]), tab2)
    return one.reshape(C1, Z1, Y1 * X1), two.reshape(C2, Z2, Y2 * X2)


def solution(mesh):
    block = P(None, "gz", ("gx", "gy"))
    return jax.shard_map(
        local,
        mesh=mesh,
        in_specs=(block,) + (P(),) * 13,
        out_specs=(block, block),
        check_vma=False,
    )
```

```python
import jax
import jax.numpy as jnp
from jax import lax
from jax.experimental import pallas as pl
from jax.experimental.pallas import tpu as pltpu
from jax.sharding import PartitionSpec as P

CX = 64
CY = 32
X1 = CX // 2
Y1 = CY // 2
X2 = X1 // 2
Y2 = Y1 // 2
Z1 = 8
Z2 = 4
C0 = 48
C1 = 64
C2 = 96
CP = 128
HALO = 2
XB = 10
YB = 6
ROWS1 = Y1 + 2 * HALO
ROWS2 = Y2 + 2 * HALO
EDGE = 16
PITCH2 = 32
BF = jnp.bfloat16
F32 = jnp.float32
NN = (((1,), (0,)), ((), ()))
NT = (((1,), (1,)), ((), ()))
VMEM_BYTES = 40 * 1024 * 1024


def mm(a, b, dims=NN):
    return lax.dot_general(a, b, dims, preferred_element_type=F32)


def iota(shape, dim):
    return lax.broadcasted_iota(jnp.int32, shape, dim)


def one_hot(flag):
    return jnp.where(flag, 1.0, 0.0).astype(BF)


def mask_rows(tab, y_start, rows, pitch, x_of, cell):
    shape = (rows, pitch, 128)
    y_block = lax.div(iota(shape, 0) + (y_start + cell), cell)
    x_block = jnp.minimum(lax.div(x_of(iota(shape, 1)) + cell, cell), XB - 1)
    hit = one_hot(y_block * XB + x_block == iota(shape, 2)).reshape(rows * pitch, 128)
    return mm(hit, tab)


def tissue_tables(t_ref):
    n_y, n_z, n_x = t_ref.shape
    here = lax.axis_index("gz")
    layers = []
    for k in (-1, 0, 1):
        z = here + k
        inside = jnp.where((z >= 0) & (z < n_z), 1.0, 0.0)
        layers.append(t_ref[:, jnp.clip(z, 0, n_z - 1), :].astype(F32) * inside)
    block = iota((128, n_y), 0)
    hot_y = one_hot((block < YB * XB) & (lax.axis_index("gy") * 4 - 1 + block // XB == iota((128, n_y), 1)))
    block = iota((128, 3 * n_x), 0)
    hot_x = lax.axis_index("gx") * 8 - 1 + block % XB == iota((128, 3 * n_x), 1) % n_x
    rows = jnp.where(hot_x, mm(hot_y, jnp.concatenate(layers, axis=1).astype(BF)), 0.0).astype(BF)
    shape = (3 * n_x, 384)
    layer, lane = iota(shape, 0) // n_x, iota(shape, 1)

    def spread(first, last):
        place = jnp.where(lane < first, 0, jnp.where(lane < last, 1, 2))
        return mm(rows, one_hot(layer == place)).astype(BF)

    return spread(64, 320), spread(128, 256)


def down1_kernel(v_ref, w_ref, b_ref, t_ref, out_ref, tab_ref, tab2_ref, wd_ref, field_ref, cells_ref, sems):
    half = v_ref.shape[2]
    kz = C0 * half
    lanes = Z1 // 2 * C1
    copies = []
    for n in range(sems.shape[0]):
        cut = (slice(None), slice(None), slice(None), slice(n * 256, n * 256 + 256))
        copies.append(pltpu.make_async_copy(v_ref.at[cut], field_ref.at[cut], sems.at[n]))
        copies[-1].start()

    tab, tab2 = tissue_tables(t_ref)
    tab_ref[...] = tab
    tab2_ref[...] = tab2
    r = iota((kz, 2 * C0), 0)
    l = iota((kz, 2 * C0), 1)
    spread = one_hot((r // half == l % C0) & (r % 2 == l // C0))
    keep = (iota((kz, lanes), 0) % half) // 2 == iota((kz, lanes), 1) // C1
    for ab in range(4):
        pair = w_ref[2 * ab : 2 * ab + 2].reshape(2 * C0, C1)
        wide = jnp.concatenate([pair] * (Z1 // 2), axis=1)
        wd_ref[ab * kz : (ab + 1) * kz, :] = jnp.where(keep, mm(spread, wide), 0.0).astype(BF)

    shape = (4 * CX, 4 * CX)
    r = iota(shape, 0)
    a, b, y, x = r // 128, (r // 64) % 2, (r // 32) % 2, r % 32
    select = one_hot((2 * y + b) * CX + 2 * x + a == iota(shape, 1))
    for n, copy in enumerate(copies):
        copy.wait()
        for h in range(2):
            v = field_ref[:, h, :, n * 256 : n * 256 + 256].reshape(kz, 256)
            cells = mm(select, v, NT).astype(BF)
            for ab in range(4):
                cells_ref[h, n * 64 : n * 64 + 64, ab * kz : (ab + 1) * kz] = cells[64 * ab : 64 * ab + 64]
    mask = mask_rows(tab[:, 128:256], 0, Y1, X1, lambda x: x, 4)
    bias = twice(b_ref)
    for h in range(2):
        acc = mm(cells_ref[h], wd_ref[...])
        for q in range(2):
            value = finish(acc[:, q * 128 : q * 128 + 128], bias, mask, Y1)
            out_ref[:, :, (2 * h + q) * 128 : (2 * h + q + 1) * 128] = value


def twice(b_ref):
    return jnp.concatenate([b_ref[...]] * 2, axis=1)


def banded(weights, group, pad):
    chan = weights.shape[1]

    def kernel(w_ref, t_ref):
        t_ref[...] = jnp.zeros_like(t_ref)
        for j in range(3):
            for i in range(3):
                for zo in range(group):
                    for k in range(3):
                        lane = i * (group + 2) * pad + (zo + k) * pad
                        t_ref[j, zo * pad : zo * pad + chan, lane : lane + chan] = w_ref[9 * i + 3 * j + k]

    return pl.pallas_call(
        kernel,
        out_shape=jax.ShapeDtypeStruct((3, group * pad, 3 * (group + 2) * pad), BF),
        compiler_params=params(),
        cost_estimate=cost(1e-6),
    )(weights)


def conv_group(taps, t_ref, y_first, rows, group_out, group_full):
    pitch = taps[0][0][0].shape[1]
    width = sum(piece[2] for piece in taps[0])
    total = None
    for j in range(3):
        parts = [ref[y_first + j : y_first + j + rows, :, lane : lane + n] for tap in taps for ref, lane, n in tap]
        left = jnp.concatenate([p.reshape(rows * pitch, p.shape[2]) for p in parts], axis=1)
        if width == group_full:
            right = t_ref[j, 0:group_out, :]
        else:
            right = jnp.concatenate([t_ref[j, 0:group_out, i * group_full : i * group_full + width] for i in range(3)], axis=1)
        term = mm(left, right, NT)
        total = term if total is None else total + term
    return total


def finish(acc, bias, mask, rows):
    value = jnp.maximum(acc + bias, 0.0) * mask
    return value.astype(BF).reshape(rows, value.shape[0] // rows, value.shape[1])


def fill_sides(left, right, lane, inner):
    cut = slice(lane, lane + inner.shape[2])
    none = jnp.zeros_like(inner[:, :1])
    left[:, :, cut] = jnp.concatenate([none, inner[:, :-1]], axis=1)
    right[:, :, cut] = jnp.concatenate([inner[:, 1:], none], axis=1)


def middle_kernel(win_ref, t_ref, b_ref, tab_ref, left_ref, right_ref, out_ref):
    for q in range(4):
        fill_sides(left_ref, right_ref, q * 128, win_ref[:, :, q * 128 : q * 128 + 128])
    rows = Y1 + 2
    mask = mask_rows(tab_ref[:, 128:256], -1, rows, X1, lambda x: x, 4)
    acc = conv_group([[(ref, 128, 384)] for ref in (left_ref, win_ref, right_ref)], t_ref, 0, rows, 256, 384)
    for q in range(2):
        cut = slice(q * 128, q * 128 + 128)
        out_ref[:, :, cut] = finish(acc[:, cut], twice(b_ref), mask, rows)


def outer_kernel(win_ref, left_ref, right_ref, zl_ref, zr_ref, t_ref, b_ref, tab_ref, low_ref, high_ref, ll, lr, hl, hr):
    fill_sides(ll, lr, 0, zl_ref[...])
    fill_sides(hl, hr, 0, zr_ref[...])
    own = (left_ref, win_ref, right_ref)
    rows = Y1 + 2
    mask = mask_rows(tab_ref[...], -1, rows, X1, lambda x: x, 4)
    taps = [[(z, 0, 128), (ref, 0, 256)] for z, ref in zip((ll, zl_ref, lr), own)]
    acc = conv_group(taps, t_ref, 0, rows, 256, 384)
    for q in range(2):
        cut = slice(q * 128, q * 128 + 128)
        low_ref[:, :, cut] = finish(acc[:, cut], twice(b_ref), mask[:, cut], rows)
    taps = [[(ref, 384, 128), (z, 0, 128)] for z, ref in zip((hl, zr_ref, hr), own)]
    acc = conv_group(taps, t_ref, 0, rows, 128, 384)
    high_ref[...] = finish(acc, twice(b_ref), mask[:, 256:384], rows)


def fill_edges(copies, pieces):
    rows, pitch, lanes = copies[0].shape
    for lane in range(0, lanes, 128):
        line = [p[:, :, lane : lane + 128] for p in pieces]
        used = sum(p.shape[1] for p in line)
        for i, copy in enumerate(copies):
            moved = [line[0][:, i:]] + line[1:] if i < line[0].shape[1] else line[1:]
            spare = jnp.zeros((rows, pitch - used + i, 128), BF)
            copy[:, :, lane : lane + 128] = jnp.concatenate(moved + [spare], axis=1)


def level_one_kernel(
    xl_ref, low_ref, high_ref, xr_ref, g1_ref, g2_ref, g3_ref, ta_ref, tb_ref, ba_ref, bb_ref, wd_ref, bd_ref, tab_ref, tab2_ref,
    one_ref, down_ref, e0, e1, e2, i0, i1, i2, feat_ref, d_ref,
):
    fill_edges((e0, e1, e2), (xl_ref, low_ref, high_ref, xr_ref))
    rows = Y1 + 2
    mask = mask_rows(tab_ref[...], -1, rows, EDGE, lambda r: jnp.where(r < 4, r - 1, r + X1 - 5), 4)
    for g, (lane, width, out) in enumerate(((0, 384, 256), (256, 384, 256), (512, 256, 128))):
        acc = conv_group([[(e, lane, width)] for e in (e0, e1, e2)], ta_ref, 0, rows, out, 384)
        for q in range(out // 128):
            chunk = 2 * g + q
            which = 0 if chunk == 0 else (2 if chunk == 4 else 1)
            edge = finish(acc[:, q * 128 : q * 128 + 128], twice(ba_ref), mask[:, which * 128 : which * 128 + 128], rows)
            inner = (g1_ref, g2_ref, g3_ref)[g][:, :, q * 128 : q * 128 + 128][:, 1:-1]
            cut = slice(chunk * 128, chunk * 128 + 128)
            i0[:, :, cut] = jnp.concatenate([edge[:, 0:2], inner], axis=1)
            i1[:, :, cut] = jnp.concatenate([edge[:, 1:2], inner, edge[:, 4:5]], axis=1)
            i2[:, :, cut] = jnp.concatenate([inner, edge[:, 4:6]], axis=1)

    mask = mask_rows(tab_ref[:, 128:256], 0, Y1, X1, lambda x: x, 4)
    for g in range(2):
        acc = conv_group([[(ref, 256 * g, 384)] for ref in (i0, i1, i2)], tb_ref, 0, Y1, 256, 384)
        for q in range(2):
            value = jnp.maximum(acc[:, q * 128 : q * 128 + 128] + twice(bb_ref), 0.0) * mask
            feat_ref[:, (2 * g + q) * 128 : (2 * g + q + 1) * 128] = value.astype(BF)

    lanes = Z1 * C1
    size = 8 * X1
    quarter = size // 4
    r = iota((size, size), 0)
    ab = r // quarter
    y = (r % quarter) // X2
    select = one_hot((2 * y + ab % 2) * X1 + 2 * (r % X2) + ab // 2 == iota((size, size), 1))
    for n in range(Y1 // 8):
        cells = mm(select, feat_ref[n * size : n * size + size, :]).astype(BF)
        for q in range(4):
            d_ref[q, n * quarter : n * quarter + quarter, :] = cells[q * quarter : (q + 1) * quarter]
    mask = mask_rows(tab2_ref[:, 128:256], 0, Y2, X2, lambda x: x, 2)
    for z in range(Z2):
        left = jnp.concatenate([d_ref[q, :, z * 128 : z * 128 + 128] for q in range(4)], axis=1)
        down_ref[:, :, z * CP : z * CP + CP] = finish(mm(left, wd_ref[...]), bd_ref[...], mask, Y2)

    r = iota((lanes, lanes), 0)
    order = one_hot((r % Z1) * C1 + r // Z1 == iota((lanes, lanes), 1))
    one_ref[...] = mm(order, feat_ref[...], NT).astype(BF)


def level_two_kernel(
    win_ref, zl_ref, zr_ref, xl_ref, xr_ref, ta_ref, tb_ref, ba_ref, bb_ref, tab_ref, out_ref, a0, a1, a2, i0, i1, i2
):
    for chunk in range(8):
        ref, lane = (zl_ref, chunk) if chunk < 2 else ((win_ref, chunk - 2) if chunk < 6 else (zr_ref, chunk - 6))
        inner = ref[:, :, lane * 128 : lane * 128 + 128]
        cut = slice(chunk * 128, chunk * 128 + 128)
        left, right = xl_ref[:, :, cut], xr_ref[:, :, cut]
        for i, copy in enumerate((a0, a1, a2)):
            spare = jnp.zeros((ROWS2, PITCH2 - X2 - 4 + i, 128), BF)
            line = [inner, right, spare] if i == 2 else [left[:, i:], inner, right, spare]
            copy[:, :, cut] = jnp.concatenate(line, axis=1)
    rows = Y2 + 2
    mask = mask_rows(tab_ref[...], -1, rows, PITCH2, lambda x: x - 1, 2)
    for g in range(3):
        acc = conv_group([[(ref, 256 * g, 512)] for ref in (a0, a1, a2)], ta_ref, 0, rows, 256, 512)
        for q in range(2):
            chunk = 2 * g + q
            which = 0 if chunk == 0 else (2 if chunk == 5 else 1)
            value = finish(acc[:, q * 128 : q * 128 + 128], ba_ref[...], mask[:, which * 128 : which * 128 + 128], rows)
            cut = slice(chunk * 128, chunk * 128 + 128)
            for s, copy in enumerate((i0, i1, i2)):
                copy[:, :, cut] = value[:, s : s + X2]
    mask = mask_rows(tab_ref[:, 128:256], 0, Y2, X2, lambda x: x, 2)
    feat = []
    for g in range(2):
        acc = conv_group([[(ref, 256 * g, 512)] for ref in (i0, i1, i2)], tb_ref, 0, Y2, 256, 512)
        for q in range(2):
            feat.append((jnp.maximum(acc[:, q * 128 : q * 128 + 128] + bb_ref[...], 0.0) * mask).astype(BF))
    shape = (C2 * Z2, Z2 * CP)
    r = iota(shape, 0)
    order = one_hot((r % Z2) * CP + r // Z2 == iota(shape, 1))
    out_ref[...] = mm(order, jnp.concatenate(feat, axis=1), NT).astype(BF)


def swap_pairs(count, cores, cores_first):
    def place(y, i):
        return y * count + i if cores_first else i * cores + y

    pairs = []
    for y in range(cores):
        for i in range(count):
            other = i + 1 if i % 2 else i - 1
            target = place(y, other) if 0 <= other < count else place(y ^ 1, i)
            pairs.append((place(y, i), target))
    return pairs


def shift_along(low_edge, high_edge, axis):
    count = lax.axis_size(axis)
    index = lax.axis_index(axis)
    even = index % 2 == 0
    one = lax.ppermute(jnp.where(even, high_edge, low_edge), axis, [(i, i ^ 1) for i in range(count)])
    two = one
    if count > 2 and axis == "gy":
        pairs = [(0, count - 1), (count - 1, 0)] + [(i, i - 1 + i % 2 * 2) for i in range(1, count - 1)]
        two = lax.ppermute(jnp.where(even, low_edge, high_edge), axis, pairs)
    elif count > 2:
        axes = ("gx", "gy") if axis == "gx" else ("gy", "gz")
        pairs = swap_pairs(count, lax.axis_size("gy"), axis == "gz")
        two = lax.ppermute(jnp.where(even, low_edge, high_edge), axes, pairs)
    below = jnp.where(index > 0, jnp.where(even, two, one), jnp.zeros_like(one))
    above = jnp.where(index < count - 1, jnp.where(even, one, two), jnp.zeros_like(one))
    return below, above


def params():
    return pltpu.CompilerParams(vmem_limit_bytes=VMEM_BYTES)


def cost(seconds):
    return pl.CostEstimate(flops=int(1e15 * seconds), bytes_accessed=0, transcendentals=0)


def shaped(*shape):
    return jax.ShapeDtypeStruct(shape, BF)


def pad_lanes(value):
    return jnp.pad(value, [(0, 0)] * (value.ndim - 1) + [(0, CP - value.shape[-1])])


def local(
    volume, tissue, w_down1, b_down1, w_conv1a, b_conv1a, w_conv1b, b_conv1b,
    w_down2, b_down2, w_conv2a, b_conv2a, w_conv2b, b_conv2b,
):
    depth = volume.shape[1]
    kz = C0 * depth
    lanes1 = Z1 * C1
    half = depth // 2
    own, tab1, tab2 = pl.pallas_call(
        down1_kernel,
        in_specs=[pl.BlockSpec(memory_space=pltpu.HBM)] + [pl.BlockSpec(memory_space=pltpu.VMEM)] * 3,
        out_shape=[shaped(Y1, X1, lanes1), shaped(128, 384), shaped(128, 384)],
        scratch_shapes=[
            pltpu.VMEM((2 * kz, lanes1 // 2), BF),
            pltpu.VMEM((C0, 2, half, volume.shape[2]), BF),
            pltpu.VMEM((2, Y1 * X1, 2 * kz), BF),
            pltpu.SemaphoreType.DMA((volume.shape[2] // 256,)),
        ],
        compiler_params=pltpu.CompilerParams(vmem_limit_bytes=62 * 1024 * 1024),
        cost_estimate=cost(4e-6),
    )(volume.reshape(C0, 2, half, -1), jnp.swapaxes(w_down1, 1, 2), b_down1[None], tissue.transpose(1, 2, 0))

    t1a = banded(w_conv1a, 4, C1)
    t1b = banded(w_conv1b, 4, C1)
    t2a = banded(w_conv2a, 2, CP)
    t2b = banded(w_conv2b, 2, CP)
    bias1a = b_conv1a[None]

    y_below, y_above = shift_along(own[:HALO], own[Y1 - HALO :], "gy")
    win = jnp.concatenate([y_below, own, y_above], axis=0)
    z_below, z_above = shift_along(win[:, :, :128], win[:, :, lanes1 - 128 :], "gz")
    rows = Y1 + 2
    left, right, g2 = pl.pallas_call(
        middle_kernel,
        out_shape=[shaped(ROWS1, X1, lanes1), shaped(ROWS1, X1, lanes1), shaped(rows, X1, 256)],
        compiler_params=params(),
        cost_estimate=cost(3e-6),
    )(win, t1a, bias1a, tab1)

    low = jnp.concatenate([z_below[:, :2], win[:, :2], z_above[:, :2]], axis=2)
    high = jnp.concatenate([z_below[:, X1 - 2 :], win[:, X1 - 2 :], z_above[:, X1 - 2 :]], axis=2)
    x_below, x_above = shift_along(low, high, "gx")
    g1, g3 = pl.pallas_call(
        outer_kernel,
        out_shape=[shaped(rows, X1, 256), shaped(rows, X1, 128)],
        scratch_shapes=[pltpu.VMEM((ROWS1, X1, 128), BF)] * 4,
        compiler_params=params(),
        cost_estimate=cost(4e-6),
    )(win, left, right, z_below, z_above, t1a, bias1a, tab1)

    one, down = pl.pallas_call(
        level_one_kernel,
        out_shape=[shaped(lanes1, Y1 * X1), shaped(Y2, X2, Z2 * CP)],
        scratch_shapes=[pltpu.VMEM((ROWS1, EDGE, (Z1 + 4) * C1), BF)] * 3
        + [pltpu.VMEM((rows, X1, (Z1 + 2) * C1), BF)] * 3
        + [pltpu.VMEM((Y1 * X1, lanes1), BF), pltpu.VMEM((4, Y2 * X2, lanes1), BF)],
        compiler_params=params(),
        cost_estimate=cost(6e-6),
    )(
        x_below, low, high, x_above, g1, g2, g3, t1a, t1b, bias1a, b_conv1b[None],
        pad_lanes(jnp.swapaxes(w_down2, 1, 2).reshape(8 * C1, C2)), pad_lanes(b_down2[None]), tab1, tab2,
    )

    y_below, y_above = shift_along(down[:HALO], down[Y2 - HALO :], "gy")
    win = jnp.concatenate([y_below, down, y_above], axis=0)
    z_below, z_above = shift_along(win[:, :, : 2 * CP], win[:, :, 2 * CP :], "gz")
    low = jnp.concatenate([z_below[:, :2], win[:, :2], z_above[:, :2]], axis=2)
    high = jnp.concatenate([z_below[:, X2 - 2 :], win[:, X2 - 2 :], z_above[:, X2 - 2 :]], axis=2)
    x_below, x_above = shift_along(low, high, "gx")
    two = pl.pallas_call(
        level_two_kernel,
        out_shape=shaped(C2 * Z2, Y2 * X2),
        scratch_shapes=[pltpu.VMEM((ROWS2, PITCH2, (Z2 + 4) * CP), BF)] * 3
        + [pltpu.VMEM((Y2 + 2, X2, (Z2 + 2) * CP), BF)] * 3,
        compiler_params=params(),
        cost_estimate=cost(5e-6),
    )(win, z_below, z_above, x_below, x_above, t2a, t2b, pad_lanes(b_conv2a[None]), pad_lanes(b_conv2b[None]), tab2)
    return one.reshape(C1, Z1, Y1 * X1), two.reshape(C2, Z2, Y2 * X2)


def solution(mesh):
    block = P(None, "gz", ("gx", "gy"))
    return jax.shard_map(
        local,
        mesh=mesh,
        in_specs=(block,) + (P(),) * 13,
        out_specs=(block, block),
        check_vma=False,
    )
```

```python
import jax
import jax.numpy as jnp
from jax import lax
from jax.experimental import pallas as pl
from jax.experimental.pallas import tpu as pltpu
from jax.sharding import PartitionSpec as P

CX = 64
CY = 32
X1 = CX // 2
Y1 = CY // 2
X2 = X1 // 2
Y2 = Y1 // 2
Z1 = 8
Z2 = 4
C0 = 48
C1 = 64
C2 = 96
CP = 128
HALO = 2
XB = 10
XB_PITCH = 16
YB = 6
ROWS1 = Y1 + 2 * HALO
ROWS2 = Y2 + 2 * HALO
EDGE = 16
PITCH2 = 32
BF = jnp.bfloat16
F32 = jnp.float32
NN = (((1,), (0,)), ((), ()))
NT = (((1,), (1,)), ((), ()))
VMEM_BYTES = 40 * 1024 * 1024


def mm(a, b, dims=NN):
    return lax.dot_general(a, b, dims, preferred_element_type=F32)


def iota(shape, dim):
    return lax.broadcasted_iota(jnp.int32, shape, dim)


def one_hot(flag):
    return jnp.where(flag, 1.0, 0.0).astype(BF)


def one_hot_rows(key, lanes):
    lane = iota(key.shape, 1)
    return jnp.concatenate([one_hot(key == lane + q) for q in range(0, lanes, 128)], axis=1)


def mask_rows(tab, y_start, rows, pitch, x_of, cell):
    bits = cell.bit_length() - 1
    shape = (rows, pitch, 128)
    y_block = (iota(shape, 0) + (y_start + cell)) >> bits
    x_block = jnp.minimum((x_of(iota(shape, 1)) + cell) >> bits, XB - 1)
    hit = one_hot(y_block * XB_PITCH + x_block == iota(shape, 2)).reshape(rows * pitch, 128)
    return mm(hit, tab)


def tissue_tables(t_ref):
    n_y, n_z, n_x = t_ref.shape
    here = lax.axis_index("gz")
    layers = []
    for k in (-1, 0, 1):
        z = here + k
        inside = jnp.where((z >= 0) & (z < n_z), 1.0, 0.0)
        layers.append(t_ref[:, jnp.clip(z, 0, n_z - 1), :].astype(F32) * inside)
    block = iota((128, n_y), 0)
    bits = XB_PITCH.bit_length() - 1
    hot_y = one_hot(lax.axis_index("gy") * 4 - 1 + (block >> bits) == iota((128, n_y), 1))
    block = iota((128, 3 * n_x), 0)
    layer = sum((iota((128, 3 * n_x), 1) >= k * n_x).astype(jnp.int32) for k in (1, 2))
    hot_x = lax.axis_index("gx") * 8 - 1 + (block & (XB_PITCH - 1)) == iota((128, 3 * n_x), 1) - layer * n_x
    rows = jnp.where(hot_x, mm(hot_y, jnp.concatenate(layers, axis=1).astype(BF)), 0.0).astype(BF)
    shape = (3 * n_x, 384)
    layer = sum((iota(shape, 0) >= k * n_x).astype(jnp.int32) for k in (1, 2))
    lane = iota(shape, 1)

    def spread(first, last):
        place = jnp.where(lane < first, 0, jnp.where(lane < last, 1, 2))
        return mm(rows, one_hot(layer == place)).astype(BF)

    return spread(64, 320), spread(128, 256)


def down1_kernel(v_ref, w_ref, b_ref, t_ref, out_ref, tab_ref, tab2_ref, wd_ref, field_ref, cells_ref, sems):
    half = v_ref.shape[2]
    kz = C0 * half
    lanes = Z1 // 2 * C1
    copies = []
    for n in range(sems.shape[0]):
        cut = (slice(None), slice(None), slice(None), slice(n * 256, n * 256 + 256))
        copies.append(pltpu.make_async_copy(v_ref.at[cut], field_ref.at[cut], sems.at[n]))
        copies[-1].start()

    tab, tab2 = tissue_tables(t_ref)
    tab_ref[...] = tab
    tab2_ref[...] = tab2
    r = iota((kz, 2 * C0), 0)
    l = iota((kz, 2 * C0), 1)
    odd = l >= C0
    spread = one_hot(((r >> 3) == jnp.where(odd, l - C0, l)) & ((r & 1) == odd.astype(jnp.int32)))
    keep = (iota((kz, lanes), 0) & 7) >> 1 == iota((kz, lanes), 1) >> 6
    for ab in range(4):
        pair = w_ref[2 * ab : 2 * ab + 2].reshape(2 * C0, C1)
        wide = jnp.concatenate([pair] * (Z1 // 2), axis=1)
        wd_ref[ab * kz : (ab + 1) * kz, :] = jnp.where(keep, mm(spread, wide), 0.0).astype(BF)

    r = iota((4 * CX, 128), 0)
    select = one_hot_rows(((r & 32) << 2) | (r & 64) | ((r & 31) << 1) | (r >> 7), 4 * CX)
    for n, copy in enumerate(copies):
        copy.wait()
        for h in range(2):
            v = field_ref[:, h, :, n * 256 : n * 256 + 256].reshape(kz, 256)
            cells = mm(select, v, NT).astype(BF)
            for ab in range(4):
                cells_ref[h, n * 64 : n * 64 + 64, ab * kz : (ab + 1) * kz] = cells[64 * ab : 64 * ab + 64]
    mask = mask_rows(tab[:, 128:256], 0, Y1, X1, lambda x: x, 4)
    bias = twice(b_ref)
    for h in range(2):
        acc = mm(cells_ref[h], wd_ref[...])
        for q in range(2):
            value = finish(acc[:, q * 128 : q * 128 + 128], bias, mask, Y1)
            out_ref[:, :, (2 * h + q) * 128 : (2 * h + q + 1) * 128] = value


def twice(b_ref):
    return jnp.concatenate([b_ref[...]] * 2, axis=1)


def fill_banded(w_ref, t_ref, group, pad):
    chan = w_ref.shape[1]
    t_ref[...] = jnp.zeros_like(t_ref)
    for j in range(3):
        for i in range(3):
            for zo in range(group):
                for k in range(3):
                    lane = i * (group + 2) * pad + (zo + k) * pad
                    t_ref[j, zo * pad : zo * pad + chan, lane : lane + chan] = w_ref[9 * i + 3 * j + k]


def banded_shape(group, pad):
    return shaped(3, group * pad, 3 * (group + 2) * pad)


def banded(weights, group, pad):
    def kernel(w_ref, t_ref):
        fill_banded(w_ref, t_ref, group, pad)

    return pl.pallas_call(
        kernel, out_shape=banded_shape(group, pad), compiler_params=params(), cost_estimate=cost(1e-6)
    )(weights)


def conv_group(taps, t_ref, y_first, rows, group_out, group_full):
    pitch = taps[0][0][0].shape[1]
    width = sum(piece[2] for piece in taps[0])
    total = None
    for j in range(3):
        parts = [ref[y_first + j : y_first + j + rows, :, lane : lane + n] for tap in taps for ref, lane, n in tap]
        left = jnp.concatenate([p.reshape(rows * pitch, p.shape[2]) for p in parts], axis=1)
        if width == group_full:
            right = t_ref[j, 0:group_out, :]
        else:
            right = jnp.concatenate([t_ref[j, 0:group_out, i * group_full : i * group_full + width] for i in range(3)], axis=1)
        term = mm(left, right, NT)
        total = term if total is None else total + term
    return total


def finish(acc, bias, mask, rows):
    value = jnp.maximum(acc + bias, 0.0) * mask
    return value.astype(BF).reshape(rows, value.shape[0] // rows, value.shape[1])


def fill_sides(left, right, lane, inner):
    cut = slice(lane, lane + inner.shape[2])
    none = jnp.zeros_like(inner[:, :1])
    left[:, :, cut] = jnp.concatenate([none, inner[:, :-1]], axis=1)
    right[:, :, cut] = jnp.concatenate([inner[:, 1:], none], axis=1)


def middle_kernel(win_ref, t_ref, b_ref, tab_ref, w_ref, left_ref, right_ref, out_ref, next_ref):
    fill_banded(w_ref, next_ref, 4, C1)
    for q in range(4):
        fill_sides(left_ref, right_ref, q * 128, win_ref[:, :, q * 128 : q * 128 + 128])
    rows = Y1 + 2
    mask = mask_rows(tab_ref[:, 128:256], -1, rows, X1, lambda x: x, 4)
    acc = conv_group([[(ref, 128, 384)] for ref in (left_ref, win_ref, right_ref)], t_ref, 0, rows, 256, 384)
    for q in range(2):
        cut = slice(q * 128, q * 128 + 128)
        out_ref[:, :, cut] = finish(acc[:, cut], twice(b_ref), mask, rows)


def outer_kernel(win_ref, left_ref, right_ref, zl_ref, zr_ref, t_ref, b_ref, tab_ref, low_ref, high_ref, ll, lr, hl, hr):
    fill_sides(ll, lr, 0, zl_ref[...])
    fill_sides(hl, hr, 0, zr_ref[...])
    own = (left_ref, win_ref, right_ref)
    rows = Y1 + 2
    mask = mask_rows(tab_ref[...], -1, rows, X1, lambda x: x, 4)
    taps = [[(z, 0, 128), (ref, 0, 256)] for z, ref in zip((ll, zl_ref, lr), own)]
    acc = conv_group(taps, t_ref, 0, rows, 256, 384)
    for q in range(2):
        cut = slice(q * 128, q * 128 + 128)
        low_ref[:, :, cut] = finish(acc[:, cut], twice(b_ref), mask[:, cut], rows)
    taps = [[(ref, 384, 128), (z, 0, 128)] for z, ref in zip((hl, zr_ref, hr), own)]
    acc = conv_group(taps, t_ref, 0, rows, 128, 384)
    high_ref[...] = finish(acc, twice(b_ref), mask[:, 256:384], rows)


def fill_edges(copies, pieces):
    rows, pitch, lanes = copies[0].shape
    for lane in range(0, lanes, 128):
        line = [p[:, :, lane : lane + 128] for p in pieces]
        used = sum(p.shape[1] for p in line)
        for i, copy in enumerate(copies):
            moved = [line[0][:, i:]] + line[1:] if i < line[0].shape[1] else line[1:]
            spare = jnp.zeros((rows, pitch - used + i, 128), BF)
            copy[:, :, lane : lane + 128] = jnp.concatenate(moved + [spare], axis=1)


def level_one_kernel(
    xl_ref, low_ref, high_ref, xr_ref, g1_ref, g2_ref, g3_ref, ta_ref, tb_ref, ba_ref, bb_ref, wd_ref, bd_ref, tab_ref, tab2_ref,
    one_ref, down_ref, e0, e1, e2, i0, i1, i2, feat_ref, d_ref,
):
    fill_edges((e0, e1, e2), (xl_ref, low_ref, high_ref, xr_ref))
    rows = Y1 + 2
    mask = mask_rows(tab_ref[...], -1, rows, EDGE, lambda r: jnp.where(r < 4, r - 1, r + X1 - 5), 4)
    for g, (lane, width, out) in enumerate(((0, 384, 256), (256, 384, 256), (512, 256, 128))):
        acc = conv_group([[(e, lane, width)] for e in (e0, e1, e2)], ta_ref, 0, rows, out, 384)
        for q in range(out // 128):
            chunk = 2 * g + q
            which = 0 if chunk == 0 else (2 if chunk == 4 else 1)
            edge = finish(acc[:, q * 128 : q * 128 + 128], twice(ba_ref), mask[:, which * 128 : which * 128 + 128], rows)
            inner = (g1_ref, g2_ref, g3_ref)[g][:, :, q * 128 : q * 128 + 128][:, 1:-1]
            cut = slice(chunk * 128, chunk * 128 + 128)
            i0[:, :, cut] = jnp.concatenate([edge[:, 0:2], inner], axis=1)
            i1[:, :, cut] = jnp.concatenate([edge[:, 1:2], inner, edge[:, 4:5]], axis=1)
            i2[:, :, cut] = jnp.concatenate([inner, edge[:, 4:6]], axis=1)

    mask = mask_rows(tab_ref[:, 128:256], 0, Y1, X1, lambda x: x, 4)
    for g in range(2):
        acc = conv_group([[(ref, 256 * g, 384)] for ref in (i0, i1, i2)], tb_ref, 0, Y1, 256, 384)
        for q in range(2):
            value = jnp.maximum(acc[:, q * 128 : q * 128 + 128] + twice(bb_ref), 0.0) * mask
            feat_ref[:, (2 * g + q) * 128 : (2 * g + q + 1) * 128] = value.astype(BF)

    lanes = Z1 * C1
    size = 8 * X1
    quarter = size // 4
    r = iota((size, 128), 0)
    select = one_hot_rows(((r & 48) << 2) | ((r & 64) >> 1) | ((r & 15) << 1) | (r >> 7), size)
    for n in range(Y1 // 8):
        cells = mm(select, feat_ref[n * size : n * size + size, :]).astype(BF)
        for q in range(4):
            d_ref[q, n * quarter : n * quarter + quarter, :] = cells[q * quarter : (q + 1) * quarter]
    mask = mask_rows(tab2_ref[:, 128:256], 0, Y2, X2, lambda x: x, 2)
    for z in range(Z2):
        left = jnp.concatenate([d_ref[q, :, z * 128 : z * 128 + 128] for q in range(4)], axis=1)
        down_ref[:, :, z * CP : z * CP + CP] = finish(mm(left, wd_ref[...]), bd_ref[...], mask, Y2)

    r = iota((lanes, 128), 0)
    order = one_hot_rows(((r & 7) << 6) | (r >> 3), lanes)
    one_ref[...] = mm(order, feat_ref[...], NT).astype(BF)


def level_two_kernel(
    win_ref, zl_ref, zr_ref, xl_ref, xr_ref, ta_ref, tb_ref, ba_ref, bb_ref, tab_ref, out_ref, a0, a1, a2, i0, i1, i2
):
    for chunk in range(8):
        ref, lane = (zl_ref, chunk) if chunk < 2 else ((win_ref, chunk - 2) if chunk < 6 else (zr_ref, chunk - 6))
        inner = ref[:, :, lane * 128 : lane * 128 + 128]
        cut = slice(chunk * 128, chunk * 128 + 128)
        left, right = xl_ref[:, :, cut], xr_ref[:, :, cut]
        for i, copy in enumerate((a0, a1, a2)):
            spare = jnp.zeros((ROWS2, PITCH2 - X2 - 4 + i, 128), BF)
            line = [inner, right, spare] if i == 2 else [left[:, i:], inner, right, spare]
            copy[:, :, cut] = jnp.concatenate(line, axis=1)
    rows = Y2 + 2
    mask = mask_rows(tab_ref[...], -1, rows, PITCH2, lambda x: x - 1, 2)
    for g in range(3):
        acc = conv_group([[(ref, 256 * g, 512)] for ref in (a0, a1, a2)], ta_ref, 0, rows, 256, 512)
        for q in range(2):
            chunk = 2 * g + q
            which = 0 if chunk == 0 else (2 if chunk == 5 else 1)
            value = finish(acc[:, q * 128 : q * 128 + 128], ba_ref[...], mask[:, which * 128 : which * 128 + 128], rows)
            cut = slice(chunk * 128, chunk * 128 + 128)
            for s, copy in enumerate((i0, i1, i2)):
                copy[:, :, cut] = value[:, s : s + X2]
    mask = mask_rows(tab_ref[:, 128:256], 0, Y2, X2, lambda x: x, 2)
    feat = []
    for g in range(2):
        acc = conv_group([[(ref, 256 * g, 512)] for ref in (i0, i1, i2)], tb_ref, 0, Y2, 256, 512)
        for q in range(2):
            feat.append((jnp.maximum(acc[:, q * 128 : q * 128 + 128] + bb_ref[...], 0.0) * mask).astype(BF))
    r = iota((C2 * Z2, 128), 0)
    order = one_hot_rows(((r & 3) << 7) | (r >> 2), Z2 * CP)
    out_ref[...] = mm(order, jnp.concatenate(feat, axis=1), NT).astype(BF)


def swap_pairs(count, cores, cores_first):
    def place(y, i):
        return y * count + i if cores_first else i * cores + y

    pairs = []
    for y in range(cores):
        for i in range(count):
            other = i + 1 if i % 2 else i - 1
            target = place(y, other) if 0 <= other < count else place(y ^ 1, i)
            pairs.append((place(y, i), target))
    return pairs


def shift_along(low_edge, high_edge, axis):
    count = lax.axis_size(axis)
    index = lax.axis_index(axis)
    even = index % 2 == 0
    one = lax.ppermute(jnp.where(even, high_edge, low_edge), axis, [(i, i ^ 1) for i in range(count)])
    two = one
    if count > 2 and axis == "gy":
        pairs = [(0, count - 1), (count - 1, 0)] + [(i, i - 1 + i % 2 * 2) for i in range(1, count - 1)]
        two = lax.ppermute(jnp.where(even, low_edge, high_edge), axis, pairs)
    elif count > 2:
        axes = ("gx", "gy") if axis == "gx" else ("gy", "gz")
        pairs = swap_pairs(count, lax.axis_size("gy"), axis == "gz")
        two = lax.ppermute(jnp.where(even, low_edge, high_edge), axes, pairs)
    below = jnp.where(index > 0, jnp.where(even, two, one), jnp.zeros_like(one))
    above = jnp.where(index < count - 1, jnp.where(even, one, two), jnp.zeros_like(one))
    return below, above


def params():
    return pltpu.CompilerParams(vmem_limit_bytes=VMEM_BYTES)


def cost(seconds):
    return pl.CostEstimate(flops=int(1e15 * seconds), bytes_accessed=0, transcendentals=0)


def shaped(*shape):
    return jax.ShapeDtypeStruct(shape, BF)


def pad_lanes(value):
    return jnp.pad(value, [(0, 0)] * (value.ndim - 1) + [(0, CP - value.shape[-1])])


def local(
    volume, tissue, w_down1, b_down1, w_conv1a, b_conv1a, w_conv1b, b_conv1b,
    w_down2, b_down2, w_conv2a, b_conv2a, w_conv2b, b_conv2b,
):
    depth = volume.shape[1]
    kz = C0 * depth
    lanes1 = Z1 * C1
    half = depth // 2
    own, tab1, tab2 = pl.pallas_call(
        down1_kernel,
        in_specs=[pl.BlockSpec(memory_space=pltpu.HBM)] + [pl.BlockSpec(memory_space=pltpu.VMEM)] * 3,
        out_shape=[shaped(Y1, X1, lanes1), shaped(128, 384), shaped(128, 384)],
        scratch_shapes=[
            pltpu.VMEM((2 * kz, lanes1 // 2), BF),
            pltpu.VMEM((C0, 2, half, volume.shape[2]), BF),
            pltpu.VMEM((2, Y1 * X1, 2 * kz), BF),
            pltpu.SemaphoreType.DMA((volume.shape[2] // 256,)),
        ],
        compiler_params=pltpu.CompilerParams(vmem_limit_bytes=123 * 512 * 1024),
        cost_estimate=cost(4e-6),
    )(volume.reshape(C0, 2, half, -1), jnp.swapaxes(w_down1, 1, 2), b_down1[None], tissue.transpose(1, 2, 0))

    t1a = banded(w_conv1a, 4, C1)
    t2a = banded(w_conv2a, 2, CP)
    t2b = banded(w_conv2b, 2, CP)
    bias1a = b_conv1a[None]

    y_below, y_above = shift_along(own[:HALO], own[Y1 - HALO :], "gy")
    win = jnp.concatenate([y_below, own, y_above], axis=0)
    z_below, z_above = shift_along(win[:, :, :128], win[:, :, lanes1 - 128 :], "gz")
    rows = Y1 + 2
    left, right, g2, t1b = pl.pallas_call(
        middle_kernel,
        out_shape=[shaped(ROWS1, X1, lanes1), shaped(ROWS1, X1, lanes1), shaped(rows, X1, 256), banded_shape(4, C1)],
        compiler_params=params(),
        cost_estimate=cost(3e-6),
    )(win, t1a, bias1a, tab1, w_conv1b)

    low = jnp.concatenate([z_below[:, :2], win[:, :2], z_above[:, :2]], axis=2)
    high = jnp.concatenate([z_below[:, X1 - 2 :], win[:, X1 - 2 :], z_above[:, X1 - 2 :]], axis=2)
    x_below, x_above = shift_along(low, high, "gx")
    g1, g3 = pl.pallas_call(
        outer_kernel,
        out_shape=[shaped(rows, X1, 256), shaped(rows, X1, 128)],
        scratch_shapes=[pltpu.VMEM((ROWS1, X1, 128), BF)] * 4,
        compiler_params=params(),
        cost_estimate=cost(4e-6),
    )(win, left, right, z_below, z_above, t1a, bias1a, tab1)

    one, down = pl.pallas_call(
        level_one_kernel,
        out_shape=[shaped(lanes1, Y1 * X1), shaped(Y2, X2, Z2 * CP)],
        scratch_shapes=[pltpu.VMEM((ROWS1, EDGE, (Z1 + 4) * C1), BF)] * 3
        + [pltpu.VMEM((rows, X1, (Z1 + 2) * C1), BF)] * 3
        + [pltpu.VMEM((Y1 * X1, lanes1), BF), pltpu.VMEM((4, Y2 * X2, lanes1), BF)],
        compiler_params=params(),
        cost_estimate=cost(6e-6),
    )(
        x_below, low, high, x_above, g1, g2, g3, t1a, t1b, bias1a, b_conv1b[None],
        pad_lanes(jnp.swapaxes(w_down2, 1, 2).reshape(8 * C1, C2)), pad_lanes(b_down2[None]), tab1, tab2,
    )

    y_below, y_above = shift_along(down[:HALO], down[Y2 - HALO :], "gy")
    win = jnp.concatenate([y_below, down, y_above], axis=0)
    z_below, z_above = shift_along(win[:, :, : 2 * CP], win[:, :, 2 * CP :], "gz")
    low = jnp.concatenate([z_below[:, :2], win[:, :2], z_above[:, :2]], axis=2)
    high = jnp.concatenate([z_below[:, X2 - 2 :], win[:, X2 - 2 :], z_above[:, X2 - 2 :]], axis=2)
    x_below, x_above = shift_along(low, high, "gx")
    two = pl.pallas_call(
        level_two_kernel,
        out_shape=shaped(C2 * Z2, Y2 * X2),
        scratch_shapes=[pltpu.VMEM((ROWS2, PITCH2, (Z2 + 4) * CP), BF)] * 3
        + [pltpu.VMEM((Y2 + 2, X2, (Z2 + 2) * CP), BF)] * 3,
        compiler_params=params(),
        cost_estimate=cost(5e-6),
    )(win, z_below, z_above, x_below, x_above, t2a, t2b, pad_lanes(b_conv2a[None]), pad_lanes(b_conv2b[None]), tab2)
    return one.reshape(C1, Z1, Y1 * X1), two.reshape(C2, Z2, Y2 * X2)


def solution(mesh):
    block = P(None, "gz", ("gx", "gy"))
    return jax.shard_map(
        local,
        mesh=mesh,
        in_specs=(block,) + (P(),) * 13,
        out_specs=(block, block),
        check_vma=False,
    )
```

```python
import jax
import jax.numpy as jnp
from jax import lax
from jax.experimental import pallas as pl
from jax.experimental.pallas import tpu as pltpu
from jax.sharding import PartitionSpec as P

CX = 64
CY = 32
X1 = CX // 2
Y1 = CY // 2
X2 = X1 // 2
Y2 = Y1 // 2
Z1 = 8
Z2 = 4
C0 = 48
C1 = 64
C2 = 96
CP = 128
HALO = 2
XB = 10
XB_PITCH = 16
YB = 6
ROWS1 = Y1 + 2 * HALO
ROWS2 = Y2 + 2 * HALO
EDGE = 16
PITCH2 = 32
BF = jnp.bfloat16
F32 = jnp.float32
NN = (((1,), (0,)), ((), ()))
NT = (((1,), (1,)), ((), ()))
VMEM_BYTES = 40 * 1024 * 1024
DOWN1_VMEM_BYTES = 52 * 1024 * 1024


def mm(a, b, dims=NN):
    return lax.dot_general(a, b, dims, preferred_element_type=F32)


def iota(shape, dim):
    return lax.broadcasted_iota(jnp.int32, shape, dim)


def one_hot(flag):
    return jnp.where(flag, 1.0, 0.0).astype(BF)


def one_hot_rows(key, lanes):
    lane = iota(key.shape, 1)
    return jnp.concatenate([one_hot(key == lane + q) for q in range(0, lanes, 128)], axis=1)


def mask_rows(tab, y_start, rows, pitch, x_of, cell):
    bits = cell.bit_length() - 1
    shape = (rows, pitch, 128)
    y_block = (iota(shape, 0) + (y_start + cell)) >> bits
    x_block = jnp.minimum((x_of(iota(shape, 1)) + cell) >> bits, XB - 1)
    hit = one_hot(y_block * XB_PITCH + x_block == iota(shape, 2)).reshape(rows * pitch, 128)
    return mm(hit, tab)


def tissue_tables(t_ref):
    n_y, n_z, n_x = t_ref.shape
    here = lax.axis_index("gz")
    layers = []
    for k in (-1, 0, 1):
        z = here + k
        inside = jnp.where((z >= 0) & (z < n_z), 1.0, 0.0)
        layers.append(t_ref[:, jnp.clip(z, 0, n_z - 1), :].astype(F32) * inside)
    block = iota((128, n_y), 0)
    bits = XB_PITCH.bit_length() - 1
    hot_y = one_hot(lax.axis_index("gy") * 4 - 1 + (block >> bits) == iota((128, n_y), 1))
    block = iota((128, 3 * n_x), 0)
    layer = sum((iota((128, 3 * n_x), 1) >= k * n_x).astype(jnp.int32) for k in (1, 2))
    hot_x = lax.axis_index("gx") * 8 - 1 + (block & (XB_PITCH - 1)) == iota((128, 3 * n_x), 1) - layer * n_x
    rows = jnp.where(hot_x, mm(hot_y, jnp.concatenate(layers, axis=1).astype(BF)), 0.0).astype(BF)
    shape = (3 * n_x, 384)
    layer = sum((iota(shape, 0) >= k * n_x).astype(jnp.int32) for k in (1, 2))
    lane = iota(shape, 1)

    def spread(first, last):
        place = jnp.where(lane < first, 0, jnp.where(lane < last, 1, 2))
        return mm(rows, one_hot(layer == place)).astype(BF)

    return spread(64, 320), spread(128, 256)


def down1_kernel(v_ref, w_ref, b_ref, t_ref, out_ref, tab_ref, tab2_ref, wd_ref, field_ref, cells_ref, sems):
    half = v_ref.shape[2]
    kz = C0 * half
    lanes = Z1 // 2 * C1
    copies = []
    for n in range(sems.shape[0]):
        cut = slice(n * 16, n * 16 + 16)
        copies.append(pltpu.make_async_copy(v_ref.at[cut], field_ref.at[cut], sems.at[n]))
        copies[-1].start()

    tab, tab2 = tissue_tables(t_ref)
    tab_ref[...] = tab
    tab2_ref[...] = tab2
    r = iota((kz, 2 * C0), 0)
    l = iota((kz, 2 * C0), 1)
    odd = l >= C0
    spread = one_hot(((r >> 3) == jnp.where(odd, l - C0, l)) & ((r & 1) == odd.astype(jnp.int32)))
    keep = (iota((kz, lanes), 0) & 7) >> 1 == iota((kz, lanes), 1) >> 6
    for ab in range(4):
        pair = w_ref[2 * ab : 2 * ab + 2].reshape(2 * C0, C1)
        wide = jnp.concatenate([pair] * (Z1 // 2), axis=1)
        wd_ref[ab * kz : (ab + 1) * kz, :] = jnp.where(keep, mm(spread, wide), 0.0).astype(BF)

    r = iota((4 * CX, 128), 0)
    select = one_hot_rows(((r & 32) << 2) | (r & 64) | ((r & 31) << 1) | (r >> 7), 4 * CX)
    part = 16 * half
    for n, copy in enumerate(copies):
        copy.wait()
        for m in range(field_ref.shape[3] // 256):
            v = [field_ref[n * 16 : n * 16 + 16, h, :, m * 256 : m * 256 + 256].reshape(part, 256) for h in range(2)]
            cells = mm(select, jnp.concatenate(v, axis=0), NT).astype(BF)
            for ab in range(4):
                lane = ab * kz + n * part
                for h in range(2):
                    piece = cells[64 * ab : 64 * ab + 64, h * part : h * part + part]
                    cells_ref[h, m * 64 : m * 64 + 64, lane : lane + part] = piece
    mask = mask_rows(tab[:, 128:256], 0, Y1, X1, lambda x: x, 4)
    bias = twice(b_ref)
    for h in range(2):
        acc = mm(cells_ref[h], wd_ref[...])
        for q in range(2):
            value = finish(acc[:, q * 128 : q * 128 + 128], bias, mask, Y1)
            out_ref[:, :, (2 * h + q) * 128 : (2 * h + q + 1) * 128] = value


def twice(b_ref):
    return jnp.concatenate([b_ref[...]] * 2, axis=1)


def fill_banded(w_ref, t_ref, group, pad):
    chan = w_ref.shape[1]
    t_ref[...] = jnp.zeros_like(t_ref)
    for j in range(3):
        for i in range(3):
            for zo in range(group):
                for k in range(3):
                    lane = i * (group + 2) * pad + (zo + k) * pad
                    t_ref[j, zo * pad : zo * pad + chan, lane : lane + chan] = w_ref[9 * i + 3 * j + k]


def banded_shape(group, pad):
    return shaped(3, group * pad, 3 * (group + 2) * pad)


def banded(weights, group, pad):
    def kernel(w_ref, t_ref):
        fill_banded(w_ref, t_ref, group, pad)

    return pl.pallas_call(
        kernel, out_shape=banded_shape(group, pad), compiler_params=params(), cost_estimate=cost(1e-6)
    )(weights)


def conv_group(taps, t_ref, y_first, rows, group_out, group_full):
    pitch = taps[0][0][0].shape[1]
    width = sum(piece[2] for piece in taps[0])
    total = None
    for j in range(3):
        parts = [ref[y_first + j : y_first + j + rows, :, lane : lane + n] for tap in taps for ref, lane, n in tap]
        left = jnp.concatenate([p.reshape(rows * pitch, p.shape[2]) for p in parts], axis=1)
        if width == group_full:
            right = t_ref[j, 0:group_out, :]
        else:
            right = jnp.concatenate([t_ref[j, 0:group_out, i * group_full : i * group_full + width] for i in range(3)], axis=1)
        term = mm(left, right, NT)
        total = term if total is None else total + term
    return total


def finish(acc, bias, mask, rows):
    value = jnp.maximum(acc + bias, 0.0) * mask
    return value.astype(BF).reshape(rows, value.shape[0] // rows, value.shape[1])


def fill_sides(left, right, lane, inner):
    cut = slice(lane, lane + inner.shape[2])
    none = jnp.zeros_like(inner[:, :1])
    left[:, :, cut] = jnp.concatenate([none, inner[:, :-1]], axis=1)
    right[:, :, cut] = jnp.concatenate([inner[:, 1:], none], axis=1)


def middle_kernel(win_ref, t_ref, b_ref, tab_ref, w_ref, left_ref, right_ref, out_ref, next_ref):
    fill_banded(w_ref, next_ref, 4, C1)
    for q in range(4):
        fill_sides(left_ref, right_ref, q * 128, win_ref[:, :, q * 128 : q * 128 + 128])
    rows = Y1 + 2
    mask = mask_rows(tab_ref[:, 128:256], -1, rows, X1, lambda x: x, 4)
    acc = conv_group([[(ref, 128, 384)] for ref in (left_ref, win_ref, right_ref)], t_ref, 0, rows, 256, 384)
    for q in range(2):
        cut = slice(q * 128, q * 128 + 128)
        out_ref[:, :, cut] = finish(acc[:, cut], twice(b_ref), mask, rows)


def outer_kernel(win_ref, left_ref, right_ref, zl_ref, zr_ref, t_ref, b_ref, tab_ref, low_ref, high_ref, ll, lr, hl, hr):
    fill_sides(ll, lr, 0, zl_ref[...])
    fill_sides(hl, hr, 0, zr_ref[...])
    own = (left_ref, win_ref, right_ref)
    rows = Y1 + 2
    mask = mask_rows(tab_ref[...], -1, rows, X1, lambda x: x, 4)
    taps = [[(z, 0, 128), (ref, 0, 256)] for z, ref in zip((ll, zl_ref, lr), own)]
    acc = conv_group(taps, t_ref, 0, rows, 256, 384)
    for q in range(2):
        cut = slice(q * 128, q * 128 + 128)
        low_ref[:, :, cut] = finish(acc[:, cut], twice(b_ref), mask[:, cut], rows)
    taps = [[(ref, 384, 128), (z, 0, 128)] for z, ref in zip((hl, zr_ref, hr), own)]
    acc = conv_group(taps, t_ref, 0, rows, 128, 384)
    high_ref[...] = finish(acc, twice(b_ref), mask[:, 256:384], rows)


def fill_edges(copies, pieces):
    rows, pitch, lanes = copies[0].shape
    for lane in range(0, lanes, 128):
        line = [p[:, :, lane : lane + 128] for p in pieces]
        used = sum(p.shape[1] for p in line)
        for i, copy in enumerate(copies):
            moved = [line[0][:, i:]] + line[1:] if i < line[0].shape[1] else line[1:]
            spare = jnp.zeros((rows, pitch - used + i, 128), BF)
            copy[:, :, lane : lane + 128] = jnp.concatenate(moved + [spare], axis=1)


def level_one_kernel(
    xl_ref, low_ref, high_ref, xr_ref, g1_ref, g2_ref, g3_ref, ta_ref, tb_ref, ba_ref, bb_ref, wd_ref, bd_ref, tab_ref, tab2_ref,
    feat_ref, down_ref, e0, e1, e2, i0, i1, i2, d_ref,
):
    fill_edges((e0, e1, e2), (xl_ref, low_ref, high_ref, xr_ref))
    rows = Y1 + 2
    mask = mask_rows(tab_ref[...], -1, rows, EDGE, lambda r: jnp.where(r < 4, r - 1, r + X1 - 5), 4)
    for g, (lane, width, out) in enumerate(((0, 384, 256), (256, 384, 256), (512, 256, 128))):
        acc = conv_group([[(e, lane, width)] for e in (e0, e1, e2)], ta_ref, 0, rows, out, 384)
        for q in range(out // 128):
            chunk = 2 * g + q
            which = 0 if chunk == 0 else (2 if chunk == 4 else 1)
            edge = finish(acc[:, q * 128 : q * 128 + 128], twice(ba_ref), mask[:, which * 128 : which * 128 + 128], rows)
            inner = (g1_ref, g2_ref, g3_ref)[g][:, :, q * 128 : q * 128 + 128][:, 1:-1]
            cut = slice(chunk * 128, chunk * 128 + 128)
            i0[:, :, cut] = jnp.concatenate([edge[:, 0:2], inner], axis=1)
            i1[:, :, cut] = jnp.concatenate([edge[:, 1:2], inner, edge[:, 4:5]], axis=1)
            i2[:, :, cut] = jnp.concatenate([inner, edge[:, 4:6]], axis=1)

    mask = mask_rows(tab_ref[:, 128:256], 0, Y1, X1, lambda x: x, 4)
    for g in range(2):
        acc = conv_group([[(ref, 256 * g, 384)] for ref in (i0, i1, i2)], tb_ref, 0, Y1, 256, 384)
        for q in range(2):
            value = jnp.maximum(acc[:, q * 128 : q * 128 + 128] + twice(bb_ref), 0.0) * mask
            feat_ref[:, (2 * g + q) * 128 : (2 * g + q + 1) * 128] = value.astype(BF)

    size = 8 * X1
    quarter = size // 4
    r = iota((size, 128), 0)
    select = one_hot_rows(((r & 48) << 2) | ((r & 64) >> 1) | ((r & 15) << 1) | (r >> 7), size)
    for n in range(Y1 // 8):
        cells = mm(select, feat_ref[n * size : n * size + size, :]).astype(BF)
        for q in range(4):
            d_ref[q, n * quarter : n * quarter + quarter, :] = cells[q * quarter : (q + 1) * quarter]
    mask = mask_rows(tab2_ref[:, 128:256], 0, Y2, X2, lambda x: x, 2)
    for z in range(Z2):
        left = jnp.concatenate([d_ref[q, :, z * 128 : z * 128 + 128] for q in range(4)], axis=1)
        down_ref[:, :, z * CP : z * CP + CP] = finish(mm(left, wd_ref[...]), bd_ref[...], mask, Y2)


def one_kernel(feat_ref, out_ref):
    lanes = feat_ref.shape[1]
    r = iota((lanes, 128), 0)
    order = one_hot_rows(((r & 7) << 6) | (r >> 3), lanes)
    out_ref[...] = mm(order, feat_ref[...], NT).astype(BF)


def level_two_kernel(
    win_ref, zl_ref, zr_ref, xl_ref, xr_ref, ta_ref, tb_ref, ba_ref, bb_ref, tab_ref, out_ref, a0, a1, a2, i0, i1, i2
):
    for chunk in range(8):
        ref, lane = (zl_ref, chunk) if chunk < 2 else ((win_ref, chunk - 2) if chunk < 6 else (zr_ref, chunk - 6))
        inner = ref[:, :, lane * 128 : lane * 128 + 128]
        cut = slice(chunk * 128, chunk * 128 + 128)
        left, right = xl_ref[:, :, cut], xr_ref[:, :, cut]
        for i, copy in enumerate((a0, a1, a2)):
            spare = jnp.zeros((ROWS2, PITCH2 - X2 - 4 + i, 128), BF)
            line = [inner, right, spare] if i == 2 else [left[:, i:], inner, right, spare]
            copy[:, :, cut] = jnp.concatenate(line, axis=1)
    rows = Y2 + 2
    mask = mask_rows(tab_ref[...], -1, rows, PITCH2, lambda x: x - 1, 2)
    for g in range(3):
        acc = conv_group([[(ref, 256 * g, 512)] for ref in (a0, a1, a2)], ta_ref, 0, rows, 256, 512)
        for q in range(2):
            chunk = 2 * g + q
            which = 0 if chunk == 0 else (2 if chunk == 5 else 1)
            value = finish(acc[:, q * 128 : q * 128 + 128], ba_ref[...], mask[:, which * 128 : which * 128 + 128], rows)
            cut = slice(chunk * 128, chunk * 128 + 128)
            for s, copy in enumerate((i0, i1, i2)):
                copy[:, :, cut] = value[:, s : s + X2]
    mask = mask_rows(tab_ref[:, 128:256], 0, Y2, X2, lambda x: x, 2)
    feat = []
    for g in range(2):
        acc = conv_group([[(ref, 256 * g, 512)] for ref in (i0, i1, i2)], tb_ref, 0, Y2, 256, 512)
        for q in range(2):
            feat.append((jnp.maximum(acc[:, q * 128 : q * 128 + 128] + bb_ref[...], 0.0) * mask).astype(BF))
    r = iota((C2 * Z2, 128), 0)
    order = one_hot_rows(((r & 3) << 7) | (r >> 2), Z2 * CP)
    out_ref[...] = mm(order, jnp.concatenate(feat, axis=1), NT).astype(BF)


def swap_pairs(count, cores, cores_first):
    def place(y, i):
        return y * count + i if cores_first else i * cores + y

    pairs = []
    for y in range(cores):
        for i in range(count):
            other = i + 1 if i % 2 else i - 1
            target = place(y, other) if 0 <= other < count else place(y ^ 1, i)
            pairs.append((place(y, i), target))
    return pairs


def shift_along(low_edge, high_edge, axis):
    count = lax.axis_size(axis)
    index = lax.axis_index(axis)
    even = index % 2 == 0
    one = lax.ppermute(jnp.where(even, high_edge, low_edge), axis, [(i, i ^ 1) for i in range(count)])
    two = one
    if count > 2 and axis == "gy":
        pairs = [(0, count - 1), (count - 1, 0)] + [(i, i - 1 + i % 2 * 2) for i in range(1, count - 1)]
        two = lax.ppermute(jnp.where(even, low_edge, high_edge), axis, pairs)
    elif count > 2:
        axes = ("gx", "gy") if axis == "gx" else ("gy", "gz")
        pairs = swap_pairs(count, lax.axis_size("gy"), axis == "gz")
        two = lax.ppermute(jnp.where(even, low_edge, high_edge), axes, pairs)
    below = jnp.where(index > 0, jnp.where(even, two, one), jnp.zeros_like(one))
    above = jnp.where(index < count - 1, jnp.where(even, one, two), jnp.zeros_like(one))
    return below, above


def params():
    return pltpu.CompilerParams(vmem_limit_bytes=VMEM_BYTES)


def cost(seconds):
    return pl.CostEstimate(flops=int(1e15 * seconds), bytes_accessed=0, transcendentals=0)


def shaped(*shape):
    return jax.ShapeDtypeStruct(shape, BF)


def pad_lanes(value):
    return jnp.pad(value, [(0, 0)] * (value.ndim - 1) + [(0, CP - value.shape[-1])])


def local(
    volume, tissue, w_down1, b_down1, w_conv1a, b_conv1a, w_conv1b, b_conv1b,
    w_down2, b_down2, w_conv2a, b_conv2a, w_conv2b, b_conv2b,
):
    depth = volume.shape[1]
    kz = C0 * depth
    lanes1 = Z1 * C1
    half = depth // 2
    own, tab1, tab2 = pl.pallas_call(
        down1_kernel,
        in_specs=[pl.BlockSpec(memory_space=pltpu.HBM)] + [pl.BlockSpec(memory_space=pltpu.VMEM)] * 3,
        out_shape=[shaped(Y1, X1, lanes1), shaped(128, 384), shaped(128, 384)],
        scratch_shapes=[
            pltpu.VMEM((2 * kz, lanes1 // 2), BF),
            pltpu.VMEM((C0, 2, half, volume.shape[2]), BF),
            pltpu.VMEM((2, Y1 * X1, 2 * kz), BF),
            pltpu.SemaphoreType.DMA((C0 // 16,)),
        ],
        compiler_params=pltpu.CompilerParams(vmem_limit_bytes=DOWN1_VMEM_BYTES),
        cost_estimate=cost(4e-6),
    )(volume.reshape(C0, 2, half, -1), jnp.swapaxes(w_down1, 1, 2), b_down1[None], tissue.transpose(1, 2, 0))

    t1a = banded(w_conv1a, 4, C1)
    t2a = banded(w_conv2a, 2, CP)
    t2b = banded(w_conv2b, 2, CP)
    bias1a = b_conv1a[None]

    y_below, y_above = shift_along(own[:HALO], own[Y1 - HALO :], "gy")
    win = jnp.concatenate([y_below, own, y_above], axis=0)
    z_below, z_above = shift_along(win[:, :, :128], win[:, :, lanes1 - 128 :], "gz")
    rows = Y1 + 2
    left, right, g2, t1b = pl.pallas_call(
        middle_kernel,
        out_shape=[shaped(ROWS1, X1, lanes1), shaped(ROWS1, X1, lanes1), shaped(rows, X1, 256), banded_shape(4, C1)],
        compiler_params=params(),
        cost_estimate=cost(3e-6),
    )(win, t1a, bias1a, tab1, w_conv1b)

    low = jnp.concatenate([z_below[:, :2], win[:, :2], z_above[:, :2]], axis=2)
    high = jnp.concatenate([z_below[:, X1 - 2 :], win[:, X1 - 2 :], z_above[:, X1 - 2 :]], axis=2)
    x_below, x_above = shift_along(low, high, "gx")
    g1, g3 = pl.pallas_call(
        outer_kernel,
        out_shape=[shaped(rows, X1, 256), shaped(rows, X1, 128)],
        scratch_shapes=[pltpu.VMEM((ROWS1, X1, 128), BF)] * 4,
        compiler_params=params(),
        cost_estimate=cost(4e-6),
    )(win, left, right, z_below, z_above, t1a, bias1a, tab1)

    feat, down = pl.pallas_call(
        level_one_kernel,
        out_shape=[shaped(Y1 * X1, lanes1), shaped(Y2, X2, Z2 * CP)],
        scratch_shapes=[pltpu.VMEM((ROWS1, EDGE, (Z1 + 4) * C1), BF)] * 3
        + [pltpu.VMEM((rows, X1, (Z1 + 2) * C1), BF)] * 3
        + [pltpu.VMEM((4, Y2 * X2, lanes1), BF)],
        compiler_params=params(),
        cost_estimate=cost(6e-6),
    )(
        x_below, low, high, x_above, g1, g2, g3, t1a, t1b, bias1a, b_conv1b[None],
        pad_lanes(jnp.swapaxes(w_down2, 1, 2).reshape(8 * C1, C2)), pad_lanes(b_down2[None]), tab1, tab2,
    )

    one = pl.pallas_call(
        one_kernel, out_shape=shaped(lanes1, Y1 * X1), compiler_params=params(), cost_estimate=cost(2e-6)
    )(feat)

    y_below, y_above = shift_along(down[:HALO], down[Y2 - HALO :], "gy")
    win = jnp.concatenate([y_below, down, y_above], axis=0)
    z_below, z_above = shift_along(win[:, :, : 2 * CP], win[:, :, 2 * CP :], "gz")
    low = jnp.concatenate([z_below[:, :2], win[:, :2], z_above[:, :2]], axis=2)
    high = jnp.concatenate([z_below[:, X2 - 2 :], win[:, X2 - 2 :], z_above[:, X2 - 2 :]], axis=2)
    x_below, x_above = shift_along(low, high, "gx")
    two = pl.pallas_call(
        level_two_kernel,
        out_shape=shaped(C2 * Z2, Y2 * X2),
        scratch_shapes=[pltpu.VMEM((ROWS2, PITCH2, (Z2 + 4) * CP), BF)] * 3
        + [pltpu.VMEM((Y2 + 2, X2, (Z2 + 2) * CP), BF)] * 3,
        compiler_params=params(),
        cost_estimate=cost(5e-6),
    )(win, z_below, z_above, x_below, x_above, t2a, t2b, pad_lanes(b_conv2a[None]), pad_lanes(b_conv2b[None]), tab2)
    return one.reshape(C1, Z1, Y1 * X1), two.reshape(C2, Z2, Y2 * X2)


def solution(mesh):
    block = P(None, "gz", ("gx", "gy"))
    return jax.shard_map(
        local,
        mesh=mesh,
        in_specs=(block,) + (P(),) * 13,
        out_specs=(block, block),
        check_vma=False,
    )
```

```python
import jax
import jax.numpy as jnp
from jax import lax
from jax.experimental import pallas as pl
from jax.experimental.pallas import tpu as pltpu
from jax.sharding import PartitionSpec as P

CX = 64
CY = 32
X1 = CX // 2
Y1 = CY // 2
X2 = X1 // 2
Y2 = Y1 // 2
Z1 = 8
Z2 = 4
C0 = 48
C1 = 64
C2 = 96
CP = 128
HALO = 2
XB = 10
XB_PITCH = 16
YB = 6
ROWS1 = Y1 + 2 * HALO
ROWS2 = Y2 + 2 * HALO
EDGE = 16
PITCH2 = 32
BF = jnp.bfloat16
F32 = jnp.float32
NN = (((1,), (0,)), ((), ()))
NT = (((1,), (1,)), ((), ()))
VMEM_BYTES = 40 * 1024 * 1024
DOWN1_VMEM_BYTES = 60 * 1024 * 1024


def mm(a, b, dims=NN):
    return lax.dot_general(a, b, dims, preferred_element_type=F32)


def iota(shape, dim):
    return lax.broadcasted_iota(jnp.int32, shape, dim)


def one_hot(flag):
    return jnp.where(flag, 1.0, 0.0).astype(BF)


def one_hot_rows(key, lanes):
    lane = iota(key.shape, 1)
    return jnp.concatenate([one_hot(key == lane + q) for q in range(0, lanes, 128)], axis=1)


def mask_rows(tab, y_start, rows, pitch, x_of, cell):
    bits = cell.bit_length() - 1
    shape = (rows, pitch, 128)
    y_block = (iota(shape, 0) + (y_start + cell)) >> bits
    x_block = jnp.minimum((x_of(iota(shape, 1)) + cell) >> bits, XB - 1)
    hit = one_hot(y_block * XB_PITCH + x_block == iota(shape, 2)).reshape(rows * pitch, 128)
    return mm(hit, tab)


def tissue_tables(t_ref):
    n_y, n_z, n_x = t_ref.shape
    here = lax.axis_index("gz")
    layers = []
    for k in (-1, 0, 1):
        z = here + k
        inside = jnp.where((z >= 0) & (z < n_z), 1.0, 0.0)
        layers.append(t_ref[:, jnp.clip(z, 0, n_z - 1), :].astype(F32) * inside)
    block = iota((128, n_y), 0)
    bits = XB_PITCH.bit_length() - 1
    hot_y = one_hot(lax.axis_index("gy") * 4 - 1 + (block >> bits) == iota((128, n_y), 1))
    block = iota((128, 3 * n_x), 0)
    layer = sum((iota((128, 3 * n_x), 1) >= k * n_x).astype(jnp.int32) for k in (1, 2))
    hot_x = lax.axis_index("gx") * 8 - 1 + (block & (XB_PITCH - 1)) == iota((128, 3 * n_x), 1) - layer * n_x
    rows = jnp.where(hot_x, mm(hot_y, jnp.concatenate(layers, axis=1).astype(BF)), 0.0).astype(BF)
    shape = (3 * n_x, 384)
    layer = sum((iota(shape, 0) >= k * n_x).astype(jnp.int32) for k in (1, 2))
    lane = iota(shape, 1)

    def spread(first, last):
        place = jnp.where(lane < first, 0, jnp.where(lane < last, 1, 2))
        return mm(rows, one_hot(layer == place)).astype(BF)

    return spread(64, 320), spread(128, 256)


def down1_kernel(v_ref, w_ref, b_ref, t_ref, out_ref, first_ref, second_ref, tab_ref, tab2_ref, wd_ref, field_ref, cells_ref, sems):
    half = v_ref.shape[2]
    kz = C0 * half
    lanes = Z1 // 2 * C1
    copies = []
    for n in range(sems.shape[0]):
        cut = slice(n * 16, n * 16 + 16)
        copies.append(pltpu.make_async_copy(v_ref.at[cut], field_ref.at[cut], sems.at[n]))
        copies[-1].start()

    tab, tab2 = tissue_tables(t_ref)
    tab_ref[...] = tab
    tab2_ref[...] = tab2
    r = iota((kz, 2 * C0), 0)
    l = iota((kz, 2 * C0), 1)
    odd = l >= C0
    spread = one_hot(((r >> 3) == jnp.where(odd, l - C0, l)) & ((r & 1) == odd.astype(jnp.int32)))
    keep = (iota((kz, lanes), 0) & 7) >> 1 == iota((kz, lanes), 1) >> 6
    for ab in range(4):
        pair = w_ref[2 * ab : 2 * ab + 2].reshape(2 * C0, C1)
        wide = jnp.concatenate([pair] * (Z1 // 2), axis=1)
        wd_ref[ab * kz : (ab + 1) * kz, :] = jnp.where(keep, mm(spread, wide), 0.0).astype(BF)

    r = iota((4 * CX, 128), 0)
    select = one_hot_rows(((r & 32) << 2) | (r & 64) | ((r & 31) << 1) | (r >> 7), 4 * CX)
    part = 16 * half
    for n, copy in enumerate(copies):
        copy.wait()
        for m in range(field_ref.shape[3] // 256):
            v = [field_ref[n * 16 : n * 16 + 16, h, :, m * 256 : m * 256 + 256].reshape(part, 256) for h in range(2)]
            cells = mm(select, jnp.concatenate(v, axis=0), NT).astype(BF)
            for ab in range(4):
                lane = ab * kz + n * part
                for h in range(2):
                    piece = cells[64 * ab : 64 * ab + 64, h * part : h * part + part]
                    cells_ref[h, m * 64 : m * 64 + 64, lane : lane + part] = piece
    mask = mask_rows(tab[:, 128:256], 0, Y1, X1, lambda x: x, 4)
    bias = twice(b_ref)
    for h in range(2):
        acc = mm(cells_ref[h], wd_ref[...])
        for q in range(2):
            value = finish(acc[:, q * 128 : q * 128 + 128], bias, mask, Y1)
            out_ref[:, :, (2 * h + q) * 128 : (2 * h + q + 1) * 128] = value
    odd = lax.axis_index("gy") & 1
    for parity, edges in enumerate(((second_ref, first_ref), (first_ref, second_ref))):

        @pl.when(odd == parity)
        def _(low=edges[0], high=edges[1]):
            low[...] = out_ref[:HALO]
            high[...] = out_ref[Y1 - HALO :]


def twice(b_ref):
    return jnp.concatenate([b_ref[...]] * 2, axis=1)


def fill_banded(w_ref, t_ref, group, pad):
    chan = w_ref.shape[1]
    t_ref[...] = jnp.zeros_like(t_ref)
    for j in range(3):
        for i in range(3):
            for zo in range(group):
                for k in range(3):
                    lane = i * (group + 2) * pad + (zo + k) * pad
                    t_ref[j, zo * pad : zo * pad + chan, lane : lane + chan] = w_ref[9 * i + 3 * j + k]


def banded_shape(group, pad):
    return shaped(3, group * pad, 3 * (group + 2) * pad)


def banded(weights, group, pad):
    def kernel(w_ref, t_ref):
        fill_banded(w_ref, t_ref, group, pad)

    return pl.pallas_call(
        kernel, out_shape=banded_shape(group, pad), compiler_params=params(), cost_estimate=cost(1e-6)
    )(weights)


def conv_group(taps, t_ref, y_first, rows, group_out, group_full):
    pitch = taps[0][0][0].shape[1]
    width = sum(piece[2] for piece in taps[0])
    total = None
    for j in range(3):
        parts = [ref[y_first + j : y_first + j + rows, :, lane : lane + n] for tap in taps for ref, lane, n in tap]
        left = jnp.concatenate([p.reshape(rows * pitch, p.shape[2]) for p in parts], axis=1)
        if width == group_full:
            right = t_ref[j, 0:group_out, :]
        else:
            right = jnp.concatenate([t_ref[j, 0:group_out, i * group_full : i * group_full + width] for i in range(3)], axis=1)
        term = mm(left, right, NT)
        total = term if total is None else total + term
    return total


def finish(acc, bias, mask, rows):
    value = jnp.maximum(acc + bias, 0.0) * mask
    return value.astype(BF).reshape(rows, value.shape[0] // rows, value.shape[1])


def fill_sides(left, right, lane, inner):
    cut = slice(lane, lane + inner.shape[2])
    none = jnp.zeros_like(inner[:, :1])
    left[:, :, cut] = jnp.concatenate([none, inner[:, :-1]], axis=1)
    right[:, :, cut] = jnp.concatenate([inner[:, 1:], none], axis=1)


def middle_kernel(win_ref, t_ref, b_ref, tab_ref, w_ref, left_ref, right_ref, out_ref, next_ref):
    fill_banded(w_ref, next_ref, 4, C1)
    for q in range(4):
        fill_sides(left_ref, right_ref, q * 128, win_ref[:, :, q * 128 : q * 128 + 128])
    rows = Y1 + 2
    mask = mask_rows(tab_ref[:, 128:256], -1, rows, X1, lambda x: x, 4)
    acc = conv_group([[(ref, 128, 384)] for ref in (left_ref, win_ref, right_ref)], t_ref, 0, rows, 256, 384)
    for q in range(2):
        cut = slice(q * 128, q * 128 + 128)
        out_ref[:, :, cut] = finish(acc[:, cut], twice(b_ref), mask, rows)


def outer_kernel(win_ref, left_ref, right_ref, zl_ref, zr_ref, t_ref, b_ref, tab_ref, low_ref, high_ref, ll, lr, hl, hr):
    fill_sides(ll, lr, 0, zl_ref[...])
    fill_sides(hl, hr, 0, zr_ref[...])
    own = (left_ref, win_ref, right_ref)
    rows = Y1 + 2
    mask = mask_rows(tab_ref[...], -1, rows, X1, lambda x: x, 4)
    taps = [[(z, 0, 128), (ref, 0, 256)] for z, ref in zip((ll, zl_ref, lr), own)]
    acc = conv_group(taps, t_ref, 0, rows, 256, 384)
    for q in range(2):
        cut = slice(q * 128, q * 128 + 128)
        low_ref[:, :, cut] = finish(acc[:, cut], twice(b_ref), mask[:, cut], rows)
    taps = [[(ref, 384, 128), (z, 0, 128)] for z, ref in zip((hl, zr_ref, hr), own)]
    acc = conv_group(taps, t_ref, 0, rows, 128, 384)
    high_ref[...] = finish(acc, twice(b_ref), mask[:, 256:384], rows)


def fill_edges(copies, pieces):
    rows, pitch, lanes = copies[0].shape
    for lane in range(0, lanes, 128):
        line = [p[:, :, lane : lane + 128] for p in pieces]
        used = sum(p.shape[1] for p in line)
        for i, copy in enumerate(copies):
            moved = [line[0][:, i:]] + line[1:] if i < line[0].shape[1] else line[1:]
            spare = jnp.zeros((rows, pitch - used + i, 128), BF)
            copy[:, :, lane : lane + 128] = jnp.concatenate(moved + [spare], axis=1)


def level_one_kernel(
    xl_ref, low_ref, high_ref, xr_ref, g1_ref, g2_ref, g3_ref, ta_ref, tb_ref, ba_ref, bb_ref, wd_ref, bd_ref, tab_ref, tab2_ref,
    feat_ref, down_ref, e0, e1, e2, i0, i1, i2, d_ref,
):
    fill_edges((e0, e1, e2), (xl_ref, low_ref, high_ref, xr_ref))
    rows = Y1 + 2
    mask = mask_rows(tab_ref[...], -1, rows, EDGE, lambda r: jnp.where(r < 4, r - 1, r + X1 - 5), 4)
    for g, (lane, width, out) in enumerate(((0, 384, 256), (256, 384, 256), (512, 256, 128))):
        acc = conv_group([[(e, lane, width)] for e in (e0, e1, e2)], ta_ref, 0, rows, out, 384)
        for q in range(out // 128):
            chunk = 2 * g + q
            which = 0 if chunk == 0 else (2 if chunk == 4 else 1)
            edge = finish(acc[:, q * 128 : q * 128 + 128], twice(ba_ref), mask[:, which * 128 : which * 128 + 128], rows)
            inner = (g1_ref, g2_ref, g3_ref)[g][:, :, q * 128 : q * 128 + 128][:, 1:-1]
            cut = slice(chunk * 128, chunk * 128 + 128)
            i0[:, :, cut] = jnp.concatenate([edge[:, 0:2], inner], axis=1)
            i1[:, :, cut] = jnp.concatenate([edge[:, 1:2], inner, edge[:, 4:5]], axis=1)
            i2[:, :, cut] = jnp.concatenate([inner, edge[:, 4:6]], axis=1)

    mask = mask_rows(tab_ref[:, 128:256], 0, Y1, X1, lambda x: x, 4)
    for g in range(2):
        acc = conv_group([[(ref, 256 * g, 384)] for ref in (i0, i1, i2)], tb_ref, 0, Y1, 256, 384)
        for q in range(2):
            value = jnp.maximum(acc[:, q * 128 : q * 128 + 128] + twice(bb_ref), 0.0) * mask
            feat_ref[:, (2 * g + q) * 128 : (2 * g + q + 1) * 128] = value.astype(BF)

    size = 8 * X1
    quarter = size // 4
    r = iota((size, 128), 0)
    select = one_hot_rows(((r & 48) << 2) | ((r & 64) >> 1) | ((r & 15) << 1) | (r >> 7), size)
    for n in range(Y1 // 8):
        cells = mm(select, feat_ref[n * size : n * size + size, :]).astype(BF)
        for q in range(4):
            d_ref[q, n * quarter : n * quarter + quarter, :] = cells[q * quarter : (q + 1) * quarter]
    mask = mask_rows(tab2_ref[:, 128:256], 0, Y2, X2, lambda x: x, 2)
    for z in range(Z2):
        left = jnp.concatenate([d_ref[q, :, z * 128 : z * 128 + 128] for q in range(4)], axis=1)
        down_ref[:, :, z * CP : z * CP + CP] = finish(mm(left, wd_ref[...]), bd_ref[...], mask, Y2)


def one_kernel(feat_ref, out_ref):
    lanes = feat_ref.shape[1]
    r = iota((lanes, 128), 0)
    order = one_hot_rows(((r & 7) << 6) | (r >> 3), lanes)
    out_ref[...] = mm(order, feat_ref[...], NT).astype(BF)


def fill_pitch(copies, wide):
    pitch = copies[0].shape[1]
    for lane in range(0, wide.shape[2], 128):
        line = wide[:, :, lane : lane + 128]
        for i, copy in enumerate(copies):
            spare = jnp.zeros((line.shape[0], pitch - line.shape[1] + i, 128), BF)
            copy[:, :, lane : lane + 128] = jnp.concatenate([line[:, i:], spare], axis=1)


def level_two_group(taps, t_ref, b_ref, masks, moved):
    rows = Y2 + 2
    acc = conv_group(taps, t_ref, 0, rows, 256, 512)
    for q in range(2):
        cut = slice(q * 128, q * 128 + 128)
        value = finish(acc[:, cut], b_ref[...], masks[q], rows)
        for i, ref in enumerate(moved):
            ref[:, :, cut] = value[:, i : i + X2]


def level_two_masks(tab_ref):
    mask = mask_rows(tab_ref[...], -1, Y2 + 2, PITCH2, lambda x: x - 1, 2)
    return [mask[:, q * 128 : q * 128 + 128] for q in range(3)]


def level_two_middle_kernel(wide_ref, t_ref, b_ref, tab_ref, a0, a1, a2, m0, m1, m2):
    fill_pitch((a0, a1, a2), wide_ref[...])
    here = level_two_masks(tab_ref)[1]
    level_two_group([[(a, 0, 512)] for a in (a0, a1, a2)], t_ref, b_ref, (here, here), (m0, m1, m2))


def level_two_kernel(
    a0, a1, a2, m0, m1, m2, zl_ref, zr_ref, ta_ref, tb_ref, ba_ref, bb_ref, tab_ref, out_ref,
    l0, l1, l2, h0, h1, h2, i0, i1, i2, j0, j1, j2,
):
    fill_pitch((l0, l1, l2), zl_ref[...])
    fill_pitch((h0, h1, h2), zr_ref[...])
    below, here, above = level_two_masks(tab_ref)
    own, mid, low, high = (a0, a1, a2), (m0, m1, m2), (i0, i1, i2), (j0, j1, j2)
    taps = [[(z, 0, 256), (a, 0, 256)] for z, a in zip((l0, l1, l2), own)]
    level_two_group(taps, ta_ref, ba_ref, (below, here), low)
    taps = [[(a, 256, 256), (z, 0, 256)] for z, a in zip((h0, h1, h2), own)]
    level_two_group(taps, ta_ref, ba_ref, (here, above), high)
    mask = mask_rows(tab_ref[:, 128:256], 0, Y2, X2, lambda x: x, 2)
    feat = []
    for pair in ((low, mid), (mid, high)):
        acc = conv_group([[(a, 0, 256), (b, 0, 256)] for a, b in zip(*pair)], tb_ref, 0, Y2, 256, 512)
        for q in range(2):
            feat.append((jnp.maximum(acc[:, q * 128 : q * 128 + 128] + bb_ref[...], 0.0) * mask).astype(BF))
    r = iota((C2 * Z2, 128), 0)
    order = one_hot_rows(((r & 3) << 7) | (r >> 2), Z2 * CP)
    out_ref[...] = mm(order, jnp.concatenate(feat, axis=1), NT).astype(BF)


def swap_pairs(count, cores, cores_first):
    def place(y, i):
        return y * count + i if cores_first else i * cores + y

    pairs = []
    for y in range(cores):
        for i in range(count):
            other = i + 1 if i % 2 else i - 1
            target = place(y, other) if 0 <= other < count else place(y ^ 1, i)
            pairs.append((place(y, i), target))
    return pairs


def trade(first, second, axis):
    count = lax.axis_size(axis)
    index = lax.axis_index(axis)
    even = index % 2 == 0
    one = lax.ppermute(first, axis, [(i, i ^ 1) for i in range(count)])
    two = one
    if count > 2 and axis == "gy":
        pairs = [(0, count - 1), (count - 1, 0)] + [(i, i - 1 + i % 2 * 2) for i in range(1, count - 1)]
        two = lax.ppermute(second, axis, pairs)
    elif count > 2:
        axes = ("gx", "gy") if axis == "gx" else ("gy", "gz")
        two = lax.ppermute(second, axes, swap_pairs(count, lax.axis_size("gy"), axis == "gz"))
    below = jnp.where(index > 0, jnp.where(even, two, one), jnp.zeros_like(one))
    above = jnp.where(index < count - 1, jnp.where(even, one, two), jnp.zeros_like(one))
    return below, above


def shift_along(low_edge, high_edge, axis):
    even = lax.axis_index(axis) % 2 == 0
    return trade(jnp.where(even, high_edge, low_edge), jnp.where(even, low_edge, high_edge), axis)


def params():
    return pltpu.CompilerParams(vmem_limit_bytes=VMEM_BYTES)


def cost(seconds):
    return pl.CostEstimate(flops=int(1e15 * seconds), bytes_accessed=0, transcendentals=0)


def shaped(*shape):
    return jax.ShapeDtypeStruct(shape, BF)


def pad_lanes(value):
    return jnp.pad(value, [(0, 0)] * (value.ndim - 1) + [(0, CP - value.shape[-1])])


def local(
    volume, tissue, w_down1, b_down1, w_conv1a, b_conv1a, w_conv1b, b_conv1b,
    w_down2, b_down2, w_conv2a, b_conv2a, w_conv2b, b_conv2b,
):
    depth = volume.shape[1]
    kz = C0 * depth
    lanes1 = Z1 * C1
    half = depth // 2
    own, first, second, tab1, tab2 = pl.pallas_call(
        down1_kernel,
        in_specs=[pl.BlockSpec(memory_space=pltpu.HBM)] + [pl.BlockSpec(memory_space=pltpu.VMEM)] * 3,
        out_shape=[shaped(Y1, X1, lanes1)] + [shaped(HALO, X1, lanes1)] * 2 + [shaped(128, 384)] * 2,
        scratch_shapes=[
            pltpu.VMEM((2 * kz, lanes1 // 2), BF),
            pltpu.VMEM((C0, 2, half, volume.shape[2]), BF),
            pltpu.VMEM((2, Y1 * X1, 2 * kz), BF),
            pltpu.SemaphoreType.DMA((C0 // 16,)),
        ],
        compiler_params=pltpu.CompilerParams(vmem_limit_bytes=DOWN1_VMEM_BYTES),
        cost_estimate=cost(4e-6),
    )(volume.reshape(C0, 2, half, -1), jnp.swapaxes(w_down1, 1, 2), b_down1[None], tissue.transpose(1, 2, 0))

    t1a = banded(w_conv1a, 4, C1)
    t2a = banded(w_conv2a, 2, CP)
    t2b = banded(w_conv2b, 2, CP)
    bias1a = b_conv1a[None]

    y_below, y_above = trade(first, second, "gy")
    win = jnp.concatenate([y_below, own, y_above], axis=0)
    z_below, z_above = shift_along(win[:, :, :128], win[:, :, lanes1 - 128 :], "gz")
    rows = Y1 + 2
    left, right, g2, t1b = pl.pallas_call(
        middle_kernel,
        out_shape=[shaped(ROWS1, X1, lanes1), shaped(ROWS1, X1, lanes1), shaped(rows, X1, 256), banded_shape(4, C1)],
        compiler_params=params(),
        cost_estimate=cost(3e-6),
    )(win, t1a, bias1a, tab1, w_conv1b)

    low = jnp.concatenate([z_below[:, :2], win[:, :2], z_above[:, :2]], axis=2)
    high = jnp.concatenate([z_below[:, X1 - 2 :], win[:, X1 - 2 :], z_above[:, X1 - 2 :]], axis=2)
    x_below, x_above = shift_along(low, high, "gx")
    g1, g3 = pl.pallas_call(
        outer_kernel,
        out_shape=[shaped(rows, X1, 256), shaped(rows, X1, 128)],
        scratch_shapes=[pltpu.VMEM((ROWS1, X1, 128), BF)] * 4,
        compiler_params=params(),
        cost_estimate=cost(4e-6),
    )(win, left, right, z_below, z_above, t1a, bias1a, tab1)

    feat, down = pl.pallas_call(
        level_one_kernel,
        out_shape=[shaped(Y1 * X1, lanes1), shaped(Y2, X2, Z2 * CP)],
        scratch_shapes=[pltpu.VMEM((ROWS1, EDGE, (Z1 + 4) * C1), BF)] * 3
        + [pltpu.VMEM((rows, X1, (Z1 + 2) * C1), BF)] * 3
        + [pltpu.VMEM((4, Y2 * X2, lanes1), BF)],
        compiler_params=params(),
        cost_estimate=cost(6e-6),
    )(
        x_below, low, high, x_above, g1, g2, g3, t1a, t1b, bias1a, b_conv1b[None],
        pad_lanes(jnp.swapaxes(w_down2, 1, 2).reshape(8 * C1, C2)), pad_lanes(b_down2[None]), tab1, tab2,
    )

    one = pl.pallas_call(
        one_kernel, out_shape=shaped(lanes1, Y1 * X1), compiler_params=params(), cost_estimate=cost(2e-6)
    )(feat)

    y_below, y_above = shift_along(down[:HALO], down[Y2 - HALO :], "gy")
    win = jnp.concatenate([y_below, down, y_above], axis=0)
    x_below, x_above = shift_along(win[:, :HALO], win[:, X2 - HALO :], "gx")
    wide = jnp.concatenate([x_below, win, x_above], axis=1)
    z_below, z_above = shift_along(wide[:, :, : 2 * CP], wide[:, :, 2 * CP :], "gz")
    bias2a = pad_lanes(b_conv2a[None])
    moved = [shaped(Y2 + 2, X2, 2 * CP)] * 3
    middle = pl.pallas_call(
        level_two_middle_kernel,
        out_shape=[shaped(ROWS2, PITCH2, Z2 * CP)] * 3 + moved,
        compiler_params=params(),
        cost_estimate=cost(3e-6),
    )(wide, t2a, bias2a, tab2)
    two = pl.pallas_call(
        level_two_kernel,
        out_shape=shaped(C2 * Z2, Y2 * X2),
        scratch_shapes=[pltpu.VMEM((ROWS2, PITCH2, 2 * CP), BF)] * 6 + [pltpu.VMEM((Y2 + 2, X2, 2 * CP), BF)] * 6,
        compiler_params=params(),
        cost_estimate=cost(5e-6),
    )(*middle, z_below, z_above, t2a, t2b, bias2a, pad_lanes(b_conv2b[None]), tab2)
    return one.reshape(C1, Z1, Y1 * X1), two.reshape(C2, Z2, Y2 * X2)


def solution(mesh):
    block = P(None, "gz", ("gx", "gy"))
    return jax.shard_map(
        local,
        mesh=mesh,
        in_specs=(block,) + (P(),) * 13,
        out_specs=(block, block),
        check_vma=False,
    )
```

```python
import jax
import jax.numpy as jnp
from jax import lax
from jax.experimental import pallas as pl
from jax.experimental.pallas import tpu as pltpu
from jax.sharding import PartitionSpec as P

CX = 64
CY = 32
X1 = CX // 2
Y1 = CY // 2
X2 = X1 // 2
Y2 = Y1 // 2
Z1 = 8
Z2 = 4
C0 = 48
C1 = 64
C2 = 96
CP = 128
HALO = 2
XB = 10
XB_PITCH = 16
YB = 6
ROWS1 = Y1 + 2 * HALO
ROWS2 = Y2 + 2 * HALO
EDGE = 16
PITCH2 = 32
BF = jnp.bfloat16
F32 = jnp.float32
NN = (((1,), (0,)), ((), ()))
NT = (((1,), (1,)), ((), ()))
VMEM_BYTES = 40 * 1024 * 1024


def mm(a, b, dims=NN):
    return lax.dot_general(a, b, dims, preferred_element_type=F32)


def iota(shape, dim):
    return lax.broadcasted_iota(jnp.int32, shape, dim)


def one_hot(flag):
    return jnp.where(flag, 1.0, 0.0).astype(BF)


def one_hot_rows(key, lanes):
    lane = iota(key.shape, 1)
    return jnp.concatenate([one_hot(key == lane + q) for q in range(0, lanes, 128)], axis=1)


def mask_rows(tab, y_start, rows, pitch, x_of, cell):
    bits = cell.bit_length() - 1
    shape = (rows, pitch, 128)
    y_block = (iota(shape, 0) + (y_start + cell)) >> bits
    x_block = jnp.minimum((x_of(iota(shape, 1)) + cell) >> bits, XB - 1)
    hit = one_hot(y_block * XB_PITCH + x_block == iota(shape, 2)).reshape(rows * pitch, 128)
    return mm(hit, tab)


def tissue_tables(t_ref):
    n_y, n_z, n_x = t_ref.shape
    here = lax.axis_index("gz")
    layers = []
    for k in (-1, 0, 1):
        z = here + k
        inside = jnp.where((z >= 0) & (z < n_z), 1.0, 0.0)
        layers.append(t_ref[:, jnp.clip(z, 0, n_z - 1), :].astype(F32) * inside)
    block = iota((128, n_y), 0)
    bits = XB_PITCH.bit_length() - 1
    hot_y = one_hot(lax.axis_index("gy") * 4 - 1 + (block >> bits) == iota((128, n_y), 1))
    block = iota((128, 3 * n_x), 0)
    layer = sum((iota((128, 3 * n_x), 1) >= k * n_x).astype(jnp.int32) for k in (1, 2))
    hot_x = lax.axis_index("gx") * 8 - 1 + (block & (XB_PITCH - 1)) == iota((128, 3 * n_x), 1) - layer * n_x
    rows = jnp.where(hot_x, mm(hot_y, jnp.concatenate(layers, axis=1).astype(BF)), 0.0).astype(BF)
    shape = (3 * n_x, 384)
    layer = sum((iota(shape, 0) >= k * n_x).astype(jnp.int32) for k in (1, 2))
    lane = iota(shape, 1)

    def spread(first, last):
        place = jnp.where(lane < first, 0, jnp.where(lane < last, 1, 2))
        return mm(rows, one_hot(layer == place)).astype(BF)

    return spread(64, 320), spread(128, 256)


def down1_kernel(v_ref, w_ref, b_ref, t_ref, order_ref, out_ref, tab_ref, tab2_ref, wd_ref, cells_ref):
    del order_ref
    half = v_ref.shape[2]
    kz = C0 * half
    lanes = Z1 // 2 * C1
    tab, tab2 = tissue_tables(t_ref)
    tab_ref[...] = tab
    tab2_ref[...] = tab2
    r = iota((kz, 2 * C0), 0)
    l = iota((kz, 2 * C0), 1)
    odd = l >= C0
    spread = one_hot(((r >> 3) == jnp.where(odd, l - C0, l)) & ((r & 1) == odd.astype(jnp.int32)))
    keep = (iota((kz, lanes), 0) & 7) >> 1 == iota((kz, lanes), 1) >> 6
    for ab in range(4):
        pair = w_ref[2 * ab : 2 * ab + 2].reshape(2 * C0, C1)
        wide = jnp.concatenate([pair] * (Z1 // 2), axis=1)
        wd_ref[ab * kz : (ab + 1) * kz, :] = jnp.where(keep, mm(spread, wide), 0.0).astype(BF)

    r = iota((4 * CX, 128), 0)
    select = one_hot_rows(((r & 32) << 2) | (r & 64) | ((r & 31) << 1) | (r >> 7), 4 * CX)
    part = 16 * half
    part = 16 * half
    for n in range(C0 // 16):
        for m in range(v_ref.shape[3] // 256):
            v = [v_ref[n * 16 : n * 16 + 16, h, :, m * 256 : m * 256 + 256].reshape(part, 256) for h in range(2)]
            cells = mm(select, jnp.concatenate(v, axis=0), NT).astype(BF)
            for ab in range(4):
                lane = ab * kz + n * part
                for h in range(2):
                    piece = cells[64 * ab : 64 * ab + 64, h * part : h * part + part]
                    cells_ref[h, m * 64 : m * 64 + 64, lane : lane + part] = piece
    mask = mask_rows(tab[:, 128:256], 0, Y1, X1, lambda x: x, 4)
    bias = twice(b_ref)
    for h in range(2):
        acc = mm(cells_ref[h], wd_ref[...])
        for q in range(2):
            value = finish(acc[:, q * 128 : q * 128 + 128], bias, mask, Y1)
            out_ref[:, :, (2 * h + q) * 128 : (2 * h + q + 1) * 128] = value


def twice(b_ref):
    return jnp.concatenate([b_ref[...]] * 2, axis=1)


def fill_banded(w_ref, t_ref, group, pad):
    chan = w_ref.shape[1]
    t_ref[...] = jnp.zeros_like(t_ref)
    for j in range(3):
        for i in range(3):
            for zo in range(group):
                for k in range(3):
                    lane = i * (group + 2) * pad + (zo + k) * pad
                    t_ref[j, zo * pad : zo * pad + chan, lane : lane + chan] = w_ref[9 * i + 3 * j + k]


def banded_shape(group, pad):
    return shaped(3, group * pad, 3 * (group + 2) * pad)


def banded(weights, group, pad):
    def kernel(w_ref, t_ref):
        fill_banded(w_ref, t_ref, group, pad)

    return pl.pallas_call(
        kernel, out_shape=banded_shape(group, pad), compiler_params=params(), cost_estimate=cost(1e-6)
    )(weights)


def conv_group(taps, t_ref, y_first, rows, group_out, group_full):
    pitch = taps[0][0][0].shape[1]
    width = sum(piece[2] for piece in taps[0])
    total = None
    for j in range(3):
        parts = [ref[y_first + j : y_first + j + rows, :, lane : lane + n] for tap in taps for ref, lane, n in tap]
        left = jnp.concatenate([p.reshape(rows * pitch, p.shape[2]) for p in parts], axis=1)
        if width == group_full:
            right = t_ref[j, 0:group_out, :]
        else:
            right = jnp.concatenate([t_ref[j, 0:group_out, i * group_full : i * group_full + width] for i in range(3)], axis=1)
        term = mm(left, right, NT)
        total = term if total is None else total + term
    return total


def finish(acc, bias, mask, rows):
    value = jnp.maximum(acc + bias, 0.0) * mask
    return value.astype(BF).reshape(rows, value.shape[0] // rows, value.shape[1])


def fill_sides(left, right, lane, inner):
    cut = slice(lane, lane + inner.shape[2])
    none = jnp.zeros_like(inner[:, :1])
    left[:, :, cut] = jnp.concatenate([none, inner[:, :-1]], axis=1)
    right[:, :, cut] = jnp.concatenate([inner[:, 1:], none], axis=1)


def middle_kernel(win_ref, t_ref, b_ref, tab_ref, w_ref, left_ref, right_ref, out_ref, next_ref):
    fill_banded(w_ref, next_ref, 4, C1)
    for q in range(4):
        fill_sides(left_ref, right_ref, q * 128, win_ref[:, :, q * 128 : q * 128 + 128])
    rows = Y1 + 2
    mask = mask_rows(tab_ref[:, 128:256], -1, rows, X1, lambda x: x, 4)
    acc = conv_group([[(ref, 128, 384)] for ref in (left_ref, win_ref, right_ref)], t_ref, 0, rows, 256, 384)
    for q in range(2):
        cut = slice(q * 128, q * 128 + 128)
        out_ref[:, :, cut] = finish(acc[:, cut], twice(b_ref), mask, rows)


def outer_kernel(win_ref, left_ref, right_ref, zl_ref, zr_ref, t_ref, b_ref, tab_ref, low_ref, high_ref, ll, lr, hl, hr):
    fill_sides(ll, lr, 0, zl_ref[...])
    fill_sides(hl, hr, 0, zr_ref[...])
    own = (left_ref, win_ref, right_ref)
    rows = Y1 + 2
    mask = mask_rows(tab_ref[...], -1, rows, X1, lambda x: x, 4)
    taps = [[(z, 0, 128), (ref, 0, 256)] for z, ref in zip((ll, zl_ref, lr), own)]
    acc = conv_group(taps, t_ref, 0, rows, 256, 384)
    for q in range(2):
        cut = slice(q * 128, q * 128 + 128)
        low_ref[:, :, cut] = finish(acc[:, cut], twice(b_ref), mask[:, cut], rows)
    taps = [[(ref, 384, 128), (z, 0, 128)] for z, ref in zip((hl, zr_ref, hr), own)]
    acc = conv_group(taps, t_ref, 0, rows, 128, 384)
    high_ref[...] = finish(acc, twice(b_ref), mask[:, 256:384], rows)


def fill_edges(copies, pieces):
    rows, pitch, lanes = copies[0].shape
    for lane in range(0, lanes, 128):
        line = [p[:, :, lane : lane + 128] for p in pieces]
        used = sum(p.shape[1] for p in line)
        for i, copy in enumerate(copies):
            moved = [line[0][:, i:]] + line[1:] if i < line[0].shape[1] else line[1:]
            spare = jnp.zeros((rows, pitch - used + i, 128), BF)
            copy[:, :, lane : lane + 128] = jnp.concatenate(moved + [spare], axis=1)


def level_one_kernel(
    xl_ref, low_ref, high_ref, xr_ref, g1_ref, g2_ref, g3_ref, ta_ref, tb_ref, ba_ref, bb_ref, wd_ref, bd_ref, tab_ref, tab2_ref,
    feat_ref, down_ref, e0, e1, e2, i0, i1, i2, d_ref,
):
    fill_edges((e0, e1, e2), (xl_ref, low_ref, high_ref, xr_ref))
    rows = Y1 + 2
    mask = mask_rows(tab_ref[...], -1, rows, EDGE, lambda r: jnp.where(r < 4, r - 1, r + X1 - 5), 4)
    for g, (lane, width, out) in enumerate(((0, 384, 256), (256, 384, 256), (512, 256, 128))):
        acc = conv_group([[(e, lane, width)] for e in (e0, e1, e2)], ta_ref, 0, rows, out, 384)
        for q in range(out // 128):
            chunk = 2 * g + q
            which = 0 if chunk == 0 else (2 if chunk == 4 else 1)
            edge = finish(acc[:, q * 128 : q * 128 + 128], twice(ba_ref), mask[:, which * 128 : which * 128 + 128], rows)
            inner = (g1_ref, g2_ref, g3_ref)[g][:, :, q * 128 : q * 128 + 128][:, 1:-1]
            cut = slice(chunk * 128, chunk * 128 + 128)
            i0[:, :, cut] = jnp.concatenate([edge[:, 0:2], inner], axis=1)
            i1[:, :, cut] = jnp.concatenate([edge[:, 1:2], inner, edge[:, 4:5]], axis=1)
            i2[:, :, cut] = jnp.concatenate([inner, edge[:, 4:6]], axis=1)

    mask = mask_rows(tab_ref[:, 128:256], 0, Y1, X1, lambda x: x, 4)
    for g in range(2):
        acc = conv_group([[(ref, 256 * g, 384)] for ref in (i0, i1, i2)], tb_ref, 0, Y1, 256, 384)
        for q in range(2):
            value = jnp.maximum(acc[:, q * 128 : q * 128 + 128] + twice(bb_ref), 0.0) * mask
            feat_ref[:, (2 * g + q) * 128 : (2 * g + q + 1) * 128] = value.astype(BF)

    size = 8 * X1
    quarter = size // 4
    r = iota((size, 128), 0)
    select = one_hot_rows(((r & 48) << 2) | ((r & 64) >> 1) | ((r & 15) << 1) | (r >> 7), size)
    for n in range(Y1 // 8):
        cells = mm(select, feat_ref[n * size : n * size + size, :]).astype(BF)
        for q in range(4):
            d_ref[q, n * quarter : n * quarter + quarter, :] = cells[q * quarter : (q + 1) * quarter]
    mask = mask_rows(tab2_ref[:, 128:256], 0, Y2, X2, lambda x: x, 2)
    for z in range(Z2):
        left = jnp.concatenate([d_ref[q, :, z * 128 : z * 128 + 128] for q in range(4)], axis=1)
        down_ref[:, :, z * CP : z * CP + CP] = finish(mm(left, wd_ref[...]), bd_ref[...], mask, Y2)


def one_kernel(feat_ref, out_ref):
    lanes = feat_ref.shape[1]
    r = iota((lanes, 128), 0)
    order = one_hot_rows(((r & 7) << 6) | (r >> 3), lanes)
    out_ref[...] = mm(order, feat_ref[...], NT).astype(BF)


def fill_pitch(copies, wide):
    pitch = copies[0].shape[1]
    for lane in range(0, wide.shape[2], 128):
        line = wide[:, :, lane : lane + 128]
        for i, copy in enumerate(copies):
            spare = jnp.zeros((line.shape[0], pitch - line.shape[1] + i, 128), BF)
            copy[:, :, lane : lane + 128] = jnp.concatenate([line[:, i:], spare], axis=1)


def level_two_group(taps, t_ref, b_ref, masks, moved):
    rows = Y2 + 2
    acc = conv_group(taps, t_ref, 0, rows, 256, 512)
    for q in range(2):
        cut = slice(q * 128, q * 128 + 128)
        value = finish(acc[:, cut], b_ref[...], masks[q], rows)
        for i, ref in enumerate(moved):
            ref[:, :, cut] = value[:, i : i + X2]


def level_two_masks(tab_ref):
    mask = mask_rows(tab_ref[...], -1, Y2 + 2, PITCH2, lambda x: x - 1, 2)
    return [mask[:, q * 128 : q * 128 + 128] for q in range(3)]


def level_two_middle_kernel(wide_ref, t_ref, b_ref, tab_ref, a0, a1, a2, m0, m1, m2):
    fill_pitch((a0, a1, a2), wide_ref[...])
    here = level_two_masks(tab_ref)[1]
    level_two_group([[(a, 0, 512)] for a in (a0, a1, a2)], t_ref, b_ref, (here, here), (m0, m1, m2))


def level_two_kernel(
    a0, a1, a2, m0, m1, m2, zl_ref, zr_ref, ta_ref, tb_ref, ba_ref, bb_ref, tab_ref, out_ref,
    l0, l1, l2, h0, h1, h2, i0, i1, i2, j0, j1, j2,
):
    fill_pitch((l0, l1, l2), zl_ref[...])
    fill_pitch((h0, h1, h2), zr_ref[...])
    below, here, above = level_two_masks(tab_ref)
    own, mid, low, high = (a0, a1, a2), (m0, m1, m2), (i0, i1, i2), (j0, j1, j2)
    taps = [[(z, 0, 256), (a, 0, 256)] for z, a in zip((l0, l1, l2), own)]
    level_two_group(taps, ta_ref, ba_ref, (below, here), low)
    taps = [[(a, 256, 256), (z, 0, 256)] for z, a in zip((h0, h1, h2), own)]
    level_two_group(taps, ta_ref, ba_ref, (here, above), high)
    mask = mask_rows(tab_ref[:, 128:256], 0, Y2, X2, lambda x: x, 2)
    feat = []
    for pair in ((low, mid), (mid, high)):
        acc = conv_group([[(a, 0, 256), (b, 0, 256)] for a, b in zip(*pair)], tb_ref, 0, Y2, 256, 512)
        for q in range(2):
            feat.append((jnp.maximum(acc[:, q * 128 : q * 128 + 128] + bb_ref[...], 0.0) * mask).astype(BF))
    r = iota((C2 * Z2, 128), 0)
    order = one_hot_rows(((r & 3) << 7) | (r >> 2), Z2 * CP)
    out_ref[...] = mm(order, jnp.concatenate(feat, axis=1), NT).astype(BF)


def swap_pairs(count, cores, cores_first):
    def place(y, i):
        return y * count + i if cores_first else i * cores + y

    pairs = []
    for y in range(cores):
        for i in range(count):
            other = i + 1 if i % 2 else i - 1
            target = place(y, other) if 0 <= other < count else place(y ^ 1, i)
            pairs.append((place(y, i), target))
    return pairs


def trade(first, second, axis):
    count = lax.axis_size(axis)
    index = lax.axis_index(axis)
    even = index % 2 == 0
    one = lax.ppermute(first, axis, [(i, i ^ 1) for i in range(count)])
    two = one
    if count > 2 and axis == "gy":
        pairs = [(0, count - 1), (count - 1, 0)] + [(i, i - 1 + i % 2 * 2) for i in range(1, count - 1)]
        two = lax.ppermute(second, axis, pairs)
    elif count > 2:
        axes = ("gx", "gy") if axis == "gx" else ("gy", "gz")
        two = lax.ppermute(second, axes, swap_pairs(count, lax.axis_size("gy"), axis == "gz"))
    below = jnp.where(index > 0, jnp.where(even, two, one), jnp.zeros_like(one))
    above = jnp.where(index < count - 1, jnp.where(even, one, two), jnp.zeros_like(one))
    return below, above


def shift_along(low_edge, high_edge, axis):
    even = lax.axis_index(axis) % 2 == 0
    return trade(jnp.where(even, high_edge, low_edge), jnp.where(even, low_edge, high_edge), axis)


def params():
    return pltpu.CompilerParams(vmem_limit_bytes=VMEM_BYTES)


def cost(seconds):
    return pl.CostEstimate(flops=int(1e15 * seconds), bytes_accessed=0, transcendentals=0)


def shaped(*shape):
    return jax.ShapeDtypeStruct(shape, BF)


def pad_lanes(value):
    return jnp.pad(value, [(0, 0)] * (value.ndim - 1) + [(0, CP - value.shape[-1])])


def local(
    volume, tissue, w_down1, b_down1, w_conv1a, b_conv1a, w_conv1b, b_conv1b,
    w_down2, b_down2, w_conv2a, b_conv2a, w_conv2b, b_conv2b,
):
    depth = volume.shape[1]
    kz = C0 * depth
    lanes1 = Z1 * C1
    half = depth // 2
    t1a = banded(w_conv1a, 4, C1)
    own, tab1, tab2 = pl.pallas_call(
        down1_kernel,
        in_specs=[pl.BlockSpec(memory_space=pltpu.VMEM)] * 4 + [pl.BlockSpec(memory_space=pl.ANY)],
        out_shape=[shaped(Y1, X1, lanes1), shaped(128, 384), shaped(128, 384)],
        scratch_shapes=[
            pltpu.VMEM((2 * kz, lanes1 // 2), BF),
            pltpu.VMEM((2, Y1 * X1, 2 * kz), BF),
        ],
        compiler_params=params(),
        cost_estimate=cost(4e-6),
    )(volume.reshape(C0, 2, half, -1), jnp.swapaxes(w_down1, 1, 2), b_down1[None], tissue.transpose(1, 2, 0), t1a)

    t2a = banded(w_conv2a, 2, CP)
    t2b = banded(w_conv2b, 2, CP)
    bias1a = b_conv1a[None]

    y_below, y_above = shift_along(own[:HALO], own[Y1 - HALO :], "gy")
    win = jnp.concatenate([y_below, own, y_above], axis=0)
    z_below, z_above = shift_along(win[:, :, :128], win[:, :, lanes1 - 128 :], "gz")
    x_below, x_above = shift_along(win[:, :HALO], win[:, X1 - HALO :], "gx")
    rows = Y1 + 2
    left, right, g2, t1b = pl.pallas_call(
        middle_kernel,
        out_shape=[shaped(ROWS1, X1, lanes1), shaped(ROWS1, X1, lanes1), shaped(rows, X1, 256), banded_shape(4, C1)],
        compiler_params=params(),
        cost_estimate=cost(3e-6),
    )(win, t1a, bias1a, tab1, w_conv1b)

    corner = jnp.concatenate([x_below, x_above], axis=1)
    corner, z_below, z_above, g2 = lax.optimization_barrier((corner, z_below, z_above, g2))
    corner_below, corner_above = shift_along(corner[:, :, :128], corner[:, :, lanes1 - 128 :], "gz")
    x_below = jnp.concatenate([corner_below[:, :HALO], x_below, corner_above[:, :HALO]], axis=2)
    x_above = jnp.concatenate([corner_below[:, HALO:], x_above, corner_above[:, HALO:]], axis=2)
    low = jnp.concatenate([z_below[:, :2], win[:, :2], z_above[:, :2]], axis=2)
    high = jnp.concatenate([z_below[:, X1 - 2 :], win[:, X1 - 2 :], z_above[:, X1 - 2 :]], axis=2)
    g1, g3 = pl.pallas_call(
        outer_kernel,
        out_shape=[shaped(rows, X1, 256), shaped(rows, X1, 128)],
        scratch_shapes=[pltpu.VMEM((ROWS1, X1, 128), BF)] * 4,
        compiler_params=params(),
        cost_estimate=cost(4e-6),
    )(win, left, right, z_below, z_above, t1a, bias1a, tab1)

    feat, down = pl.pallas_call(
        level_one_kernel,
        out_shape=[shaped(Y1 * X1, lanes1), shaped(Y2, X2, Z2 * CP)],
        scratch_shapes=[pltpu.VMEM((ROWS1, EDGE, (Z1 + 4) * C1), BF)] * 3
        + [pltpu.VMEM((rows, X1, (Z1 + 2) * C1), BF)] * 3
        + [pltpu.VMEM((4, Y2 * X2, lanes1), BF)],
        compiler_params=params(),
        cost_estimate=cost(6e-6),
    )(
        x_below, low, high, x_above, g1, g2, g3, t1a, t1b, bias1a, b_conv1b[None],
        pad_lanes(jnp.swapaxes(w_down2, 1, 2).reshape(8 * C1, C2)), pad_lanes(b_down2[None]), tab1, tab2,
    )

    one = pl.pallas_call(
        one_kernel, out_shape=shaped(lanes1, Y1 * X1), compiler_params=params(), cost_estimate=cost(2e-6)
    )(feat)

    y_below, y_above = shift_along(down[:HALO], down[Y2 - HALO :], "gy")
    win = jnp.concatenate([y_below, down, y_above], axis=0)
    x_below, x_above = shift_along(win[:, :HALO], win[:, X2 - HALO :], "gx")
    wide = jnp.concatenate([x_below, win, x_above], axis=1)
    z_below, z_above = shift_along(wide[:, :, : 2 * CP], wide[:, :, 2 * CP :], "gz")
    bias2a = pad_lanes(b_conv2a[None])
    moved = [shaped(Y2 + 2, X2, 2 * CP)] * 3
    middle = pl.pallas_call(
        level_two_middle_kernel,
        out_shape=[shaped(ROWS2, PITCH2, Z2 * CP)] * 3 + moved,
        compiler_params=params(),
        cost_estimate=cost(3e-6),
    )(wide, t2a, bias2a, tab2)
    two = pl.pallas_call(
        level_two_kernel,
        out_shape=shaped(C2 * Z2, Y2 * X2),
        scratch_shapes=[pltpu.VMEM((ROWS2, PITCH2, 2 * CP), BF)] * 6 + [pltpu.VMEM((Y2 + 2, X2, 2 * CP), BF)] * 6,
        compiler_params=params(),
        cost_estimate=cost(5e-6),
    )(*middle, z_below, z_above, t2a, t2b, bias2a, pad_lanes(b_conv2b[None]), tab2)
    return one.reshape(C1, Z1, Y1 * X1), two.reshape(C2, Z2, Y2 * X2)


def solution(mesh):
    block = P(None, "gz", ("gx", "gy"))
    return jax.shard_map(
        local,
        mesh=mesh,
        in_specs=(block,) + (P(),) * 13,
        out_specs=(block, block),
        check_vma=False,
    )
```

```python
import jax
import jax.numpy as jnp
from jax import lax
from jax.experimental import pallas as pl
from jax.experimental.pallas import tpu as pltpu
from jax.sharding import PartitionSpec as P

CX = 64
CY = 32
X1 = CX // 2
Y1 = CY // 2
X2 = X1 // 2
Y2 = Y1 // 2
Z1 = 8
Z2 = 4
C0 = 48
C1 = 64
C2 = 96
CP = 128
HALO = 2
HALO_X = 6
HALO_X2 = 2
XB = 12
XB_BELOW = 2
XB_PITCH = 16
YB = 6
ROWS1 = Y1 + 2 * HALO
ROWS2 = Y2 + 2 * HALO
EDGE = 16
PITCH2 = 32
BF = jnp.bfloat16
F32 = jnp.float32
NN = (((1,), (0,)), ((), ()))
NT = (((1,), (1,)), ((), ()))
VMEM_BYTES = 40 * 1024 * 1024


def mm(a, b, dims=NN):
    return lax.dot_general(a, b, dims, preferred_element_type=F32)


def iota(shape, dim):
    return lax.broadcasted_iota(jnp.int32, shape, dim)


def one_hot(flag):
    return jnp.where(flag, 1.0, 0.0).astype(BF)


def one_hot_rows(key, lanes):
    lane = iota(key.shape, 1)
    return jnp.concatenate([one_hot(key == lane + q) for q in range(0, lanes, 128)], axis=1)


def mask_rows(tab, y_start, rows, pitch, x_of, cell):
    bits = cell.bit_length() - 1
    shape = (rows, pitch, 128)
    y_block = (iota(shape, 0) + (y_start + cell)) >> bits
    x_block = jnp.minimum((x_of(iota(shape, 1)) + XB_BELOW * cell) >> bits, XB - 1)
    hit = one_hot(y_block * XB_PITCH + x_block == iota(shape, 2)).reshape(rows * pitch, 128)
    return mm(hit, tab)


def tissue_tables(t_ref):
    n_y, n_z, n_x = t_ref.shape
    here = lax.axis_index("gz")
    layers = []
    for k in (-1, 0, 1):
        z = here + k
        inside = jnp.where((z >= 0) & (z < n_z), 1.0, 0.0)
        layers.append(t_ref[:, jnp.clip(z, 0, n_z - 1), :].astype(F32) * inside)
    block = iota((128, n_y), 0)
    bits = XB_PITCH.bit_length() - 1
    hot_y = one_hot(lax.axis_index("gy") * 4 - 1 + (block >> bits) == iota((128, n_y), 1))
    block = iota((128, 3 * n_x), 0)
    layer = sum((iota((128, 3 * n_x), 1) >= k * n_x).astype(jnp.int32) for k in (1, 2))
    hot_x = lax.axis_index("gx") * 8 - XB_BELOW + (block & (XB_PITCH - 1)) == iota((128, 3 * n_x), 1) - layer * n_x
    rows = jnp.where(hot_x, mm(hot_y, jnp.concatenate(layers, axis=1).astype(BF)), 0.0).astype(BF)
    shape = (3 * n_x, 384)
    layer = sum((iota(shape, 0) >= k * n_x).astype(jnp.int32) for k in (1, 2))
    lane = iota(shape, 1)

    def spread(first, last):
        place = jnp.where(lane < first, 0, jnp.where(lane < last, 1, 2))
        return mm(rows, one_hot(layer == place)).astype(BF)

    return spread(64, 320), spread(128, 256)


def down1_kernel(
    v_hbm, wd_hbm, b_hbm, t_hbm, wa_hbm, out_ref, ta_ref, tab_ref, tab2_ref,
    v_ref, w_ref, b_ref, t_ref, wa_ref, wd_ref, cells_ref, sems,
):
    half = v_ref.shape[2]
    kz = C0 * half
    lanes = Z1 // 2 * C1
    small = ((t_hbm, t_ref), (wd_hbm, w_ref), (b_hbm, b_ref), (wa_hbm, wa_ref))
    copies = [pltpu.make_async_copy(src, dst, sems.at[n]) for n, (src, dst) in enumerate(small)]
    for n in range(C0 // 16):
        cut = slice(n * 16, n * 16 + 16)
        copies.append(pltpu.make_async_copy(v_hbm.at[cut], v_ref.at[cut], sems.at[len(small) + n]))
    for copy in copies:
        copy.start()

    copies[0].wait()
    tab, tab2 = tissue_tables(t_ref)
    tab_ref[...] = tab
    tab2_ref[...] = tab2
    copies[1].wait()
    copies[2].wait()
    r = iota((kz, 2 * C0), 0)
    l = iota((kz, 2 * C0), 1)
    odd = l >= C0
    spread = one_hot(((r >> 3) == jnp.where(odd, l - C0, l)) & ((r & 1) == odd.astype(jnp.int32)))
    keep = (iota((kz, lanes), 0) & 7) >> 1 == iota((kz, lanes), 1) >> 6
    for ab in range(4):
        pair = w_ref[2 * ab : 2 * ab + 2].reshape(2 * C0, C1)
        wide = jnp.concatenate([pair] * (Z1 // 2), axis=1)
        wd_ref[ab * kz : (ab + 1) * kz, :] = jnp.where(keep, mm(spread, wide), 0.0).astype(BF)

    copies[3].wait()
    fill_banded(wa_ref, ta_ref, 4, C1)
    r = iota((4 * CX, 128), 0)
    select = one_hot_rows(((r & 32) << 2) | (r & 64) | ((r & 31) << 1) | (r >> 7), 4 * CX)
    part = 16 * half
    part = 16 * half
    for n, copy in enumerate(copies[4:]):
        copy.wait()
        for m in range(v_ref.shape[3] // 256):
            v = [v_ref[n * 16 : n * 16 + 16, h, :, m * 256 : m * 256 + 256].reshape(part, 256) for h in range(2)]
            cells = mm(select, jnp.concatenate(v, axis=0), NT).astype(BF)
            for ab in range(4):
                lane = ab * kz + n * part
                for h in range(2):
                    piece = cells[64 * ab : 64 * ab + 64, h * part : h * part + part]
                    cells_ref[h, m * 64 : m * 64 + 64, lane : lane + part] = piece
    mask = mask_rows(tab[:, 128:256], 0, Y1, X1, lambda x: x, 4)
    bias = twice(b_ref)
    for h in range(2):
        acc = mm(cells_ref[h], wd_ref[...])
        for q in range(2):
            value = finish(acc[:, q * 128 : q * 128 + 128], bias, mask, Y1)
            out_ref[:, :, (2 * h + q) * 128 : (2 * h + q + 1) * 128] = value


def twice(b_ref):
    return jnp.concatenate([b_ref[...]] * 2, axis=1)


def fill_banded(w_ref, t_ref, group, pad):
    chan = w_ref.shape[1]
    t_ref[...] = jnp.zeros_like(t_ref)
    for j in range(3):
        for i in range(3):
            for zo in range(group):
                for k in range(3):
                    lane = i * (group + 2) * pad + (zo + k) * pad
                    t_ref[j, zo * pad : zo * pad + chan, lane : lane + chan] = w_ref[9 * i + 3 * j + k]


def banded_shape(group, pad):
    return shaped(3, group * pad, 3 * (group + 2) * pad)


def banded(weights, group, pad):
    def kernel(w_ref, t_ref):
        fill_banded(w_ref, t_ref, group, pad)

    return pl.pallas_call(
        kernel, out_shape=banded_shape(group, pad), compiler_params=params(), cost_estimate=cost(1e-6)
    )(weights)


def conv_group(taps, t_ref, y_first, rows, group_out, group_full):
    pitch = taps[0][0][0].shape[1]
    width = sum(piece[2] for piece in taps[0])
    total = None
    for j in range(3):
        parts = [ref[y_first + j : y_first + j + rows, :, lane : lane + n] for tap in taps for ref, lane, n in tap]
        left = jnp.concatenate([p.reshape(rows * pitch, p.shape[2]) for p in parts], axis=1)
        if width == group_full:
            right = t_ref[j, 0:group_out, :]
        else:
            right = jnp.concatenate([t_ref[j, 0:group_out, i * group_full : i * group_full + width] for i in range(3)], axis=1)
        term = mm(left, right, NT)
        total = term if total is None else total + term
    return total


def finish(acc, bias, mask, rows):
    value = jnp.maximum(acc + bias, 0.0) * mask
    return value.astype(BF).reshape(rows, value.shape[0] // rows, value.shape[1])


def fill_sides(left, right, lane, inner):
    cut = slice(lane, lane + inner.shape[2])
    none = jnp.zeros_like(inner[:, :1])
    left[:, :, cut] = jnp.concatenate([none, inner[:, :-1]], axis=1)
    right[:, :, cut] = jnp.concatenate([inner[:, 1:], none], axis=1)


def middle_kernel(win_ref, t_ref, b_ref, tab_ref, w_ref, left_ref, right_ref, out_ref, next_ref):
    fill_banded(w_ref, next_ref, 4, C1)
    for q in range(4):
        fill_sides(left_ref, right_ref, q * 128, win_ref[:, :, q * 128 : q * 128 + 128])
    rows = Y1 + 2
    mask = mask_rows(tab_ref[:, 128:256], -1, rows, X1, lambda x: x, 4)
    acc = conv_group([[(ref, 128, 384)] for ref in (left_ref, win_ref, right_ref)], t_ref, 0, rows, 256, 384)
    for q in range(2):
        cut = slice(q * 128, q * 128 + 128)
        out_ref[:, :, cut] = finish(acc[:, cut], twice(b_ref), mask, rows)


def outer_kernel(win_ref, left_ref, right_ref, zl_ref, zr_ref, t_ref, b_ref, tab_ref, low_ref, high_ref, ll, lr, hl, hr):
    fill_sides(ll, lr, 0, zl_ref[...])
    fill_sides(hl, hr, 0, zr_ref[...])
    own = (left_ref, win_ref, right_ref)
    rows = Y1 + 2
    mask = mask_rows(tab_ref[...], -1, rows, X1, lambda x: x, 4)
    taps = [[(z, 0, 128), (ref, 0, 256)] for z, ref in zip((ll, zl_ref, lr), own)]
    acc = conv_group(taps, t_ref, 0, rows, 256, 384)
    for q in range(2):
        cut = slice(q * 128, q * 128 + 128)
        low_ref[:, :, cut] = finish(acc[:, cut], twice(b_ref), mask[:, cut], rows)
    taps = [[(ref, 384, 128), (z, 0, 128)] for z, ref in zip((hl, zr_ref, hr), own)]
    acc = conv_group(taps, t_ref, 0, rows, 128, 384)
    high_ref[...] = finish(acc, twice(b_ref), mask[:, 256:384], rows)


def fill_edges(copies, pieces):
    rows, pitch, lanes = copies[0].shape
    for lane in range(0, lanes, 128):
        line = [p[:, :, lane : lane + 128] for p in pieces]
        used = sum(p.shape[1] for p in line)
        for i, copy in enumerate(copies):
            moved = [line[0][:, i:]] + line[1:] if i < line[0].shape[1] else line[1:]
            spare = [jnp.zeros((rows, pitch - used + i, 128), BF)] if pitch - used + i else []
            copy[:, :, lane : lane + 128] = jnp.concatenate(moved + spare, axis=1)


def level_one_kernel(
    xl_ref, low_ref, high_ref, xr_ref, g1_ref, g2_ref, g3_ref, ta_ref, tb_ref, ba_ref, bb_ref, wd_ref, bd_ref, tab_ref, tab2_ref,
    feat_ref, down_ref, e0, e1, e2, i0, i1, i2, side_ref, d_ref,
):
    fill_edges((e0, e1, e2), (xl_ref, low_ref, high_ref, xr_ref))
    rows = Y1 + 2
    mask = mask_rows(tab_ref[...], -1, rows, EDGE, lambda r: jnp.where(r < 8, r - 5, r + X1 - 9), 4)
    for g, (lane, width, out) in enumerate(((0, 384, 256), (256, 384, 256), (512, 256, 128))):
        acc = conv_group([[(e, lane, width)] for e in (e0, e1, e2)], ta_ref, 0, rows, out, 384)
        for q in range(out // 128):
            chunk = 2 * g + q
            which = 0 if chunk == 0 else (2 if chunk == 4 else 1)
            edge = finish(acc[:, q * 128 : q * 128 + 128], twice(ba_ref), mask[:, which * 128 : which * 128 + 128], rows)
            inner = (g1_ref, g2_ref, g3_ref)[g][:, :, q * 128 : q * 128 + 128][:, 1:-1]
            cut = slice(chunk * 128, chunk * 128 + 128)
            i0[:, :X1, cut] = jnp.concatenate([edge[:, 4:6], inner], axis=1)
            i1[:, :X1, cut] = jnp.concatenate([edge[:, 5:6], inner, edge[:, 8:9]], axis=1)
            i2[:, :X1, cut] = jnp.concatenate([inner, edge[:, 8:10]], axis=1)
            i0[:, X1:, cut] = edge
            for i, copy in ((1, i1), (2, i2)):
                copy[:, X1:, cut] = jnp.concatenate([edge[:, i:], jnp.zeros((rows, i, 128), BF)], axis=1)

    def cell_of(r):
        return jnp.where(r < X1, r, jnp.where(r < X1 + 8, r - X1 - 4, r - 8))

    mask = mask_rows(tab_ref[:, 128:256], 0, Y1, X1 + EDGE, cell_of, 4)
    for g in range(2):
        acc = conv_group([[(ref, 256 * g, 384)] for ref in (i0, i1, i2)], tb_ref, 0, Y1, 256, 384)
        for q in range(2):
            value = finish(acc[:, q * 128 : q * 128 + 128], twice(bb_ref), mask, Y1)
            cut = slice((2 * g + q) * 128, (2 * g + q + 1) * 128)
            feat_ref[:, cut] = value[:, :X1].reshape(Y1 * X1, 128)
            side_ref[:, cut] = value[:, X1:].reshape(Y1 * EDGE, 128)

    size = 8 * X1
    quarter = size // 4
    r = iota((size, 128), 0)
    select = one_hot_rows(((r & 48) << 2) | ((r & 64) >> 1) | ((r & 15) << 1) | (r >> 7), size)
    for n in range(Y1 // 8):
        cells = mm(select, feat_ref[n * size : n * size + size, :]).astype(BF)
        for q in range(4):
            d_ref[q, n * quarter : n * quarter + quarter, :] = cells[q * quarter : (q + 1) * quarter]
    select = one_hot_rows(((r & 56) << 2) | ((r & 64) >> 2) | ((r & 7) << 1) | (r >> 7), size)
    cells = mm(select, side_ref[...]).astype(BF)
    for q in range(4):
        d_ref[q, Y2 * X2 :, :] = cells[q * quarter : (q + 1) * quarter]
    inner_mask = mask_rows(tab2_ref[:, 128:256], 0, Y2, X2, lambda x: x, 2)
    side_mask = mask_rows(tab2_ref[:, 128:256], 0, Y2, EDGE // 2, lambda r: jnp.where(r < 4, r - 2, r + X2 - 4), 2)
    for z in range(Z2):
        left = jnp.concatenate([d_ref[q, :, z * 128 : z * 128 + 128] for q in range(4)], axis=1)
        acc = mm(left, wd_ref[...])
        inner = finish(acc[: Y2 * X2], bd_ref[...], inner_mask, Y2)
        side = finish(acc[Y2 * X2 :], bd_ref[...], side_mask, Y2)
        down_ref[:, :, z * CP : z * CP + CP] = jnp.concatenate([side[:, 0:2], inner, side[:, 4:6]], axis=1)


def one_kernel(feat_ref, out_ref):
    lanes = feat_ref.shape[1]
    r = iota((lanes, 128), 0)
    order = one_hot_rows(((r & 7) << 6) | (r >> 3), lanes)
    out_ref[...] = mm(order, feat_ref[...], NT).astype(BF)


def fill_pitch(copies, wide):
    pitch = copies[0].shape[1]
    for lane in range(0, wide.shape[2], 128):
        line = wide[:, :, lane : lane + 128]
        for i, copy in enumerate(copies):
            spare = jnp.zeros((line.shape[0], pitch - line.shape[1] + i, 128), BF)
            copy[:, :, lane : lane + 128] = jnp.concatenate([line[:, i:], spare], axis=1)


def level_two_group(taps, t_ref, b_ref, masks, moved):
    rows = Y2 + 2
    acc = conv_group(taps, t_ref, 0, rows, 256, 512)
    for q in range(2):
        cut = slice(q * 128, q * 128 + 128)
        value = finish(acc[:, cut], b_ref[...], masks[q], rows)
        for i, ref in enumerate(moved):
            ref[:, :, cut] = value[:, i : i + X2]


def level_two_masks(tab_ref):
    mask = mask_rows(tab_ref[...], -1, Y2 + 2, PITCH2, lambda x: x - 1, 2)
    return [mask[:, q * 128 : q * 128 + 128] for q in range(3)]


def level_two_middle_kernel(wide_ref, t_ref, b_ref, tab_ref, a0, a1, a2, m0, m1, m2):
    fill_pitch((a0, a1, a2), wide_ref[...])
    here = level_two_masks(tab_ref)[1]
    level_two_group([[(a, 0, 512)] for a in (a0, a1, a2)], t_ref, b_ref, (here, here), (m0, m1, m2))


def level_two_kernel(
    a0, a1, a2, m0, m1, m2, zl_ref, zr_ref, ta_ref, tb_ref, ba_ref, bb_ref, tab_ref, out_ref,
    l0, l1, l2, h0, h1, h2, i0, i1, i2, j0, j1, j2,
):
    fill_pitch((l0, l1, l2), zl_ref[...])
    fill_pitch((h0, h1, h2), zr_ref[...])
    below, here, above = level_two_masks(tab_ref)
    own, mid, low, high = (a0, a1, a2), (m0, m1, m2), (i0, i1, i2), (j0, j1, j2)
    taps = [[(z, 0, 256), (a, 0, 256)] for z, a in zip((l0, l1, l2), own)]
    level_two_group(taps, ta_ref, ba_ref, (below, here), low)
    taps = [[(a, 256, 256), (z, 0, 256)] for z, a in zip((h0, h1, h2), own)]
    level_two_group(taps, ta_ref, ba_ref, (here, above), high)
    mask = mask_rows(tab_ref[:, 128:256], 0, Y2, X2, lambda x: x, 2)
    feat = []
    for pair in ((low, mid), (mid, high)):
        acc = conv_group([[(a, 0, 256), (b, 0, 256)] for a, b in zip(*pair)], tb_ref, 0, Y2, 256, 512)
        for q in range(2):
            feat.append((jnp.maximum(acc[:, q * 128 : q * 128 + 128] + bb_ref[...], 0.0) * mask).astype(BF))
    r = iota((C2 * Z2, 128), 0)
    order = one_hot_rows(((r & 3) << 7) | (r >> 2), Z2 * CP)
    out_ref[...] = mm(order, jnp.concatenate(feat, axis=1), NT).astype(BF)


def swap_pairs(count, cores, cores_first):
    def place(y, i):
        return y * count + i if cores_first else i * cores + y

    pairs = []
    for y in range(cores):
        for i in range(count):
            other = i + 1 if i % 2 else i - 1
            target = place(y, other) if 0 <= other < count else place(y ^ 1, i)
            pairs.append((place(y, i), target))
    return pairs


def trade(first, second, axis):
    count = lax.axis_size(axis)
    index = lax.axis_index(axis)
    even = index % 2 == 0
    one = lax.ppermute(first, axis, [(i, i ^ 1) for i in range(count)])
    two = one
    if count > 2 and axis == "gy":
        pairs = [(0, count - 1), (count - 1, 0)] + [(i, i - 1 + i % 2 * 2) for i in range(1, count - 1)]
        two = lax.ppermute(second, axis, pairs)
    elif count > 2:
        axes = ("gx", "gy") if axis == "gx" else ("gy", "gz")
        two = lax.ppermute(second, axes, swap_pairs(count, lax.axis_size("gy"), axis == "gz"))
    below = jnp.where(index > 0, jnp.where(even, two, one), jnp.zeros_like(one))
    above = jnp.where(index < count - 1, jnp.where(even, one, two), jnp.zeros_like(one))
    return below, above


def shift_along(low_edge, high_edge, axis):
    even = lax.axis_index(axis) % 2 == 0
    return trade(jnp.where(even, high_edge, low_edge), jnp.where(even, low_edge, high_edge), axis)


def params():
    return pltpu.CompilerParams(vmem_limit_bytes=VMEM_BYTES)


def cost(seconds):
    return pl.CostEstimate(flops=int(1e15 * seconds), bytes_accessed=0, transcendentals=0)


def shaped(*shape):
    return jax.ShapeDtypeStruct(shape, BF)


def pad_lanes(value):
    return jnp.pad(value, [(0, 0)] * (value.ndim - 1) + [(0, CP - value.shape[-1])])


def local(
    volume, tissue, w_down1, b_down1, w_conv1a, b_conv1a, w_conv1b, b_conv1b,
    w_down2, b_down2, w_conv2a, b_conv2a, w_conv2b, b_conv2b,
):
    depth = volume.shape[1]
    kz = C0 * depth
    lanes1 = Z1 * C1
    half = depth // 2
    operands = [volume.reshape(C0, 2, half, -1), jnp.swapaxes(w_down1, 1, 2), b_down1[None], tissue.transpose(1, 2, 0), w_conv1a]
    operands = [pltpu.with_memory_space_constraint(x, pltpu.HBM) for x in operands]
    own, t1a, tab1, tab2 = pl.pallas_call(
        down1_kernel,
        in_specs=[pl.BlockSpec(memory_space=pltpu.HBM)] * 5,
        out_shape=[shaped(Y1, X1, lanes1), banded_shape(4, C1), shaped(128, 384), shaped(128, 384)],
        scratch_shapes=[pltpu.VMEM(x.shape, x.dtype) for x in operands]
        + [
            pltpu.VMEM((2 * kz, lanes1 // 2), BF),
            pltpu.VMEM((2, Y1 * X1, 2 * kz), BF),
            pltpu.SemaphoreType.DMA((4 + C0 // 16,)),
        ],
        compiler_params=params(),
        cost_estimate=cost(4e-6),
    )(*operands)

    t2a = banded(w_conv2a, 2, CP)
    t2b = banded(w_conv2b, 2, CP)
    bias1a = b_conv1a[None]

    y_below, y_above = shift_along(own[:HALO], own[Y1 - HALO :], "gy")
    win = jnp.concatenate([y_below, own, y_above], axis=0)
    z_below, z_above = shift_along(win[:, :, :128], win[:, :, lanes1 - 128 :], "gz")
    x_below, x_above = shift_along(win[:, :HALO_X], win[:, X1 - HALO_X :], "gx")
    rows = Y1 + 2
    left, right, g2, t1b = pl.pallas_call(
        middle_kernel,
        out_shape=[shaped(ROWS1, X1, lanes1), shaped(ROWS1, X1, lanes1), shaped(rows, X1, 256), banded_shape(4, C1)],
        compiler_params=params(),
        cost_estimate=cost(3e-6),
    )(win, t1a, bias1a, tab1, w_conv1b)

    corner = jnp.concatenate([x_below, x_above], axis=1)
    corner, z_below, z_above, g2 = lax.optimization_barrier((corner, z_below, z_above, g2))
    corner_below, corner_above = shift_along(corner[:, :, :128], corner[:, :, lanes1 - 128 :], "gz")
    x_below = jnp.concatenate([corner_below[:, :HALO_X], x_below, corner_above[:, :HALO_X]], axis=2)
    x_above = jnp.concatenate([corner_below[:, HALO_X:], x_above, corner_above[:, HALO_X:]], axis=2)
    low = jnp.concatenate([z_below[:, :2], win[:, :2], z_above[:, :2]], axis=2)
    high = jnp.concatenate([z_below[:, X1 - 2 :], win[:, X1 - 2 :], z_above[:, X1 - 2 :]], axis=2)
    g1, g3 = pl.pallas_call(
        outer_kernel,
        out_shape=[shaped(rows, X1, 256), shaped(rows, X1, 128)],
        scratch_shapes=[pltpu.VMEM((ROWS1, X1, 128), BF)] * 4,
        compiler_params=params(),
        cost_estimate=cost(4e-6),
    )(win, left, right, z_below, z_above, t1a, bias1a, tab1)

    feat, down = pl.pallas_call(
        level_one_kernel,
        out_shape=[shaped(Y1 * X1, lanes1), shaped(Y2, X2 + 2 * HALO_X2, Z2 * CP)],
        scratch_shapes=[pltpu.VMEM((ROWS1, EDGE, (Z1 + 4) * C1), BF)] * 3
        + [pltpu.VMEM((rows, X1 + EDGE, (Z1 + 2) * C1), BF)] * 3
        + [pltpu.VMEM((Y1 * EDGE, lanes1), BF), pltpu.VMEM((4, Y2 * (X2 + EDGE // 2), lanes1), BF)],
        compiler_params=params(),
        cost_estimate=cost(6e-6),
    )(
        x_below, low, high, x_above, g1, g2, g3, t1a, t1b, bias1a, b_conv1b[None],
        pad_lanes(jnp.swapaxes(w_down2, 1, 2).reshape(8 * C1, C2)), pad_lanes(b_down2[None]), tab1, tab2,
    )

    y_below, y_above = shift_along(down[:HALO], down[Y2 - HALO :], "gy")
    wide = jnp.concatenate([y_below, down, y_above], axis=0)
    feat, wide = lax.optimization_barrier((feat, wide))
    one = pl.pallas_call(
        one_kernel, out_shape=shaped(lanes1, Y1 * X1), compiler_params=params(), cost_estimate=cost(2e-6)
    )(feat)
    z_below, z_above = shift_along(wide[:, :, : 2 * CP], wide[:, :, 2 * CP :], "gz")
    bias2a = pad_lanes(b_conv2a[None])
    moved = [shaped(Y2 + 2, X2, 2 * CP)] * 3
    middle = pl.pallas_call(
        level_two_middle_kernel,
        out_shape=[shaped(ROWS2, PITCH2, Z2 * CP)] * 3 + moved,
        compiler_params=params(),
        cost_estimate=cost(3e-6),
    )(wide, t2a, bias2a, tab2)
    two = pl.pallas_call(
        level_two_kernel,
        out_shape=shaped(C2 * Z2, Y2 * X2),
        scratch_shapes=[pltpu.VMEM((ROWS2, PITCH2, 2 * CP), BF)] * 6 + [pltpu.VMEM((Y2 + 2, X2, 2 * CP), BF)] * 6,
        compiler_params=params(),
        cost_estimate=cost(5e-6),
    )(*middle, z_below, z_above, t2a, t2b, bias2a, pad_lanes(b_conv2b[None]), tab2)
    return one.reshape(C1, Z1, Y1 * X1), two.reshape(C2, Z2, Y2 * X2)


def solution(mesh):
    block = P(None, "gz", ("gx", "gy"))
    return jax.shard_map(
        local,
        mesh=mesh,
        in_specs=(block,) + (P(),) * 13,
        out_specs=(block, block),
        check_vma=False,
    )
```

```python
import jax
import jax.numpy as jnp
from jax import lax
from jax.experimental import pallas as pl
from jax.experimental.pallas import tpu as pltpu
from jax.sharding import PartitionSpec as P

CX = 64
CY = 32
X1 = CX // 2
Y1 = CY // 2
X2 = X1 // 2
Y2 = Y1 // 2
Z1 = 8
Z2 = 4
C0 = 48
C1 = 64
C2 = 96
CP = 128
HALO = 2
HALO_X = 6
HALO_X2 = 2
XB = 12
XB_BELOW = 2
XB_PITCH = 16
YB = 6
ROWS1 = Y1 + 2 * HALO
ROWS2 = Y2 + 2 * HALO
EDGE = 16
PITCH2 = 32
BF = jnp.bfloat16
F32 = jnp.float32
NN = (((1,), (0,)), ((), ()))
NT = (((1,), (1,)), ((), ()))
VMEM_BYTES = 40 * 1024 * 1024


def mm(a, b, dims=NN):
    return lax.dot_general(a, b, dims, preferred_element_type=F32)


def iota(shape, dim):
    return lax.broadcasted_iota(jnp.int32, shape, dim)


def one_hot(flag):
    return jnp.where(flag, 1.0, 0.0).astype(BF)


def one_hot_rows(key, lanes):
    lane = iota(key.shape, 1)
    return jnp.concatenate([one_hot(key == lane + q) for q in range(0, lanes, 128)], axis=1)


def mask_rows(tab, y_start, rows, pitch, x_of, cell):
    bits = cell.bit_length() - 1
    shape = (rows, pitch, 128)
    y_block = (iota(shape, 0) + (y_start + cell)) >> bits
    x_block = jnp.minimum((x_of(iota(shape, 1)) + XB_BELOW * cell) >> bits, XB - 1)
    hit = one_hot(y_block * XB_PITCH + x_block == iota(shape, 2)).reshape(rows * pitch, 128)
    return mm(hit, tab)


def tissue_tables(t_ref):
    n_y, n_z, n_x = t_ref.shape
    here = lax.axis_index("gz")
    layers = []
    for k in (-1, 0, 1):
        z = here + k
        inside = jnp.where((z >= 0) & (z < n_z), 1.0, 0.0)
        layers.append(t_ref[:, jnp.clip(z, 0, n_z - 1), :].astype(F32) * inside)
    block = iota((128, n_y), 0)
    bits = XB_PITCH.bit_length() - 1
    hot_y = one_hot(lax.axis_index("gy") * 4 - 1 + (block >> bits) == iota((128, n_y), 1))
    block = iota((128, 3 * n_x), 0)
    layer = sum((iota((128, 3 * n_x), 1) >= k * n_x).astype(jnp.int32) for k in (1, 2))
    hot_x = lax.axis_index("gx") * 8 - XB_BELOW + (block & (XB_PITCH - 1)) == iota((128, 3 * n_x), 1) - layer * n_x
    rows = jnp.where(hot_x, mm(hot_y, jnp.concatenate(layers, axis=1).astype(BF)), 0.0).astype(BF)
    shape = (3 * n_x, 384)
    layer = sum((iota(shape, 0) >= k * n_x).astype(jnp.int32) for k in (1, 2))
    lane = iota(shape, 1)

    def spread(first, last):
        place = jnp.where(lane < first, 0, jnp.where(lane < last, 1, 2))
        return mm(rows, one_hot(layer == place)).astype(BF)

    return spread(64, 320), spread(128, 256)


def down1_kernel(
    v_hbm, wd_hbm, b_hbm, t_hbm, wa_hbm, out_ref, ta_ref, tab_ref, tab2_ref,
    v_ref, w_ref, b_ref, t_ref, wa_ref, wd_ref, cells_ref, sems,
):
    half = v_ref.shape[2]
    kz = C0 * half
    part = 16 * half
    lanes = Z1 // 2 * C1
    small = ((t_hbm, t_ref), (wd_hbm, w_ref), (b_hbm, b_ref), (wa_hbm, wa_ref))
    copies = [pltpu.make_async_copy(src, dst, sems.at[n]) for n, (src, dst) in enumerate(small)]
    for n in range(C0 // 16):
        cut = slice(n * 16, n * 16 + 16)
        copies.append(pltpu.make_async_copy(v_hbm.at[cut], v_ref.at[cut], sems.at[len(small) + n]))
    for copy in copies:
        copy.start()

    copies[0].wait()
    tab, tab2 = tissue_tables(t_ref)
    tab_ref[...] = tab
    tab2_ref[...] = tab2
    copies[1].wait()
    copies[2].wait()
    r = iota((kz, 2 * C0), 0)
    l = iota((kz, 2 * C0), 1)
    odd = l >= C0
    spread = one_hot(((r >> 3) == jnp.where(odd, l - C0, l)) & ((r & 1) == odd.astype(jnp.int32)))
    keep = (iota((kz, lanes), 0) & 7) >> 1 == iota((kz, lanes), 1) >> 6
    for ab in range(4):
        pair = w_ref[2 * ab : 2 * ab + 2].reshape(2 * C0, C1)
        wide = jnp.concatenate([pair] * (Z1 // 2), axis=1)
        block = jnp.where(keep, mm(spread, wide), 0.0).astype(BF)
        for n in range(C0 // 16):
            wd_ref[n, ab * part : ab * part + part, :] = block[n * part : n * part + part]

    copies[3].wait()
    fill_banded(wa_ref, ta_ref, 4, C1)
    r = iota((4 * CX, 128), 0)
    select = one_hot_rows(((r & 32) << 2) | (r & 64) | ((r & 31) << 1) | (r >> 7), 4 * CX)
    part = 16 * half
    acc = [0.0, 0.0]
    for n, copy in enumerate(copies[4:]):
        copy.wait()
        for m in range(v_ref.shape[3] // 256):
            v = [v_ref[n * 16 : n * 16 + 16, h, :, m * 256 : m * 256 + 256].reshape(part, 256) for h in range(2)]
            cells = mm(select, jnp.concatenate(v, axis=0), NT).astype(BF)
            for ab in range(4):
                for h in range(2):
                    piece = cells[64 * ab : 64 * ab + 64, h * part : h * part + part]
                    cells_ref[n, h, m * 64 : m * 64 + 64, ab * part : ab * part + part] = piece
        acc = [acc[h] + mm(cells_ref[n, h], wd_ref[n]) for h in range(2)]
    mask = mask_rows(tab[:, 128:256], 0, Y1, X1, lambda x: x, 4)
    bias = twice(b_ref)
    for h in range(2):
        for q in range(2):
            value = finish(acc[h][:, q * 128 : q * 128 + 128], bias, mask, Y1)
            out_ref[:, :, (2 * h + q) * 128 : (2 * h + q + 1) * 128] = value


def twice(b_ref):
    return jnp.concatenate([b_ref[...]] * 2, axis=1)


def fill_banded(w_ref, t_ref, group, pad):
    chan = w_ref.shape[1]
    t_ref[...] = jnp.zeros_like(t_ref)
    for j in range(3):
        for i in range(3):
            for zo in range(group):
                for k in range(3):
                    lane = i * (group + 2) * pad + (zo + k) * pad
                    t_ref[j, zo * pad : zo * pad + chan, lane : lane + chan] = w_ref[9 * i + 3 * j + k]


def banded_shape(group, pad):
    return shaped(3, group * pad, 3 * (group + 2) * pad)


def banded(weights, group, pad):
    def kernel(w_ref, t_ref):
        fill_banded(w_ref, t_ref, group, pad)

    return pl.pallas_call(
        kernel, out_shape=banded_shape(group, pad), compiler_params=params(), cost_estimate=cost(1e-6)
    )(weights)


def conv_group(taps, t_ref, y_first, rows, group_out, group_full):
    pitch = taps[0][0][0].shape[1]
    width = sum(piece[2] for piece in taps[0])
    total = None
    for j in range(3):
        parts = [ref[y_first + j : y_first + j + rows, :, lane : lane + n] for tap in taps for ref, lane, n in tap]
        left = jnp.concatenate([p.reshape(rows * pitch, p.shape[2]) for p in parts], axis=1)
        if width == group_full:
            right = t_ref[j, 0:group_out, :]
        else:
            right = jnp.concatenate([t_ref[j, 0:group_out, i * group_full : i * group_full + width] for i in range(3)], axis=1)
        term = mm(left, right, NT)
        total = term if total is None else total + term
    return total


def finish(acc, bias, mask, rows):
    value = jnp.maximum(acc + bias, 0.0) * mask
    return value.astype(BF).reshape(rows, value.shape[0] // rows, value.shape[1])


def fill_sides(left, right, lane, inner):
    cut = slice(lane, lane + inner.shape[2])
    none = jnp.zeros_like(inner[:, :1])
    left[:, :, cut] = jnp.concatenate([none, inner[:, :-1]], axis=1)
    right[:, :, cut] = jnp.concatenate([inner[:, 1:], none], axis=1)


def middle_kernel(win_ref, t_ref, b_ref, tab_ref, w_ref, left_ref, right_ref, out_ref, next_ref):
    fill_banded(w_ref, next_ref, 4, C1)
    for q in range(4):
        fill_sides(left_ref, right_ref, q * 128, win_ref[:, :, q * 128 : q * 128 + 128])
    rows = Y1 + 2
    mask = mask_rows(tab_ref[:, 128:256], -1, rows, X1, lambda x: x, 4)
    acc = conv_group([[(ref, 128, 384)] for ref in (left_ref, win_ref, right_ref)], t_ref, 0, rows, 256, 384)
    for q in range(2):
        cut = slice(q * 128, q * 128 + 128)
        out_ref[:, :, cut] = finish(acc[:, cut], twice(b_ref), mask, rows)


def outer_kernel(win_ref, left_ref, right_ref, zl_ref, zr_ref, t_ref, b_ref, tab_ref, low_ref, high_ref, ll, lr, hl, hr):
    fill_sides(ll, lr, 0, zl_ref[...])
    fill_sides(hl, hr, 0, zr_ref[...])
    own = (left_ref, win_ref, right_ref)
    rows = Y1 + 2
    mask = mask_rows(tab_ref[...], -1, rows, X1, lambda x: x, 4)
    taps = [[(z, 0, 128), (ref, 0, 256)] for z, ref in zip((ll, zl_ref, lr), own)]
    acc = conv_group(taps, t_ref, 0, rows, 256, 384)
    for q in range(2):
        cut = slice(q * 128, q * 128 + 128)
        low_ref[:, :, cut] = finish(acc[:, cut], twice(b_ref), mask[:, cut], rows)
    taps = [[(ref, 384, 128), (z, 0, 128)] for z, ref in zip((hl, zr_ref, hr), own)]
    acc = conv_group(taps, t_ref, 0, rows, 128, 384)
    high_ref[...] = finish(acc, twice(b_ref), mask[:, 256:384], rows)


def fill_edges(copies, pieces):
    pitch = copies[0].shape[1]
    for i, copy in enumerate(copies):
        line = [pieces[0][:, i:]] + pieces[1:]
        if i:
            line.append(jnp.zeros((copy.shape[0], i, pieces[0].shape[2]), BF))
        copy[...] = jnp.concatenate(line, axis=1)


def edge_masks(tab_ref):
    mask = mask_rows(tab_ref[...], -1, Y1 + 2, EDGE, lambda r: jnp.where(r < 8, r - 5, r + X1 - 9), 4)
    return [mask[:, q * 128 : q * 128 + 128] for q in range(3)]


def edge_group(taps, t_ref, b_ref, masks, inner_ref, moved):
    rows = Y1 + 2
    acc = conv_group(taps, t_ref, 0, rows, 128 * len(masks), 384)
    i0, i1, i2 = moved
    for q, mask in enumerate(masks):
        cut = slice(q * 128, q * 128 + 128)
        edge = finish(acc[:, cut], twice(b_ref), mask, rows)
        inner = inner_ref[:, :, cut][:, 1:-1]
        i0[:, :X1, cut] = jnp.concatenate([edge[:, 4:6], inner], axis=1)
        i1[:, :X1, cut] = jnp.concatenate([edge[:, 5:6], inner, edge[:, 8:9]], axis=1)
        i2[:, :X1, cut] = jnp.concatenate([inner, edge[:, 8:10]], axis=1)
        i0[:, X1:, cut] = edge
        for i, copy in ((1, i1), (2, i2)):
            copy[:, X1:, cut] = jnp.concatenate([edge[:, i:], jnp.zeros((rows, i, 128), BF)], axis=1)


def edge_middle_kernel(xl_ref, win_ref, xr_ref, g_ref, t_ref, b_ref, tab_ref, e0, e1, e2, m0, m1, m2):
    for lane in range(0, Z1 * C1, 128):
        cut = slice(lane, lane + 128)
        inner = win_ref[:, :, cut]
        pieces = [xl_ref[:, :, cut], inner[:, :2], inner[:, X1 - 2 :], xr_ref[:, :, cut]]
        fill_edges([e.at[:, :, cut] for e in (e0, e1, e2)], pieces)
    here = edge_masks(tab_ref)[1]
    edge_group([[(e, 128, 384)] for e in (e0, e1, e2)], t_ref, b_ref, (here, here), g_ref, (m0, m1, m2))


def level_one_kernel(
    zl_ref, zr_ref, cl_ref, cr_ref, e0, e1, e2, m0, m1, m2, g1_ref, g3_ref, ta_ref, tb_ref, ba_ref, bb_ref, wd_ref, bd_ref, tab_ref,
    tab2_ref, feat_ref, down_ref, l0, l1, l2, h0, h1, h2, i0, i1, i2, j0, j1, j2, side_ref, d_ref,
):
    own, mid, low, high = (e0, e1, e2), (m0, m1, m2), (i0, i1, i2), (j0, j1, j2)
    for z_ref, c_ref, copies in ((zl_ref, cl_ref, (l0, l1, l2)), (zr_ref, cr_ref, (h0, h1, h2))):
        inner, corner = z_ref[...], c_ref[...]
        fill_edges(copies, [corner[:, :HALO_X], inner[:, :2], inner[:, X1 - 2 :], corner[:, HALO_X:]])
    below, here, above = edge_masks(tab_ref)
    taps = [[(z, 0, 128), (e, 0, 256)] for z, e in zip((l0, l1, l2), own)]
    edge_group(taps, ta_ref, ba_ref, (below, here), g1_ref, low)
    taps = [[(e, 384, 128), (z, 0, 128)] for z, e in zip((h0, h1, h2), own)]
    edge_group(taps, ta_ref, ba_ref, (above,), g3_ref, high)

    def cell_of(r):
        return jnp.where(r < X1, r, jnp.where(r < X1 + 8, r - X1 - 4, r - 8))

    mask = mask_rows(tab_ref[:, 128:256], 0, Y1, X1 + EDGE, cell_of, 4)
    first = [[(a, 0, 256), (b, 0, 128)] for a, b in zip(low, mid)]
    second = [[(a, 0, 256), (b, 0, 128)] for a, b in zip(mid, high)]
    for g, taps in enumerate((first, second)):
        acc = conv_group(taps, tb_ref, 0, Y1, 256, 384)
        for q in range(2):
            value = finish(acc[:, q * 128 : q * 128 + 128], twice(bb_ref), mask, Y1)
            cut = slice((2 * g + q) * 128, (2 * g + q + 1) * 128)
            feat_ref[:, cut] = value[:, :X1].reshape(Y1 * X1, 128)
            side_ref[:, cut] = value[:, X1:].reshape(Y1 * EDGE, 128)

    size = 8 * X1
    quarter = size // 4
    r = iota((size, 128), 0)
    select = one_hot_rows(((r & 48) << 2) | ((r & 64) >> 1) | ((r & 15) << 1) | (r >> 7), size)
    for n in range(Y1 // 8):
        cells = mm(select, feat_ref[n * size : n * size + size, :]).astype(BF)
        for q in range(4):
            d_ref[q, n * quarter : n * quarter + quarter, :] = cells[q * quarter : (q + 1) * quarter]
    select = one_hot_rows(((r & 56) << 2) | ((r & 64) >> 2) | ((r & 7) << 1) | (r >> 7), size)
    cells = mm(select, side_ref[...]).astype(BF)
    for q in range(4):
        d_ref[q, Y2 * X2 :, :] = cells[q * quarter : (q + 1) * quarter]
    inner_mask = mask_rows(tab2_ref[:, 128:256], 0, Y2, X2, lambda x: x, 2)
    side_mask = mask_rows(tab2_ref[:, 128:256], 0, Y2, EDGE // 2, lambda r: jnp.where(r < 4, r - 2, r + X2 - 4), 2)
    for z in range(Z2):
        left = jnp.concatenate([d_ref[q, :, z * 128 : z * 128 + 128] for q in range(4)], axis=1)
        acc = mm(left, wd_ref[...])
        inner = finish(acc[: Y2 * X2], bd_ref[...], inner_mask, Y2)
        side = finish(acc[Y2 * X2 :], bd_ref[...], side_mask, Y2)
        down_ref[:, :, z * CP : z * CP + CP] = jnp.concatenate([side[:, 0:2], inner, side[:, 4:6]], axis=1)


def one_kernel(feat_ref, out_ref):
    lanes = feat_ref.shape[1]
    r = iota((lanes, 128), 0)
    order = one_hot_rows(((r & 7) << 6) | (r >> 3), lanes)
    out_ref[...] = mm(order, feat_ref[...], NT).astype(BF)


def fill_pitch(copies, wide):
    pitch = copies[0].shape[1]
    for lane in range(0, wide.shape[2], 128):
        line = wide[:, :, lane : lane + 128]
        for i, copy in enumerate(copies):
            spare = jnp.zeros((line.shape[0], pitch - line.shape[1] + i, 128), BF)
            copy[:, :, lane : lane + 128] = jnp.concatenate([line[:, i:], spare], axis=1)


def level_two_group(taps, t_ref, b_ref, masks, moved):
    rows = Y2 + 2
    acc = conv_group(taps, t_ref, 0, rows, 256, 512)
    for q in range(2):
        cut = slice(q * 128, q * 128 + 128)
        value = finish(acc[:, cut], b_ref[...], masks[q], rows)
        for i, ref in enumerate(moved):
            ref[:, :, cut] = value[:, i : i + X2]


def level_two_masks(tab_ref):
    mask = mask_rows(tab_ref[...], -1, Y2 + 2, PITCH2, lambda x: x - 1, 2)
    return [mask[:, q * 128 : q * 128 + 128] for q in range(3)]


def level_two_middle_kernel(wide_ref, t_ref, b_ref, tab_ref, a0, a1, a2, m0, m1, m2):
    fill_pitch((a0, a1, a2), wide_ref[...])
    here = level_two_masks(tab_ref)[1]
    level_two_group([[(a, 0, 512)] for a in (a0, a1, a2)], t_ref, b_ref, (here, here), (m0, m1, m2))


def level_two_kernel(
    a0, a1, a2, m0, m1, m2, zl_ref, zr_ref, ta_ref, tb_ref, ba_ref, bb_ref, tab_ref, out_ref,
    l0, l1, l2, h0, h1, h2, i0, i1, i2, j0, j1, j2,
):
    fill_pitch((l0, l1, l2), zl_ref[...])
    fill_pitch((h0, h1, h2), zr_ref[...])
    below, here, above = level_two_masks(tab_ref)
    own, mid, low, high = (a0, a1, a2), (m0, m1, m2), (i0, i1, i2), (j0, j1, j2)
    taps = [[(z, 0, 256), (a, 0, 256)] for z, a in zip((l0, l1, l2), own)]
    level_two_group(taps, ta_ref, ba_ref, (below, here), low)
    taps = [[(a, 256, 256), (z, 0, 256)] for z, a in zip((h0, h1, h2), own)]
    level_two_group(taps, ta_ref, ba_ref, (here, above), high)
    mask = mask_rows(tab_ref[:, 128:256], 0, Y2, X2, lambda x: x, 2)
    feat = []
    for pair in ((low, mid), (mid, high)):
        acc = conv_group([[(a, 0, 256), (b, 0, 256)] for a, b in zip(*pair)], tb_ref, 0, Y2, 256, 512)
        for q in range(2):
            feat.append((jnp.maximum(acc[:, q * 128 : q * 128 + 128] + bb_ref[...], 0.0) * mask).astype(BF))
    r = iota((C2 * Z2, 128), 0)
    order = one_hot_rows(((r & 3) << 7) | (r >> 2), Z2 * CP)
    out_ref[...] = mm(order, jnp.concatenate(feat, axis=1), NT).astype(BF)


def swap_pairs(count, cores, cores_first):
    def place(y, i):
        return y * count + i if cores_first else i * cores + y

    pairs = []
    for y in range(cores):
        for i in range(count):
            other = i + 1 if i % 2 else i - 1
            target = place(y, other) if 0 <= other < count else place(y ^ 1, i)
            pairs.append((place(y, i), target))
    return pairs


def trade(first, second, axis):
    count = lax.axis_size(axis)
    index = lax.axis_index(axis)
    even = index % 2 == 0
    one = lax.ppermute(first, axis, [(i, i ^ 1) for i in range(count)])
    two = one
    if count > 2 and axis == "gy":
        pairs = [(0, count - 1), (count - 1, 0)] + [(i, i - 1 + i % 2 * 2) for i in range(1, count - 1)]
        two = lax.ppermute(second, axis, pairs)
    elif count > 2:
        axes = ("gx", "gy") if axis == "gx" else ("gy", "gz")
        two = lax.ppermute(second, axes, swap_pairs(count, lax.axis_size("gy"), axis == "gz"))
    below = jnp.where(index > 0, jnp.where(even, two, one), jnp.zeros_like(one))
    above = jnp.where(index < count - 1, jnp.where(even, one, two), jnp.zeros_like(one))
    return below, above


def shift_along(low_edge, high_edge, axis):
    shape = low_edge.shape
    low, high = (edge.reshape(-1, shape[-1]) for edge in (low_edge, high_edge))
    even = lax.axis_index(axis) % 2 == 0
    below, above = trade(jnp.where(even, high, low), jnp.where(even, low, high), axis)
    return below.reshape(shape), above.reshape(shape)


def params():
    return pltpu.CompilerParams(vmem_limit_bytes=VMEM_BYTES)


def cost(seconds):
    return pl.CostEstimate(flops=int(1e15 * seconds), bytes_accessed=0, transcendentals=0)


def shaped(*shape):
    return jax.ShapeDtypeStruct(shape, BF)


def pad_lanes(value):
    return jnp.pad(value, [(0, 0)] * (value.ndim - 1) + [(0, CP - value.shape[-1])])


def local(
    volume, tissue, w_down1, b_down1, w_conv1a, b_conv1a, w_conv1b, b_conv1b,
    w_down2, b_down2, w_conv2a, b_conv2a, w_conv2b, b_conv2b,
):
    depth = volume.shape[1]
    lanes1 = Z1 * C1
    half = depth // 2
    operands = [volume.reshape(C0, 2, half, -1), jnp.swapaxes(w_down1, 1, 2), b_down1[None], tissue.transpose(1, 2, 0), w_conv1a]
    operands = [pltpu.with_memory_space_constraint(x, pltpu.HBM) for x in operands]
    own, t1a, tab1, tab2 = pl.pallas_call(
        down1_kernel,
        in_specs=[pl.BlockSpec(memory_space=pltpu.HBM)] * 5,
        out_shape=[shaped(Y1, X1, lanes1), banded_shape(4, C1), shaped(128, 384), shaped(128, 384)],
        scratch_shapes=[pltpu.VMEM(x.shape, x.dtype) for x in operands]
        + [
            pltpu.VMEM((C0 // 16, 64 * half, lanes1 // 2), BF),
            pltpu.VMEM((C0 // 16, 2, Y1 * X1, 64 * half), BF),
            pltpu.SemaphoreType.DMA((4 + C0 // 16,)),
        ],
        compiler_params=params(),
        cost_estimate=cost(4e-6),
    )(*operands)

    t2a = banded(w_conv2a, 2, CP)
    t2b = banded(w_conv2b, 2, CP)
    bias1a = b_conv1a[None]

    y_below, y_above = shift_along(own[:HALO], own[Y1 - HALO :], "gy")
    win = jnp.concatenate([y_below, own, y_above], axis=0)
    z_below, z_above = shift_along(win[:, :, :128], win[:, :, lanes1 - 128 :], "gz")
    x_below, x_above = shift_along(win[:, :HALO_X], win[:, X1 - HALO_X :], "gx")
    rows = Y1 + 2
    left, right, g2, t1b = pl.pallas_call(
        middle_kernel,
        out_shape=[shaped(ROWS1, X1, lanes1), shaped(ROWS1, X1, lanes1), shaped(rows, X1, 256), banded_shape(4, C1)],
        compiler_params=params(),
        cost_estimate=cost(3e-6),
    )(win, t1a, bias1a, tab1, w_conv1b)

    corner = jnp.concatenate([x_below, x_above], axis=1)
    corner, z_below, z_above, g2 = lax.optimization_barrier((corner, z_below, z_above, g2))
    corner_below, corner_above = shift_along(corner[:, :, :128], corner[:, :, lanes1 - 128 :], "gz")
    g1, g3 = pl.pallas_call(
        outer_kernel,
        out_shape=[shaped(rows, X1, 256), shaped(rows, X1, 128)],
        scratch_shapes=[pltpu.VMEM((ROWS1, X1, 128), BF)] * 4,
        compiler_params=params(),
        cost_estimate=cost(4e-6),
    )(win, left, right, z_below, z_above, t1a, bias1a, tab1)

    wide_x = X1 + EDGE
    edges = pl.pallas_call(
        edge_middle_kernel,
        out_shape=[shaped(ROWS1, EDGE, lanes1)] * 3 + [shaped(rows, wide_x, 256)] * 3,
        compiler_params=params(),
        cost_estimate=cost(3e-6),
    )(x_below, win, x_above, g2, t1a, bias1a, tab1)
    feat, down = pl.pallas_call(
        level_one_kernel,
        out_shape=[shaped(Y1 * X1, lanes1), shaped(Y2, X2 + 2 * HALO_X2, Z2 * CP)],
        scratch_shapes=[pltpu.VMEM((ROWS1, EDGE, 128), BF)] * 6
        + [pltpu.VMEM((rows, wide_x, 256), BF)] * 3
        + [pltpu.VMEM((rows, wide_x, 128), BF)] * 3
        + [pltpu.VMEM((Y1 * EDGE, lanes1), BF), pltpu.VMEM((4, Y2 * (X2 + EDGE // 2), lanes1), BF)],
        compiler_params=params(),
        cost_estimate=cost(6e-6),
    )(
        z_below, z_above, corner_below, corner_above, *edges, g1, g3, t1a, t1b, bias1a, b_conv1b[None],
        pad_lanes(jnp.swapaxes(w_down2, 1, 2).reshape(8 * C1, C2)), pad_lanes(b_down2[None]), tab1, tab2,
    )

    y_below, y_above = shift_along(down[:HALO], down[Y2 - HALO :], "gy")
    wide = jnp.concatenate([y_below, down, y_above], axis=0)
    feat, wide = lax.optimization_barrier((feat, wide))
    one = pl.pallas_call(
        one_kernel, out_shape=shaped(lanes1, Y1 * X1), compiler_params=params(), cost_estimate=cost(2e-6)
    )(feat)
    z_below, z_above = shift_along(wide[:, :, : 2 * CP], wide[:, :, 2 * CP :], "gz")
    bias2a = pad_lanes(b_conv2a[None])
    moved = [shaped(Y2 + 2, X2, 2 * CP)] * 3
    middle = pl.pallas_call(
        level_two_middle_kernel,
        out_shape=[shaped(ROWS2, PITCH2, Z2 * CP)] * 3 + moved,
        compiler_params=params(),
        cost_estimate=cost(3e-6),
    )(wide, t2a, bias2a, tab2)
    two = pl.pallas_call(
        level_two_kernel,
        out_shape=shaped(C2 * Z2, Y2 * X2),
        scratch_shapes=[pltpu.VMEM((ROWS2, PITCH2, 2 * CP), BF)] * 6 + [pltpu.VMEM((Y2 + 2, X2, 2 * CP), BF)] * 6,
        compiler_params=params(),
        cost_estimate=cost(5e-6),
    )(*middle, z_below, z_above, t2a, t2b, bias2a, pad_lanes(b_conv2b[None]), tab2)
    return one.reshape(C1, Z1, Y1 * X1), two.reshape(C2, Z2, Y2 * X2)


def solution(mesh):
    block = P(None, "gz", ("gx", "gy"))
    return jax.shard_map(
        local,
        mesh=mesh,
        in_specs=(block,) + (P(),) * 13,
        out_specs=(block, block),
        check_vma=False,
    )
```

```python
import jax
import jax.numpy as jnp
from jax import lax
from jax.experimental import pallas as pl
from jax.experimental.pallas import tpu as pltpu
from jax.sharding import PartitionSpec as P

CX = 64
CY = 32
X1 = CX // 2
Y1 = CY // 2
X2 = X1 // 2
Y2 = Y1 // 2
Z1 = 8
Z2 = 4
C0 = 48
C1 = 64
C2 = 96
CP = 128
HALO = 2
HALO_X = 6
HALO_X2 = 2
XB = 12
XB_BELOW = 2
XB_PITCH = 16
YB = 6
ROWS1 = Y1 + 2 * HALO
ROWS2 = Y2 + 2 * HALO
EDGE = 16
PITCH2 = 32
BF = jnp.bfloat16
F32 = jnp.float32
NN = (((1,), (0,)), ((), ()))
NT = (((1,), (1,)), ((), ()))
VMEM_BYTES = 20 * 1024 * 1024


def mm(a, b, dims=NN):
    return lax.dot_general(a, b, dims, preferred_element_type=F32)


def iota(shape, dim):
    return lax.broadcasted_iota(jnp.int32, shape, dim)


def one_hot(flag):
    return jnp.where(flag, 1.0, 0.0).astype(BF)


def one_hot_rows(key, lanes):
    lane = iota(key.shape, 1)
    return jnp.concatenate([one_hot(key == lane + q) for q in range(0, lanes, 128)], axis=1)


def mask_rows(tab, y_start, rows, pitch, x_of, cell):
    bits = cell.bit_length() - 1
    shape = (rows, pitch, 128)
    y_block = (iota(shape, 0) + (y_start + cell)) >> bits
    x_block = jnp.minimum((x_of(iota(shape, 1)) + XB_BELOW * cell) >> bits, XB - 1)
    hit = one_hot(y_block * XB_PITCH + x_block == iota(shape, 2)).reshape(rows * pitch, 128)
    return mm(hit, tab)


def tissue_tables(t_ref):
    n_y, n_z, n_x = t_ref.shape
    here = lax.axis_index("gz")
    layers = []
    for k in (-1, 0, 1):
        z = here + k
        inside = jnp.where((z >= 0) & (z < n_z), 1.0, 0.0)
        layers.append(t_ref[:, jnp.clip(z, 0, n_z - 1), :].astype(F32) * inside)
    block = iota((128, n_y), 0)
    bits = XB_PITCH.bit_length() - 1
    hot_y = one_hot(lax.axis_index("gy") * 4 - 1 + (block >> bits) == iota((128, n_y), 1))
    block = iota((128, 3 * n_x), 0)
    layer = sum((iota((128, 3 * n_x), 1) >= k * n_x).astype(jnp.int32) for k in (1, 2))
    hot_x = lax.axis_index("gx") * 8 - XB_BELOW + (block & (XB_PITCH - 1)) == iota((128, 3 * n_x), 1) - layer * n_x
    rows = jnp.where(hot_x, mm(hot_y, jnp.concatenate(layers, axis=1).astype(BF)), 0.0).astype(BF)
    shape = (3 * n_x, 384)
    layer = sum((iota(shape, 0) >= k * n_x).astype(jnp.int32) for k in (1, 2))
    lane = iota(shape, 1)

    def spread(first, last):
        place = jnp.where(lane < first, 0, jnp.where(lane < last, 1, 2))
        return mm(rows, one_hot(layer == place)).astype(BF)

    return spread(64, 320), spread(128, 256)


def down1_kernel(
    v_hbm, wd_hbm, b_hbm, t_hbm, wa_hbm, out_ref, ta_ref, tab_ref, tab2_ref,
    v_ref, w_ref, b_ref, t_ref, wa_ref, wd_ref, cells_ref, sems,
):
    half = v_ref.shape[2]
    kz = C0 * half
    part = 16 * half
    lanes = Z1 // 2 * C1
    small = ((t_hbm, t_ref), (wd_hbm, w_ref), (b_hbm, b_ref), (wa_hbm, wa_ref))
    copies = [pltpu.make_async_copy(src, dst, sems.at[n]) for n, (src, dst) in enumerate(small)]
    for n in range(C0 // 16):
        cut = slice(n * 16, n * 16 + 16)
        copies.append(pltpu.make_async_copy(v_hbm.at[cut], v_ref.at[cut], sems.at[len(small) + n]))
    for copy in copies:
        copy.start()

    copies[0].wait()
    tab, tab2 = tissue_tables(t_ref)
    tab_ref[...] = tab
    tab2_ref[...] = tab2
    copies[1].wait()
    copies[2].wait()
    r = iota((kz, 2 * C0), 0)
    l = iota((kz, 2 * C0), 1)
    odd = l >= C0
    spread = one_hot(((r >> 3) == jnp.where(odd, l - C0, l)) & ((r & 1) == odd.astype(jnp.int32)))
    keep = (iota((kz, lanes), 0) & 7) >> 1 == iota((kz, lanes), 1) >> 6
    for ab in range(4):
        pair = w_ref[2 * ab : 2 * ab + 2].reshape(2 * C0, C1)
        wide = jnp.concatenate([pair] * (Z1 // 2), axis=1)
        block = jnp.where(keep, mm(spread, wide), 0.0).astype(BF)
        for n in range(C0 // 16):
            wd_ref[n, ab * part : ab * part + part, :] = block[n * part : n * part + part]

    copies[3].wait()
    fill_banded(wa_ref, ta_ref, 4, C1)
    r = iota((4 * CX, 128), 0)
    select = one_hot_rows(((r & 32) << 2) | (r & 64) | ((r & 31) << 1) | (r >> 7), 4 * CX)
    part = 16 * half
    acc = [0.0, 0.0]
    for n, copy in enumerate(copies[4:]):
        copy.wait()
        for m in range(v_ref.shape[3] // 256):
            v = [v_ref[n * 16 : n * 16 + 16, h, :, m * 256 : m * 256 + 256].reshape(part, 256) for h in range(2)]
            cells = mm(select, jnp.concatenate(v, axis=0), NT).astype(BF)
            for ab in range(4):
                for h in range(2):
                    piece = cells[64 * ab : 64 * ab + 64, h * part : h * part + part]
                    cells_ref[n, h, m * 64 : m * 64 + 64, ab * part : ab * part + part] = piece
        acc = [acc[h] + mm(cells_ref[n, h], wd_ref[n]) for h in range(2)]
    mask = mask_rows(tab[:, 128:256], 0, Y1, X1, lambda x: x, 4)
    bias = twice(b_ref)
    for h in range(2):
        for q in range(2):
            value = finish(acc[h][:, q * 128 : q * 128 + 128], bias, mask, Y1)
            out_ref[:, :, (2 * h + q) * 128 : (2 * h + q + 1) * 128] = value


def twice(b_ref):
    return jnp.concatenate([b_ref[...]] * 2, axis=1)


def fill_banded(w_ref, t_ref, group, pad):
    chan = w_ref.shape[1]
    t_ref[...] = jnp.zeros_like(t_ref)
    for j in range(3):
        for i in range(3):
            for zo in range(group):
                for k in range(3):
                    lane = i * (group + 2) * pad + (zo + k) * pad
                    t_ref[j, zo * pad : zo * pad + chan, lane : lane + chan] = w_ref[9 * i + 3 * j + k]


def banded_shape(group, pad):
    return shaped(3, group * pad, 3 * (group + 2) * pad)


def banded(weights, group, pad):
    def kernel(w_ref, t_ref):
        fill_banded(w_ref, t_ref, group, pad)

    return pl.pallas_call(
        kernel, out_shape=banded_shape(group, pad), compiler_params=params(), cost_estimate=cost(1e-6)
    )(weights)


def conv_group(taps, t_ref, y_first, rows, group_out, group_full):
    pitch = taps[0][0][0].shape[1]
    width = sum(piece[2] for piece in taps[0])
    total = None
    for j in range(3):
        parts = [ref[y_first + j : y_first + j + rows, :, lane : lane + n] for tap in taps for ref, lane, n in tap]
        left = jnp.concatenate([p.reshape(rows * pitch, p.shape[2]) for p in parts], axis=1)
        if width == group_full:
            right = t_ref[j, 0:group_out, :]
        else:
            right = jnp.concatenate([t_ref[j, 0:group_out, i * group_full : i * group_full + width] for i in range(3)], axis=1)
        term = mm(left, right, NT)
        total = term if total is None else total + term
    return total


def finish(acc, bias, mask, rows):
    value = jnp.maximum(acc + bias, 0.0) * mask
    return value.astype(BF).reshape(rows, value.shape[0] // rows, value.shape[1])


def fill_sides(left, right, lane, inner):
    cut = slice(lane, lane + inner.shape[2])
    none = jnp.zeros_like(inner[:, :1])
    left[:, :, cut] = jnp.concatenate([none, inner[:, :-1]], axis=1)
    right[:, :, cut] = jnp.concatenate([inner[:, 1:], none], axis=1)


def middle_kernel(win_ref, t_ref, b_ref, tab_ref, w_ref, left_ref, right_ref, out_ref, next_ref):
    fill_banded(w_ref, next_ref, 4, C1)
    for q in range(4):
        fill_sides(left_ref, right_ref, q * 128, win_ref[:, :, q * 128 : q * 128 + 128])
    rows = Y1 + 2
    mask = mask_rows(tab_ref[:, 128:256], -1, rows, X1, lambda x: x, 4)
    acc = conv_group([[(ref, 128, 384)] for ref in (left_ref, win_ref, right_ref)], t_ref, 0, rows, 256, 384)
    for q in range(2):
        cut = slice(q * 128, q * 128 + 128)
        out_ref[:, :, cut] = finish(acc[:, cut], twice(b_ref), mask, rows)


def outer_kernel(win_ref, left_ref, right_ref, zl_ref, zr_ref, t_ref, b_ref, tab_ref, low_ref, high_ref, ll, lr, hl, hr):
    fill_sides(ll, lr, 0, zl_ref[...])
    fill_sides(hl, hr, 0, zr_ref[...])
    own = (left_ref, win_ref, right_ref)
    rows = Y1 + 2
    mask = mask_rows(tab_ref[...], -1, rows, X1, lambda x: x, 4)
    taps = [[(z, 0, 128), (ref, 0, 256)] for z, ref in zip((ll, zl_ref, lr), own)]
    acc = conv_group(taps, t_ref, 0, rows, 256, 384)
    for q in range(2):
        cut = slice(q * 128, q * 128 + 128)
        low_ref[:, :, cut] = finish(acc[:, cut], twice(b_ref), mask[:, cut], rows)
    taps = [[(ref, 384, 128), (z, 0, 128)] for z, ref in zip((hl, zr_ref, hr), own)]
    acc = conv_group(taps, t_ref, 0, rows, 128, 384)
    high_ref[...] = finish(acc, twice(b_ref), mask[:, 256:384], rows)


def fill_edges(copies, pieces):
    pitch = copies[0].shape[1]
    for i, copy in enumerate(copies):
        line = [pieces[0][:, i:]] + pieces[1:]
        if i:
            line.append(jnp.zeros((copy.shape[0], i, pieces[0].shape[2]), BF))
        copy[...] = jnp.concatenate(line, axis=1)


def edge_masks(tab_ref):
    mask = mask_rows(tab_ref[...], -1, Y1 + 2, EDGE, lambda r: jnp.where(r < 8, r - 5, r + X1 - 9), 4)
    return [mask[:, q * 128 : q * 128 + 128] for q in range(3)]


def edge_group(taps, t_ref, b_ref, masks, inner_ref, moved):
    rows = Y1 + 2
    acc = conv_group(taps, t_ref, 0, rows, 128 * len(masks), 384)
    i0, i1, i2 = moved
    for q, mask in enumerate(masks):
        cut = slice(q * 128, q * 128 + 128)
        edge = finish(acc[:, cut], twice(b_ref), mask, rows)
        inner = inner_ref[:, :, cut][:, 1:-1]
        i0[:, :X1, cut] = jnp.concatenate([edge[:, 4:6], inner], axis=1)
        i1[:, :X1, cut] = jnp.concatenate([edge[:, 5:6], inner, edge[:, 8:9]], axis=1)
        i2[:, :X1, cut] = jnp.concatenate([inner, edge[:, 8:10]], axis=1)
        i0[:, X1:, cut] = edge
        for i, copy in ((1, i1), (2, i2)):
            copy[:, X1:, cut] = jnp.concatenate([edge[:, i:], jnp.zeros((rows, i, 128), BF)], axis=1)


def edge_middle_kernel(xl_ref, win_ref, xr_ref, g_ref, t_ref, b_ref, tab_ref, e0, e1, e2, m0, m1, m2):
    for lane in range(0, Z1 * C1, 128):
        cut = slice(lane, lane + 128)
        inner = win_ref[:, :, cut]
        pieces = [xl_ref[:, :, cut], inner[:, :2], inner[:, X1 - 2 :], xr_ref[:, :, cut]]
        fill_edges([e.at[:, :, cut] for e in (e0, e1, e2)], pieces)
    here = edge_masks(tab_ref)[1]
    edge_group([[(e, 128, 384)] for e in (e0, e1, e2)], t_ref, b_ref, (here, here), g_ref, (m0, m1, m2))


def level_one_kernel(
    zl_ref, zr_ref, cl_ref, cr_ref, e0, e1, e2, m0, m1, m2, g1_ref, g3_ref, ta_ref, tb_ref, ba_ref, bb_ref, wd_ref, bd_ref, tab_ref,
    tab2_ref, feat_ref, down_ref, l0, l1, l2, h0, h1, h2, i0, i1, i2, j0, j1, j2, side_ref, d_ref,
):
    own, mid, low, high = (e0, e1, e2), (m0, m1, m2), (i0, i1, i2), (j0, j1, j2)
    for z_ref, c_ref, copies in ((zl_ref, cl_ref, (l0, l1, l2)), (zr_ref, cr_ref, (h0, h1, h2))):
        inner, corner = z_ref[...], c_ref[...]
        fill_edges(copies, [corner[:, :HALO_X], inner[:, :2], inner[:, X1 - 2 :], corner[:, HALO_X:]])
    below, here, above = edge_masks(tab_ref)
    taps = [[(z, 0, 128), (e, 0, 256)] for z, e in zip((l0, l1, l2), own)]
    edge_group(taps, ta_ref, ba_ref, (below, here), g1_ref, low)
    taps = [[(e, 384, 128), (z, 0, 128)] for z, e in zip((h0, h1, h2), own)]
    edge_group(taps, ta_ref, ba_ref, (above,), g3_ref, high)

    def cell_of(r):
        return jnp.where(r < X1, r, jnp.where(r < X1 + 8, r - X1 - 4, r - 8))

    mask = mask_rows(tab_ref[:, 128:256], 0, Y1, X1 + EDGE, cell_of, 4)
    first = [[(a, 0, 256), (b, 0, 128)] for a, b in zip(low, mid)]
    second = [[(a, 0, 256), (b, 0, 128)] for a, b in zip(mid, high)]
    for g, taps in enumerate((first, second)):
        acc = conv_group(taps, tb_ref, 0, Y1, 256, 384)
        for q in range(2):
            value = finish(acc[:, q * 128 : q * 128 + 128], twice(bb_ref), mask, Y1)
            cut = slice((2 * g + q) * 128, (2 * g + q + 1) * 128)
            feat_ref[:, cut] = value[:, :X1].reshape(Y1 * X1, 128)
            side_ref[:, cut] = value[:, X1:].reshape(Y1 * EDGE, 128)

    size = 8 * X1
    quarter = size // 4
    r = iota((size, 128), 0)
    select = one_hot_rows(((r & 48) << 2) | ((r & 64) >> 1) | ((r & 15) << 1) | (r >> 7), size)
    for n in range(Y1 // 8):
        cells = mm(select, feat_ref[n * size : n * size + size, :]).astype(BF)
        for q in range(4):
            d_ref[q, n * quarter : n * quarter + quarter, :] = cells[q * quarter : (q + 1) * quarter]
    select = one_hot_rows(((r & 56) << 2) | ((r & 64) >> 2) | ((r & 7) << 1) | (r >> 7), size)
    cells = mm(select, side_ref[...]).astype(BF)
    for q in range(4):
        d_ref[q, Y2 * X2 :, :] = cells[q * quarter : (q + 1) * quarter]
    inner_mask = mask_rows(tab2_ref[:, 128:256], 0, Y2, X2, lambda x: x, 2)
    side_mask = mask_rows(tab2_ref[:, 128:256], 0, Y2, EDGE // 2, lambda r: jnp.where(r < 4, r - 2, r + X2 - 4), 2)
    for z in range(Z2):
        left = jnp.concatenate([d_ref[q, :, z * 128 : z * 128 + 128] for q in range(4)], axis=1)
        acc = mm(left, wd_ref[...])
        inner = finish(acc[: Y2 * X2], bd_ref[...], inner_mask, Y2)
        side = finish(acc[Y2 * X2 :], bd_ref[...], side_mask, Y2)
        down_ref[:, :, z * CP : z * CP + CP] = jnp.concatenate([side[:, 0:2], inner, side[:, 4:6]], axis=1)


def one_kernel(feat_ref, out_ref):
    lanes = feat_ref.shape[1]
    r = iota((lanes, 128), 0)
    order = one_hot_rows(((r & 7) << 6) | (r >> 3), lanes)
    out_ref[...] = mm(order, feat_ref[...], NT).astype(BF)


def fill_pitch(copies, wide):
    pitch = copies[0].shape[1]
    for lane in range(0, wide.shape[2], 128):
        line = wide[:, :, lane : lane + 128]
        for i, copy in enumerate(copies):
            spare = jnp.zeros((line.shape[0], pitch - line.shape[1] + i, 128), BF)
            copy[:, :, lane : lane + 128] = jnp.concatenate([line[:, i:], spare], axis=1)


def level_two_group(taps, t_ref, b_ref, masks, moved):
    rows = Y2 + 2
    acc = conv_group(taps, t_ref, 0, rows, 256, 512)
    for q in range(2):
        cut = slice(q * 128, q * 128 + 128)
        value = finish(acc[:, cut], b_ref[...], masks[q], rows)
        for i, ref in enumerate(moved):
            ref[:, :, cut] = value[:, i : i + X2]


def level_two_masks(tab_ref):
    mask = mask_rows(tab_ref[...], -1, Y2 + 2, PITCH2, lambda x: x - 1, 2)
    return [mask[:, q * 128 : q * 128 + 128] for q in range(3)]


def level_two_middle_kernel(wide_ref, t_ref, b_ref, tab_ref, a0, a1, a2, m0, m1, m2):
    fill_pitch((a0, a1, a2), wide_ref[...])
    here = level_two_masks(tab_ref)[1]
    level_two_group([[(a, 0, 512)] for a in (a0, a1, a2)], t_ref, b_ref, (here, here), (m0, m1, m2))


def level_two_kernel(
    a0, a1, a2, m0, m1, m2, zl_ref, zr_ref, ta_ref, tb_ref, ba_ref, bb_ref, tab_ref, out_ref,
    l0, l1, l2, h0, h1, h2, i0, i1, i2, j0, j1, j2,
):
    fill_pitch((l0, l1, l2), zl_ref[...])
    fill_pitch((h0, h1, h2), zr_ref[...])
    below, here, above = level_two_masks(tab_ref)
    own, mid, low, high = (a0, a1, a2), (m0, m1, m2), (i0, i1, i2), (j0, j1, j2)
    taps = [[(z, 0, 256), (a, 0, 256)] for z, a in zip((l0, l1, l2), own)]
    level_two_group(taps, ta_ref, ba_ref, (below, here), low)
    taps = [[(a, 256, 256), (z, 0, 256)] for z, a in zip((h0, h1, h2), own)]
    level_two_group(taps, ta_ref, ba_ref, (here, above), high)
    mask = mask_rows(tab_ref[:, 128:256], 0, Y2, X2, lambda x: x, 2)
    feat = []
    for pair in ((low, mid), (mid, high)):
        acc = conv_group([[(a, 0, 256), (b, 0, 256)] for a, b in zip(*pair)], tb_ref, 0, Y2, 256, 512)
        for q in range(2):
            feat.append((jnp.maximum(acc[:, q * 128 : q * 128 + 128] + bb_ref[...], 0.0) * mask).astype(BF))
    r = iota((C2 * Z2, 128), 0)
    order = one_hot_rows(((r & 3) << 7) | (r >> 2), Z2 * CP)
    out_ref[...] = mm(order, jnp.concatenate(feat, axis=1), NT).astype(BF)


def swap_pairs(count, cores, cores_first):
    def place(y, i):
        return y * count + i if cores_first else i * cores + y

    pairs = []
    for y in range(cores):
        for i in range(count):
            other = i + 1 if i % 2 else i - 1
            target = place(y, other) if 0 <= other < count else place(y ^ 1, i)
            pairs.append((place(y, i), target))
    return pairs


def trade(first, second, axis):
    count = lax.axis_size(axis)
    index = lax.axis_index(axis)
    even = index % 2 == 0
    one = lax.ppermute(first, axis, [(i, i ^ 1) for i in range(count)])
    two = one
    if count > 2 and axis == "gy":
        pairs = [(0, count - 1), (count - 1, 0)] + [(i, i - 1 + i % 2 * 2) for i in range(1, count - 1)]
        two = lax.ppermute(second, axis, pairs)
    elif count > 2:
        axes = ("gx", "gy") if axis == "gx" else ("gy", "gz")
        two = lax.ppermute(second, axes, swap_pairs(count, lax.axis_size("gy"), axis == "gz"))
    below = jnp.where(index > 0, jnp.where(even, two, one), jnp.zeros_like(one))
    above = jnp.where(index < count - 1, jnp.where(even, one, two), jnp.zeros_like(one))
    return below, above


def shift_along(low_edge, high_edge, axis):
    shape = low_edge.shape
    low, high = (edge.reshape(-1, shape[-1]) for edge in (low_edge, high_edge))
    even = lax.axis_index(axis) % 2 == 0
    below, above = trade(jnp.where(even, high, low), jnp.where(even, low, high), axis)
    return below.reshape(shape), above.reshape(shape)


def params():
    return pltpu.CompilerParams(vmem_limit_bytes=VMEM_BYTES)


def cost(seconds):
    return pl.CostEstimate(flops=int(1e15 * seconds), bytes_accessed=0, transcendentals=0)


def shaped(*shape):
    return jax.ShapeDtypeStruct(shape, BF)


def pad_lanes(value):
    return jnp.pad(value, [(0, 0)] * (value.ndim - 1) + [(0, CP - value.shape[-1])])


def local(
    volume, tissue, w_down1, b_down1, w_conv1a, b_conv1a, w_conv1b, b_conv1b,
    w_down2, b_down2, w_conv2a, b_conv2a, w_conv2b, b_conv2b,
):
    depth = volume.shape[1]
    lanes1 = Z1 * C1
    half = depth // 2
    operands = [volume.reshape(C0, 2, half, -1), jnp.swapaxes(w_down1, 1, 2), b_down1[None], tissue.transpose(1, 2, 0), w_conv1a]
    operands = [pltpu.with_memory_space_constraint(x, pltpu.HBM) for x in operands]
    own, t1a, tab1, tab2 = pl.pallas_call(
        down1_kernel,
        in_specs=[pl.BlockSpec(memory_space=pltpu.HBM)] * 5,
        out_shape=[shaped(Y1, X1, lanes1), banded_shape(4, C1), shaped(128, 384), shaped(128, 384)],
        scratch_shapes=[pltpu.VMEM(x.shape, x.dtype) for x in operands]
        + [
            pltpu.VMEM((C0 // 16, 64 * half, lanes1 // 2), BF),
            pltpu.VMEM((C0 // 16, 2, Y1 * X1, 64 * half), BF),
            pltpu.SemaphoreType.DMA((4 + C0 // 16,)),
        ],
        compiler_params=params(),
        cost_estimate=cost(4e-6),
    )(*operands)

    t2a = banded(w_conv2a, 2, CP)
    t2b = banded(w_conv2b, 2, CP)
    bias1a = b_conv1a[None]

    y_below, y_above = shift_along(own[:HALO], own[Y1 - HALO :], "gy")
    win = jnp.concatenate([y_below, own, y_above], axis=0)
    z_below, z_above = shift_along(win[:, :, :128], win[:, :, lanes1 - 128 :], "gz")
    x_below, x_above = shift_along(win[:, :HALO_X], win[:, X1 - HALO_X :], "gx")
    rows = Y1 + 2
    left, right, g2, t1b = pl.pallas_call(
        middle_kernel,
        out_shape=[shaped(ROWS1, X1, lanes1), shaped(ROWS1, X1, lanes1), shaped(rows, X1, 256), banded_shape(4, C1)],
        compiler_params=params(),
        cost_estimate=cost(3e-6),
    )(win, t1a, bias1a, tab1, w_conv1b)

    corner = jnp.concatenate([x_below, x_above], axis=1)
    corner, z_below, z_above, g2 = lax.optimization_barrier((corner, z_below, z_above, g2))
    corner_below, corner_above = shift_along(corner[:, :, :128], corner[:, :, lanes1 - 128 :], "gz")
    g1, g3 = pl.pallas_call(
        outer_kernel,
        out_shape=[shaped(rows, X1, 256), shaped(rows, X1, 128)],
        scratch_shapes=[pltpu.VMEM((ROWS1, X1, 128), BF)] * 4,
        compiler_params=params(),
        cost_estimate=cost(4e-6),
    )(win, left, right, z_below, z_above, t1a, bias1a, tab1)

    wide_x = X1 + EDGE
    edges = pl.pallas_call(
        edge_middle_kernel,
        out_shape=[shaped(ROWS1, EDGE, lanes1)] * 3 + [shaped(rows, wide_x, 256)] * 3,
        compiler_params=params(),
        cost_estimate=cost(3e-6),
    )(x_below, win, x_above, g2, t1a, bias1a, tab1)
    feat, down = pl.pallas_call(
        level_one_kernel,
        out_shape=[shaped(Y1 * X1, lanes1), shaped(Y2, X2 + 2 * HALO_X2, Z2 * CP)],
        scratch_shapes=[pltpu.VMEM((ROWS1, EDGE, 128), BF)] * 6
        + [pltpu.VMEM((rows, wide_x, 256), BF)] * 3
        + [pltpu.VMEM((rows, wide_x, 128), BF)] * 3
        + [pltpu.VMEM((Y1 * EDGE, lanes1), BF), pltpu.VMEM((4, Y2 * (X2 + EDGE // 2), lanes1), BF)],
        compiler_params=params(),
        cost_estimate=cost(6e-6),
    )(
        z_below, z_above, corner_below, corner_above, *edges, g1, g3, t1a, t1b, bias1a, b_conv1b[None],
        pad_lanes(jnp.swapaxes(w_down2, 1, 2).reshape(8 * C1, C2)), pad_lanes(b_down2[None]), tab1, tab2,
    )

    y_below, y_above = shift_along(down[:HALO], down[Y2 - HALO :], "gy")
    wide = jnp.concatenate([y_below, down, y_above], axis=0)
    feat, wide = lax.optimization_barrier((feat, wide))
    one = pl.pallas_call(
        one_kernel, out_shape=shaped(lanes1, Y1 * X1), compiler_params=params(), cost_estimate=cost(2e-6)
    )(feat)
    z_below, z_above = shift_along(wide[:, :, : 2 * CP], wide[:, :, 2 * CP :], "gz")
    bias2a = pad_lanes(b_conv2a[None])
    moved = [shaped(Y2 + 2, X2, 2 * CP)] * 3
    middle = pl.pallas_call(
        level_two_middle_kernel,
        out_shape=[shaped(ROWS2, PITCH2, Z2 * CP)] * 3 + moved,
        compiler_params=params(),
        cost_estimate=cost(3e-6),
    )(wide, t2a, bias2a, tab2)
    two = pl.pallas_call(
        level_two_kernel,
        out_shape=shaped(C2 * Z2, Y2 * X2),
        scratch_shapes=[pltpu.VMEM((ROWS2, PITCH2, 2 * CP), BF)] * 6 + [pltpu.VMEM((Y2 + 2, X2, 2 * CP), BF)] * 6,
        compiler_params=params(),
        cost_estimate=cost(5e-6),
    )(*middle, z_below, z_above, t2a, t2b, bias2a, pad_lanes(b_conv2b[None]), tab2)
    return one.reshape(C1, Z1, Y1 * X1), two.reshape(C2, Z2, Y2 * X2)


def solution(mesh):
    block = P(None, "gz", ("gx", "gy"))
    return jax.shard_map(
        local,
        mesh=mesh,
        in_specs=(block,) + (P(),) * 13,
        out_specs=(block, block),
        check_vma=False,
    )
```

```python
import jax
import jax.numpy as jnp
from jax import lax
from jax.experimental import pallas as pl
from jax.experimental.pallas import tpu as pltpu
from jax.sharding import PartitionSpec as P

CX = 64
CY = 32
X1 = CX // 2
Y1 = CY // 2
X2 = X1 // 2
Y2 = Y1 // 2
Z1 = 8
Z2 = 4
C0 = 48
C1 = 64
C2 = 96
CP = 128
HALO = 2
HALO_X = 6
HALO_X2 = 2
XB = 12
XB_BELOW = 2
XB_PITCH = 16
YB = 6
ROWS1 = Y1 + 2 * HALO
ROWS2 = Y2 + 2 * HALO
EDGE = 16
PITCH2 = 32
BF = jnp.bfloat16
F32 = jnp.float32
NN = (((1,), (0,)), ((), ()))
NT = (((1,), (1,)), ((), ()))
VMEM_BYTES = 20 * 1024 * 1024


def mm(a, b, dims=NN):
    return lax.dot_general(a, b, dims, preferred_element_type=F32)


def iota(shape, dim):
    return lax.broadcasted_iota(jnp.int32, shape, dim)


def one_hot(flag):
    return jnp.where(flag, 1.0, 0.0).astype(BF)


def one_hot_rows(key, lanes):
    lane = iota(key.shape, 1)
    return jnp.concatenate([one_hot(key == lane + q) for q in range(0, lanes, 128)], axis=1)


def mask_rows(tab, y_start, rows, pitch, x_of, cell):
    bits = cell.bit_length() - 1
    shape = (rows, pitch, 128)
    y_block = (iota(shape, 0) + (y_start + cell)) >> bits
    x_block = jnp.minimum((x_of(iota(shape, 1)) + XB_BELOW * cell) >> bits, XB - 1)
    hit = one_hot(y_block * XB_PITCH + x_block == iota(shape, 2)).reshape(rows * pitch, 128)
    return mm(hit, tab)


def tissue_tables(t_ref):
    n_y, n_z, n_x = t_ref.shape
    here = lax.axis_index("gz")
    layers = []
    for k in (-1, 0, 1):
        z = here + k
        inside = jnp.where((z >= 0) & (z < n_z), 1.0, 0.0)
        layers.append(t_ref[:, jnp.clip(z, 0, n_z - 1), :].astype(F32) * inside)
    block = iota((128, n_y), 0)
    bits = XB_PITCH.bit_length() - 1
    hot_y = one_hot(lax.axis_index("gy") * 4 - 1 + (block >> bits) == iota((128, n_y), 1))
    block = iota((128, 3 * n_x), 0)
    layer = sum((iota((128, 3 * n_x), 1) >= k * n_x).astype(jnp.int32) for k in (1, 2))
    hot_x = lax.axis_index("gx") * 8 - XB_BELOW + (block & (XB_PITCH - 1)) == iota((128, 3 * n_x), 1) - layer * n_x
    rows = jnp.where(hot_x, mm(hot_y, jnp.concatenate(layers, axis=1).astype(BF)), 0.0).astype(BF)
    shape = (3 * n_x, 384)
    layer = sum((iota(shape, 0) >= k * n_x).astype(jnp.int32) for k in (1, 2))
    lane = iota(shape, 1)

    def spread(first, last):
        place = jnp.where(lane < first, 0, jnp.where(lane < last, 1, 2))
        return mm(rows, one_hot(layer == place)).astype(BF)

    return spread(64, 320), spread(128, 256)


def down1_kernel(
    v_hbm, wd_hbm, b_hbm, t_hbm, wa_hbm, out_ref, ta_ref, tab_ref, tab2_ref,
    v_ref, w_ref, b_ref, t_ref, wa_ref, wd_ref, cells_ref, sems,
):
    half = v_ref.shape[2]
    kz = C0 * half
    part = 16 * half
    lanes = Z1 // 2 * C1
    small = ((t_hbm, t_ref), (wd_hbm, w_ref), (b_hbm, b_ref), (wa_hbm, wa_ref))
    copies = [pltpu.make_async_copy(src, dst, sems.at[n]) for n, (src, dst) in enumerate(small)]
    for n in range(C0 // 16):
        cut = slice(n * 16, n * 16 + 16)
        copies.append(pltpu.make_async_copy(v_hbm.at[cut], v_ref.at[cut], sems.at[len(small) + n]))
    for copy in copies:
        copy.start()

    copies[0].wait()
    tab, tab2 = tissue_tables(t_ref)
    tab_ref[...] = tab
    tab2_ref[...] = tab2
    copies[1].wait()
    copies[2].wait()
    r = iota((kz, 2 * C0), 0)
    l = iota((kz, 2 * C0), 1)
    odd = l >= C0
    spread = one_hot(((r >> 3) == jnp.where(odd, l - C0, l)) & ((r & 1) == odd.astype(jnp.int32)))
    keep = (iota((kz, lanes), 0) & 7) >> 1 == iota((kz, lanes), 1) >> 6
    for ab in range(4):
        pair = w_ref[2 * ab : 2 * ab + 2].reshape(2 * C0, C1)
        wide = jnp.concatenate([pair] * (Z1 // 2), axis=1)
        block = jnp.where(keep, mm(spread, wide), 0.0).astype(BF)
        for n in range(C0 // 16):
            wd_ref[n, ab * part : ab * part + part, :] = block[n * part : n * part + part]

    copies[3].wait()
    fill_banded(wa_ref, ta_ref, 4, C1)
    r = iota((4 * CX, 128), 0)
    select = one_hot_rows(((r & 32) << 2) | (r & 64) | ((r & 31) << 1) | (r >> 7), 4 * CX)
    part = 16 * half
    acc = [0.0, 0.0]
    for n, copy in enumerate(copies[4:]):
        copy.wait()
        for m in range(v_ref.shape[3] // 256):
            v = [v_ref[n * 16 : n * 16 + 16, h, :, m * 256 : m * 256 + 256].reshape(part, 256) for h in range(2)]
            cells = mm(select, jnp.concatenate(v, axis=0), NT).astype(BF)
            for ab in range(4):
                for h in range(2):
                    piece = cells[64 * ab : 64 * ab + 64, h * part : h * part + part]
                    cells_ref[n, h, m * 64 : m * 64 + 64, ab * part : ab * part + part] = piece
        acc = [acc[h] + mm(cells_ref[n, h], wd_ref[n]) for h in range(2)]
    mask = mask_rows(tab[:, 128:256], 0, Y1, X1, lambda x: x, 4)
    bias = twice(b_ref)
    for h in range(2):
        for q in range(2):
            value = finish(acc[h][:, q * 128 : q * 128 + 128], bias, mask, Y1)
            out_ref[:, :, (2 * h + q) * 128 : (2 * h + q + 1) * 128] = value


def twice(b_ref):
    return jnp.concatenate([b_ref[...]] * 2, axis=1)


def fill_banded(w_ref, t_ref, group, pad):
    chan = w_ref.shape[1]
    t_ref[...] = jnp.zeros_like(t_ref)
    for j in range(3):
        for i in range(3):
            for zo in range(group):
                for k in range(3):
                    lane = i * (group + 2) * pad + (zo + k) * pad
                    t_ref[j, zo * pad : zo * pad + chan, lane : lane + chan] = w_ref[9 * i + 3 * j + k]


def banded_shape(group, pad):
    return shaped(3, group * pad, 3 * (group + 2) * pad)


def banded(weights, group, pad):
    def kernel(w_ref, t_ref):
        fill_banded(w_ref, t_ref, group, pad)

    return pl.pallas_call(
        kernel, out_shape=banded_shape(group, pad), compiler_params=params(), cost_estimate=cost(1e-6)
    )(weights)


def conv_group(taps, t_ref, y_first, rows, group_out, group_full):
    pitch = taps[0][0][0].shape[1]
    width = sum(piece[2] for piece in taps[0])
    total = None
    for j in range(3):
        parts = [ref[y_first + j : y_first + j + rows, :, lane : lane + n] for tap in taps for ref, lane, n in tap]
        left = jnp.concatenate([p.reshape(rows * pitch, p.shape[2]) for p in parts], axis=1)
        if width == group_full:
            right = t_ref[j, 0:group_out, :]
        else:
            right = jnp.concatenate([t_ref[j, 0:group_out, i * group_full : i * group_full + width] for i in range(3)], axis=1)
        term = mm(left, right, NT)
        total = term if total is None else total + term
    return total


def finish(acc, bias, mask, rows):
    value = jnp.maximum(acc + bias, 0.0) * mask
    return value.astype(BF).reshape(rows, value.shape[0] // rows, value.shape[1])


def fill_sides(left, right, lane, inner):
    cut = slice(lane, lane + inner.shape[2])
    none = jnp.zeros_like(inner[:, :1])
    left[:, :, cut] = jnp.concatenate([none, inner[:, :-1]], axis=1)
    right[:, :, cut] = jnp.concatenate([inner[:, 1:], none], axis=1)


def middle_kernel(win_ref, t_ref, b_ref, tab_ref, w_ref, left_ref, right_ref, out_ref, next_ref):
    fill_banded(w_ref, next_ref, 4, C1)
    for q in range(4):
        fill_sides(left_ref, right_ref, q * 128, win_ref[:, :, q * 128 : q * 128 + 128])
    rows = Y1 + 2
    mask = mask_rows(tab_ref[:, 128:256], -1, rows, X1, lambda x: x, 4)
    acc = conv_group([[(ref, 128, 384)] for ref in (left_ref, win_ref, right_ref)], t_ref, 0, rows, 256, 384)
    for q in range(2):
        cut = slice(q * 128, q * 128 + 128)
        out_ref[:, :, cut] = finish(acc[:, cut], twice(b_ref), mask, rows)


def outer_kernel(win_ref, left_ref, right_ref, zl_ref, zr_ref, t_ref, b_ref, tab_ref, low_ref, high_ref, ll, lr, hl, hr):
    fill_sides(ll, lr, 0, zl_ref[...])
    fill_sides(hl, hr, 0, zr_ref[...])
    own = (left_ref, win_ref, right_ref)
    rows = Y1 + 2
    mask = mask_rows(tab_ref[...], -1, rows, X1, lambda x: x, 4)
    taps = [[(z, 0, 128), (ref, 0, 256)] for z, ref in zip((ll, zl_ref, lr), own)]
    acc = conv_group(taps, t_ref, 0, rows, 256, 384)
    for q in range(2):
        cut = slice(q * 128, q * 128 + 128)
        low_ref[:, :, cut] = finish(acc[:, cut], twice(b_ref), mask[:, cut], rows)
    taps = [[(ref, 384, 128), (z, 0, 128)] for z, ref in zip((hl, zr_ref, hr), own)]
    acc = conv_group(taps, t_ref, 0, rows, 128, 384)
    high_ref[...] = finish(acc, twice(b_ref), mask[:, 256:384], rows)


def fill_edges(copies, pieces):
    pitch = copies[0].shape[1]
    for i, copy in enumerate(copies):
        line = [pieces[0][:, i:]] + pieces[1:]
        if i:
            line.append(jnp.zeros((copy.shape[0], i, pieces[0].shape[2]), BF))
        copy[...] = jnp.concatenate(line, axis=1)


def edge_masks(tab_ref):
    mask = mask_rows(tab_ref[...], -1, Y1 + 2, EDGE, lambda r: jnp.where(r < 8, r - 5, r + X1 - 9), 4)
    return [mask[:, q * 128 : q * 128 + 128] for q in range(3)]


def edge_group(taps, t_ref, b_ref, masks, inner_ref, moved):
    rows = Y1 + 2
    acc = conv_group(taps, t_ref, 0, rows, 128 * len(masks), 384)
    i0, i1, i2 = moved
    for q, mask in enumerate(masks):
        cut = slice(q * 128, q * 128 + 128)
        edge = finish(acc[:, cut], twice(b_ref), mask, rows)
        inner = inner_ref[:, :, cut][:, 1:-1]
        i0[:, :X1, cut] = jnp.concatenate([edge[:, 4:6], inner], axis=1)
        i1[:, :X1, cut] = jnp.concatenate([edge[:, 5:6], inner, edge[:, 8:9]], axis=1)
        i2[:, :X1, cut] = jnp.concatenate([inner, edge[:, 8:10]], axis=1)
        i0[:, X1:, cut] = edge
        for i, copy in ((1, i1), (2, i2)):
            copy[:, X1:, cut] = jnp.concatenate([edge[:, i:], jnp.zeros((rows, i, 128), BF)], axis=1)


def edge_middle_kernel(xl_ref, win_ref, xr_ref, g_ref, t_ref, b_ref, tab_ref, e0, e1, e2, m0, m1, m2):
    for lane in range(0, Z1 * C1, 128):
        cut = slice(lane, lane + 128)
        inner = win_ref[:, :, cut]
        pieces = [xl_ref[:, :, cut], inner[:, :2], inner[:, X1 - 2 :], xr_ref[:, :, cut]]
        fill_edges([e.at[:, :, cut] for e in (e0, e1, e2)], pieces)
    here = edge_masks(tab_ref)[1]
    edge_group([[(e, 128, 384)] for e in (e0, e1, e2)], t_ref, b_ref, (here, here), g_ref, (m0, m1, m2))


def level_one_kernel(
    zl_ref, zr_ref, cl_ref, cr_ref, e0, e1, e2, m0, m1, m2, g1_ref, g3_ref, ta_ref, tb_ref, ba_ref, bb_ref, wd_ref, bd_ref, tab_ref,
    tab2_ref, feat_ref, down_ref, l0, l1, l2, h0, h1, h2, i0, i1, i2, j0, j1, j2, side_ref, d_ref,
):
    own, mid, low, high = (e0, e1, e2), (m0, m1, m2), (i0, i1, i2), (j0, j1, j2)
    for z_ref, c_ref, copies in ((zl_ref, cl_ref, (l0, l1, l2)), (zr_ref, cr_ref, (h0, h1, h2))):
        inner, corner = z_ref[...], c_ref[...]
        fill_edges(copies, [corner[:, :HALO_X], inner[:, :2], inner[:, X1 - 2 :], corner[:, HALO_X:]])
    below, here, above = edge_masks(tab_ref)
    taps = [[(z, 0, 128), (e, 0, 256)] for z, e in zip((l0, l1, l2), own)]
    edge_group(taps, ta_ref, ba_ref, (below, here), g1_ref, low)
    taps = [[(e, 384, 128), (z, 0, 128)] for z, e in zip((h0, h1, h2), own)]
    edge_group(taps, ta_ref, ba_ref, (above,), g3_ref, high)

    def cell_of(r):
        return jnp.where(r < X1, r, jnp.where(r < X1 + 8, r - X1 - 4, r - 8))

    mask = mask_rows(tab_ref[:, 128:256], 0, Y1, X1 + EDGE, cell_of, 4)
    first = [[(a, 0, 256), (b, 0, 128)] for a, b in zip(low, mid)]
    second = [[(a, 0, 256), (b, 0, 128)] for a, b in zip(mid, high)]
    for g, taps in enumerate((first, second)):
        acc = conv_group(taps, tb_ref, 0, Y1, 256, 384)
        for q in range(2):
            value = finish(acc[:, q * 128 : q * 128 + 128], twice(bb_ref), mask, Y1)
            cut = slice((2 * g + q) * 128, (2 * g + q + 1) * 128)
            feat_ref[:, cut] = value[:, :X1].reshape(Y1 * X1, 128)
            side_ref[:, cut] = value[:, X1:].reshape(Y1 * EDGE, 128)

    size = 8 * X1
    quarter = size // 4
    r = iota((size, 128), 0)
    select = one_hot_rows(((r & 48) << 2) | ((r & 64) >> 1) | ((r & 15) << 1) | (r >> 7), size)
    for n in range(Y1 // 8):
        cells = mm(select, feat_ref[n * size : n * size + size, :]).astype(BF)
        for q in range(4):
            d_ref[q, n * quarter : n * quarter + quarter, :] = cells[q * quarter : (q + 1) * quarter]
    select = one_hot_rows(((r & 56) << 2) | ((r & 64) >> 2) | ((r & 7) << 1) | (r >> 7), size)
    cells = mm(select, side_ref[...]).astype(BF)
    for q in range(4):
        d_ref[q, Y2 * X2 :, :] = cells[q * quarter : (q + 1) * quarter]
    inner_mask = mask_rows(tab2_ref[:, 128:256], 0, Y2, X2, lambda x: x, 2)
    side_mask = mask_rows(tab2_ref[:, 128:256], 0, Y2, EDGE // 2, lambda r: jnp.where(r < 4, r - 2, r + X2 - 4), 2)
    for z in range(Z2):
        left = jnp.concatenate([d_ref[q, :, z * 128 : z * 128 + 128] for q in range(4)], axis=1)
        acc = mm(left, wd_ref[...])
        inner = finish(acc[: Y2 * X2], bd_ref[...], inner_mask, Y2)
        side = finish(acc[Y2 * X2 :], bd_ref[...], side_mask, Y2)
        down_ref[:, :, z * CP : z * CP + CP] = jnp.concatenate([side[:, 0:2], inner, side[:, 4:6]], axis=1)


def one_kernel(feat_ref, out_ref):
    lanes = feat_ref.shape[1]
    r = iota((lanes, 128), 0)
    order = one_hot_rows(((r & 7) << 6) | (r >> 3), lanes)
    out_ref[...] = mm(order, feat_ref[...], NT).astype(BF)


def fill_pitch(copies, wide):
    pitch = copies[0].shape[1]
    for lane in range(0, wide.shape[2], 128):
        line = wide[:, :, lane : lane + 128]
        for i, copy in enumerate(copies):
            spare = jnp.zeros((line.shape[0], pitch - line.shape[1] + i, 128), BF)
            copy[:, :, lane : lane + 128] = jnp.concatenate([line[:, i:], spare], axis=1)


def level_two_group(taps, t_ref, b_ref, masks, moved):
    rows = Y2 + 2
    acc = conv_group(taps, t_ref, 0, rows, 256, 512)
    for q in range(2):
        cut = slice(q * 128, q * 128 + 128)
        value = finish(acc[:, cut], b_ref[...], masks[q], rows)
        for i, ref in enumerate(moved):
            ref[:, :, cut] = value[:, i : i + X2]


def level_two_masks(tab_ref):
    mask = mask_rows(tab_ref[...], -1, Y2 + 2, PITCH2, lambda x: x - 1, 2)
    return [mask[:, q * 128 : q * 128 + 128] for q in range(3)]


def level_two_middle_kernel(wide_ref, t_ref, b_ref, tab_ref, a0, a1, a2, m0, m1, m2):
    fill_pitch((a0, a1, a2), wide_ref[...])
    here = level_two_masks(tab_ref)[1]
    level_two_group([[(a, 0, 512)] for a in (a0, a1, a2)], t_ref, b_ref, (here, here), (m0, m1, m2))


def level_two_kernel(
    a0, a1, a2, m0, m1, m2, zl_ref, zr_ref, ta_ref, tb_ref, ba_ref, bb_ref, tab_ref, out_ref,
    l0, l1, l2, h0, h1, h2, i0, i1, i2, j0, j1, j2,
):
    fill_pitch((l0, l1, l2), zl_ref[...])
    fill_pitch((h0, h1, h2), zr_ref[...])
    below, here, above = level_two_masks(tab_ref)
    own, mid, low, high = (a0, a1, a2), (m0, m1, m2), (i0, i1, i2), (j0, j1, j2)
    taps = [[(z, 0, 256), (a, 0, 256)] for z, a in zip((l0, l1, l2), own)]
    level_two_group(taps, ta_ref, ba_ref, (below, here), low)
    taps = [[(a, 256, 256), (z, 0, 256)] for z, a in zip((h0, h1, h2), own)]
    level_two_group(taps, ta_ref, ba_ref, (here, above), high)
    mask = mask_rows(tab_ref[:, 128:256], 0, Y2, X2, lambda x: x, 2)
    feat = []
    for pair in ((low, mid), (mid, high)):
        acc = conv_group([[(a, 0, 256), (b, 0, 256)] for a, b in zip(*pair)], tb_ref, 0, Y2, 256, 512)
        for q in range(2):
            feat.append((jnp.maximum(acc[:, q * 128 : q * 128 + 128] + bb_ref[...], 0.0) * mask).astype(BF))
    r = iota((C2 * Z2, 128), 0)
    order = one_hot_rows(((r & 3) << 7) | (r >> 2), Z2 * CP)
    out_ref[...] = mm(order, jnp.concatenate(feat, axis=1), NT).astype(BF)


def swap_pairs(count, cores, cores_first):
    def place(y, i):
        return y * count + i if cores_first else i * cores + y

    pairs = []
    for y in range(cores):
        for i in range(count):
            other = i + 1 if i % 2 else i - 1
            target = place(y, other) if 0 <= other < count else place(y ^ 1, i)
            pairs.append((place(y, i), target))
    return pairs


def trade(first, second, axis):
    count = lax.axis_size(axis)
    index = lax.axis_index(axis)
    even = index % 2 == 0
    one = lax.ppermute(first, axis, [(i, i ^ 1) for i in range(count)])
    two = one
    if count > 2 and axis == "gy":
        pairs = [(0, count - 1), (count - 1, 0)] + [(i, i - 1 + i % 2 * 2) for i in range(1, count - 1)]
        two = lax.ppermute(second, axis, pairs)
    elif count > 2:
        axes = ("gx", "gy") if axis == "gx" else ("gy", "gz")
        two = lax.ppermute(second, axes, swap_pairs(count, lax.axis_size("gy"), axis == "gz"))
    below = jnp.where(index > 0, jnp.where(even, two, one), jnp.zeros_like(one))
    above = jnp.where(index < count - 1, jnp.where(even, one, two), jnp.zeros_like(one))
    return below, above


def shift_along(low_edge, high_edge, axis):
    even = lax.axis_index(axis) % 2 == 0
    return trade(jnp.where(even, high_edge, low_edge), jnp.where(even, low_edge, high_edge), axis)


def params():
    return pltpu.CompilerParams(vmem_limit_bytes=VMEM_BYTES)


def cost(seconds):
    return pl.CostEstimate(flops=int(1e15 * seconds), bytes_accessed=0, transcendentals=0)


def shaped(*shape):
    return jax.ShapeDtypeStruct(shape, BF)


def pad_lanes(value):
    return jnp.pad(value, [(0, 0)] * (value.ndim - 1) + [(0, CP - value.shape[-1])])


def local(
    volume, tissue, w_down1, b_down1, w_conv1a, b_conv1a, w_conv1b, b_conv1b,
    w_down2, b_down2, w_conv2a, b_conv2a, w_conv2b, b_conv2b,
):
    depth = volume.shape[1]
    lanes1 = Z1 * C1
    half = depth // 2
    operands = [volume.reshape(C0, 2, half, -1), jnp.swapaxes(w_down1, 1, 2), b_down1[None], tissue.transpose(1, 2, 0), w_conv1a]
    operands = [pltpu.with_memory_space_constraint(x, pltpu.HBM) for x in operands]
    own, t1a, tab1, tab2 = pl.pallas_call(
        down1_kernel,
        in_specs=[pl.BlockSpec(memory_space=pltpu.HBM)] * 5,
        out_shape=[shaped(Y1, X1, lanes1), banded_shape(4, C1), shaped(128, 384), shaped(128, 384)],
        scratch_shapes=[pltpu.VMEM(x.shape, x.dtype) for x in operands]
        + [
            pltpu.VMEM((C0 // 16, 64 * half, lanes1 // 2), BF),
            pltpu.VMEM((C0 // 16, 2, Y1 * X1, 64 * half), BF),
            pltpu.SemaphoreType.DMA((4 + C0 // 16,)),
        ],
        compiler_params=params(),
        cost_estimate=cost(4e-6),
    )(*operands)

    t2a = banded(w_conv2a, 2, CP)
    t2b = banded(w_conv2b, 2, CP)
    bias1a = b_conv1a[None]

    y_below, y_above = shift_along(own[:HALO], own[Y1 - HALO :], "gy")
    win = jnp.concatenate([y_below, own, y_above], axis=0)
    z_below, z_above = shift_along(win[:, :, :128], win[:, :, lanes1 - 128 :], "gz")
    x_below, x_above = shift_along(win[:, :HALO_X], win[:, X1 - HALO_X :], "gx")
    rows = Y1 + 2
    left, right, g2, t1b = pl.pallas_call(
        middle_kernel,
        out_shape=[shaped(ROWS1, X1, lanes1), shaped(ROWS1, X1, lanes1), shaped(rows, X1, 256), banded_shape(4, C1)],
        compiler_params=params(),
        cost_estimate=cost(3e-6),
    )(win, t1a, bias1a, tab1, w_conv1b)

    corner = jnp.concatenate([x_below, x_above], axis=1)
    corner, z_below, z_above, g2 = lax.optimization_barrier((corner, z_below, z_above, g2))
    corner_below, corner_above = shift_along(corner[:, :, :128], corner[:, :, lanes1 - 128 :], "gz")
    g1, g3 = pl.pallas_call(
        outer_kernel,
        out_shape=[shaped(rows, X1, 256), shaped(rows, X1, 128)],
        scratch_shapes=[pltpu.VMEM((ROWS1, X1, 128), BF)] * 4,
        compiler_params=params(),
        cost_estimate=cost(4e-6),
    )(win, left, right, z_below, z_above, t1a, bias1a, tab1)

    wide_x = X1 + EDGE
    edges = pl.pallas_call(
        edge_middle_kernel,
        out_shape=[shaped(ROWS1, EDGE, lanes1)] * 3 + [shaped(rows, wide_x, 256)] * 3,
        compiler_params=params(),
        cost_estimate=cost(3e-6),
    )(x_below, win, x_above, g2, t1a, bias1a, tab1)
    feat, down = pl.pallas_call(
        level_one_kernel,
        out_shape=[shaped(Y1 * X1, lanes1), shaped(Y2, X2 + 2 * HALO_X2, Z2 * CP)],
        scratch_shapes=[pltpu.VMEM((ROWS1, EDGE, 128), BF)] * 6
        + [pltpu.VMEM((rows, wide_x, 256), BF)] * 3
        + [pltpu.VMEM((rows, wide_x, 128), BF)] * 3
        + [pltpu.VMEM((Y1 * EDGE, lanes1), BF), pltpu.VMEM((4, Y2 * (X2 + EDGE // 2), lanes1), BF)],
        compiler_params=params(),
        cost_estimate=cost(6e-6),
    )(
        z_below, z_above, corner_below, corner_above, *edges, g1, g3, t1a, t1b, bias1a, b_conv1b[None],
        pad_lanes(jnp.swapaxes(w_down2, 1, 2).reshape(8 * C1, C2)), pad_lanes(b_down2[None]), tab1, tab2,
    )

    y_below, y_above = shift_along(down[:HALO], down[Y2 - HALO :], "gy")
    wide = jnp.concatenate([y_below, down, y_above], axis=0)
    feat, wide = lax.optimization_barrier((feat, wide))
    one = pl.pallas_call(
        one_kernel, out_shape=shaped(lanes1, Y1 * X1), compiler_params=params(), cost_estimate=cost(2e-6)
    )(feat)
    z_below, z_above = shift_along(wide[:, :, : 2 * CP], wide[:, :, 2 * CP :], "gz")
    bias2a = pad_lanes(b_conv2a[None])
    moved = [shaped(Y2 + 2, X2, 2 * CP)] * 3
    middle = pl.pallas_call(
        level_two_middle_kernel,
        out_shape=[shaped(ROWS2, PITCH2, Z2 * CP)] * 3 + moved,
        compiler_params=params(),
        cost_estimate=cost(3e-6),
    )(wide, t2a, bias2a, tab2)
    two = pl.pallas_call(
        level_two_kernel,
        out_shape=shaped(C2 * Z2, Y2 * X2),
        scratch_shapes=[pltpu.VMEM((ROWS2, PITCH2, 2 * CP), BF)] * 6 + [pltpu.VMEM((Y2 + 2, X2, 2 * CP), BF)] * 6,
        compiler_params=params(),
        cost_estimate=cost(5e-6),
    )(*middle, z_below, z_above, t2a, t2b, bias2a, pad_lanes(b_conv2b[None]), tab2)
    return one.reshape(C1, Z1, Y1 * X1), two.reshape(C2, Z2, Y2 * X2)


def solution(mesh):
    block = P(None, "gz", ("gx", "gy"))
    return jax.shard_map(
        local,
        mesh=mesh,
        in_specs=(block,) + (P(),) * 13,
        out_specs=(block, block),
        check_vma=False,
    )
```

```python
import itertools

import jax
import jax.numpy as jnp
from jax import lax
from jax.experimental import pallas as pl
from jax.experimental.pallas import tpu as pltpu
from jax.sharding import PartitionSpec as P

CX = 64
CY = 32
X1 = CX // 2
Y1 = CY // 2
X2 = X1 // 2
Y2 = Y1 // 2
Z1 = 8
Z2 = 4
C0 = 48
C1 = 64
C2 = 96
CP = 128
HALO = 2
HALO_X = 6
HALO_X2 = 2
XB = 12
XB_BELOW = 2
XB_PITCH = 16
YB = 6
ROWS1 = Y1 + 2 * HALO
ROWS2 = Y2 + 2 * HALO
EDGE = 16
PITCH2 = 32
BF = jnp.bfloat16
F32 = jnp.float32
NN = (((1,), (0,)), ((), ()))
NT = (((1,), (1,)), ((), ()))
VMEM_BYTES = 20 * 1024 * 1024


def mm(a, b, dims=NN):
    return lax.dot_general(a, b, dims, preferred_element_type=F32)


def iota(shape, dim):
    return lax.broadcasted_iota(jnp.int32, shape, dim)


def one_hot(flag):
    return jnp.where(flag, 1.0, 0.0).astype(BF)


def one_hot_rows(key, lanes):
    lane = iota(key.shape, 1)
    return jnp.concatenate([one_hot(key == lane + q) for q in range(0, lanes, 128)], axis=1)


def mask_rows(tab, y_start, rows, pitch, x_of, cell):
    bits = cell.bit_length() - 1
    shape = (rows, pitch, 128)
    y_block = (iota(shape, 0) + (y_start + cell)) >> bits
    x_block = jnp.minimum((x_of(iota(shape, 1)) + XB_BELOW * cell) >> bits, XB - 1)
    hit = one_hot(y_block * XB_PITCH + x_block == iota(shape, 2)).reshape(rows * pitch, 128)
    return mm(hit, tab)


def tissue_tables(t_ref):
    n_y, n_z, n_x = t_ref.shape
    here = lax.axis_index("gz")
    layers = []
    for k in (-1, 0, 1):
        z = here + k
        inside = jnp.where((z >= 0) & (z < n_z), 1.0, 0.0)
        layers.append(t_ref[:, jnp.clip(z, 0, n_z - 1), :].astype(F32) * inside)
    block = iota((128, n_y), 0)
    bits = XB_PITCH.bit_length() - 1
    hot_y = one_hot(lax.axis_index("gy") * 4 - 1 + (block >> bits) == iota((128, n_y), 1))
    block = iota((128, 3 * n_x), 0)
    layer = sum((iota((128, 3 * n_x), 1) >= k * n_x).astype(jnp.int32) for k in (1, 2))
    hot_x = lax.axis_index("gx") * 8 - XB_BELOW + (block & (XB_PITCH - 1)) == iota((128, 3 * n_x), 1) - layer * n_x
    rows = jnp.where(hot_x, mm(hot_y, jnp.concatenate(layers, axis=1).astype(BF)), 0.0).astype(BF)
    shape = (3 * n_x, 384)
    layer = sum((iota(shape, 0) >= k * n_x).astype(jnp.int32) for k in (1, 2))
    lane = iota(shape, 1)

    def spread(first, last):
        place = jnp.where(lane < first, 0, jnp.where(lane < last, 1, 2))
        return mm(rows, one_hot(layer == place)).astype(BF)

    return spread(64, 320), spread(128, 256)


def down1_kernel(
    v_hbm, wd_hbm, b_hbm, t_hbm, wa_hbm, out_ref, ta_ref, tab_ref, tab2_ref,
    v_ref, w_ref, b_ref, t_ref, wa_ref, wd_ref, cells_ref, sems,
):
    half = v_ref.shape[2]
    kz = C0 * half
    part = 16 * half
    lanes = Z1 // 2 * C1
    small = ((t_hbm, t_ref), (wd_hbm, w_ref), (b_hbm, b_ref), (wa_hbm, wa_ref))
    copies = [pltpu.make_async_copy(src, dst, sems.at[n]) for n, (src, dst) in enumerate(small)]
    for n in range(C0 // 16):
        cut = slice(n * 16, n * 16 + 16)
        copies.append(pltpu.make_async_copy(v_hbm.at[cut], v_ref.at[cut], sems.at[len(small) + n]))
    for copy in copies:
        copy.start()

    copies[0].wait()
    tab, tab2 = tissue_tables(t_ref)
    tab_ref[...] = tab
    tab2_ref[...] = tab2
    copies[1].wait()
    copies[2].wait()
    r = iota((kz, 2 * C0), 0)
    l = iota((kz, 2 * C0), 1)
    odd = l >= C0
    spread = one_hot(((r >> 3) == jnp.where(odd, l - C0, l)) & ((r & 1) == odd.astype(jnp.int32)))
    keep = (iota((kz, lanes), 0) & 7) >> 1 == iota((kz, lanes), 1) >> 6
    for ab in range(4):
        pair = w_ref[2 * ab : 2 * ab + 2].reshape(2 * C0, C1)
        wide = jnp.concatenate([pair] * (Z1 // 2), axis=1)
        block = jnp.where(keep, mm(spread, wide), 0.0).astype(BF)
        for n in range(C0 // 16):
            wd_ref[n, ab * part : ab * part + part, :] = block[n * part : n * part + part]

    copies[3].wait()
    fill_banded(wa_ref, ta_ref, 4, C1)
    r = iota((4 * CX, 128), 0)
    select = one_hot_rows(((r & 32) << 2) | (r & 64) | ((r & 31) << 1) | (r >> 7), 4 * CX)
    part = 16 * half
    acc = [0.0, 0.0]
    for n, copy in enumerate(copies[4:]):
        copy.wait()
        for m in range(v_ref.shape[3] // 256):
            v = [v_ref[n * 16 : n * 16 + 16, h, :, m * 256 : m * 256 + 256].reshape(part, 256) for h in range(2)]
            cells = mm(select, jnp.concatenate(v, axis=0), NT).astype(BF)
            for ab in range(4):
                for h in range(2):
                    piece = cells[64 * ab : 64 * ab + 64, h * part : h * part + part]
                    cells_ref[n, h, m * 64 : m * 64 + 64, ab * part : ab * part + part] = piece
        acc = [acc[h] + mm(cells_ref[n, h], wd_ref[n]) for h in range(2)]
    mask = mask_rows(tab[:, 128:256], 0, Y1, X1, lambda x: x, 4)
    bias = twice(b_ref)
    for h in range(2):
        for q in range(2):
            value = finish(acc[h][:, q * 128 : q * 128 + 128], bias, mask, Y1)
            out_ref[:, :, (2 * h + q) * 128 : (2 * h + q + 1) * 128] = value


def twice(b_ref):
    return jnp.concatenate([b_ref[...]] * 2, axis=1)


def fill_banded(w_ref, t_ref, group, pad):
    chan = w_ref.shape[1]
    t_ref[...] = jnp.zeros_like(t_ref)
    for j in range(3):
        for i in range(3):
            for zo in range(group):
                for k in range(3):
                    lane = i * (group + 2) * pad + (zo + k) * pad
                    t_ref[j, zo * pad : zo * pad + chan, lane : lane + chan] = w_ref[9 * i + 3 * j + k]


def banded_shape(group, pad):
    return shaped(3, group * pad, 3 * (group + 2) * pad)


def banded(weights, group, pad):
    def kernel(w_ref, t_ref):
        fill_banded(w_ref, t_ref, group, pad)

    return pl.pallas_call(
        kernel, out_shape=banded_shape(group, pad), compiler_params=params(), cost_estimate=cost(1e-6)
    )(weights)


def conv_group(taps, t_ref, y_first, rows, group_out, group_full):
    pitch = taps[0][0][0].shape[1]
    width = sum(piece[2] for piece in taps[0])
    total = None
    for j in range(3):
        parts = [ref[y_first + j : y_first + j + rows, :, lane : lane + n] for tap in taps for ref, lane, n in tap]
        left = jnp.concatenate([p.reshape(rows * pitch, p.shape[2]) for p in parts], axis=1)
        if width == group_full:
            right = t_ref[j, 0:group_out, :]
        else:
            right = jnp.concatenate([t_ref[j, 0:group_out, i * group_full : i * group_full + width] for i in range(3)], axis=1)
        term = mm(left, right, NT)
        total = term if total is None else total + term
    return total


def finish(acc, bias, mask, rows):
    value = jnp.maximum(acc + bias, 0.0) * mask
    return value.astype(BF).reshape(rows, value.shape[0] // rows, value.shape[1])


def fill_sides(left, right, lane, inner):
    cut = slice(lane, lane + inner.shape[2])
    none = jnp.zeros_like(inner[:, :1])
    left[:, :, cut] = jnp.concatenate([none, inner[:, :-1]], axis=1)
    right[:, :, cut] = jnp.concatenate([inner[:, 1:], none], axis=1)


def middle_kernel(win_ref, t_ref, b_ref, tab_ref, w_ref, left_ref, right_ref, out_ref, next_ref):
    fill_banded(w_ref, next_ref, 4, C1)
    for q in range(4):
        fill_sides(left_ref, right_ref, q * 128, win_ref[:, :, q * 128 : q * 128 + 128])
    rows = Y1 + 2
    mask = mask_rows(tab_ref[:, 128:256], -1, rows, X1, lambda x: x, 4)
    acc = conv_group([[(ref, 128, 384)] for ref in (left_ref, win_ref, right_ref)], t_ref, 0, rows, 256, 384)
    for q in range(2):
        cut = slice(q * 128, q * 128 + 128)
        out_ref[:, :, cut] = finish(acc[:, cut], twice(b_ref), mask, rows)


def outer_kernel(win_ref, left_ref, right_ref, zl_ref, zr_ref, t_ref, b_ref, tab_ref, low_ref, high_ref, ll, lr, hl, hr):
    fill_sides(ll, lr, 0, zl_ref[...])
    fill_sides(hl, hr, 0, zr_ref[...])
    own = (left_ref, win_ref, right_ref)
    rows = Y1 + 2
    mask = mask_rows(tab_ref[...], -1, rows, X1, lambda x: x, 4)
    taps = [[(z, 0, 128), (ref, 0, 256)] for z, ref in zip((ll, zl_ref, lr), own)]
    acc = conv_group(taps, t_ref, 0, rows, 256, 384)
    for q in range(2):
        cut = slice(q * 128, q * 128 + 128)
        low_ref[:, :, cut] = finish(acc[:, cut], twice(b_ref), mask[:, cut], rows)
    taps = [[(ref, 384, 128), (z, 0, 128)] for z, ref in zip((hl, zr_ref, hr), own)]
    acc = conv_group(taps, t_ref, 0, rows, 128, 384)
    high_ref[...] = finish(acc, twice(b_ref), mask[:, 256:384], rows)


def fill_edges(copies, pieces):
    for i, copy in enumerate(copies):
        line = [pieces[0][:, i:]] + pieces[1:] if i < 2 else pieces[1:]
        if i:
            line.append(jnp.zeros((copy.shape[0], i, pieces[0].shape[2]), BF))
        copy[...] = jnp.concatenate(line, axis=1)


def edge_masks(tab_ref):
    mask = mask_rows(tab_ref[...], -1, Y1 + 2, EDGE, lambda r: jnp.where(r < 8, r - 5, r + X1 - 9), 4)
    return [mask[:, q * 128 : q * 128 + 128] for q in range(3)]


def edge_group(taps, t_ref, b_ref, masks, inner_ref, moved):
    rows = Y1 + 2
    acc = conv_group(taps, t_ref, 0, rows, 128 * len(masks), 384)
    i0, i1, i2 = moved
    for q, mask in enumerate(masks):
        cut = slice(q * 128, q * 128 + 128)
        edge = finish(acc[:, cut], twice(b_ref), mask, rows)
        inner = inner_ref[:, :, cut][:, 1:-1]
        i0[:, :X1, cut] = jnp.concatenate([edge[:, 4:6], inner], axis=1)
        i1[:, :X1, cut] = jnp.concatenate([edge[:, 5:6], inner, edge[:, 8:9]], axis=1)
        i2[:, :X1, cut] = jnp.concatenate([inner, edge[:, 8:10]], axis=1)
        i0[:, X1:, cut] = edge
        for i, copy in ((1, i1), (2, i2)):
            copy[:, X1:, cut] = jnp.concatenate([edge[:, i:], jnp.zeros((rows, i, 128), BF)], axis=1)


def column_lanes(field, lane, stride=Z1 * C1):
    return [field[:, :, first : first + 128] for first in range(lane, field.shape[2], stride)]


def edge_middle_kernel(xl_ref, win_ref, xr_ref, g_ref, t_ref, b_ref, tab_ref, e0, e1, e2, m0, m1, m2):
    for lane in range(0, Z1 * C1, 128):
        cut = slice(lane, lane + 128)
        inner = win_ref[:, :, cut]
        left, right = (column_lanes(ref, lane) for ref in (xl_ref, xr_ref))
        pieces = left + [inner[:, :2], inner[:, X1 - 2 :]] + right
        fill_edges([e.at[:, :, cut] for e in (e0, e1, e2)], pieces)
    here = edge_masks(tab_ref)[1]
    edge_group([[(e, 128, 384)] for e in (e0, e1, e2)], t_ref, b_ref, (here, here), g_ref, (m0, m1, m2))


def level_one_kernel(
    zl_ref, zr_ref, cl_ref, cr_ref, e0, e1, e2, m0, m1, m2, g1_ref, g3_ref, ta_ref, tb_ref, ba_ref, bb_ref, wd_ref, bd_ref, tab_ref,
    tab2_ref, feat_ref, down_ref, l0, l1, l2, h0, h1, h2, i0, i1, i2, j0, j1, j2, side_ref, d_ref,
):
    own, mid, low, high = (e0, e1, e2), (m0, m1, m2), (i0, i1, i2), (j0, j1, j2)
    for z_ref, c_ref, copies in ((zl_ref, cl_ref, (l0, l1, l2)), (zr_ref, cr_ref, (h0, h1, h2))):
        inner = z_ref[...]
        corner = column_lanes(c_ref, 0, 128)
        fill_edges(copies, corner[:3] + [inner[:, :2], inner[:, X1 - 2 :]] + corner[3:])
    below, here, above = edge_masks(tab_ref)
    taps = [[(z, 0, 128), (e, 0, 256)] for z, e in zip((l0, l1, l2), own)]
    edge_group(taps, ta_ref, ba_ref, (below, here), g1_ref, low)
    taps = [[(e, 384, 128), (z, 0, 128)] for z, e in zip((h0, h1, h2), own)]
    edge_group(taps, ta_ref, ba_ref, (above,), g3_ref, high)

    def cell_of(r):
        return jnp.where(r < X1, r, jnp.where(r < X1 + 8, r - X1 - 4, r - 8))

    mask = mask_rows(tab_ref[:, 128:256], 0, Y1, X1 + EDGE, cell_of, 4)
    first = [[(a, 0, 256), (b, 0, 128)] for a, b in zip(low, mid)]
    second = [[(a, 0, 256), (b, 0, 128)] for a, b in zip(mid, high)]
    for g, taps in enumerate((first, second)):
        acc = conv_group(taps, tb_ref, 0, Y1, 256, 384)
        for q in range(2):
            value = finish(acc[:, q * 128 : q * 128 + 128], twice(bb_ref), mask, Y1)
            cut = slice((2 * g + q) * 128, (2 * g + q + 1) * 128)
            feat_ref[:, cut] = value[:, :X1].reshape(Y1 * X1, 128)
            side_ref[:, cut] = value[:, X1:].reshape(Y1 * EDGE, 128)

    size = 8 * X1
    quarter = size // 4
    r = iota((size, 128), 0)
    select = one_hot_rows(((r & 48) << 2) | ((r & 64) >> 1) | ((r & 15) << 1) | (r >> 7), size)
    for n in range(Y1 // 8):
        cells = mm(select, feat_ref[n * size : n * size + size, :]).astype(BF)
        for q in range(4):
            d_ref[q, n * quarter : n * quarter + quarter, :] = cells[q * quarter : (q + 1) * quarter]
    select = one_hot_rows(((r & 56) << 2) | ((r & 64) >> 2) | ((r & 7) << 1) | (r >> 7), size)
    cells = mm(select, side_ref[...]).astype(BF)
    for q in range(4):
        d_ref[q, Y2 * X2 :, :] = cells[q * quarter : (q + 1) * quarter]
    inner_mask = mask_rows(tab2_ref[:, 128:256], 0, Y2, X2, lambda x: x, 2)
    side_mask = mask_rows(tab2_ref[:, 128:256], 0, Y2, EDGE // 2, lambda r: jnp.where(r < 4, r - 2, r + X2 - 4), 2)
    for z in range(Z2):
        left = jnp.concatenate([d_ref[q, :, z * 128 : z * 128 + 128] for q in range(4)], axis=1)
        acc = mm(left, wd_ref[...])
        inner = finish(acc[: Y2 * X2], bd_ref[...], inner_mask, Y2)
        side = finish(acc[Y2 * X2 :], bd_ref[...], side_mask, Y2)
        down_ref[:, :, z * CP : z * CP + CP] = jnp.concatenate([side[:, 0:2], inner, side[:, 4:6]], axis=1)


def one_kernel(feat_ref, out_ref):
    lanes = feat_ref.shape[1]
    r = iota((lanes, 128), 0)
    order = one_hot_rows(((r & 7) << 6) | (r >> 3), lanes)
    out_ref[...] = mm(order, feat_ref[...], NT).astype(BF)


def fill_pitch(copies, wide):
    pitch = copies[0].shape[1]
    for lane in range(0, wide.shape[2], 128):
        line = wide[:, :, lane : lane + 128]
        for i, copy in enumerate(copies):
            spare = jnp.zeros((line.shape[0], pitch - line.shape[1] + i, 128), BF)
            copy[:, :, lane : lane + 128] = jnp.concatenate([line[:, i:], spare], axis=1)


def level_two_group(taps, t_ref, b_ref, masks, moved):
    rows = Y2 + 2
    acc = conv_group(taps, t_ref, 0, rows, 256, 512)
    for q in range(2):
        cut = slice(q * 128, q * 128 + 128)
        value = finish(acc[:, cut], b_ref[...], masks[q], rows)
        for i, ref in enumerate(moved):
            ref[:, :, cut] = value[:, i : i + X2]


def level_two_masks(tab_ref):
    mask = mask_rows(tab_ref[...], -1, Y2 + 2, PITCH2, lambda x: x - 1, 2)
    return [mask[:, q * 128 : q * 128 + 128] for q in range(3)]


def level_two_middle_kernel(wide_ref, t_ref, b_ref, tab_ref, a0, a1, a2, m0, m1, m2):
    fill_pitch((a0, a1, a2), wide_ref[...])
    here = level_two_masks(tab_ref)[1]
    level_two_group([[(a, 0, 512)] for a in (a0, a1, a2)], t_ref, b_ref, (here, here), (m0, m1, m2))


def level_two_kernel(
    a0, a1, a2, m0, m1, m2, zl_ref, zr_ref, ta_ref, tb_ref, ba_ref, bb_ref, tab_ref, out_ref,
    l0, l1, l2, h0, h1, h2, i0, i1, i2, j0, j1, j2,
):
    fill_pitch((l0, l1, l2), zl_ref[...])
    fill_pitch((h0, h1, h2), zr_ref[...])
    below, here, above = level_two_masks(tab_ref)
    own, mid, low, high = (a0, a1, a2), (m0, m1, m2), (i0, i1, i2), (j0, j1, j2)
    taps = [[(z, 0, 256), (a, 0, 256)] for z, a in zip((l0, l1, l2), own)]
    level_two_group(taps, ta_ref, ba_ref, (below, here), low)
    taps = [[(a, 256, 256), (z, 0, 256)] for z, a in zip((h0, h1, h2), own)]
    level_two_group(taps, ta_ref, ba_ref, (here, above), high)
    mask = mask_rows(tab_ref[:, 128:256], 0, Y2, X2, lambda x: x, 2)
    feat = []
    for pair in ((low, mid), (mid, high)):
        acc = conv_group([[(a, 0, 256), (b, 0, 256)] for a, b in zip(*pair)], tb_ref, 0, Y2, 256, 512)
        for q in range(2):
            feat.append((jnp.maximum(acc[:, q * 128 : q * 128 + 128] + bb_ref[...], 0.0) * mask).astype(BF))
    r = iota((C2 * Z2, 128), 0)
    order = one_hot_rows(((r & 3) << 7) | (r >> 2), Z2 * CP)
    out_ref[...] = mm(order, jnp.concatenate(feat, axis=1), NT).astype(BF)


def partner(index, second, count):
    other = index + 1 if index % 2 == second else index - 1
    return other if 0 <= other < count else None


def swap(value, moves):
    axes = ("gx", "gy", "gz")
    sizes = [lax.axis_size(axis) for axis in axes]
    pairs = []
    for source in itertools.product(*(range(size) for size in sizes)):
        target = [partner(i, moves[axis], size) if axis in moves else i for i, axis, size in zip(source, axes, sizes)]
        if None in target:
            other = sizes[1] - 1 - source[1] if "gy" in moves else source[1] ^ 1
            target = [source[0], other, source[2]]
        pairs.append(tuple((x * sizes[1] + y) * sizes[2] + z for x, y, z in (source, target)))
    return lax.ppermute(value, axes, pairs)


def parity(axis):
    return lax.axis_index(axis) % 2 == 0


def sides(first, second, axis):
    index = lax.axis_index(axis)
    even = parity(axis)
    below = jnp.where(index > 0, jnp.where(even, second, first), jnp.zeros_like(first))
    above = jnp.where(index < lax.axis_size(axis) - 1, jnp.where(even, first, second), jnp.zeros_like(first))
    return below, above


def shift_along(low_edge, high_edge, axis):
    even = parity(axis)
    first = swap(jnp.where(even, high_edge, low_edge), {axis: 0})
    second = swap(jnp.where(even, low_edge, high_edge), {axis: 1}) if lax.axis_size(axis) > 2 else first
    return sides(first, second, axis)


def column_pairs(field):
    return jnp.concatenate([field[:, i : i + 2] for i in range(0, field.shape[1], 2)], axis=2)


def params():
    return pltpu.CompilerParams(vmem_limit_bytes=VMEM_BYTES)


def cost(seconds):
    return pl.CostEstimate(flops=int(1e15 * seconds), bytes_accessed=0, transcendentals=0)


def shaped(*shape):
    return jax.ShapeDtypeStruct(shape, BF)


def pad_lanes(value):
    return jnp.pad(value, [(0, 0)] * (value.ndim - 1) + [(0, CP - value.shape[-1])])


def local(
    volume, tissue, w_down1, b_down1, w_conv1a, b_conv1a, w_conv1b, b_conv1b,
    w_down2, b_down2, w_conv2a, b_conv2a, w_conv2b, b_conv2b,
):
    depth = volume.shape[1]
    lanes1 = Z1 * C1
    half = depth // 2
    operands = [volume.reshape(C0, 2, half, -1), jnp.swapaxes(w_down1, 1, 2), b_down1[None], tissue.transpose(1, 2, 0), w_conv1a]
    operands = [pltpu.with_memory_space_constraint(x, pltpu.HBM) for x in operands]
    own, t1a, tab1, tab2 = pl.pallas_call(
        down1_kernel,
        in_specs=[pl.BlockSpec(memory_space=pltpu.HBM)] * 5,
        out_shape=[shaped(Y1, X1, lanes1), banded_shape(4, C1), shaped(128, 384), shaped(128, 384)],
        scratch_shapes=[pltpu.VMEM(x.shape, x.dtype) for x in operands]
        + [
            pltpu.VMEM((C0 // 16, 64 * half, lanes1 // 2), BF),
            pltpu.VMEM((C0 // 16, 2, Y1 * X1, 64 * half), BF),
            pltpu.SemaphoreType.DMA((4 + C0 // 16,)),
        ],
        compiler_params=params(),
        cost_estimate=cost(4e-6),
    )(*operands)

    t2a = banded(w_conv2a, 2, CP)
    t2b = banded(w_conv2b, 2, CP)
    bias1a = b_conv1a[None]

    y_below, y_above = shift_along(own[:HALO], own[Y1 - HALO :], "gy")
    win = jnp.concatenate([y_below, own, y_above], axis=0)
    z_below, z_above = shift_along(win[:, :, :128], win[:, :, lanes1 - 128 :], "gz")
    low, high = win[:, :HALO_X], win[:, X1 - HALO_X :]
    x_below, x_above = shift_along(column_pairs(low), column_pairs(high), "gx")
    rows = Y1 + 2
    left, right, g2, t1b = pl.pallas_call(
        middle_kernel,
        out_shape=[shaped(ROWS1, X1, lanes1), shaped(ROWS1, X1, lanes1), shaped(rows, X1, 256), banded_shape(4, C1)],
        compiler_params=params(),
        cost_estimate=cost(1e-7),
    )(win, t1a, bias1a, tab1, w_conv1b)

    corner = [jnp.concatenate(column_lanes(x, at), axis=2) for at in (0, lanes1 - 128) for x in (x_below, x_above)]
    low, high = jnp.concatenate(corner[:2], axis=2), jnp.concatenate(corner[2:], axis=2)
    low, high, g2 = lax.optimization_barrier((low, high, g2))
    corner_below, corner_above = shift_along(low, high, "gz")
    g1, g3 = pl.pallas_call(
        outer_kernel,
        out_shape=[shaped(rows, X1, 256), shaped(rows, X1, 128)],
        scratch_shapes=[pltpu.VMEM((ROWS1, X1, 128), BF)] * 4,
        compiler_params=params(),
        cost_estimate=cost(4e-6),
    )(win, left, right, z_below, z_above, t1a, bias1a, tab1)

    wide_x = X1 + EDGE
    edges = pl.pallas_call(
        edge_middle_kernel,
        out_shape=[shaped(ROWS1, EDGE, lanes1)] * 3 + [shaped(rows, wide_x, 256)] * 3,
        compiler_params=params(),
        cost_estimate=cost(3e-6),
    )(x_below, win, x_above, g2, t1a, bias1a, tab1)
    feat, down = pl.pallas_call(
        level_one_kernel,
        out_shape=[shaped(Y1 * X1, lanes1), shaped(Y2, X2 + 2 * HALO_X2, Z2 * CP)],
        scratch_shapes=[pltpu.VMEM((ROWS1, EDGE, 128), BF)] * 6
        + [pltpu.VMEM((rows, wide_x, 256), BF)] * 3
        + [pltpu.VMEM((rows, wide_x, 128), BF)] * 3
        + [pltpu.VMEM((Y1 * EDGE, lanes1), BF), pltpu.VMEM((4, Y2 * (X2 + EDGE // 2), lanes1), BF)],
        compiler_params=params(),
        cost_estimate=cost(6e-6),
    )(
        z_below, z_above, corner_below, corner_above, *edges, g1, g3, t1a, t1b, bias1a, b_conv1b[None],
        pad_lanes(jnp.swapaxes(w_down2, 1, 2).reshape(8 * C1, C2)), pad_lanes(b_down2[None]), tab1, tab2,
    )

    y_below, y_above = shift_along(down[:HALO], down[Y2 - HALO :], "gy")
    wide = jnp.concatenate([y_below, down, y_above], axis=0)
    feat, wide = lax.optimization_barrier((feat, wide))
    one = pl.pallas_call(
        one_kernel, out_shape=shaped(lanes1, Y1 * X1), compiler_params=params(), cost_estimate=cost(2e-6)
    )(feat)
    z_below, z_above = shift_along(wide[:, :, : 2 * CP], wide[:, :, 2 * CP :], "gz")
    bias2a = pad_lanes(b_conv2a[None])
    moved = [shaped(Y2 + 2, X2, 2 * CP)] * 3
    middle = pl.pallas_call(
        level_two_middle_kernel,
        out_shape=[shaped(ROWS2, PITCH2, Z2 * CP)] * 3 + moved,
        compiler_params=params(),
        cost_estimate=cost(3e-6),
    )(wide, t2a, bias2a, tab2)
    two = pl.pallas_call(
        level_two_kernel,
        out_shape=shaped(C2 * Z2, Y2 * X2),
        scratch_shapes=[pltpu.VMEM((ROWS2, PITCH2, 2 * CP), BF)] * 6 + [pltpu.VMEM((Y2 + 2, X2, 2 * CP), BF)] * 6,
        compiler_params=params(),
        cost_estimate=cost(5e-6),
    )(*middle, z_below, z_above, t2a, t2b, bias2a, pad_lanes(b_conv2b[None]), tab2)
    return one.reshape(C1, Z1, Y1 * X1), two.reshape(C2, Z2, Y2 * X2)


def solution(mesh):
    block = P(None, "gz", ("gx", "gy"))
    return jax.shard_map(
        local,
        mesh=mesh,
        in_specs=(block,) + (P(),) * 13,
        out_specs=(block, block),
        check_vma=False,
    )
```

```python
import itertools

import jax
import jax.numpy as jnp
from jax import lax
from jax.experimental import pallas as pl
from jax.experimental.pallas import tpu as pltpu
from jax.sharding import PartitionSpec as P

CX = 64
CY = 32
X1 = CX // 2
Y1 = CY // 2
X2 = X1 // 2
Y2 = Y1 // 2
Z1 = 8
Z2 = 4
C0 = 48
C1 = 64
C2 = 96
CP = 128
HALO = 2
HALO_X = 6
HALO_X2 = 2
XB = 12
XB_BELOW = 2
XB_PITCH = 16
YB = 6
ROWS1 = Y1 + 2 * HALO
ROWS2 = Y2 + 2 * HALO
EDGE = 16
PITCH2 = 32
BF = jnp.bfloat16
F32 = jnp.float32
NN = (((1,), (0,)), ((), ()))
NT = (((1,), (1,)), ((), ()))
VMEM_BYTES = 20 * 1024 * 1024


def mm(a, b, dims=NN):
    return lax.dot_general(a, b, dims, preferred_element_type=F32)


def iota(shape, dim):
    return lax.broadcasted_iota(jnp.int32, shape, dim)


def one_hot(flag):
    return jnp.where(flag, 1.0, 0.0).astype(BF)


def one_hot_rows(key, lanes):
    lane = iota(key.shape, 1)
    return jnp.concatenate([one_hot(key == lane + q) for q in range(0, lanes, 128)], axis=1)


def mask_rows(tab, y_start, rows, pitch, x_of, cell):
    bits = cell.bit_length() - 1
    shape = (rows, pitch, 128)
    y_block = (iota(shape, 0) + (y_start + cell)) >> bits
    x_block = jnp.minimum((x_of(iota(shape, 1)) + XB_BELOW * cell) >> bits, XB - 1)
    hit = one_hot(y_block * XB_PITCH + x_block == iota(shape, 2)).reshape(rows * pitch, 128)
    return mm(hit, tab)


def tissue_tables(t_ref):
    n_y, n_z, n_x = t_ref.shape
    here = lax.axis_index("gz")
    layers = []
    for k in (-1, 0, 1):
        z = here + k
        inside = jnp.where((z >= 0) & (z < n_z), 1.0, 0.0)
        layers.append(t_ref[:, jnp.clip(z, 0, n_z - 1), :].astype(F32) * inside)
    block = iota((128, n_y), 0)
    bits = XB_PITCH.bit_length() - 1
    hot_y = one_hot(lax.axis_index("gy") * 4 - 1 + (block >> bits) == iota((128, n_y), 1))
    block = iota((128, 3 * n_x), 0)
    layer = sum((iota((128, 3 * n_x), 1) >= k * n_x).astype(jnp.int32) for k in (1, 2))
    hot_x = lax.axis_index("gx") * 8 - XB_BELOW + (block & (XB_PITCH - 1)) == iota((128, 3 * n_x), 1) - layer * n_x
    rows = jnp.where(hot_x, mm(hot_y, jnp.concatenate(layers, axis=1).astype(BF)), 0.0).astype(BF)
    shape = (3 * n_x, 384)
    layer = sum((iota(shape, 0) >= k * n_x).astype(jnp.int32) for k in (1, 2))
    lane = iota(shape, 1)

    def spread(first, last):
        place = jnp.where(lane < first, 0, jnp.where(lane < last, 1, 2))
        return mm(rows, one_hot(layer == place)).astype(BF)

    return spread(64, 320), spread(128, 256)


def down1_kernel(
    v_hbm, wd_hbm, b_hbm, t_hbm, out_ref, tab_ref, tab2_ref, v_ref, w_ref, b_ref, t_ref, wd_ref, cells_ref, sems
):
    half = v_ref.shape[2]
    kz = C0 * half
    part = 16 * half
    lanes = Z1 // 2 * C1
    small = ((t_hbm, t_ref), (wd_hbm, w_ref), (b_hbm, b_ref))
    copies = [pltpu.make_async_copy(src, dst, sems.at[n]) for n, (src, dst) in enumerate(small)]
    for n in range(C0 // 16):
        cut = slice(n * 16, n * 16 + 16)
        copies.append(pltpu.make_async_copy(v_hbm.at[cut], v_ref.at[cut], sems.at[len(small) + n]))
    for copy in copies:
        copy.start()

    copies[0].wait()
    tab, tab2 = tissue_tables(t_ref)
    tab_ref[...] = tab
    tab2_ref[...] = tab2
    copies[1].wait()
    copies[2].wait()
    r = iota((kz, 2 * C0), 0)
    l = iota((kz, 2 * C0), 1)
    odd = l >= C0
    spread = one_hot(((r >> 3) == jnp.where(odd, l - C0, l)) & ((r & 1) == odd.astype(jnp.int32)))
    keep = (iota((kz, lanes), 0) & 7) >> 1 == iota((kz, lanes), 1) >> 6
    for ab in range(4):
        pair = w_ref[2 * ab : 2 * ab + 2].reshape(2 * C0, C1)
        wide = jnp.concatenate([pair] * (Z1 // 2), axis=1)
        block = jnp.where(keep, mm(spread, wide), 0.0).astype(BF)
        for n in range(C0 // 16):
            wd_ref[n, ab * part : ab * part + part, :] = block[n * part : n * part + part]

    r = iota((4 * CX, 128), 0)
    select = one_hot_rows(((r & 32) << 2) | (r & 64) | ((r & 31) << 1) | (r >> 7), 4 * CX)
    part = 16 * half
    acc = [0.0, 0.0]
    for n, copy in enumerate(copies[3:]):
        copy.wait()
        for m in range(v_ref.shape[3] // 256):
            v = [v_ref[n * 16 : n * 16 + 16, h, :, m * 256 : m * 256 + 256].reshape(part, 256) for h in range(2)]
            cells = mm(select, jnp.concatenate(v, axis=0), NT).astype(BF)
            for ab in range(4):
                for h in range(2):
                    piece = cells[64 * ab : 64 * ab + 64, h * part : h * part + part]
                    cells_ref[n, h, m * 64 : m * 64 + 64, ab * part : ab * part + part] = piece
        acc = [acc[h] + mm(cells_ref[n, h], wd_ref[n]) for h in range(2)]
    mask = mask_rows(tab[:, 128:256], 0, Y1, X1, lambda x: x, 4)
    bias = twice(b_ref)
    for h in range(2):
        for q in range(2):
            value = finish(acc[h][:, q * 128 : q * 128 + 128], bias, mask, Y1)
            out_ref[:, :, (2 * h + q) * 128 : (2 * h + q + 1) * 128] = value


def twice(b_ref):
    return jnp.concatenate([b_ref[...]] * 2, axis=1)


def fill_banded(w_ref, t_ref, group, pad):
    chan = w_ref.shape[1]
    t_ref[...] = jnp.zeros_like(t_ref)
    for j in range(3):
        for i in range(3):
            for zo in range(group):
                for k in range(3):
                    lane = i * (group + 2) * pad + (zo + k) * pad
                    t_ref[j, zo * pad : zo * pad + chan, lane : lane + chan] = w_ref[9 * i + 3 * j + k]


def banded_shape(group, pad):
    return shaped(3, group * pad, 3 * (group + 2) * pad)


def banded(weights, group, pad):
    def kernel(w_ref, t_ref):
        fill_banded(w_ref, t_ref, group, pad)

    return pl.pallas_call(
        kernel, out_shape=banded_shape(group, pad), compiler_params=params(), cost_estimate=cost(1e-6)
    )(weights)


def conv_groups(groups, t_ref, rows, group_out, group_full):
    pitch = groups[0][0][0][0].shape[1]
    width = sum(piece[2] for piece in groups[0][0])
    total = None
    for j in range(3):
        left = []
        for taps in groups:
            parts = [ref[j : j + rows, :, lane : lane + n] for tap in taps for ref, lane, n in tap]
            left.append(jnp.concatenate([p.reshape(rows * pitch, p.shape[2]) for p in parts], axis=1))
        if width == group_full:
            right = t_ref[j, 0:group_out, :]
        else:
            right = jnp.concatenate([t_ref[j, 0:group_out, i * group_full : i * group_full + width] for i in range(3)], axis=1)
        term = mm(jnp.concatenate(left, axis=0), right, NT)
        total = term if total is None else total + term
    size = rows * pitch
    return [total[g * size : g * size + size] for g in range(len(groups))]


def conv_group(taps, t_ref, rows, group_out, group_full):
    return conv_groups([taps], t_ref, rows, group_out, group_full)[0]


def finish(acc, bias, mask, rows):
    value = jnp.maximum(acc + bias, 0.0) * mask
    return value.astype(BF).reshape(rows, value.shape[0] // rows, value.shape[1])


def fill_sides(left, right, lane, inner):
    cut = slice(lane, lane + inner.shape[2])
    none = jnp.zeros_like(inner[:, :1])
    left[:, :, cut] = jnp.concatenate([none, inner[:, :-1]], axis=1)
    right[:, :, cut] = jnp.concatenate([inner[:, 1:], none], axis=1)


def middle_kernel(win_ref, t_ref, b_ref, tab_ref, w_ref, left_ref, right_ref, out_ref, next_ref):
    fill_banded(w_ref, next_ref, 4, C1)
    for q in range(4):
        fill_sides(left_ref, right_ref, q * 128, win_ref[:, :, q * 128 : q * 128 + 128])
    rows = Y1 + 2
    mask = mask_rows(tab_ref[:, 128:256], -1, rows, X1, lambda x: x, 4)
    acc = conv_group([[(ref, 128, 384)] for ref in (left_ref, win_ref, right_ref)], t_ref, rows, 256, 384)
    for q in range(2):
        cut = slice(q * 128, q * 128 + 128)
        out_ref[:, :, cut] = finish(acc[:, cut], twice(b_ref), mask, rows)


def outer_kernel(win_ref, left_ref, right_ref, zl_ref, zr_ref, t_ref, b_ref, tab_ref, low_ref, high_ref, ll, lr, hl, hr):
    fill_sides(ll, lr, 0, zl_ref[...])
    fill_sides(hl, hr, 0, zr_ref[...])
    own = (left_ref, win_ref, right_ref)
    rows = Y1 + 2
    mask = mask_rows(tab_ref[...], -1, rows, X1, lambda x: x, 4)
    taps = [[(z, 0, 128), (ref, 0, 256)] for z, ref in zip((ll, zl_ref, lr), own)]
    acc = conv_group(taps, t_ref, rows, 256, 384)
    for q in range(2):
        cut = slice(q * 128, q * 128 + 128)
        low_ref[:, :, cut] = finish(acc[:, cut], twice(b_ref), mask[:, cut], rows)
    taps = [[(ref, 384, 128), (z, 0, 128)] for z, ref in zip((hl, zr_ref, hr), own)]
    acc = conv_group(taps, t_ref, rows, 128, 384)
    high_ref[...] = finish(acc, twice(b_ref), mask[:, 256:384], rows)


def fill_edges(copies, pieces):
    line = jnp.concatenate(pieces, axis=1)
    copies[0][...] = line
    for i in (1, 2):
        copies[i][...] = jnp.concatenate([line[:, i:], jnp.zeros_like(line[:, :i])], axis=1)


def edge_masks(tab_ref):
    mask = mask_rows(tab_ref[...], -1, Y1 + 2, EDGE, lambda r: jnp.where(r < 8, r - 5, r + X1 - 9), 4)
    return [mask[:, q * 128 : q * 128 + 128] for q in range(3)]


def edge_group(taps, t_ref, b_ref, masks, inner_ref, moved):
    rows = Y1 + 2
    acc = conv_group(taps, t_ref, rows, 128 * len(masks), 384)
    i0, i1, i2 = moved
    for q, mask in enumerate(masks):
        cut = slice(q * 128, q * 128 + 128)
        edge = finish(acc[:, cut], twice(b_ref), mask, rows)
        inner = inner_ref[:, :, cut][:, 1:-1]
        i0[:, :X1, cut] = jnp.concatenate([edge[:, 4:6], inner], axis=1)
        i1[:, :X1, cut] = jnp.concatenate([edge[:, 5:6], inner, edge[:, 8:9]], axis=1)
        i2[:, :X1, cut] = jnp.concatenate([inner, edge[:, 8:10]], axis=1)
        i0[:, X1:, cut] = edge
        for i, copy in ((1, i1), (2, i2)):
            copy[:, X1:, cut] = jnp.concatenate([edge[:, i:], jnp.zeros((rows, i, 128), BF)], axis=1)


def column_lanes(field, lane, stride=Z1 * C1):
    return [field[:, :, first : first + 128] for first in range(lane, field.shape[2], stride)]


def edge_middle_kernel(xl_ref, win_ref, xr_ref, g_ref, t_ref, b_ref, tab_ref, e0, e1, e2, m0, m1, m2):
    for lane in range(0, Z1 * C1, 128):
        cut = slice(lane, lane + 128)
        inner = win_ref[:, :, cut]
        left, right = (column_lanes(ref, lane) for ref in (xl_ref, xr_ref))
        pieces = left + [inner[:, :2], inner[:, X1 - 2 :]] + right
        fill_edges([e.at[:, :, cut] for e in (e0, e1, e2)], pieces)
    here = edge_masks(tab_ref)[1]
    edge_group([[(e, 128, 384)] for e in (e0, e1, e2)], t_ref, b_ref, (here, here), g_ref, (m0, m1, m2))


def level_one_kernel(
    zl_ref, zr_ref, cl_ref, cr_ref, e0, e1, e2, m0, m1, m2, g1_ref, g3_ref, ta_ref, tb_ref, ba_ref, bb_ref, wd_ref, bd_ref, tab_ref,
    tab2_ref, feat_ref, down_ref, l0, l1, l2, h0, h1, h2, i0, i1, i2, j0, j1, j2, side_ref, d_ref,
):
    own, mid, low, high = (e0, e1, e2), (m0, m1, m2), (i0, i1, i2), (j0, j1, j2)
    for z_ref, c_ref, copies in ((zl_ref, cl_ref, (l0, l1, l2)), (zr_ref, cr_ref, (h0, h1, h2))):
        inner = z_ref[...]
        corner = column_lanes(c_ref, 0, 128)
        fill_edges(copies, corner[:3] + [inner[:, :2], inner[:, X1 - 2 :]] + corner[3:])
    below, here, above = edge_masks(tab_ref)
    taps = [[(z, 0, 128), (e, 0, 256)] for z, e in zip((l0, l1, l2), own)]
    edge_group(taps, ta_ref, ba_ref, (below, here), g1_ref, low)
    taps = [[(e, 384, 128), (z, 0, 128)] for z, e in zip((h0, h1, h2), own)]
    edge_group(taps, ta_ref, ba_ref, (above,), g3_ref, high)

    def cell_of(r):
        return jnp.where(r < X1, r, jnp.where(r < X1 + 8, r - X1 - 4, r - 8))

    mask = mask_rows(tab_ref[:, 128:256], 0, Y1, X1 + EDGE, cell_of, 4)
    first = [[(a, 0, 256), (b, 0, 128)] for a, b in zip(low, mid)]
    second = [[(a, 0, 256), (b, 0, 128)] for a, b in zip(mid, high)]
    for g, taps in enumerate((first, second)):
        acc = conv_group(taps, tb_ref, Y1, 256, 384)
        for q in range(2):
            value = finish(acc[:, q * 128 : q * 128 + 128], twice(bb_ref), mask, Y1)
            cut = slice((2 * g + q) * 128, (2 * g + q + 1) * 128)
            feat_ref[:, cut] = value[:, :X1].reshape(Y1 * X1, 128)
            side_ref[:, cut] = value[:, X1:].reshape(Y1 * EDGE, 128)

    size = 8 * X1
    quarter = size // 4
    r = iota((size, 128), 0)
    select = one_hot_rows(((r & 48) << 2) | ((r & 64) >> 1) | ((r & 15) << 1) | (r >> 7), size)
    for n in range(Y1 // 8):
        cells = mm(select, feat_ref[n * size : n * size + size, :]).astype(BF)
        for q in range(4):
            d_ref[q, n * quarter : n * quarter + quarter, :] = cells[q * quarter : (q + 1) * quarter]
    select = one_hot_rows(((r & 56) << 2) | ((r & 64) >> 2) | ((r & 7) << 1) | (r >> 7), size)
    cells = mm(select, side_ref[...]).astype(BF)
    for q in range(4):
        d_ref[q, Y2 * X2 :, :] = cells[q * quarter : (q + 1) * quarter]
    inner_mask = mask_rows(tab2_ref[:, 128:256], 0, Y2, X2, lambda x: x, 2)
    side_mask = mask_rows(tab2_ref[:, 128:256], 0, Y2, EDGE // 2, lambda r: jnp.where(r < 4, r - 2, r + X2 - 4), 2)
    for z in range(Z2):
        left = jnp.concatenate([d_ref[q, :, z * 128 : z * 128 + 128] for q in range(4)], axis=1)
        acc = mm(left, wd_ref[...])
        inner = finish(acc[: Y2 * X2], bd_ref[...], inner_mask, Y2)
        side = finish(acc[Y2 * X2 :], bd_ref[...], side_mask, Y2)
        down_ref[:, :, z * CP : z * CP + CP] = jnp.concatenate([side[:, 0:2], inner, side[:, 4:6]], axis=1)


def one_kernel(feat_ref, out_ref):
    lanes = feat_ref.shape[1]
    r = iota((lanes, 128), 0)
    order = one_hot_rows(((r & 7) << 6) | (r >> 3), lanes)
    out_ref[...] = mm(order, feat_ref[...], NT).astype(BF)


def fill_pitch(copies, wide):
    pitch = copies[0].shape[1]
    for lane in range(0, wide.shape[2], 128):
        line = wide[:, :, lane : lane + 128]
        for i, copy in enumerate(copies):
            spare = jnp.zeros((line.shape[0], pitch - line.shape[1] + i, 128), BF)
            copy[:, :, lane : lane + 128] = jnp.concatenate([line[:, i:], spare], axis=1)


def level_two_groups(groups, t_ref, b_ref, masks, moved):
    rows = Y2 + 2
    for g, acc in enumerate(conv_groups(groups, t_ref, rows, 256, 512)):
        for q in range(2):
            cut = slice(q * 128, q * 128 + 128)
            value = finish(acc[:, cut], b_ref[...], masks[g][q], rows)
            for i, ref in enumerate(moved[g]):
                ref[:, :, cut] = value[:, i : i + X2]


def level_two_masks(tab_ref):
    mask = mask_rows(tab_ref[...], -1, Y2 + 2, PITCH2, lambda x: x - 1, 2)
    return [mask[:, q * 128 : q * 128 + 128] for q in range(3)]


def level_two_middle_kernel(wide_ref, t_ref, b_ref, tab_ref, a0, a1, a2, m0, m1, m2):
    fill_pitch((a0, a1, a2), wide_ref[...])
    here = level_two_masks(tab_ref)[1]
    level_two_groups([[[(a, 0, 512)] for a in (a0, a1, a2)]], t_ref, b_ref, [(here, here)], [(m0, m1, m2)])


def level_two_kernel(
    a0, a1, a2, m0, m1, m2, zl_ref, zr_ref, ta_ref, tb_ref, ba_ref, bb_ref, tab_ref, out_ref,
    l0, l1, l2, h0, h1, h2, i0, i1, i2, j0, j1, j2,
):
    fill_pitch((l0, l1, l2), zl_ref[...])
    fill_pitch((h0, h1, h2), zr_ref[...])
    below, here, above = level_two_masks(tab_ref)
    own, mid, low, high = (a0, a1, a2), (m0, m1, m2), (i0, i1, i2), (j0, j1, j2)
    first = [[(z, 0, 256), (a, 0, 256)] for z, a in zip((l0, l1, l2), own)]
    second = [[(a, 256, 256), (z, 0, 256)] for z, a in zip((h0, h1, h2), own)]
    level_two_groups([first, second], ta_ref, ba_ref, [(below, here), (here, above)], [low, high])
    mask = mask_rows(tab_ref[:, 128:256], 0, Y2, X2, lambda x: x, 2)
    groups = [[[(a, 0, 256), (b, 0, 256)] for a, b in zip(*pair)] for pair in ((low, mid), (mid, high))]
    feat = []
    for acc in conv_groups(groups, tb_ref, Y2, 256, 512):
        for q in range(2):
            feat.append((jnp.maximum(acc[:, q * 128 : q * 128 + 128] + bb_ref[...], 0.0) * mask).astype(BF))
    r = iota((C2 * Z2, 128), 0)
    order = one_hot_rows(((r & 3) << 7) | (r >> 2), Z2 * CP)
    out_ref[...] = mm(order, jnp.concatenate(feat, axis=1), NT).astype(BF)


def partner(index, second, count):
    other = index + 1 if index % 2 == second else index - 1
    return other if 0 <= other < count else None


def swap(value, moves):
    axes = ("gx", "gy", "gz")
    sizes = [lax.axis_size(axis) for axis in axes]
    pairs = []
    for source in itertools.product(*(range(size) for size in sizes)):
        target = [partner(i, moves[axis], size) if axis in moves else i for i, axis, size in zip(source, axes, sizes)]
        if None in target:
            other = sizes[1] - 1 - source[1] if "gy" in moves else source[1] ^ 1
            target = [source[0], other, source[2]]
        pairs.append(tuple((x * sizes[1] + y) * sizes[2] + z for x, y, z in (source, target)))
    return lax.ppermute(value, axes, pairs)


def parity(axis):
    return lax.axis_index(axis) % 2 == 0


def sides(first, second, axis):
    index = lax.axis_index(axis)
    even = parity(axis)
    below = jnp.where(index > 0, jnp.where(even, second, first), jnp.zeros_like(first))
    above = jnp.where(index < lax.axis_size(axis) - 1, jnp.where(even, first, second), jnp.zeros_like(first))
    return below, above


def shift_along(low_edge, high_edge, axis):
    even = parity(axis)
    first = swap(jnp.where(even, high_edge, low_edge), {axis: 0})
    second = swap(jnp.where(even, low_edge, high_edge), {axis: 1}) if lax.axis_size(axis) > 2 else first
    return sides(first, second, axis)


def column_pairs(field):
    return jnp.concatenate([field[:, i : i + 2] for i in range(0, field.shape[1], 2)], axis=2)


def params():
    return pltpu.CompilerParams(vmem_limit_bytes=VMEM_BYTES)


def cost(seconds):
    return pl.CostEstimate(flops=int(1e15 * seconds), bytes_accessed=0, transcendentals=0)


def shaped(*shape):
    return jax.ShapeDtypeStruct(shape, BF)


def pad_lanes(value):
    return jnp.pad(value, [(0, 0)] * (value.ndim - 1) + [(0, CP - value.shape[-1])])


def local(
    volume, tissue, w_down1, b_down1, w_conv1a, b_conv1a, w_conv1b, b_conv1b,
    w_down2, b_down2, w_conv2a, b_conv2a, w_conv2b, b_conv2b,
):
    depth = volume.shape[1]
    lanes1 = Z1 * C1
    half = depth // 2
    operands = [volume.reshape(C0, 2, half, -1), jnp.swapaxes(w_down1, 1, 2), b_down1[None], tissue.transpose(1, 2, 0)]
    operands = [pltpu.with_memory_space_constraint(x, pltpu.HBM) for x in operands]
    own, tab1, tab2 = pl.pallas_call(
        down1_kernel,
        in_specs=[pl.BlockSpec(memory_space=pltpu.HBM)] * 4,
        out_shape=[shaped(Y1, X1, lanes1), shaped(128, 384), shaped(128, 384)],
        scratch_shapes=[pltpu.VMEM(x.shape, x.dtype) for x in operands]
        + [
            pltpu.VMEM((C0 // 16, 64 * half, lanes1 // 2), BF),
            pltpu.VMEM((C0 // 16, 2, Y1 * X1, 64 * half), BF),
            pltpu.SemaphoreType.DMA((3 + C0 // 16,)),
        ],
        compiler_params=params(),
        cost_estimate=cost(4e-6),
    )(*operands)

    t1a = banded(w_conv1a, 4, C1)
    bias1a = b_conv1a[None]

    y_below, y_above = shift_along(own[:HALO], own[Y1 - HALO :], "gy")
    win = jnp.concatenate([y_below, own, y_above], axis=0)
    z_below, z_above = shift_along(win[:, :, :128], win[:, :, lanes1 - 128 :], "gz")
    low, high = win[:, :HALO_X], win[:, X1 - HALO_X :]
    x_below, x_above = shift_along(column_pairs(low), column_pairs(high), "gx")
    rows = Y1 + 2
    left, right, g2, t1b = pl.pallas_call(
        middle_kernel,
        out_shape=[shaped(ROWS1, X1, lanes1), shaped(ROWS1, X1, lanes1), shaped(rows, X1, 256), banded_shape(4, C1)],
        compiler_params=params(),
        cost_estimate=cost(1e-7),
    )(win, t1a, bias1a, tab1, w_conv1b)

    corner = [jnp.concatenate(column_lanes(x, at), axis=2) for at in (0, lanes1 - 128) for x in (x_below, x_above)]
    low, high = jnp.concatenate(corner[:2], axis=2), jnp.concatenate(corner[2:], axis=2)
    low, high, g2 = lax.optimization_barrier((low, high, g2))
    corner_below, corner_above = shift_along(low, high, "gz")
    g1, g3 = pl.pallas_call(
        outer_kernel,
        out_shape=[shaped(rows, X1, 256), shaped(rows, X1, 128)],
        scratch_shapes=[pltpu.VMEM((ROWS1, X1, 128), BF)] * 4,
        compiler_params=params(),
        cost_estimate=cost(4e-6),
    )(win, left, right, z_below, z_above, t1a, bias1a, tab1)

    wide_x = X1 + EDGE
    edges = pl.pallas_call(
        edge_middle_kernel,
        out_shape=[shaped(ROWS1, EDGE, lanes1)] * 3 + [shaped(rows, wide_x, 256)] * 3,
        compiler_params=params(),
        cost_estimate=cost(3e-6),
    )(x_below, win, x_above, g2, t1a, bias1a, tab1)
    feat, down = pl.pallas_call(
        level_one_kernel,
        out_shape=[shaped(Y1 * X1, lanes1), shaped(Y2, X2 + 2 * HALO_X2, Z2 * CP)],
        scratch_shapes=[pltpu.VMEM((ROWS1, EDGE, 128), BF)] * 6
        + [pltpu.VMEM((rows, wide_x, 256), BF)] * 3
        + [pltpu.VMEM((rows, wide_x, 128), BF)] * 3
        + [pltpu.VMEM((Y1 * EDGE, lanes1), BF), pltpu.VMEM((4, Y2 * (X2 + EDGE // 2), lanes1), BF)],
        compiler_params=params(),
        cost_estimate=cost(6e-6),
    )(
        z_below, z_above, corner_below, corner_above, *edges, g1, g3, t1a, t1b, bias1a, b_conv1b[None],
        pad_lanes(jnp.swapaxes(w_down2, 1, 2).reshape(8 * C1, C2)), pad_lanes(b_down2[None]), tab1, tab2,
    )

    down, w_conv2a = lax.optimization_barrier((down, w_conv2a))
    t2a = banded(w_conv2a, 2, CP)
    y_below, y_above = shift_along(down[:HALO], down[Y2 - HALO :], "gy")
    wide = jnp.concatenate([y_below, down, y_above], axis=0)
    feat, wide, w_conv2b = lax.optimization_barrier((feat, wide, w_conv2b))
    t2b = banded(w_conv2b, 2, CP)
    one = pl.pallas_call(
        one_kernel, out_shape=shaped(lanes1, Y1 * X1), compiler_params=params(), cost_estimate=cost(2e-6)
    )(feat)
    z_below, z_above = shift_along(wide[:, :, : 2 * CP], wide[:, :, 2 * CP :], "gz")
    bias2a = pad_lanes(b_conv2a[None])
    moved = [shaped(Y2 + 2, X2, 2 * CP)] * 3
    middle = pl.pallas_call(
        level_two_middle_kernel,
        out_shape=[shaped(ROWS2, PITCH2, Z2 * CP)] * 3 + moved,
        compiler_params=params(),
        cost_estimate=cost(3e-6),
    )(wide, t2a, bias2a, tab2)
    two = pl.pallas_call(
        level_two_kernel,
        out_shape=shaped(C2 * Z2, Y2 * X2),
        scratch_shapes=[pltpu.VMEM((ROWS2, PITCH2, 2 * CP), BF)] * 6 + [pltpu.VMEM((Y2 + 2, X2, 2 * CP), BF)] * 6,
        compiler_params=params(),
        cost_estimate=cost(5e-6),
    )(*middle, z_below, z_above, t2a, t2b, bias2a, pad_lanes(b_conv2b[None]), tab2)
    return one.reshape(C1, Z1, Y1 * X1), two.reshape(C2, Z2, Y2 * X2)


def solution(mesh):
    block = P(None, "gz", ("gx", "gy"))
    return jax.shard_map(
        local,
        mesh=mesh,
        in_specs=(block,) + (P(),) * 13,
        out_specs=(block, block),
        check_vma=False,
    )
```

```python
import itertools

import jax
import jax.numpy as jnp
from jax import lax
from jax.experimental import pallas as pl
from jax.experimental.pallas import tpu as pltpu
from jax.sharding import PartitionSpec as P

CX = 64
CY = 32
X1 = CX // 2
Y1 = CY // 2
X2 = X1 // 2
Y2 = Y1 // 2
Z1 = 8
Z2 = 4
C0 = 48
C1 = 64
C2 = 96
CP = 128
HALO = 2
HALO_X = 6
HALO_X2 = 2
XB = 12
XB_BELOW = 2
XB_PITCH = 16
YB = 6
ROWS1 = Y1 + 2 * HALO
ROWS2 = Y2 + 2 * HALO
EDGE = 16
PITCH2 = 32
BF = jnp.bfloat16
F32 = jnp.float32
NN = (((1,), (0,)), ((), ()))
NT = (((1,), (1,)), ((), ()))
VMEM_BYTES = 20 * 1024 * 1024


def mm(a, b, dims=NN):
    return lax.dot_general(a, b, dims, preferred_element_type=F32)


def iota(shape, dim):
    return lax.broadcasted_iota(jnp.int32, shape, dim)


def one_hot(flag):
    return jnp.where(flag, 1.0, 0.0).astype(BF)


def one_hot_rows(key, lanes):
    lane = iota(key.shape, 1)
    return jnp.concatenate([one_hot(key == lane + q) for q in range(0, lanes, 128)], axis=1)


def mask_rows(tab, y_start, rows, pitch, x_of, cell):
    bits = cell.bit_length() - 1
    shape = (rows, pitch, 128)
    y_block = (iota(shape, 0) + (y_start + cell)) >> bits
    x_block = jnp.minimum((x_of(iota(shape, 1)) + XB_BELOW * cell) >> bits, XB - 1)
    hit = one_hot(y_block * XB_PITCH + x_block == iota(shape, 2)).reshape(rows * pitch, 128)
    return mm(hit, tab)


def tissue_tables(t_ref):
    n_y, n_z, n_x = t_ref.shape
    here = lax.axis_index("gz")
    layers = []
    for k in (-1, 0, 1):
        z = here + k
        inside = jnp.where((z >= 0) & (z < n_z), 1.0, 0.0)
        layers.append(t_ref[:, jnp.clip(z, 0, n_z - 1), :].astype(F32) * inside)
    block = iota((128, n_y), 0)
    bits = XB_PITCH.bit_length() - 1
    hot_y = one_hot(lax.axis_index("gy") * 4 - 1 + (block >> bits) == iota((128, n_y), 1))
    block = iota((128, 3 * n_x), 0)
    layer = sum((iota((128, 3 * n_x), 1) >= k * n_x).astype(jnp.int32) for k in (1, 2))
    hot_x = lax.axis_index("gx") * 8 - XB_BELOW + (block & (XB_PITCH - 1)) == iota((128, 3 * n_x), 1) - layer * n_x
    rows = jnp.where(hot_x, mm(hot_y, jnp.concatenate(layers, axis=1).astype(BF)), 0.0).astype(BF)
    shape = (3 * n_x, 384)
    layer = sum((iota(shape, 0) >= k * n_x).astype(jnp.int32) for k in (1, 2))
    lane = iota(shape, 1)

    def spread(first, last):
        place = jnp.where(lane < first, 0, jnp.where(lane < last, 1, 2))
        return mm(rows, one_hot(layer == place)).astype(BF)

    return spread(64, 320), spread(128, 256)


def down1_kernel(
    v_hbm, wd_hbm, b_hbm, t_hbm, out_ref, tab_ref, tab2_ref, v_ref, w_ref, b_ref, t_ref, wd_ref, cells_ref, sems
):
    half = v_ref.shape[2]
    kz = C0 * half
    part = 16 * half
    lanes = Z1 // 2 * C1
    small = ((t_hbm, t_ref), (wd_hbm, w_ref), (b_hbm, b_ref))
    copies = [pltpu.make_async_copy(src, dst, sems.at[n]) for n, (src, dst) in enumerate(small)]
    for n in range(C0 // 16):
        cut = slice(n * 16, n * 16 + 16)
        copies.append(pltpu.make_async_copy(v_hbm.at[cut], v_ref.at[cut], sems.at[len(small) + n]))
    for copy in copies:
        copy.start()

    copies[0].wait()
    tab, tab2 = tissue_tables(t_ref)
    tab_ref[...] = tab
    tab2_ref[...] = tab2
    copies[1].wait()
    copies[2].wait()
    r = iota((kz, 2 * C0), 0)
    l = iota((kz, 2 * C0), 1)
    odd = l >= C0
    spread = one_hot(((r >> 3) == jnp.where(odd, l - C0, l)) & ((r & 1) == odd.astype(jnp.int32)))
    keep = (iota((kz, lanes), 0) & 7) >> 1 == iota((kz, lanes), 1) >> 6
    for ab in range(4):
        pair = w_ref[2 * ab : 2 * ab + 2].reshape(2 * C0, C1)
        wide = jnp.concatenate([pair] * (Z1 // 2), axis=1)
        block = jnp.where(keep, mm(spread, wide), 0.0).astype(BF)
        for n in range(C0 // 16):
            wd_ref[n, ab * part : ab * part + part, :] = block[n * part : n * part + part]

    r = iota((4 * CX, 128), 0)
    select = one_hot_rows(((r & 32) << 2) | (r & 64) | ((r & 31) << 1) | (r >> 7), 4 * CX)
    part = 16 * half
    acc = [0.0, 0.0]
    for n, copy in enumerate(copies[3:]):
        copy.wait()
        for m in range(v_ref.shape[3] // 256):
            v = [v_ref[n * 16 : n * 16 + 16, h, :, m * 256 : m * 256 + 256].reshape(part, 256) for h in range(2)]
            cells = mm(select, jnp.concatenate(v, axis=0), NT).astype(BF)
            for ab in range(4):
                for h in range(2):
                    piece = cells[64 * ab : 64 * ab + 64, h * part : h * part + part]
                    cells_ref[n, h, m * 64 : m * 64 + 64, ab * part : ab * part + part] = piece
        acc = [acc[h] + mm(cells_ref[n, h], wd_ref[n]) for h in range(2)]
    mask = mask_rows(tab[:, 128:256], 0, Y1, X1, lambda x: x, 4)
    bias = twice(b_ref)
    for h in range(2):
        for q in range(2):
            value = finish(acc[h][:, q * 128 : q * 128 + 128], bias, mask, Y1)
            out_ref[:, :, (2 * h + q) * 128 : (2 * h + q + 1) * 128] = value


def twice(b_ref):
    return jnp.concatenate([b_ref[...]] * 2, axis=1)


def fill_banded(w_ref, t_ref, group, pad):
    chan = w_ref.shape[1]
    t_ref[...] = jnp.zeros_like(t_ref)
    for j in range(3):
        for i in range(3):
            for zo in range(group):
                for k in range(3):
                    lane = (3 * j + i) * (group + 2) * pad + (zo + k) * pad
                    t_ref[zo * pad : zo * pad + chan, lane : lane + chan] = w_ref[9 * i + 3 * j + k]


def banded_shape(group, pad):
    return shaped(group * pad, 9 * (group + 2) * pad)


def banded(weights, group, pad):
    def kernel(w_ref, t_ref):
        fill_banded(w_ref, t_ref, group, pad)

    return pl.pallas_call(
        kernel, out_shape=banded_shape(group, pad), compiler_params=params(), cost_estimate=cost(1e-6)
    )(weights)


def conv_group(taps, t_ref, rows, group_out, group_full):
    pitch = taps[0][0][0].shape[1]
    width = sum(piece[2] for piece in taps[0])
    parts = [ref[j : j + rows, :, lane : lane + n] for j in range(3) for tap in taps for ref, lane, n in tap]
    left = jnp.concatenate([p.reshape(rows * pitch, p.shape[2]) for p in parts], axis=1)
    if width == group_full:
        right = t_ref[0:group_out, :]
    else:
        right = jnp.concatenate([t_ref[0:group_out, n * group_full : n * group_full + width] for n in range(9)], axis=1)
    return mm(left, right, NT)


def finish(acc, bias, mask, rows):
    value = jnp.maximum(acc + bias, 0.0) * mask
    return value.astype(BF).reshape(rows, value.shape[0] // rows, value.shape[1])


def fill_sides(left, right, lane, inner):
    cut = slice(lane, lane + inner.shape[2])
    none = jnp.zeros_like(inner[:, :1])
    left[:, :, cut] = jnp.concatenate([none, inner[:, :-1]], axis=1)
    right[:, :, cut] = jnp.concatenate([inner[:, 1:], none], axis=1)


def middle_kernel(win_ref, t_ref, b_ref, tab_ref, w_ref, left_ref, right_ref, out_ref, next_ref):
    fill_banded(w_ref, next_ref, 4, C1)
    for q in range(4):
        fill_sides(left_ref, right_ref, q * 128, win_ref[:, :, q * 128 : q * 128 + 128])
    rows = Y1 + 2
    mask = mask_rows(tab_ref[:, 128:256], -1, rows, X1, lambda x: x, 4)
    acc = conv_group([[(ref, 128, 384)] for ref in (left_ref, win_ref, right_ref)], t_ref, rows, 256, 384)
    for q in range(2):
        cut = slice(q * 128, q * 128 + 128)
        out_ref[:, :, cut] = finish(acc[:, cut], twice(b_ref), mask, rows)


def outer_kernel(win_ref, left_ref, right_ref, zl_ref, zr_ref, t_ref, b_ref, tab_ref, low_ref, high_ref, ll, lr, hl, hr):
    fill_sides(ll, lr, 0, zl_ref[...])
    fill_sides(hl, hr, 0, zr_ref[...])
    own = (left_ref, win_ref, right_ref)
    rows = Y1 + 2
    mask = mask_rows(tab_ref[...], -1, rows, X1, lambda x: x, 4)
    taps = [[(z, 0, 128), (ref, 0, 256)] for z, ref in zip((ll, zl_ref, lr), own)]
    acc = conv_group(taps, t_ref, rows, 256, 384)
    for q in range(2):
        cut = slice(q * 128, q * 128 + 128)
        low_ref[:, :, cut] = finish(acc[:, cut], twice(b_ref), mask[:, cut], rows)
    taps = [[(ref, 384, 128), (z, 0, 128)] for z, ref in zip((hl, zr_ref, hr), own)]
    acc = conv_group(taps, t_ref, rows, 128, 384)
    high_ref[...] = finish(acc, twice(b_ref), mask[:, 256:384], rows)


def fill_edges(copies, pieces):
    line = jnp.concatenate(pieces, axis=1)
    copies[0][...] = line
    for i in (1, 2):
        copies[i][...] = jnp.concatenate([line[:, i:], jnp.zeros_like(line[:, :i])], axis=1)


def edge_masks(tab_ref):
    mask = mask_rows(tab_ref[...], -1, Y1 + 2, EDGE, lambda r: jnp.where(r < 8, r - 5, r + X1 - 9), 4)
    return [mask[:, q * 128 : q * 128 + 128] for q in range(3)]


def edge_group(taps, t_ref, b_ref, masks, inner_ref, moved):
    rows = Y1 + 2
    acc = conv_group(taps, t_ref, rows, 128 * len(masks), 384)
    i0, i1, i2 = moved
    for q, mask in enumerate(masks):
        cut = slice(q * 128, q * 128 + 128)
        edge = finish(acc[:, cut], twice(b_ref), mask, rows)
        inner = inner_ref[:, :, cut][:, 1:-1]
        i0[:, :X1, cut] = jnp.concatenate([edge[:, 4:6], inner], axis=1)
        i1[:, :X1, cut] = jnp.concatenate([edge[:, 5:6], inner, edge[:, 8:9]], axis=1)
        i2[:, :X1, cut] = jnp.concatenate([inner, edge[:, 8:10]], axis=1)
        i0[:, X1:, cut] = edge
        for i, copy in ((1, i1), (2, i2)):
            copy[:, X1:, cut] = jnp.concatenate([edge[:, i:], jnp.zeros((rows, i, 128), BF)], axis=1)


def column_lanes(field, lane, stride=Z1 * C1):
    return [field[:, :, first : first + 128] for first in range(lane, field.shape[2], stride)]


def edge_middle_kernel(xl_ref, win_ref, xr_ref, g_ref, t_ref, b_ref, tab_ref, e0, e1, e2, m0, m1, m2):
    for lane in range(0, Z1 * C1, 128):
        cut = slice(lane, lane + 128)
        inner = win_ref[:, :, cut]
        left, right = (column_lanes(ref, lane) for ref in (xl_ref, xr_ref))
        pieces = left + [inner[:, :2], inner[:, X1 - 2 :]] + right
        fill_edges([e.at[:, :, cut] for e in (e0, e1, e2)], pieces)
    here = edge_masks(tab_ref)[1]
    edge_group([[(e, 128, 384)] for e in (e0, e1, e2)], t_ref, b_ref, (here, here), g_ref, (m0, m1, m2))


def level_one_kernel(
    zl_ref, zr_ref, cl_ref, cr_ref, e0, e1, e2, m0, m1, m2, g1_ref, g3_ref, ta_ref, tb_ref, ba_ref, bb_ref, wd_ref, bd_ref, tab_ref,
    tab2_ref, feat_ref, down_ref, l0, l1, l2, h0, h1, h2, i0, i1, i2, j0, j1, j2, side_ref, d_ref,
):
    own, mid, low, high = (e0, e1, e2), (m0, m1, m2), (i0, i1, i2), (j0, j1, j2)
    for z_ref, c_ref, copies in ((zl_ref, cl_ref, (l0, l1, l2)), (zr_ref, cr_ref, (h0, h1, h2))):
        inner = z_ref[...]
        corner = column_lanes(c_ref, 0, 128)
        fill_edges(copies, corner[:3] + [inner[:, :2], inner[:, X1 - 2 :]] + corner[3:])
    below, here, above = edge_masks(tab_ref)
    taps = [[(z, 0, 128), (e, 0, 256)] for z, e in zip((l0, l1, l2), own)]
    edge_group(taps, ta_ref, ba_ref, (below, here), g1_ref, low)
    taps = [[(e, 384, 128), (z, 0, 128)] for z, e in zip((h0, h1, h2), own)]
    edge_group(taps, ta_ref, ba_ref, (above,), g3_ref, high)

    def cell_of(r):
        return jnp.where(r < X1, r, jnp.where(r < X1 + 8, r - X1 - 4, r - 8))

    mask = mask_rows(tab_ref[:, 128:256], 0, Y1, X1 + EDGE, cell_of, 4)
    first = [[(a, 0, 256), (b, 0, 128)] for a, b in zip(low, mid)]
    second = [[(a, 0, 256), (b, 0, 128)] for a, b in zip(mid, high)]
    for g, taps in enumerate((first, second)):
        acc = conv_group(taps, tb_ref, Y1, 256, 384)
        for q in range(2):
            value = finish(acc[:, q * 128 : q * 128 + 128], twice(bb_ref), mask, Y1)
            cut = slice((2 * g + q) * 128, (2 * g + q + 1) * 128)
            feat_ref[:, cut] = value[:, :X1].reshape(Y1 * X1, 128)
            side_ref[:, cut] = value[:, X1:].reshape(Y1 * EDGE, 128)

    size = 8 * X1
    quarter = size // 4
    r = iota((size, 128), 0)
    select = one_hot_rows(((r & 48) << 2) | ((r & 64) >> 1) | ((r & 15) << 1) | (r >> 7), size)
    for n in range(Y1 // 8):
        cells = mm(select, feat_ref[n * size : n * size + size, :]).astype(BF)
        for q in range(4):
            d_ref[q, n * quarter : n * quarter + quarter, :] = cells[q * quarter : (q + 1) * quarter]
    select = one_hot_rows(((r & 56) << 2) | ((r & 64) >> 2) | ((r & 7) << 1) | (r >> 7), size)
    cells = mm(select, side_ref[...]).astype(BF)
    for q in range(4):
        d_ref[q, Y2 * X2 :, :] = cells[q * quarter : (q + 1) * quarter]
    inner_mask = mask_rows(tab2_ref[:, 128:256], 0, Y2, X2, lambda x: x, 2)
    side_mask = mask_rows(tab2_ref[:, 128:256], 0, Y2, EDGE // 2, lambda r: jnp.where(r < 4, r - 2, r + X2 - 4), 2)
    for z in range(Z2):
        left = jnp.concatenate([d_ref[q, :, z * 128 : z * 128 + 128] for q in range(4)], axis=1)
        acc = mm(left, wd_ref[...])
        inner = finish(acc[: Y2 * X2], bd_ref[...], inner_mask, Y2)
        side = finish(acc[Y2 * X2 :], bd_ref[...], side_mask, Y2)
        down_ref[:, :, z * CP : z * CP + CP] = jnp.concatenate([side[:, 0:2], inner, side[:, 4:6]], axis=1)


def one_kernel(feat_ref, out_ref):
    lanes = feat_ref.shape[1]
    r = iota((lanes, 128), 0)
    order = one_hot_rows(((r & 7) << 6) | (r >> 3), lanes)
    out_ref[...] = mm(order, feat_ref[...], NT).astype(BF)


def fill_pitch(copies, wide):
    pitch = copies[0].shape[1]
    for lane in range(0, wide.shape[2], 128):
        line = wide[:, :, lane : lane + 128]
        for i, copy in enumerate(copies):
            spare = jnp.zeros((line.shape[0], pitch - line.shape[1] + i, 128), BF)
            copy[:, :, lane : lane + 128] = jnp.concatenate([line[:, i:], spare], axis=1)


def level_two_group(taps, t_ref, b_ref, masks, moved):
    rows = Y2 + 2
    acc = conv_group(taps, t_ref, rows, 256, 512)
    for q in range(2):
        cut = slice(q * 128, q * 128 + 128)
        value = finish(acc[:, cut], b_ref[...], masks[q], rows)
        for i, ref in enumerate(moved):
            ref[:, :, cut] = value[:, i : i + X2]


def level_two_masks(tab_ref):
    mask = mask_rows(tab_ref[...], -1, Y2 + 2, PITCH2, lambda x: x - 1, 2)
    return [mask[:, q * 128 : q * 128 + 128] for q in range(3)]


def level_two_middle_kernel(wide_ref, t_ref, b_ref, tab_ref, a0, a1, a2, m0, m1, m2):
    fill_pitch((a0, a1, a2), wide_ref[...])
    here = level_two_masks(tab_ref)[1]
    level_two_group([[(a, 0, 512)] for a in (a0, a1, a2)], t_ref, b_ref, (here, here), (m0, m1, m2))


def level_two_kernel(
    a0, a1, a2, m0, m1, m2, zl_ref, zr_ref, ta_ref, tb_ref, ba_ref, bb_ref, tab_ref, out_ref,
    l0, l1, l2, h0, h1, h2, i0, i1, i2, j0, j1, j2,
):
    fill_pitch((l0, l1, l2), zl_ref[...])
    fill_pitch((h0, h1, h2), zr_ref[...])
    below, here, above = level_two_masks(tab_ref)
    own, mid, low, high = (a0, a1, a2), (m0, m1, m2), (i0, i1, i2), (j0, j1, j2)
    taps = [[(z, 0, 256), (a, 0, 256)] for z, a in zip((l0, l1, l2), own)]
    level_two_group(taps, ta_ref, ba_ref, (below, here), low)
    taps = [[(a, 256, 256), (z, 0, 256)] for z, a in zip((h0, h1, h2), own)]
    level_two_group(taps, ta_ref, ba_ref, (here, above), high)
    mask = mask_rows(tab_ref[:, 128:256], 0, Y2, X2, lambda x: x, 2)
    feat = []
    for pair in ((low, mid), (mid, high)):
        acc = conv_group([[(a, 0, 256), (b, 0, 256)] for a, b in zip(*pair)], tb_ref, Y2, 256, 512)
        for q in range(2):
            feat.append((jnp.maximum(acc[:, q * 128 : q * 128 + 128] + bb_ref[...], 0.0) * mask).astype(BF))
    r = iota((C2 * Z2, 128), 0)
    order = one_hot_rows(((r & 3) << 7) | (r >> 2), Z2 * CP)
    out_ref[...] = mm(order, jnp.concatenate(feat, axis=1), NT).astype(BF)


def partner(index, second, count):
    other = index + 1 if index % 2 == second else index - 1
    return other if 0 <= other < count else None


def swap(value, moves):
    axes = ("gx", "gy", "gz")
    sizes = [lax.axis_size(axis) for axis in axes]
    pairs = []
    for source in itertools.product(*(range(size) for size in sizes)):
        target = [partner(i, moves[axis], size) if axis in moves else i for i, axis, size in zip(source, axes, sizes)]
        if None in target:
            other = sizes[1] - 1 - source[1] if "gy" in moves else source[1] ^ 1
            target = [source[0], other, source[2]]
        pairs.append(tuple((x * sizes[1] + y) * sizes[2] + z for x, y, z in (source, target)))
    return lax.ppermute(value, axes, pairs)


def parity(axis):
    return lax.axis_index(axis) % 2 == 0


def sides(first, second, axis):
    index = lax.axis_index(axis)
    even = parity(axis)
    below = jnp.where(index > 0, jnp.where(even, second, first), jnp.zeros_like(first))
    above = jnp.where(index < lax.axis_size(axis) - 1, jnp.where(even, first, second), jnp.zeros_like(first))
    return below, above


def swaps(low_edge, high_edge, axis):
    even = parity(axis)
    first = swap(jnp.where(even, high_edge, low_edge), {axis: 0})
    second = swap(jnp.where(even, low_edge, high_edge), {axis: 1}) if lax.axis_size(axis) > 2 else first
    return first, second


def shift_along(low_edge, high_edge, axis):
    return sides(*swaps(low_edge, high_edge, axis), axis)


def column_pairs(field):
    return jnp.concatenate([field[:, i : i + 2] for i in range(0, field.shape[1], 2)], axis=2)


def params():
    return pltpu.CompilerParams(vmem_limit_bytes=VMEM_BYTES)


def cost(seconds):
    return pl.CostEstimate(flops=int(1e15 * seconds), bytes_accessed=0, transcendentals=0)


def shaped(*shape):
    return jax.ShapeDtypeStruct(shape, BF)


def pad_lanes(value):
    return jnp.pad(value, [(0, 0)] * (value.ndim - 1) + [(0, CP - value.shape[-1])])


def local(
    volume, tissue, w_down1, b_down1, w_conv1a, b_conv1a, w_conv1b, b_conv1b,
    w_down2, b_down2, w_conv2a, b_conv2a, w_conv2b, b_conv2b,
):
    depth = volume.shape[1]
    lanes1 = Z1 * C1
    half = depth // 2
    operands = [volume.reshape(C0, 2, half, -1), jnp.swapaxes(w_down1, 1, 2), b_down1[None], tissue.transpose(1, 2, 0)]
    operands = [pltpu.with_memory_space_constraint(x, pltpu.HBM) for x in operands]
    own, tab1, tab2 = pl.pallas_call(
        down1_kernel,
        in_specs=[pl.BlockSpec(memory_space=pltpu.HBM)] * 4,
        out_shape=[shaped(Y1, X1, lanes1), shaped(128, 384), shaped(128, 384)],
        scratch_shapes=[pltpu.VMEM(x.shape, x.dtype) for x in operands]
        + [
            pltpu.VMEM((C0 // 16, 64 * half, lanes1 // 2), BF),
            pltpu.VMEM((C0 // 16, 2, Y1 * X1, 64 * half), BF),
            pltpu.SemaphoreType.DMA((3 + C0 // 16,)),
        ],
        compiler_params=params(),
        cost_estimate=cost(4e-6),
    )(*operands)

    t1a = banded(w_conv1a, 4, C1)
    bias1a = b_conv1a[None]

    y_below, y_above = shift_along(own[:HALO], own[Y1 - HALO :], "gy")
    win = jnp.concatenate([y_below, own, y_above], axis=0)
    z_below, z_above = shift_along(win[:, :, :128], win[:, :, lanes1 - 128 :], "gz")
    low, high = win[:, :HALO_X], win[:, X1 - HALO_X :]
    x_got = lax.optimization_barrier(swaps(column_pairs(low), column_pairs(high), "gx"))
    rows = Y1 + 2
    left, right, g2, t1b = pl.pallas_call(
        middle_kernel,
        out_shape=[shaped(ROWS1, X1, lanes1), shaped(ROWS1, X1, lanes1), shaped(rows, X1, 256), banded_shape(4, C1)],
        compiler_params=params(),
        cost_estimate=cost(1e-7),
    )(win, t1a, bias1a, tab1, w_conv1b)

    corner = []
    for lane in (0, lanes1 - 128):
        cut = [jnp.concatenate(column_lanes(got, lane), axis=2) for got in x_got]
        corner.append(jnp.concatenate(sides(*cut, "gx"), axis=2))
    low, high = corner
    low, high, g2, *x_got = lax.optimization_barrier((low, high, g2, *x_got))
    x_below, x_above = sides(*x_got, "gx")
    corner_below, corner_above = shift_along(low, high, "gz")
    g1, g3 = pl.pallas_call(
        outer_kernel,
        out_shape=[shaped(rows, X1, 256), shaped(rows, X1, 128)],
        scratch_shapes=[pltpu.VMEM((ROWS1, X1, 128), BF)] * 4,
        compiler_params=params(),
        cost_estimate=cost(4e-6),
    )(win, left, right, z_below, z_above, t1a, bias1a, tab1)

    wide_x = X1 + EDGE
    edges = pl.pallas_call(
        edge_middle_kernel,
        out_shape=[shaped(ROWS1, EDGE, lanes1)] * 3 + [shaped(rows, wide_x, 256)] * 3,
        compiler_params=params(),
        cost_estimate=cost(3e-6),
    )(x_below, win, x_above, g2, t1a, bias1a, tab1)
    feat, down = pl.pallas_call(
        level_one_kernel,
        out_shape=[shaped(Y1 * X1, lanes1), shaped(Y2, X2 + 2 * HALO_X2, Z2 * CP)],
        scratch_shapes=[pltpu.VMEM((ROWS1, EDGE, 128), BF)] * 6
        + [pltpu.VMEM((rows, wide_x, 256), BF)] * 3
        + [pltpu.VMEM((rows, wide_x, 128), BF)] * 3
        + [pltpu.VMEM((Y1 * EDGE, lanes1), BF), pltpu.VMEM((4, Y2 * (X2 + EDGE // 2), lanes1), BF)],
        compiler_params=params(),
        cost_estimate=cost(6e-6),
    )(
        z_below, z_above, corner_below, corner_above, *edges, g1, g3, t1a, t1b, bias1a, b_conv1b[None],
        pad_lanes(jnp.swapaxes(w_down2, 1, 2).reshape(8 * C1, C2)), pad_lanes(b_down2[None]), tab1, tab2,
    )

    down, w_conv2a = lax.optimization_barrier((down, w_conv2a))
    t2a = banded(w_conv2a, 2, CP)
    y_below, y_above = shift_along(down[:HALO], down[Y2 - HALO :], "gy")
    wide = jnp.concatenate([y_below, down, y_above], axis=0)
    feat, wide, w_conv2b = lax.optimization_barrier((feat, wide, w_conv2b))
    t2b = banded(w_conv2b, 2, CP)
    one = pl.pallas_call(
        one_kernel, out_shape=shaped(lanes1, Y1 * X1), compiler_params=params(), cost_estimate=cost(2e-6)
    )(feat)
    z_below, z_above = shift_along(wide[:, :, : 2 * CP], wide[:, :, 2 * CP :], "gz")
    bias2a = pad_lanes(b_conv2a[None])
    moved = [shaped(Y2 + 2, X2, 2 * CP)] * 3
    middle = pl.pallas_call(
        level_two_middle_kernel,
        out_shape=[shaped(ROWS2, PITCH2, Z2 * CP)] * 3 + moved,
        compiler_params=params(),
        cost_estimate=cost(3e-6),
    )(wide, t2a, bias2a, tab2)
    two = pl.pallas_call(
        level_two_kernel,
        out_shape=shaped(C2 * Z2, Y2 * X2),
        scratch_shapes=[pltpu.VMEM((ROWS2, PITCH2, 2 * CP), BF)] * 6 + [pltpu.VMEM((Y2 + 2, X2, 2 * CP), BF)] * 6,
        compiler_params=params(),
        cost_estimate=cost(5e-6),
    )(*middle, z_below, z_above, t2a, t2b, bias2a, pad_lanes(b_conv2b[None]), tab2)
    return one.reshape(C1, Z1, Y1 * X1), two.reshape(C2, Z2, Y2 * X2)


def solution(mesh):
    block = P(None, "gz", ("gx", "gy"))
    return jax.shard_map(
        local,
        mesh=mesh,
        in_specs=(block,) + (P(),) * 13,
        out_specs=(block, block),
        check_vma=False,
    )
```

```python
import itertools

import jax
import jax.numpy as jnp
from jax import lax
from jax.experimental import pallas as pl
from jax.experimental.pallas import tpu as pltpu
from jax.sharding import PartitionSpec as P

CX = 64
CY = 32
X1 = CX // 2
Y1 = CY // 2
X2 = X1 // 2
Y2 = Y1 // 2
Z1 = 8
Z2 = 4
C0 = 48
C1 = 64
C2 = 96
CP = 128
HALO = 2
HALO_X = 6
HALO_X2 = 2
XB = 12
XB_BELOW = 2
XB_PITCH = 16
YB = 6
ROWS1 = Y1 + 2 * HALO
ROWS2 = Y2 + 2 * HALO
EDGE = 16
PITCH2 = 32
FACE = HALO_X // 2 * Z1 * C1
BF = jnp.bfloat16
F32 = jnp.float32
NN = (((1,), (0,)), ((), ()))
NT = (((1,), (1,)), ((), ()))
VMEM_BYTES = 20 * 1024 * 1024


def mm(a, b, dims=NN):
    return lax.dot_general(a, b, dims, preferred_element_type=F32)


def iota(shape, dim):
    return lax.broadcasted_iota(jnp.int32, shape, dim)


def one_hot(flag):
    return jnp.where(flag, 1.0, 0.0).astype(BF)


def one_hot_rows(key, lanes):
    lane = iota(key.shape, 1)
    return jnp.concatenate([one_hot(key == lane + q) for q in range(0, lanes, 128)], axis=1)


def mask_rows(tab, y_start, rows, pitch, x_of, cell):
    bits = cell.bit_length() - 1
    shape = (rows, pitch, 128)
    y_block = (iota(shape, 0) + (y_start + cell)) >> bits
    x_block = jnp.minimum((x_of(iota(shape, 1)) + XB_BELOW * cell) >> bits, XB - 1)
    hit = one_hot(y_block * XB_PITCH + x_block == iota(shape, 2)).reshape(rows * pitch, 128)
    return mm(hit, tab).astype(BF)


def tissue_tables(t_ref):
    n_y, n_z, n_x = t_ref.shape
    here = lax.axis_index("gz")
    layers = []
    for k in (-1, 0, 1):
        z = here + k
        inside = jnp.where((z >= 0) & (z < n_z), 1.0, 0.0)
        layers.append(t_ref[:, jnp.clip(z, 0, n_z - 1), :].astype(F32) * inside)
    block = iota((128, n_y), 0)
    bits = XB_PITCH.bit_length() - 1
    hot_y = one_hot(lax.axis_index("gy") * 4 - 1 + (block >> bits) == iota((128, n_y), 1))
    block = iota((128, 3 * n_x), 0)
    layer = sum((iota((128, 3 * n_x), 1) >= k * n_x).astype(jnp.int32) for k in (1, 2))
    hot_x = lax.axis_index("gx") * 8 - XB_BELOW + (block & (XB_PITCH - 1)) == iota((128, 3 * n_x), 1) - layer * n_x
    rows = jnp.where(hot_x, mm(hot_y, jnp.concatenate(layers, axis=1).astype(BF)), 0.0).astype(BF)
    shape = (3 * n_x, 384)
    layer = sum((iota(shape, 0) >= k * n_x).astype(jnp.int32) for k in (1, 2))
    lane = iota(shape, 1)

    def spread(first, last):
        place = jnp.where(lane < first, 0, jnp.where(lane < last, 1, 2))
        return mm(rows, one_hot(layer == place)).astype(BF)

    return spread(64, 320), spread(128, 256)


def second_cell(r):
    return jnp.where(r < X1, r, jnp.where(r < X1 + 8, r - X1 - 4, r - 8))


def down1_kernel(
    v_hbm, wd_hbm, b_hbm, t_hbm, out_ref, face_ref, inner_ref, edge_ref, second_ref, down_ref, two_ref, last_ref,
    v_ref, w_ref, b_ref, t_ref, wd_ref, cells_ref, sems,
):
    half = v_ref.shape[2]
    kz = C0 * half
    part = 16 * half
    lanes = Z1 // 2 * C1
    small = ((t_hbm, t_ref), (wd_hbm, w_ref), (b_hbm, b_ref))
    copies = [pltpu.make_async_copy(src, dst, sems.at[n]) for n, (src, dst) in enumerate(small)]
    for n in range(C0 // 16):
        cut = slice(n * 16, n * 16 + 16)
        copies.append(pltpu.make_async_copy(v_hbm.at[cut], v_ref.at[cut], sems.at[len(small) + n]))
    for copy in copies:
        copy.start()

    copies[0].wait()
    tab, tab2 = tissue_tables(t_ref)
    here, here2 = tab[:, 128:256], tab2[:, 128:256]
    inner_ref[...] = mask_rows(tab, -1, Y1 + 2, X1, lambda x: x, 4)
    edge_ref[...] = mask_rows(tab, -1, Y1 + 2, EDGE, lambda r: jnp.where(r < 8, r - 5, r + X1 - 9), 4)
    second_ref[...] = mask_rows(here, 0, Y1, X1 + EDGE, second_cell, 4)
    down_ref[: Y2 * X2] = mask_rows(here2, 0, Y2, X2, lambda x: x, 2)
    down_ref[Y2 * X2 :] = mask_rows(here2, 0, Y2, EDGE // 2, lambda r: jnp.where(r < 4, r - 2, r + X2 - 4), 2)
    two_ref[...] = mask_rows(tab2, -1, Y2 + 2, PITCH2, lambda x: x - 1, 2)
    last_ref[...] = mask_rows(here2, 0, Y2, X2, lambda x: x, 2)
    copies[1].wait()
    copies[2].wait()
    r = iota((kz, 2 * C0), 0)
    l = iota((kz, 2 * C0), 1)
    odd = l >= C0
    spread = one_hot(((r >> 3) == jnp.where(odd, l - C0, l)) & ((r & 1) == odd.astype(jnp.int32)))
    keep = (iota((kz, lanes), 0) & 7) >> 1 == iota((kz, lanes), 1) >> 6
    for ab in range(4):
        pair = w_ref[2 * ab : 2 * ab + 2].reshape(2 * C0, C1)
        wide = jnp.concatenate([pair] * (Z1 // 2), axis=1)
        block = jnp.where(keep, mm(spread, wide), 0.0).astype(BF)
        for n in range(C0 // 16):
            wd_ref[n, ab * part : ab * part + part, :] = block[n * part : n * part + part]

    r = iota((4 * CX, 128), 0)
    select = one_hot_rows(((r & 32) << 2) | (r & 64) | ((r & 31) << 1) | (r >> 7), 4 * CX)
    part = 16 * half
    acc = [0.0, 0.0]
    for n, copy in enumerate(copies[3:]):
        copy.wait()
        for m in range(v_ref.shape[3] // 256):
            v = [v_ref[n * 16 : n * 16 + 16, h, :, m * 256 : m * 256 + 256].reshape(part, 256) for h in range(2)]
            cells = mm(select, jnp.concatenate(v, axis=0), NT).astype(BF)
            for ab in range(4):
                for h in range(2):
                    piece = cells[64 * ab : 64 * ab + 64, h * part : h * part + part]
                    cells_ref[n, h, m * 64 : m * 64 + 64, ab * part : ab * part + part] = piece
        acc = [acc[h] + mm(cells_ref[n, h], wd_ref[n]) for h in range(2)]
    mask = inner_ref[X1 : X1 + Y1 * X1, 128:256]
    bias = twice(b_ref)
    for h in range(2):
        for q in range(2):
            value = finish(acc[h][:, q * 128 : q * 128 + 128], bias, mask, Y1)
            chunk = 2 * h + q
            out_ref[:, :, chunk * 128 : chunk * 128 + 128] = value
            for side, start in enumerate((0, X1 - HALO_X)):
                for pair in range(HALO_X // 2):
                    lane = side * FACE + (chunk * (HALO_X // 2) + pair) * 128
                    face_ref[:, :, lane : lane + 128] = value[:, start + 2 * pair : start + 2 * pair + 2]


def twice(b_ref):
    return jnp.concatenate([b_ref[...]] * 2, axis=1)


def fill_banded(w_ref, t_ref, group, pad):
    chan = w_ref.shape[1]
    t_ref[...] = jnp.zeros_like(t_ref)
    for j in range(3):
        for i in range(3):
            for zo in range(group):
                for k in range(3):
                    lane = (3 * j + i) * (group + 2) * pad + (zo + k) * pad
                    t_ref[zo * pad : zo * pad + chan, lane : lane + chan] = w_ref[9 * i + 3 * j + k]


def banded_shape(group, pad):
    return shaped(group * pad, 9 * (group + 2) * pad)


def banded(weights, group, pad):
    def kernel(w_ref, t_ref):
        fill_banded(w_ref, t_ref, group, pad)

    return pl.pallas_call(
        kernel, out_shape=banded_shape(group, pad), compiler_params=params(), cost_estimate=cost(1e-6)
    )(weights)


def conv_group(taps, t_ref, rows, group_out, group_full, split=False):
    pitch = taps[0][0][0].shape[1]
    width = sum(piece[2] for piece in taps[0])
    total = 0.0
    for js in ((0,), (1,), (2,)) if split else ((0, 1, 2),):
        parts = [ref[j : j + rows, :, lane : lane + n] for j in js for tap in taps for ref, lane, n in tap]
        left = jnp.concatenate([p.reshape(rows * pitch, p.shape[2]) for p in parts], axis=1)
        first, last = 3 * js[0], 3 * js[-1] + 3
        if width == group_full:
            right = t_ref[0:group_out, first * group_full : last * group_full]
        else:
            right = jnp.concatenate([t_ref[0:group_out, n * group_full : n * group_full + width] for n in range(first, last)], axis=1)
        total = total + mm(left, right, NT)
    return total


def finish(acc, bias, mask, rows):
    value = jnp.maximum(acc + bias, 0.0) * mask
    return value.astype(BF).reshape(rows, value.shape[0] // rows, value.shape[1])


def fill_sides(left, right, lane, inner):
    cut = slice(lane, lane + inner.shape[2])
    none = jnp.zeros_like(inner[:, :1])
    left[:, :, cut] = jnp.concatenate([none, inner[:, :-1]], axis=1)
    right[:, :, cut] = jnp.concatenate([inner[:, 1:], none], axis=1)


def middle_kernel(win_ref, t_ref, b_ref, mask_ref, w_ref, left_ref, right_ref, out_ref, next_ref):
    fill_banded(w_ref, next_ref, 4, C1)
    for q in range(4):
        fill_sides(left_ref, right_ref, q * 128, win_ref[:, :, q * 128 : q * 128 + 128])
    rows = Y1 + 2
    mask = mask_ref[:, 128:256]
    acc = conv_group([[(ref, 128, 384)] for ref in (left_ref, win_ref, right_ref)], t_ref, rows, 256, 384)
    for q in range(2):
        cut = slice(q * 128, q * 128 + 128)
        out_ref[:, :, cut] = finish(acc[:, cut], twice(b_ref), mask, rows)


def outer_kernel(win_ref, left_ref, right_ref, zl_ref, zr_ref, t_ref, b_ref, mask, low_ref, high_ref, ll, lr, hl, hr):
    fill_sides(ll, lr, 0, zl_ref[...])
    fill_sides(hl, hr, 0, zr_ref[...])
    own = (left_ref, win_ref, right_ref)
    rows = Y1 + 2
    taps = [[(z, 0, 128), (ref, 0, 256)] for z, ref in zip((ll, zl_ref, lr), own)]
    acc = conv_group(taps, t_ref, rows, 256, 384)
    for q in range(2):
        cut = slice(q * 128, q * 128 + 128)
        low_ref[:, :, cut] = finish(acc[:, cut], twice(b_ref), mask[:, cut], rows)
    taps = [[(ref, 384, 128), (z, 0, 128)] for z, ref in zip((hl, zr_ref, hr), own)]
    acc = conv_group(taps, t_ref, rows, 128, 384)
    high_ref[...] = finish(acc, twice(b_ref), mask[:, 256:384], rows)


def fill_edges(copies, pieces):
    line = jnp.concatenate(pieces, axis=1)
    copies[0][...] = line
    for i in (1, 2):
        copies[i][...] = jnp.concatenate([line[:, i:], jnp.zeros_like(line[:, :i])], axis=1)


def lane_chunks(ref):
    return [ref[:, lane : lane + 128] for lane in range(0, ref.shape[1], 128)]


def edge_group(taps, t_ref, b_ref, masks, inner_ref, moved):
    rows = Y1 + 2
    acc = conv_group(taps, t_ref, rows, 128 * len(masks), 384)
    i0, i1, i2 = moved
    for q, mask in enumerate(masks):
        cut = slice(q * 128, q * 128 + 128)
        edge = finish(acc[:, cut], twice(b_ref), mask, rows)
        inner = inner_ref[:, :, cut][:, 1:-1]
        i0[:, :X1, cut] = jnp.concatenate([edge[:, 4:6], inner], axis=1)
        i1[:, :X1, cut] = jnp.concatenate([edge[:, 5:6], inner, edge[:, 8:9]], axis=1)
        i2[:, :X1, cut] = jnp.concatenate([inner, edge[:, 8:10]], axis=1)
        i0[:, X1:, cut] = edge
        for i, copy in ((1, i1), (2, i2)):
            copy[:, X1:, cut] = jnp.concatenate([edge[:, i:], jnp.zeros((rows, i, 128), BF)], axis=1)


def column_pieces(ref, chunk, side=0):
    first = (side + chunk) * (HALO_X // 2) * 128
    return [ref[:, :, lane : lane + 128] for lane in range(first, first + HALO_X // 2 * 128, 128)]


def edge_middle_kernel(xl_ref, win_ref, xr_ref, g_ref, t_ref, b_ref, mask_ref, e0, e1, e2, m0, m1, m2):
    for lane in range(0, Z1 * C1, 128):
        cut = slice(lane, lane + 128)
        inner = win_ref[:, :, cut]
        left, right = (column_pieces(ref, lane // 128) for ref in (xl_ref, xr_ref))
        pieces = left + [inner[:, :2], inner[:, X1 - 2 :]] + right
        fill_edges([e.at[:, :, cut] for e in (e0, e1, e2)], pieces)
    here = mask_ref[:, 128:256]
    edge_group([[(e, 128, 384)] for e in (e0, e1, e2)], t_ref, b_ref, (here, here), g_ref, (m0, m1, m2))


def level_one_kernel(
    zl_ref, zr_ref, cl_ref, cr_ref, e0, e1, e2, m0, m1, m2, g1_ref, g3_ref, ta_ref, tb_ref, ba_ref, bb_ref, wd_ref, bd_ref, edge_ref,
    second_ref, last_ref, feat_ref, down_ref, l0, l1, l2, h0, h1, h2, i0, i1, i2, j0, j1, j2, side_ref, d_ref,
):
    own, mid, low, high = (e0, e1, e2), (m0, m1, m2), (i0, i1, i2), (j0, j1, j2)
    for z_ref, c_ref, copies in ((zl_ref, cl_ref, (l0, l1, l2)), (zr_ref, cr_ref, (h0, h1, h2))):
        inner = z_ref[...]
        fill_edges(copies, column_pieces(c_ref, 0) + [inner[:, :2], inner[:, X1 - 2 :]] + column_pieces(c_ref, 1))
    below, here, above = lane_chunks(edge_ref)
    taps = [[(z, 0, 128), (e, 0, 256)] for z, e in zip((l0, l1, l2), own)]
    edge_group(taps, ta_ref, ba_ref, (below, here), g1_ref, low)
    taps = [[(e, 384, 128), (z, 0, 128)] for z, e in zip((h0, h1, h2), own)]
    edge_group(taps, ta_ref, ba_ref, (above,), g3_ref, high)

    first = [[(a, 0, 256), (b, 0, 128)] for a, b in zip(low, mid)]
    second = [[(a, 0, 256), (b, 0, 128)] for a, b in zip(mid, high)]
    for g, taps in enumerate((first, second)):
        acc = conv_group(taps, tb_ref, Y1, 256, 384)
        for q in range(2):
            value = finish(acc[:, q * 128 : q * 128 + 128], twice(bb_ref), second_ref[...], Y1)
            cut = slice((2 * g + q) * 128, (2 * g + q + 1) * 128)
            feat_ref[:, cut] = value[:, :X1].reshape(Y1 * X1, 128)
            side_ref[:, cut] = value[:, X1:].reshape(Y1 * EDGE, 128)

    size = 8 * X1
    quarter = size // 4
    r = iota((size, 128), 0)
    select = one_hot_rows(((r & 48) << 2) | ((r & 64) >> 1) | ((r & 15) << 1) | (r >> 7), size)
    for n in range(Y1 // 8):
        cells = mm(select, feat_ref[n * size : n * size + size, :]).astype(BF)
        for q in range(4):
            d_ref[q, n * quarter : n * quarter + quarter, :] = cells[q * quarter : (q + 1) * quarter]
    select = one_hot_rows(((r & 56) << 2) | ((r & 64) >> 2) | ((r & 7) << 1) | (r >> 7), size)
    cells = mm(select, side_ref[...]).astype(BF)
    for q in range(4):
        d_ref[q, Y2 * X2 :, :] = cells[q * quarter : (q + 1) * quarter]
    for z in range(Z2):
        left = jnp.concatenate([d_ref[q, :, z * 128 : z * 128 + 128] for q in range(4)], axis=1)
        acc = mm(left, wd_ref[...])
        inner = finish(acc[: Y2 * X2], bd_ref[...], last_ref[: Y2 * X2], Y2)
        side = finish(acc[Y2 * X2 :], bd_ref[...], last_ref[Y2 * X2 :], Y2)
        down_ref[:, :, z * CP : z * CP + CP] = jnp.concatenate([side[:, 0:2], inner, side[:, 4:6]], axis=1)


def one_kernel(feat_ref, out_ref):
    lanes = feat_ref.shape[1]
    r = iota((lanes, 128), 0)
    order = one_hot_rows(((r & 7) << 6) | (r >> 3), lanes)
    out_ref[...] = mm(order, feat_ref[...], NT).astype(BF)


def fill_pitch(copies, wide):
    pitch = copies[0].shape[1]
    for lane in range(0, wide.shape[2], 128):
        line = wide[:, :, lane : lane + 128]
        for i, copy in enumerate(copies):
            spare = jnp.zeros((line.shape[0], pitch - line.shape[1] + i, 128), BF)
            copy[:, :, lane : lane + 128] = jnp.concatenate([line[:, i:], spare], axis=1)


def level_two_group(taps, t_ref, b_ref, masks, moved):
    rows = Y2 + 2
    acc = conv_group(taps, t_ref, rows, 256, 512, split=True)
    for q in range(2):
        cut = slice(q * 128, q * 128 + 128)
        value = finish(acc[:, cut], b_ref[...], masks[q], rows)
        for i, ref in enumerate(moved):
            ref[:, :, cut] = value[:, i : i + X2]


def level_two_middle_kernel(wide_ref, t_ref, b_ref, mask_ref, a0, a1, a2, m0, m1, m2):
    fill_pitch((a0, a1, a2), wide_ref[...])
    here = mask_ref[:, 128:256]
    level_two_group([[(a, 0, 512)] for a in (a0, a1, a2)], t_ref, b_ref, (here, here), (m0, m1, m2))


def level_two_kernel(
    a0, a1, a2, m0, m1, m2, zl_ref, zr_ref, ta_ref, tb_ref, ba_ref, bb_ref, mask_ref, last_ref, out_ref,
    l0, l1, l2, h0, h1, h2, i0, i1, i2, j0, j1, j2,
):
    fill_pitch((l0, l1, l2), zl_ref[...])
    fill_pitch((h0, h1, h2), zr_ref[...])
    below, here, above = lane_chunks(mask_ref)
    own, mid, low, high = (a0, a1, a2), (m0, m1, m2), (i0, i1, i2), (j0, j1, j2)
    taps = [[(z, 0, 256), (a, 0, 256)] for z, a in zip((l0, l1, l2), own)]
    level_two_group(taps, ta_ref, ba_ref, (below, here), low)
    taps = [[(a, 256, 256), (z, 0, 256)] for z, a in zip((h0, h1, h2), own)]
    level_two_group(taps, ta_ref, ba_ref, (here, above), high)
    feat = []
    for pair in ((low, mid), (mid, high)):
        acc = conv_group([[(a, 0, 256), (b, 0, 256)] for a, b in zip(*pair)], tb_ref, Y2, 256, 512, split=True)
        for q in range(2):
            feat.append(finish(acc[:, q * 128 : q * 128 + 128], bb_ref[...], last_ref[...], 1)[0])
    r = iota((C2 * Z2, 128), 0)
    order = one_hot_rows(((r & 3) << 7) | (r >> 2), Z2 * CP)
    out_ref[...] = mm(order, jnp.concatenate(feat, axis=1), NT).astype(BF)


def partner(index, second, count):
    other = index + 1 if index % 2 == second else index - 1
    return other if 0 <= other < count else None


def swap(value, moves):
    axes = ("gx", "gy", "gz")
    sizes = [lax.axis_size(axis) for axis in axes]
    pairs = []
    for source in itertools.product(*(range(size) for size in sizes)):
        target = [partner(i, moves[axis], size) if axis in moves else i for i, axis, size in zip(source, axes, sizes)]
        if None in target:
            other = sizes[1] - 1 - source[1] if "gy" in moves else source[1] ^ 1
            target = [source[0], other, source[2]]
        pairs.append(tuple((x * sizes[1] + y) * sizes[2] + z for x, y, z in (source, target)))
    return lax.ppermute(value, axes, pairs)


def parity(axis):
    return lax.axis_index(axis) % 2 == 0


def sides(first, second, axis):
    index = lax.axis_index(axis)
    even = parity(axis)
    below = jnp.where(index > 0, jnp.where(even, second, first), jnp.zeros_like(first))
    above = jnp.where(index < lax.axis_size(axis) - 1, jnp.where(even, first, second), jnp.zeros_like(first))
    return below, above


def swaps(low_edge, high_edge, axis):
    even = parity(axis)
    first = swap(jnp.where(even, high_edge, low_edge), {axis: 0})
    second = swap(jnp.where(even, low_edge, high_edge), {axis: 1}) if lax.axis_size(axis) > 2 else first
    return first, second


def shift_along(low_edge, high_edge, axis):
    return sides(*swaps(low_edge, high_edge, axis), axis)


def params():
    return pltpu.CompilerParams(vmem_limit_bytes=VMEM_BYTES)


def cost(seconds):
    return pl.CostEstimate(flops=int(1e15 * seconds), bytes_accessed=0, transcendentals=0)


def shaped(*shape):
    return jax.ShapeDtypeStruct(shape, BF)


def pad_lanes(value):
    return jnp.pad(value, [(0, 0)] * (value.ndim - 1) + [(0, CP - value.shape[-1])])


def local(
    volume, tissue, w_down1, b_down1, w_conv1a, b_conv1a, w_conv1b, b_conv1b,
    w_down2, b_down2, w_conv2a, b_conv2a, w_conv2b, b_conv2b,
):
    depth = volume.shape[1]
    lanes1 = Z1 * C1
    half = depth // 2
    operands = [volume.reshape(C0, 2, half, -1), jnp.swapaxes(w_down1, 1, 2), b_down1[None], tissue.transpose(1, 2, 0)]
    operands = [pltpu.with_memory_space_constraint(x, pltpu.HBM) for x in operands]
    own, faces, inner_mask, edge_mask, second_mask, down_mask, two_mask, last_mask = pl.pallas_call(
        down1_kernel,
        in_specs=[pl.BlockSpec(memory_space=pltpu.HBM)] * 4,
        out_shape=[
            shaped(Y1, X1, lanes1),
            shaped(Y1, 2, 2 * FACE),
            shaped((Y1 + 2) * X1, 384),
            shaped((Y1 + 2) * EDGE, 384),
            shaped(Y1 * (X1 + EDGE), 128),
            shaped(Y2 * (X2 + EDGE // 2), 128),
            shaped((Y2 + 2) * PITCH2, 384),
            shaped(Y2 * X2, 128),
        ],
        scratch_shapes=[pltpu.VMEM(x.shape, x.dtype) for x in operands]
        + [
            pltpu.VMEM((C0 // 16, 64 * half, lanes1 // 2), BF),
            pltpu.VMEM((C0 // 16, 2, Y1 * X1, 64 * half), BF),
            pltpu.SemaphoreType.DMA((3 + C0 // 16,)),
        ],
        compiler_params=params(),
        cost_estimate=cost(4e-6),
    )(*operands)

    t1a = banded(w_conv1a, 4, C1)
    bias1a = b_conv1a[None]

    def with_halo(field):
        below, above = shift_along(field[:HALO], field[field.shape[0] - HALO :], "gy")
        return jnp.concatenate([below, field, above], axis=0)

    faces = with_halo(faces)
    win = with_halo(own)
    z_below, z_above = shift_along(win[:, :, :128], win[:, :, lanes1 - 128 :], "gz")
    x_got = lax.optimization_barrier(swaps(faces[:, :, :FACE], faces[:, :, FACE:], "gx"))
    rows = Y1 + 2
    left, right, g2, t1b = pl.pallas_call(
        middle_kernel,
        out_shape=[shaped(ROWS1, X1, lanes1), shaped(ROWS1, X1, lanes1), shaped(rows, X1, 256), banded_shape(4, C1)],
        compiler_params=params(),
        cost_estimate=cost(1e-7),
    )(win, t1a, bias1a, inner_mask, w_conv1b)

    corner = HALO_X // 2 * 2 * C1
    low, high = (jnp.concatenate([got[:, :, cut] for got in x_got], axis=2) for cut in (slice(corner), slice(FACE - corner, FACE)))
    low, high, g2, *x_got = lax.optimization_barrier((low, high, g2, *x_got))
    x_below, x_above = sides(*x_got, "gx")
    corner_got = swaps(low, high, "gz")
    g1, g3 = pl.pallas_call(
        outer_kernel,
        out_shape=[shaped(rows, X1, 256), shaped(rows, X1, 128)],
        scratch_shapes=[pltpu.VMEM((ROWS1, X1, 128), BF)] * 4,
        compiler_params=params(),
        cost_estimate=cost(4e-6),
    )(win, left, right, z_below, z_above, t1a, bias1a, inner_mask)

    *corner_got, g1, g3 = lax.optimization_barrier((*corner_got, g1, g3))
    corner_below, corner_above = (
        jnp.concatenate(sides(got[:, :, :corner], got[:, :, corner:], "gx"), axis=2) for got in sides(*corner_got, "gz")
    )
    wide_x = X1 + EDGE
    edges = pl.pallas_call(
        edge_middle_kernel,
        out_shape=[shaped(ROWS1, EDGE, lanes1)] * 3 + [shaped(rows, wide_x, 256)] * 3,
        compiler_params=params(),
        cost_estimate=cost(3e-6),
    )(x_below, win, x_above, g2, t1a, bias1a, edge_mask)
    feat, down = pl.pallas_call(
        level_one_kernel,
        out_shape=[shaped(Y1 * X1, lanes1), shaped(Y2, X2 + 2 * HALO_X2, Z2 * CP)],
        scratch_shapes=[pltpu.VMEM((ROWS1, EDGE, 128), BF)] * 6
        + [pltpu.VMEM((rows, wide_x, 256), BF)] * 3
        + [pltpu.VMEM((rows, wide_x, 128), BF)] * 3
        + [pltpu.VMEM((Y1 * EDGE, lanes1), BF), pltpu.VMEM((4, Y2 * (X2 + EDGE // 2), lanes1), BF)],
        compiler_params=params(),
        cost_estimate=cost(6e-6),
    )(
        z_below, z_above, corner_below, corner_above, *edges, g1, g3, t1a, t1b, bias1a, b_conv1b[None],
        pad_lanes(jnp.swapaxes(w_down2, 1, 2).reshape(8 * C1, C2)), pad_lanes(b_down2[None]), edge_mask, second_mask, down_mask,
    )

    down, w_conv2a = lax.optimization_barrier((down, w_conv2a))
    t2a = banded(w_conv2a, 2, CP)
    wide = with_halo(down)
    feat, wide, w_conv2b = lax.optimization_barrier((feat, wide, w_conv2b))
    t2b = banded(w_conv2b, 2, CP)
    one = pl.pallas_call(
        one_kernel, out_shape=shaped(lanes1, Y1 * X1), compiler_params=params(), cost_estimate=cost(2e-6)
    )(feat)
    z_below, z_above = shift_along(wide[:, :, : 2 * CP], wide[:, :, 2 * CP :], "gz")
    bias2a = pad_lanes(b_conv2a[None])
    moved = [shaped(Y2 + 2, X2, 2 * CP)] * 3
    middle = pl.pallas_call(
        level_two_middle_kernel,
        out_shape=[shaped(ROWS2, PITCH2, Z2 * CP)] * 3 + moved,
        compiler_params=params(),
        cost_estimate=cost(3e-6),
    )(wide, t2a, bias2a, two_mask)
    two = pl.pallas_call(
        level_two_kernel,
        out_shape=shaped(C2 * Z2, Y2 * X2),
        scratch_shapes=[pltpu.VMEM((ROWS2, PITCH2, 2 * CP), BF)] * 6 + [pltpu.VMEM((Y2 + 2, X2, 2 * CP), BF)] * 6,
        compiler_params=params(),
        cost_estimate=cost(5e-6),
    )(*middle, z_below, z_above, t2a, t2b, bias2a, pad_lanes(b_conv2b[None]), two_mask, last_mask)
    return one.reshape(C1, Z1, Y1 * X1), two.reshape(C2, Z2, Y2 * X2)


def solution(mesh):
    block = P(None, "gz", ("gx", "gy"))
    return jax.shard_map(
        local,
        mesh=mesh,
        in_specs=(block,) + (P(),) * 13,
        out_specs=(block, block),
        check_vma=False,
    )
```

```python
import itertools

import jax
import jax.numpy as jnp
from jax import lax
from jax.experimental import pallas as pl
from jax.experimental.pallas import tpu as pltpu
from jax.sharding import PartitionSpec as P

CX = 64
CY = 32
X1 = CX // 2
Y1 = CY // 2
X2 = X1 // 2
Y2 = Y1 // 2
Z1 = 8
Z2 = 4
C0 = 48
C1 = 64
C2 = 96
CP = 128
HALO = 2
HALO_X = 6
HALO_X2 = 2
XB = 12
XB_BELOW = 2
XB_PITCH = 16
YB = 6
ROWS1 = Y1 + 2 * HALO
ROWS2 = Y2 + 2 * HALO
EDGE = 16
PITCH2 = 32
FACE = HALO_X // 2 * Z1 * C1
BF = jnp.bfloat16
F32 = jnp.float32
NN = (((1,), (0,)), ((), ()))
NT = (((1,), (1,)), ((), ()))
VMEM_BYTES = 20 * 1024 * 1024


def mm(a, b, dims=NN):
    return lax.dot_general(a, b, dims, preferred_element_type=F32)


def iota(shape, dim):
    return lax.broadcasted_iota(jnp.int32, shape, dim)


def one_hot(flag):
    return jnp.where(flag, 1.0, 0.0).astype(BF)


def one_hot_rows(key, lanes):
    lane = iota(key.shape, 1)
    return jnp.concatenate([one_hot(key == lane + q) for q in range(0, lanes, 128)], axis=1)


def mask_rows(tab, y_start, rows, pitch, x_of, cell):
    bits = cell.bit_length() - 1
    shape = (rows, pitch, 128)
    y_block = (iota(shape, 0) + (y_start + cell)) >> bits
    x_block = jnp.minimum((x_of(iota(shape, 1)) + XB_BELOW * cell) >> bits, XB - 1)
    hit = one_hot(y_block * XB_PITCH + x_block == iota(shape, 2)).reshape(rows * pitch, 128)
    return mm(hit, tab)


def tissue_tables(t_ref):
    n_y, n_z, n_x = t_ref.shape
    here = lax.axis_index("gz")
    layers = []
    for k in (-1, 0, 1):
        z = here + k
        inside = jnp.where((z >= 0) & (z < n_z), 1.0, 0.0)
        layers.append(t_ref[:, jnp.clip(z, 0, n_z - 1), :].astype(F32) * inside)
    block = iota((128, n_y), 0)
    bits = XB_PITCH.bit_length() - 1
    hot_y = one_hot(lax.axis_index("gy") * 4 - 1 + (block >> bits) == iota((128, n_y), 1))
    block = iota((128, 3 * n_x), 0)
    layer = sum((iota((128, 3 * n_x), 1) >= k * n_x).astype(jnp.int32) for k in (1, 2))
    hot_x = lax.axis_index("gx") * 8 - XB_BELOW + (block & (XB_PITCH - 1)) == iota((128, 3 * n_x), 1) - layer * n_x
    rows = jnp.where(hot_x, mm(hot_y, jnp.concatenate(layers, axis=1).astype(BF)), 0.0).astype(BF)
    shape = (3 * n_x, 384)
    layer = sum((iota(shape, 0) >= k * n_x).astype(jnp.int32) for k in (1, 2))
    lane = iota(shape, 1)

    def spread(first, last):
        place = jnp.where(lane < first, 0, jnp.where(lane < last, 1, 2))
        return mm(rows, one_hot(layer == place)).astype(BF)

    return spread(64, 320), spread(128, 256)


def down1_kernel(
    v_hbm, wd_hbm, b_hbm, t_hbm, out_ref, face_ref, tab_ref, tab2_ref, v_ref, w_ref, b_ref, t_ref, wd_ref, cells_ref, sems
):
    half = v_ref.shape[2]
    kz = C0 * half
    part = 16 * half
    lanes = Z1 // 2 * C1
    small = ((t_hbm, t_ref), (wd_hbm, w_ref), (b_hbm, b_ref))
    copies = [pltpu.make_async_copy(src, dst, sems.at[n]) for n, (src, dst) in enumerate(small)]
    for n in range(C0 // 16):
        cut = slice(n * 16, n * 16 + 16)
        copies.append(pltpu.make_async_copy(v_hbm.at[cut], v_ref.at[cut], sems.at[len(small) + n]))
    for copy in copies:
        copy.start()

    copies[0].wait()
    tab, tab2 = tissue_tables(t_ref)
    tab_ref[...] = tab
    tab2_ref[...] = tab2
    copies[1].wait()
    copies[2].wait()
    r = iota((kz, 2 * C0), 0)
    l = iota((kz, 2 * C0), 1)
    odd = l >= C0
    spread = one_hot(((r >> 3) == jnp.where(odd, l - C0, l)) & ((r & 1) == odd.astype(jnp.int32)))
    keep = (iota((kz, lanes), 0) & 7) >> 1 == iota((kz, lanes), 1) >> 6
    for ab in range(4):
        pair = w_ref[2 * ab : 2 * ab + 2].reshape(2 * C0, C1)
        wide = jnp.concatenate([pair] * (Z1 // 2), axis=1)
        block = jnp.where(keep, mm(spread, wide), 0.0).astype(BF)
        for n in range(C0 // 16):
            wd_ref[n, ab * part : ab * part + part, :] = block[n * part : n * part + part]

    r = iota((4 * CX, 128), 0)
    select = one_hot_rows(((r & 32) << 2) | (r & 64) | ((r & 31) << 1) | (r >> 7), 4 * CX)
    part = 16 * half
    acc = [0.0, 0.0]
    for n, copy in enumerate(copies[3:]):
        copy.wait()
        for m in range(v_ref.shape[3] // 256):
            v = [v_ref[n * 16 : n * 16 + 16, h, :, m * 256 : m * 256 + 256].reshape(part, 256) for h in range(2)]
            cells = mm(select, jnp.concatenate(v, axis=0), NT).astype(BF)
            for ab in range(4):
                for h in range(2):
                    piece = cells[64 * ab : 64 * ab + 64, h * part : h * part + part]
                    cells_ref[n, h, m * 64 : m * 64 + 64, ab * part : ab * part + part] = piece
        acc = [acc[h] + mm(cells_ref[n, h], wd_ref[n]) for h in range(2)]
    mask = mask_rows(tab[:, 128:256], 0, Y1, X1, lambda x: x, 4)
    bias = twice(b_ref)
    for h in range(2):
        for q in range(2):
            value = finish(acc[h][:, q * 128 : q * 128 + 128], bias, mask, Y1)
            chunk = 2 * h + q
            out_ref[:, :, chunk * 128 : chunk * 128 + 128] = value
            for side, start in enumerate((0, X1 - HALO_X)):
                for pair in range(HALO_X // 2):
                    lane = side * FACE + (chunk * (HALO_X // 2) + pair) * 128
                    face_ref[:, :, lane : lane + 128] = value[:, start + 2 * pair : start + 2 * pair + 2]


def twice(b_ref):
    return jnp.concatenate([b_ref[...]] * 2, axis=1)


def fill_banded(w_ref, t_ref, group, pad):
    chan = w_ref.shape[1]
    t_ref[...] = jnp.zeros_like(t_ref)
    for j in range(3):
        for i in range(3):
            for zo in range(group):
                for k in range(3):
                    lane = (3 * j + i) * (group + 2) * pad + (zo + k) * pad
                    t_ref[zo * pad : zo * pad + chan, lane : lane + chan] = w_ref[9 * i + 3 * j + k]


def banded_shape(group, pad):
    return shaped(group * pad, 9 * (group + 2) * pad)


def banded(weights, group, pad):
    def kernel(w_ref, t_ref):
        fill_banded(w_ref, t_ref, group, pad)

    return pl.pallas_call(
        kernel, out_shape=banded_shape(group, pad), compiler_params=params(), cost_estimate=cost(1e-6)
    )(weights)


def conv_group(taps, t_ref, rows, group_out, group_full):
    pitch = taps[0][0][0].shape[1]
    width = sum(piece[2] for piece in taps[0])
    parts = [ref[j : j + rows, :, lane : lane + n] for j in range(3) for tap in taps for ref, lane, n in tap]
    left = jnp.concatenate([p.reshape(rows * pitch, p.shape[2]) for p in parts], axis=1)
    if width == group_full:
        right = t_ref[0:group_out, :]
    else:
        right = jnp.concatenate([t_ref[0:group_out, n * group_full : n * group_full + width] for n in range(9)], axis=1)
    return mm(left, right, NT)


def finish(acc, bias, mask, rows):
    value = jnp.maximum(acc + bias, 0.0) * mask
    return value.astype(BF).reshape(rows, value.shape[0] // rows, value.shape[1])


def fill_sides(left, right, lane, inner):
    cut = slice(lane, lane + inner.shape[2])
    none = jnp.zeros_like(inner[:, :1])
    left[:, :, cut] = jnp.concatenate([none, inner[:, :-1]], axis=1)
    right[:, :, cut] = jnp.concatenate([inner[:, 1:], none], axis=1)


def middle_kernel(win_ref, t_ref, b_ref, tab_ref, w_ref, left_ref, right_ref, out_ref, next_ref):
    fill_banded(w_ref, next_ref, 4, C1)
    for q in range(4):
        fill_sides(left_ref, right_ref, q * 128, win_ref[:, :, q * 128 : q * 128 + 128])
    rows = Y1 + 2
    mask = mask_rows(tab_ref[:, 128:256], -1, rows, X1, lambda x: x, 4)
    acc = conv_group([[(ref, 128, 384)] for ref in (left_ref, win_ref, right_ref)], t_ref, rows, 256, 384)
    for q in range(2):
        cut = slice(q * 128, q * 128 + 128)
        out_ref[:, :, cut] = finish(acc[:, cut], twice(b_ref), mask, rows)


def outer_kernel(win_ref, left_ref, right_ref, zl_ref, zr_ref, t_ref, b_ref, tab_ref, low_ref, high_ref, ll, lr, hl, hr):
    fill_sides(ll, lr, 0, zl_ref[...])
    fill_sides(hl, hr, 0, zr_ref[...])
    own = (left_ref, win_ref, right_ref)
    rows = Y1 + 2
    mask = mask_rows(tab_ref[...], -1, rows, X1, lambda x: x, 4)
    taps = [[(z, 0, 128), (ref, 0, 256)] for z, ref in zip((ll, zl_ref, lr), own)]
    acc = conv_group(taps, t_ref, rows, 256, 384)
    for q in range(2):
        cut = slice(q * 128, q * 128 + 128)
        low_ref[:, :, cut] = finish(acc[:, cut], twice(b_ref), mask[:, cut], rows)
    taps = [[(ref, 384, 128), (z, 0, 128)] for z, ref in zip((hl, zr_ref, hr), own)]
    acc = conv_group(taps, t_ref, rows, 128, 384)
    high_ref[...] = finish(acc, twice(b_ref), mask[:, 256:384], rows)


def fill_edges(copies, pieces):
    line = jnp.concatenate(pieces, axis=1)
    copies[0][...] = line
    for i in (1, 2):
        copies[i][...] = jnp.concatenate([line[:, i:], jnp.zeros_like(line[:, :i])], axis=1)


def edge_masks(tab_ref):
    mask = mask_rows(tab_ref[...], -1, Y1 + 2, EDGE, lambda r: jnp.where(r < 8, r - 5, r + X1 - 9), 4)
    return [mask[:, q * 128 : q * 128 + 128] for q in range(3)]


def edge_group(taps, t_ref, b_ref, masks, inner_ref, moved):
    rows = Y1 + 2
    acc = conv_group(taps, t_ref, rows, 128 * len(masks), 384)
    i0, i1, i2 = moved
    for q, mask in enumerate(masks):
        cut = slice(q * 128, q * 128 + 128)
        edge = finish(acc[:, cut], twice(b_ref), mask, rows)
        inner = inner_ref[:, :, cut][:, 1:-1]
        i0[:, :X1, cut] = jnp.concatenate([edge[:, 4:6], inner], axis=1)
        i1[:, :X1, cut] = jnp.concatenate([edge[:, 5:6], inner, edge[:, 8:9]], axis=1)
        i2[:, :X1, cut] = jnp.concatenate([inner, edge[:, 8:10]], axis=1)
        i0[:, X1:, cut] = edge
        for i, copy in ((1, i1), (2, i2)):
            copy[:, X1:, cut] = jnp.concatenate([edge[:, i:], jnp.zeros((rows, i, 128), BF)], axis=1)


def column_pieces(ref, chunk):
    first = chunk * (HALO_X // 2) * 128
    return [ref[:, :, lane : lane + 128] for lane in range(first, first + HALO_X // 2 * 128, 128)]


def edge_middle_kernel(xl_ref, win_ref, xr_ref, g_ref, t_ref, b_ref, tab_ref, e0, e1, e2, m0, m1, m2):
    for lane in range(0, Z1 * C1, 128):
        cut = slice(lane, lane + 128)
        inner = win_ref[:, :, cut]
        left, right = (column_pieces(ref, lane // 128) for ref in (xl_ref, xr_ref))
        pieces = left + [inner[:, :2], inner[:, X1 - 2 :]] + right
        fill_edges([e.at[:, :, cut] for e in (e0, e1, e2)], pieces)
    here = edge_masks(tab_ref)[1]
    edge_group([[(e, 128, 384)] for e in (e0, e1, e2)], t_ref, b_ref, (here, here), g_ref, (m0, m1, m2))


def level_one_kernel(
    zl_ref, zr_ref, cl_ref, cr_ref, e0, e1, e2, m0, m1, m2, g1_ref, g3_ref, ta_ref, tb_ref, ba_ref, bb_ref, wd_ref, bd_ref, tab_ref,
    tab2_ref, feat_ref, down_ref, l0, l1, l2, h0, h1, h2, i0, i1, i2, j0, j1, j2, side_ref, d_ref,
):
    own, mid, low, high = (e0, e1, e2), (m0, m1, m2), (i0, i1, i2), (j0, j1, j2)
    for z_ref, c_ref, copies in ((zl_ref, cl_ref, (l0, l1, l2)), (zr_ref, cr_ref, (h0, h1, h2))):
        inner = z_ref[...]
        fill_edges(copies, column_pieces(c_ref, 0) + [inner[:, :2], inner[:, X1 - 2 :]] + column_pieces(c_ref, 1))
    below, here, above = edge_masks(tab_ref)
    taps = [[(z, 0, 128), (e, 0, 256)] for z, e in zip((l0, l1, l2), own)]
    edge_group(taps, ta_ref, ba_ref, (below, here), g1_ref, low)
    taps = [[(e, 384, 128), (z, 0, 128)] for z, e in zip((h0, h1, h2), own)]
    edge_group(taps, ta_ref, ba_ref, (above,), g3_ref, high)

    def cell_of(r):
        return jnp.where(r < X1, r, jnp.where(r < X1 + 8, r - X1 - 4, r - 8))

    mask = mask_rows(tab_ref[:, 128:256], 0, Y1, X1 + EDGE, cell_of, 4)
    first = [[(a, 0, 256), (b, 0, 128)] for a, b in zip(low, mid)]
    second = [[(a, 0, 256), (b, 0, 128)] for a, b in zip(mid, high)]
    for g, taps in enumerate((first, second)):
        acc = conv_group(taps, tb_ref, Y1, 256, 384)
        for q in range(2):
            value = finish(acc[:, q * 128 : q * 128 + 128], twice(bb_ref), mask, Y1)
            cut = slice((2 * g + q) * 128, (2 * g + q + 1) * 128)
            feat_ref[:, cut] = value[:, :X1].reshape(Y1 * X1, 128)
            side_ref[:, cut] = value[:, X1:].reshape(Y1 * EDGE, 128)

    size = 8 * X1
    quarter = size // 4
    r = iota((size, 128), 0)
    select = one_hot_rows(((r & 48) << 2) | ((r & 64) >> 1) | ((r & 15) << 1) | (r >> 7), size)
    for n in range(Y1 // 8):
        cells = mm(select, feat_ref[n * size : n * size + size, :]).astype(BF)
        for q in range(4):
            d_ref[q, n * quarter : n * quarter + quarter, :] = cells[q * quarter : (q + 1) * quarter]
    select = one_hot_rows(((r & 56) << 2) | ((r & 64) >> 2) | ((r & 7) << 1) | (r >> 7), size)
    cells = mm(select, side_ref[...]).astype(BF)
    for q in range(4):
        d_ref[q, Y2 * X2 :, :] = cells[q * quarter : (q + 1) * quarter]
    inner_mask = mask_rows(tab2_ref[:, 128:256], 0, Y2, X2, lambda x: x, 2)
    side_mask = mask_rows(tab2_ref[:, 128:256], 0, Y2, EDGE // 2, lambda r: jnp.where(r < 4, r - 2, r + X2 - 4), 2)
    for z in range(Z2):
        left = jnp.concatenate([d_ref[q, :, z * 128 : z * 128 + 128] for q in range(4)], axis=1)
        acc = mm(left, wd_ref[...])
        inner = finish(acc[: Y2 * X2], bd_ref[...], inner_mask, Y2)
        side = finish(acc[Y2 * X2 :], bd_ref[...], side_mask, Y2)
        down_ref[:, :, z * CP : z * CP + CP] = jnp.concatenate([side[:, 0:2], inner, side[:, 4:6]], axis=1)


def one_kernel(feat_ref, out_ref):
    lanes = feat_ref.shape[1]
    r = iota((lanes, 128), 0)
    order = one_hot_rows(((r & 7) << 6) | (r >> 3), lanes)
    out_ref[...] = mm(order, feat_ref[...], NT).astype(BF)


def fill_pitch(copies, wide):
    pitch = copies[0].shape[1]
    for lane in range(0, wide.shape[2], 128):
        line = wide[:, :, lane : lane + 128]
        for i, copy in enumerate(copies):
            spare = jnp.zeros((line.shape[0], pitch - line.shape[1] + i, 128), BF)
            copy[:, :, lane : lane + 128] = jnp.concatenate([line[:, i:], spare], axis=1)


def level_two_group(taps, t_ref, b_ref, masks, moved):
    rows = Y2 + 2
    acc = conv_group(taps, t_ref, rows, 256, 512)
    for q in range(2):
        cut = slice(q * 128, q * 128 + 128)
        value = finish(acc[:, cut], b_ref[...], masks[q], rows)
        for i, ref in enumerate(moved):
            ref[:, :, cut] = value[:, i : i + X2]


def level_two_masks(tab_ref):
    mask = mask_rows(tab_ref[...], -1, Y2 + 2, PITCH2, lambda x: x - 1, 2)
    return [mask[:, q * 128 : q * 128 + 128] for q in range(3)]


def level_two_middle_kernel(wide_ref, t_ref, b_ref, tab_ref, a0, a1, a2, m0, m1, m2):
    fill_pitch((a0, a1, a2), wide_ref[...])
    here = level_two_masks(tab_ref)[1]
    level_two_group([[(a, 0, 512)] for a in (a0, a1, a2)], t_ref, b_ref, (here, here), (m0, m1, m2))


def level_two_kernel(
    a0, a1, a2, m0, m1, m2, zl_ref, zr_ref, ta_ref, tb_ref, ba_ref, bb_ref, tab_ref, out_ref,
    l0, l1, l2, h0, h1, h2, i0, i1, i2, j0, j1, j2,
):
    fill_pitch((l0, l1, l2), zl_ref[...])
    fill_pitch((h0, h1, h2), zr_ref[...])
    below, here, above = level_two_masks(tab_ref)
    own, mid, low, high = (a0, a1, a2), (m0, m1, m2), (i0, i1, i2), (j0, j1, j2)
    taps = [[(z, 0, 256), (a, 0, 256)] for z, a in zip((l0, l1, l2), own)]
    level_two_group(taps, ta_ref, ba_ref, (below, here), low)
    taps = [[(a, 256, 256), (z, 0, 256)] for z, a in zip((h0, h1, h2), own)]
    level_two_group(taps, ta_ref, ba_ref, (here, above), high)
    mask = mask_rows(tab_ref[:, 128:256], 0, Y2, X2, lambda x: x, 2)
    feat = []
    for pair in ((low, mid), (mid, high)):
        acc = conv_group([[(a, 0, 256), (b, 0, 256)] for a, b in zip(*pair)], tb_ref, Y2, 256, 512)
        for q in range(2):
            feat.append((jnp.maximum(acc[:, q * 128 : q * 128 + 128] + bb_ref[...], 0.0) * mask).astype(BF))
    r = iota((C2 * Z2, 128), 0)
    order = one_hot_rows(((r & 3) << 7) | (r >> 2), Z2 * CP)
    out_ref[...] = mm(order, jnp.concatenate(feat, axis=1), NT).astype(BF)


def partner(index, second, count):
    other = index + 1 if index % 2 == second else index - 1
    return other if 0 <= other < count else None


def swap(value, moves):
    axes = ("gx", "gy", "gz")
    sizes = [lax.axis_size(axis) for axis in axes]
    pairs = []
    for source in itertools.product(*(range(size) for size in sizes)):
        target = [partner(i, moves[axis], size) if axis in moves else i for i, axis, size in zip(source, axes, sizes)]
        if None in target:
            other = sizes[1] - 1 - source[1] if "gy" in moves else source[1] ^ 1
            target = [source[0], other, source[2]]
        pairs.append(tuple((x * sizes[1] + y) * sizes[2] + z for x, y, z in (source, target)))
    return lax.ppermute(value, axes, pairs)


def positions():
    found = {}
    for axis in ("gx", "gy", "gz"):
        index = lax.axis_index(axis)
        found[axis] = ((index & 1) == 0, index > 0, index < lax.axis_size(axis) - 1)
    return found


def sides(first, second, position):
    even, has_below, has_above = position
    below = jnp.where(has_below, jnp.where(even, second, first), jnp.zeros_like(first))
    above = jnp.where(has_above, jnp.where(even, first, second), jnp.zeros_like(first))
    return below, above


def swaps(low_edge, high_edge, axis, position):
    even = position[0]
    first = swap(jnp.where(even, high_edge, low_edge), {axis: 0})
    second = swap(jnp.where(even, low_edge, high_edge), {axis: 1}) if lax.axis_size(axis) > 2 else first
    return first, second


def shift_along(low_edge, high_edge, axis, position):
    return sides(*swaps(low_edge, high_edge, axis, position), position)


def params():
    return pltpu.CompilerParams(vmem_limit_bytes=VMEM_BYTES)


def cost(seconds):
    return pl.CostEstimate(flops=int(1e15 * seconds), bytes_accessed=0, transcendentals=0)


def shaped(*shape):
    return jax.ShapeDtypeStruct(shape, BF)


def pad_lanes(value):
    return jnp.pad(value, [(0, 0)] * (value.ndim - 1) + [(0, CP - value.shape[-1])])


def local(
    volume, tissue, w_down1, b_down1, w_conv1a, b_conv1a, w_conv1b, b_conv1b,
    w_down2, b_down2, w_conv2a, b_conv2a, w_conv2b, b_conv2b,
):
    depth = volume.shape[1]
    lanes1 = Z1 * C1
    half = depth // 2
    operands = [volume.reshape(C0, 2, half, -1), jnp.swapaxes(w_down1, 1, 2), b_down1[None], tissue.transpose(1, 2, 0)]
    at, operands = lax.optimization_barrier((positions(), operands))
    operands = [pltpu.with_memory_space_constraint(x, pltpu.HBM) for x in operands]
    own, faces, tab1, tab2 = pl.pallas_call(
        down1_kernel,
        in_specs=[pl.BlockSpec(memory_space=pltpu.HBM)] * 4,
        out_shape=[shaped(Y1, X1, lanes1), shaped(Y1, 2, 2 * FACE), shaped(128, 384), shaped(128, 384)],
        scratch_shapes=[pltpu.VMEM(x.shape, x.dtype) for x in operands]
        + [
            pltpu.VMEM((C0 // 16, 64 * half, lanes1 // 2), BF),
            pltpu.VMEM((C0 // 16, 2, Y1 * X1, 64 * half), BF),
            pltpu.SemaphoreType.DMA((3 + C0 // 16,)),
        ],
        compiler_params=params(),
        cost_estimate=cost(4e-6),
    )(*operands)

    t1a = banded(w_conv1a, 4, C1)
    bias1a = b_conv1a[None]

    def with_halo(field):
        below, above = shift_along(field[:HALO], field[field.shape[0] - HALO :], "gy", at["gy"])
        return jnp.concatenate([below, field, above], axis=0)

    faces = with_halo(faces)
    win = with_halo(own)
    z_below, z_above = shift_along(win[:, :, :128], win[:, :, lanes1 - 128 :], "gz", at["gz"])
    x_got = lax.optimization_barrier(swaps(faces[:, :, :FACE], faces[:, :, FACE:], "gx", at["gx"]))
    rows = Y1 + 2
    left, right, g2, t1b = pl.pallas_call(
        middle_kernel,
        out_shape=[shaped(ROWS1, X1, lanes1), shaped(ROWS1, X1, lanes1), shaped(rows, X1, 256), banded_shape(4, C1)],
        compiler_params=params(),
        cost_estimate=cost(1e-7),
    )(win, t1a, bias1a, tab1, w_conv1b)

    corner = HALO_X // 2 * 2 * C1
    low, high = (
        jnp.concatenate(sides(*(got[:, :, cut] for got in x_got), at["gx"]), axis=2) for cut in (slice(corner), slice(FACE - corner, FACE))
    )
    low, high, g2, *x_got = lax.optimization_barrier((low, high, g2, *x_got))
    x_below, x_above = sides(*x_got, at["gx"])
    corner_got = swaps(low, high, "gz", at["gz"])
    g1, g3 = pl.pallas_call(
        outer_kernel,
        out_shape=[shaped(rows, X1, 256), shaped(rows, X1, 128)],
        scratch_shapes=[pltpu.VMEM((ROWS1, X1, 128), BF)] * 4,
        compiler_params=params(),
        cost_estimate=cost(4e-6),
    )(win, left, right, z_below, z_above, t1a, bias1a, tab1)

    *corner_got, g1, g3 = lax.optimization_barrier((*corner_got, g1, g3))
    corner_below, corner_above = sides(*corner_got, at["gz"])
    wide_x = X1 + EDGE
    edges = pl.pallas_call(
        edge_middle_kernel,
        out_shape=[shaped(ROWS1, EDGE, lanes1)] * 3 + [shaped(rows, wide_x, 256)] * 3,
        compiler_params=params(),
        cost_estimate=cost(3e-6),
    )(x_below, win, x_above, g2, t1a, bias1a, tab1)
    feat, down = pl.pallas_call(
        level_one_kernel,
        out_shape=[shaped(Y1 * X1, lanes1), shaped(Y2, X2 + 2 * HALO_X2, Z2 * CP)],
        scratch_shapes=[pltpu.VMEM((ROWS1, EDGE, 128), BF)] * 6
        + [pltpu.VMEM((rows, wide_x, 256), BF)] * 3
        + [pltpu.VMEM((rows, wide_x, 128), BF)] * 3
        + [pltpu.VMEM((Y1 * EDGE, lanes1), BF), pltpu.VMEM((4, Y2 * (X2 + EDGE // 2), lanes1), BF)],
        compiler_params=params(),
        cost_estimate=cost(6e-6),
    )(
        z_below, z_above, corner_below, corner_above, *edges, g1, g3, t1a, t1b, bias1a, b_conv1b[None],
        pad_lanes(jnp.swapaxes(w_down2, 1, 2).reshape(8 * C1, C2)), pad_lanes(b_down2[None]), tab1, tab2,
    )

    down, w_conv2a = lax.optimization_barrier((down, w_conv2a))
    t2a = banded(w_conv2a, 2, CP)
    wide = with_halo(down)
    feat, wide, w_conv2b = lax.optimization_barrier((feat, wide, w_conv2b))
    t2b = banded(w_conv2b, 2, CP)
    one = pl.pallas_call(
        one_kernel, out_shape=shaped(lanes1, Y1 * X1), compiler_params=params(), cost_estimate=cost(2e-6)
    )(feat)
    z_below, z_above = shift_along(wide[:, :, : 2 * CP], wide[:, :, 2 * CP :], "gz", at["gz"])
    bias2a = pad_lanes(b_conv2a[None])
    moved = [shaped(Y2 + 2, X2, 2 * CP)] * 3
    middle = pl.pallas_call(
        level_two_middle_kernel,
        out_shape=[shaped(ROWS2, PITCH2, Z2 * CP)] * 3 + moved,
        compiler_params=params(),
        cost_estimate=cost(3e-6),
    )(wide, t2a, bias2a, tab2)
    two = pl.pallas_call(
        level_two_kernel,
        out_shape=shaped(C2 * Z2, Y2 * X2),
        scratch_shapes=[pltpu.VMEM((ROWS2, PITCH2, 2 * CP), BF)] * 6 + [pltpu.VMEM((Y2 + 2, X2, 2 * CP), BF)] * 6,
        compiler_params=params(),
        cost_estimate=cost(5e-6),
    )(*middle, z_below, z_above, t2a, t2b, bias2a, pad_lanes(b_conv2b[None]), tab2)
    return one.reshape(C1, Z1, Y1 * X1), two.reshape(C2, Z2, Y2 * X2)


def solution(mesh):
    block = P(None, "gz", ("gx", "gy"))
    return jax.shard_map(
        local,
        mesh=mesh,
        in_specs=(block,) + (P(),) * 13,
        out_specs=(block, block),
        check_vma=False,
    )
```

```python
import itertools

import jax
import jax.numpy as jnp
from jax import lax
from jax.experimental import pallas as pl
from jax.experimental.pallas import tpu as pltpu
from jax.sharding import PartitionSpec as P

CX = 64
CY = 32
X1 = CX // 2
Y1 = CY // 2
X2 = X1 // 2
Y2 = Y1 // 2
Z1 = 8
Z2 = 4
C0 = 48
C1 = 64
C2 = 96
CP = 128
HALO = 2
HALO_X = 6
HALO_X2 = 2
XB = 12
XB_BELOW = 2
XB_PITCH = 16
YB = 6
ROWS1 = Y1 + 2 * HALO
ROWS2 = Y2 + 2 * HALO
EDGE = 16
PITCH2 = 32
BF = jnp.bfloat16
F32 = jnp.float32
NN = (((1,), (0,)), ((), ()))
NT = (((1,), (1,)), ((), ()))
VMEM_BYTES = 20 * 1024 * 1024


def mm(a, b, dims=NN):
    return lax.dot_general(a, b, dims, preferred_element_type=F32)


def iota(shape, dim):
    return lax.broadcasted_iota(jnp.int32, shape, dim)


def one_hot(flag):
    return jnp.where(flag, 1.0, 0.0).astype(BF)


def one_hot_rows(key, lanes):
    lane = iota(key.shape, 1)
    return jnp.concatenate([one_hot(key == lane + q) for q in range(0, lanes, 128)], axis=1)


def mask_rows(tab, y_start, rows, pitch, x_of, cell):
    bits = cell.bit_length() - 1
    shape = (rows, pitch, 128)
    y_block = (iota(shape, 0) + (y_start + cell)) >> bits
    x_block = jnp.minimum((x_of(iota(shape, 1)) + XB_BELOW * cell) >> bits, XB - 1)
    hit = one_hot(y_block * XB_PITCH + x_block == iota(shape, 2)).reshape(rows * pitch, 128)
    return mm(hit, tab)


def tissue_tables(t_ref):
    n_y, n_z, n_x = t_ref.shape
    here = lax.axis_index("gz")
    layers = []
    for k in (-1, 0, 1):
        z = here + k
        inside = jnp.where((z >= 0) & (z < n_z), 1.0, 0.0)
        layers.append(t_ref[:, jnp.clip(z, 0, n_z - 1), :].astype(F32) * inside)
    block = iota((128, n_y), 0)
    bits = XB_PITCH.bit_length() - 1
    hot_y = one_hot(lax.axis_index("gy") * 4 - 1 + (block >> bits) == iota((128, n_y), 1))
    block = iota((128, 3 * n_x), 0)
    layer = sum((iota((128, 3 * n_x), 1) >= k * n_x).astype(jnp.int32) for k in (1, 2))
    hot_x = lax.axis_index("gx") * 8 - XB_BELOW + (block & (XB_PITCH - 1)) == iota((128, 3 * n_x), 1) - layer * n_x
    rows = jnp.where(hot_x, mm(hot_y, jnp.concatenate(layers, axis=1).astype(BF)), 0.0).astype(BF)
    shape = (3 * n_x, 384)
    layer = sum((iota(shape, 0) >= k * n_x).astype(jnp.int32) for k in (1, 2))
    lane = iota(shape, 1)

    def spread(first, last):
        place = jnp.where(lane < first, 0, jnp.where(lane < last, 1, 2))
        return mm(rows, one_hot(layer == place)).astype(BF)

    return spread(64, 320), spread(128, 256)


def down1_kernel(
    v_hbm, wd_hbm, b_hbm, t_hbm, out_ref, tab_ref, tab2_ref, v_ref, w_ref, b_ref, t_ref, wd_ref, cells_ref, sems
):
    half = v_ref.shape[2]
    kz = C0 * half
    part = 16 * half
    lanes = Z1 // 2 * C1
    small = ((t_hbm, t_ref), (wd_hbm, w_ref), (b_hbm, b_ref))
    copies = [pltpu.make_async_copy(src, dst, sems.at[n]) for n, (src, dst) in enumerate(small)]
    for n in range(C0 // 16):
        cut = slice(n * 16, n * 16 + 16)
        copies.append(pltpu.make_async_copy(v_hbm.at[cut], v_ref.at[cut], sems.at[len(small) + n]))
    for copy in copies:
        copy.start()

    copies[0].wait()
    tab, tab2 = tissue_tables(t_ref)
    tab_ref[...] = tab
    tab2_ref[...] = tab2
    copies[1].wait()
    copies[2].wait()
    r = iota((kz, 2 * C0), 0)
    l = iota((kz, 2 * C0), 1)
    odd = l >= C0
    spread = one_hot(((r >> 3) == jnp.where(odd, l - C0, l)) & ((r & 1) == odd.astype(jnp.int32)))
    keep = (iota((kz, lanes), 0) & 7) >> 1 == iota((kz, lanes), 1) >> 6
    for ab in range(4):
        pair = w_ref[2 * ab : 2 * ab + 2].reshape(2 * C0, C1)
        wide = jnp.concatenate([pair] * (Z1 // 2), axis=1)
        block = jnp.where(keep, mm(spread, wide), 0.0).astype(BF)
        for n in range(C0 // 16):
            wd_ref[n, ab * part : ab * part + part, :] = block[n * part : n * part + part]

    r = iota((4 * CX, 128), 0)
    select = one_hot_rows(((r & 32) << 2) | (r & 64) | ((r & 31) << 1) | (r >> 7), 4 * CX)
    part = 16 * half
    acc = [0.0, 0.0]
    for n, copy in enumerate(copies[3:]):
        copy.wait()
        for m in range(v_ref.shape[3] // 256):
            v = [v_ref[n * 16 : n * 16 + 16, h, :, m * 256 : m * 256 + 256].reshape(part, 256) for h in range(2)]
            cells = mm(select, jnp.concatenate(v, axis=0), NT).astype(BF)
            for ab in range(4):
                for h in range(2):
                    piece = cells[64 * ab : 64 * ab + 64, h * part : h * part + part]
                    cells_ref[n, h, m * 64 : m * 64 + 64, ab * part : ab * part + part] = piece
        acc = [acc[h] + mm(cells_ref[n, h], wd_ref[n]) for h in range(2)]
    mask = mask_rows(tab[:, 128:256], 0, Y1, X1, lambda x: x, 4)
    bias = twice(b_ref)
    for h in range(2):
        for q in range(2):
            value = finish(acc[h][:, q * 128 : q * 128 + 128], bias, mask, Y1)
            out_ref[:, :, (2 * h + q) * 128 : (2 * h + q + 1) * 128] = value


def twice(b_ref):
    return jnp.concatenate([b_ref[...]] * 2, axis=1)


def fill_banded(w_ref, t_ref, group, pad):
    chan = w_ref.shape[1]
    t_ref[...] = jnp.zeros_like(t_ref)
    for j in range(3):
        for i in range(3):
            for zo in range(group):
                for k in range(3):
                    lane = (3 * j + i) * (group + 2) * pad + (zo + k) * pad
                    cut, lane = divmod(lane, t_ref.shape[2])
                    t_ref[cut, zo * pad : zo * pad + chan, lane : lane + chan] = w_ref[9 * i + 3 * j + k]


def banded_shape(group, pad, cuts):
    return shaped(cuts, group * pad, 9 * (group + 2) * pad // cuts)


def banded(weights, group, pad, cuts):
    def kernel(w_ref, t_ref):
        fill_banded(w_ref, t_ref, group, pad)

    return pl.pallas_call(
        kernel, out_shape=banded_shape(group, pad, cuts), compiler_params=params(), cost_estimate=cost(1e-6)
    )(weights)


def conv_group(taps, t_ref, rows, group_out, group_full):
    pitch = taps[0][0][0].shape[1]
    width = sum(piece[2] for piece in taps[0])
    cuts = t_ref.shape[0]
    total = None
    for cut in range(cuts):
        js = range(3 * cut // cuts, 3 * (cut + 1) // cuts)
        parts = [ref[j : j + rows, :, lane : lane + n] for j in js for tap in taps for ref, lane, n in tap]
        left = jnp.concatenate([p.reshape(rows * pitch, p.shape[2]) for p in parts], axis=1)
        if width == group_full:
            right = t_ref[cut, 0:group_out, :]
        else:
            starts = range(0, t_ref.shape[2], group_full)
            right = jnp.concatenate([t_ref[cut, 0:group_out, lane : lane + width] for lane in starts], axis=1)
        term = mm(left, right, NT)
        total = term if total is None else total + term
    return total


def finish(acc, bias, mask, rows):
    value = jnp.maximum(acc + bias, 0.0) * mask
    return value.astype(BF).reshape(rows, value.shape[0] // rows, value.shape[1])


def fill_sides(left, right, lane, inner):
    cut = slice(lane, lane + inner.shape[2])
    none = jnp.zeros_like(inner[:, :1])
    left[:, :, cut] = jnp.concatenate([none, inner[:, :-1]], axis=1)
    right[:, :, cut] = jnp.concatenate([inner[:, 1:], none], axis=1)


def middle_kernel(win_ref, t_ref, b_ref, tab_ref, w_ref, left_ref, right_ref, out_ref, next_ref):
    fill_banded(w_ref, next_ref, 4, C1)
    for q in range(4):
        fill_sides(left_ref, right_ref, q * 128, win_ref[:, :, q * 128 : q * 128 + 128])
    rows = Y1 + 2
    mask = mask_rows(tab_ref[:, 128:256], -1, rows, X1, lambda x: x, 4)
    acc = conv_group([[(ref, 128, 384)] for ref in (left_ref, win_ref, right_ref)], t_ref, rows, 256, 384)
    for q in range(2):
        cut = slice(q * 128, q * 128 + 128)
        out_ref[:, :, cut] = finish(acc[:, cut], twice(b_ref), mask, rows)


def outer_kernel(win_ref, left_ref, right_ref, zl_ref, zr_ref, t_ref, b_ref, tab_ref, low_ref, high_ref, ll, lr, hl, hr):
    fill_sides(ll, lr, 0, zl_ref[...])
    fill_sides(hl, hr, 0, zr_ref[...])
    own = (left_ref, win_ref, right_ref)
    rows = Y1 + 2
    mask = mask_rows(tab_ref[...], -1, rows, X1, lambda x: x, 4)
    taps = [[(z, 0, 128), (ref, 0, 256)] for z, ref in zip((ll, zl_ref, lr), own)]
    acc = conv_group(taps, t_ref, rows, 256, 384)
    for q in range(2):
        cut = slice(q * 128, q * 128 + 128)
        low_ref[:, :, cut] = finish(acc[:, cut], twice(b_ref), mask[:, cut], rows)
    taps = [[(ref, 384, 128), (z, 0, 128)] for z, ref in zip((hl, zr_ref, hr), own)]
    acc = conv_group(taps, t_ref, rows, 128, 384)
    high_ref[...] = finish(acc, twice(b_ref), mask[:, 256:384], rows)


def fill_edges(copies, pieces):
    line = jnp.concatenate(pieces, axis=1)
    copies[0][...] = line
    for i in (1, 2):
        copies[i][...] = jnp.concatenate([line[:, i:], jnp.zeros_like(line[:, :i])], axis=1)


def edge_masks(tab_ref):
    mask = mask_rows(tab_ref[...], -1, Y1 + 2, EDGE, lambda r: jnp.where(r < 8, r - 5, r + X1 - 9), 4)
    return [mask[:, q * 128 : q * 128 + 128] for q in range(3)]


def edge_group(taps, t_ref, b_ref, masks, inner_ref, moved):
    rows = Y1 + 2
    acc = conv_group(taps, t_ref, rows, 128 * len(masks), 384)
    i0, i1, i2 = moved
    for q, mask in enumerate(masks):
        cut = slice(q * 128, q * 128 + 128)
        edge = finish(acc[:, cut], twice(b_ref), mask, rows)
        inner = inner_ref[:, :, cut][:, 1:-1]
        i0[:, :X1, cut] = jnp.concatenate([edge[:, 4:6], inner], axis=1)
        i1[:, :X1, cut] = jnp.concatenate([edge[:, 5:6], inner, edge[:, 8:9]], axis=1)
        i2[:, :X1, cut] = jnp.concatenate([inner, edge[:, 8:10]], axis=1)
        i0[:, X1:, cut] = edge
        for i, copy in ((1, i1), (2, i2)):
            copy[:, X1:, cut] = jnp.concatenate([edge[:, i:], jnp.zeros((rows, i, 128), BF)], axis=1)


def column_lanes(field, lane, stride=Z1 * C1):
    return [field[:, :, first : first + 128] for first in range(lane, field.shape[2], stride)]


def edge_middle_kernel(xl_ref, win_ref, xr_ref, g_ref, t_ref, b_ref, tab_ref, e0, e1, e2, m0, m1, m2):
    for lane in range(0, Z1 * C1, 128):
        cut = slice(lane, lane + 128)
        inner = win_ref[:, :, cut]
        left, right = (column_lanes(ref, lane) for ref in (xl_ref, xr_ref))
        pieces = left + [inner[:, :2], inner[:, X1 - 2 :]] + right
        fill_edges([e.at[:, :, cut] for e in (e0, e1, e2)], pieces)
    here = edge_masks(tab_ref)[1]
    edge_group([[(e, 128, 384)] for e in (e0, e1, e2)], t_ref, b_ref, (here, here), g_ref, (m0, m1, m2))


def level_one_kernel(
    zl_ref, zr_ref, cl_ref, cr_ref, e0, e1, e2, m0, m1, m2, g1_ref, g3_ref, ta_ref, tb_ref, ba_ref, bb_ref, wd_ref, bd_ref, tab_ref,
    tab2_ref, feat_ref, down_ref, l0, l1, l2, h0, h1, h2, i0, i1, i2, j0, j1, j2, side_ref, d_ref,
):
    own, mid, low, high = (e0, e1, e2), (m0, m1, m2), (i0, i1, i2), (j0, j1, j2)
    for z_ref, c_ref, copies in ((zl_ref, cl_ref, (l0, l1, l2)), (zr_ref, cr_ref, (h0, h1, h2))):
        inner = z_ref[...]
        corner = column_lanes(c_ref, 0, 128)
        fill_edges(copies, corner[:3] + [inner[:, :2], inner[:, X1 - 2 :]] + corner[3:])
    below, here, above = edge_masks(tab_ref)
    taps = [[(z, 0, 128), (e, 0, 256)] for z, e in zip((l0, l1, l2), own)]
    edge_group(taps, ta_ref, ba_ref, (below, here), g1_ref, low)
    taps = [[(e, 384, 128), (z, 0, 128)] for z, e in zip((h0, h1, h2), own)]
    edge_group(taps, ta_ref, ba_ref, (above,), g3_ref, high)

    def cell_of(r):
        return jnp.where(r < X1, r, jnp.where(r < X1 + 8, r - X1 - 4, r - 8))

    mask = mask_rows(tab_ref[:, 128:256], 0, Y1, X1 + EDGE, cell_of, 4)
    first = [[(a, 0, 256), (b, 0, 128)] for a, b in zip(low, mid)]
    second = [[(a, 0, 256), (b, 0, 128)] for a, b in zip(mid, high)]
    for g, taps in enumerate((first, second)):
        acc = conv_group(taps, tb_ref, Y1, 256, 384)
        for q in range(2):
            value = finish(acc[:, q * 128 : q * 128 + 128], twice(bb_ref), mask, Y1)
            cut = slice((2 * g + q) * 128, (2 * g + q + 1) * 128)
            feat_ref[:, cut] = value[:, :X1].reshape(Y1 * X1, 128)
            side_ref[:, cut] = value[:, X1:].reshape(Y1 * EDGE, 128)

    size = 8 * X1
    quarter = size // 4
    r = iota((size, 128), 0)
    select = one_hot_rows(((r & 48) << 2) | ((r & 64) >> 1) | ((r & 15) << 1) | (r >> 7), size)
    for n in range(Y1 // 8):
        cells = mm(select, feat_ref[n * size : n * size + size, :]).astype(BF)
        for q in range(4):
            d_ref[q, n * quarter : n * quarter + quarter, :] = cells[q * quarter : (q + 1) * quarter]
    select = one_hot_rows(((r & 56) << 2) | ((r & 64) >> 2) | ((r & 7) << 1) | (r >> 7), size)
    cells = mm(select, side_ref[...]).astype(BF)
    for q in range(4):
        d_ref[q, Y2 * X2 :, :] = cells[q * quarter : (q + 1) * quarter]
    inner_mask = mask_rows(tab2_ref[:, 128:256], 0, Y2, X2, lambda x: x, 2)
    side_mask = mask_rows(tab2_ref[:, 128:256], 0, Y2, EDGE // 2, lambda r: jnp.where(r < 4, r - 2, r + X2 - 4), 2)
    for z in range(Z2):
        left = jnp.concatenate([d_ref[q, :, z * 128 : z * 128 + 128] for q in range(4)], axis=1)
        acc = mm(left, wd_ref[...])
        inner = finish(acc[: Y2 * X2], bd_ref[...], inner_mask, Y2)
        side = finish(acc[Y2 * X2 :], bd_ref[...], side_mask, Y2)
        down_ref[:, :, z * CP : z * CP + CP] = jnp.concatenate([side[:, 0:2], inner, side[:, 4:6]], axis=1)


def one_kernel(feat_ref, out_ref):
    lanes = feat_ref.shape[1]
    r = iota((lanes, 128), 0)
    order = one_hot_rows(((r & 7) << 6) | (r >> 3), lanes)
    out_ref[...] = mm(order, feat_ref[...], NT).astype(BF)


def fill_pitch(copies, wide):
    pitch = copies[0].shape[1]
    for lane in range(0, wide.shape[2], 128):
        line = wide[:, :, lane : lane + 128]
        for i, copy in enumerate(copies):
            spare = jnp.zeros((line.shape[0], pitch - line.shape[1] + i, 128), BF)
            copy[:, :, lane : lane + 128] = jnp.concatenate([line[:, i:], spare], axis=1)


def level_two_group(taps, t_ref, b_ref, masks, moved):
    rows = Y2 + 2
    acc = conv_group(taps, t_ref, rows, 256, 512)
    for q in range(2):
        cut = slice(q * 128, q * 128 + 128)
        value = finish(acc[:, cut], b_ref[...], masks[q], rows)
        for i, ref in enumerate(moved):
            ref[:, :, cut] = value[:, i : i + X2]


def level_two_masks(tab_ref):
    mask = mask_rows(tab_ref[...], -1, Y2 + 2, PITCH2, lambda x: x - 1, 2)
    return [mask[:, q * 128 : q * 128 + 128] for q in range(3)]


def level_two_middle_kernel(wide_ref, t_ref, b_ref, tab_ref, a0, a1, a2, m0, m1, m2):
    fill_pitch((a0, a1, a2), wide_ref[...])
    here = level_two_masks(tab_ref)[1]
    level_two_group([[(a, 0, 512)] for a in (a0, a1, a2)], t_ref, b_ref, (here, here), (m0, m1, m2))


def level_two_kernel(
    a0, a1, a2, m0, m1, m2, zl_ref, zr_ref, ta_ref, tb_ref, ba_ref, bb_ref, tab_ref, out_ref,
    l0, l1, l2, h0, h1, h2, i0, i1, i2, j0, j1, j2,
):
    fill_pitch((l0, l1, l2), zl_ref[...])
    fill_pitch((h0, h1, h2), zr_ref[...])
    below, here, above = level_two_masks(tab_ref)
    own, mid, low, high = (a0, a1, a2), (m0, m1, m2), (i0, i1, i2), (j0, j1, j2)
    taps = [[(z, 0, 256), (a, 0, 256)] for z, a in zip((l0, l1, l2), own)]
    level_two_group(taps, ta_ref, ba_ref, (below, here), low)
    taps = [[(a, 256, 256), (z, 0, 256)] for z, a in zip((h0, h1, h2), own)]
    level_two_group(taps, ta_ref, ba_ref, (here, above), high)
    mask = mask_rows(tab_ref[:, 128:256], 0, Y2, X2, lambda x: x, 2)
    feat = []
    for pair in ((low, mid), (mid, high)):
        acc = conv_group([[(a, 0, 256), (b, 0, 256)] for a, b in zip(*pair)], tb_ref, Y2, 256, 512)
        for q in range(2):
            feat.append((jnp.maximum(acc[:, q * 128 : q * 128 + 128] + bb_ref[...], 0.0) * mask).astype(BF))
    r = iota((C2 * Z2, 128), 0)
    order = one_hot_rows(((r & 3) << 7) | (r >> 2), Z2 * CP)
    out_ref[...] = mm(order, jnp.concatenate(feat, axis=1), NT).astype(BF)


def partner(index, second, count):
    other = index + 1 if index % 2 == second else index - 1
    return other if 0 <= other < count else None


def swap(value, moves):
    axes = ("gx", "gy", "gz")
    sizes = [lax.axis_size(axis) for axis in axes]
    pairs = []
    for source in itertools.product(*(range(size) for size in sizes)):
        target = [partner(i, moves[axis], size) if axis in moves else i for i, axis, size in zip(source, axes, sizes)]
        if None in target:
            other = sizes[1] - 1 - source[1] if "gy" in moves else source[1] ^ 1
            target = [source[0], other, source[2]]
        pairs.append(tuple((x * sizes[1] + y) * sizes[2] + z for x, y, z in (source, target)))
    return lax.ppermute(value, axes, pairs)


def parity(axis):
    return lax.axis_index(axis) % 2 == 0


def sides(first, second, axis):
    index = lax.axis_index(axis)
    even = parity(axis)
    below = jnp.where(index > 0, jnp.where(even, second, first), jnp.zeros_like(first))
    above = jnp.where(index < lax.axis_size(axis) - 1, jnp.where(even, first, second), jnp.zeros_like(first))
    return below, above


def swaps(low_edge, high_edge, axis):
    even = parity(axis)
    first = swap(jnp.where(even, high_edge, low_edge), {axis: 0})
    second = swap(jnp.where(even, low_edge, high_edge), {axis: 1}) if lax.axis_size(axis) > 2 else first
    return first, second


def shift_along(low_edge, high_edge, axis):
    return sides(*swaps(low_edge, high_edge, axis), axis)


def column_pairs(field):
    return jnp.concatenate([field[:, i : i + 2] for i in range(0, field.shape[1], 2)], axis=2)


def params():
    return pltpu.CompilerParams(vmem_limit_bytes=VMEM_BYTES)


def cost(seconds):
    return pl.CostEstimate(flops=int(1e15 * seconds), bytes_accessed=0, transcendentals=0)


def shaped(*shape):
    return jax.ShapeDtypeStruct(shape, BF)


def pad_lanes(value):
    return jnp.pad(value, [(0, 0)] * (value.ndim - 1) + [(0, CP - value.shape[-1])])


def local(
    volume, tissue, w_down1, b_down1, w_conv1a, b_conv1a, w_conv1b, b_conv1b,
    w_down2, b_down2, w_conv2a, b_conv2a, w_conv2b, b_conv2b,
):
    depth = volume.shape[1]
    lanes1 = Z1 * C1
    half = depth // 2
    operands = [volume.reshape(C0, 2, half, -1), jnp.swapaxes(w_down1, 1, 2), b_down1[None], tissue.transpose(1, 2, 0)]
    operands = [pltpu.with_memory_space_constraint(x, pltpu.HBM) for x in operands]
    own, tab1, tab2 = pl.pallas_call(
        down1_kernel,
        in_specs=[pl.BlockSpec(memory_space=pltpu.HBM)] * 4,
        out_shape=[shaped(Y1, X1, lanes1), shaped(128, 384), shaped(128, 384)],
        scratch_shapes=[pltpu.VMEM(x.shape, x.dtype) for x in operands]
        + [
            pltpu.VMEM((C0 // 16, 64 * half, lanes1 // 2), BF),
            pltpu.VMEM((C0 // 16, 2, Y1 * X1, 64 * half), BF),
            pltpu.SemaphoreType.DMA((3 + C0 // 16,)),
        ],
        compiler_params=params(),
        cost_estimate=cost(4e-6),
    )(*operands)

    t1a = banded(w_conv1a, 4, C1, 1)
    bias1a = b_conv1a[None]

    y_below, y_above = shift_along(own[:HALO], own[Y1 - HALO :], "gy")
    win = jnp.concatenate([y_below, own, y_above], axis=0)
    z_below, z_above = shift_along(win[:, :, :128], win[:, :, lanes1 - 128 :], "gz")
    low, high = win[:, :HALO_X], win[:, X1 - HALO_X :]
    x_got = lax.optimization_barrier(swaps(column_pairs(low), column_pairs(high), "gx"))
    rows = Y1 + 2
    left, right, g2, t1b = pl.pallas_call(
        middle_kernel,
        out_shape=[shaped(ROWS1, X1, lanes1), shaped(ROWS1, X1, lanes1), shaped(rows, X1, 256), banded_shape(4, C1, 1)],
        compiler_params=params(),
        cost_estimate=cost(1e-7),
    )(win, t1a, bias1a, tab1, w_conv1b)

    corner = []
    for lane in (0, lanes1 - 128):
        cut = [jnp.concatenate(column_lanes(got, lane), axis=2) for got in x_got]
        corner.append(jnp.concatenate(sides(*cut, "gx"), axis=2))
    low, high = corner
    low, high, g2, *x_got = lax.optimization_barrier((low, high, g2, *x_got))
    x_below, x_above = sides(*x_got, "gx")
    corner_below, corner_above = shift_along(low, high, "gz")
    g1, g3 = pl.pallas_call(
        outer_kernel,
        out_shape=[shaped(rows, X1, 256), shaped(rows, X1, 128)],
        scratch_shapes=[pltpu.VMEM((ROWS1, X1, 128), BF)] * 4,
        compiler_params=params(),
        cost_estimate=cost(4e-6),
    )(win, left, right, z_below, z_above, t1a, bias1a, tab1)

    wide_x = X1 + EDGE
    edges = pl.pallas_call(
        edge_middle_kernel,
        out_shape=[shaped(ROWS1, EDGE, lanes1)] * 3 + [shaped(rows, wide_x, 256)] * 3,
        compiler_params=params(),
        cost_estimate=cost(3e-6),
    )(x_below, win, x_above, g2, t1a, bias1a, tab1)
    feat, down = pl.pallas_call(
        level_one_kernel,
        out_shape=[shaped(Y1 * X1, lanes1), shaped(Y2, X2 + 2 * HALO_X2, Z2 * CP)],
        scratch_shapes=[pltpu.VMEM((ROWS1, EDGE, 128), BF)] * 6
        + [pltpu.VMEM((rows, wide_x, 256), BF)] * 3
        + [pltpu.VMEM((rows, wide_x, 128), BF)] * 3
        + [pltpu.VMEM((Y1 * EDGE, lanes1), BF), pltpu.VMEM((4, Y2 * (X2 + EDGE // 2), lanes1), BF)],
        compiler_params=params(),
        cost_estimate=cost(6e-6),
    )(
        z_below, z_above, corner_below, corner_above, *edges, g1, g3, t1a, t1b, bias1a, b_conv1b[None],
        pad_lanes(jnp.swapaxes(w_down2, 1, 2).reshape(8 * C1, C2)), pad_lanes(b_down2[None]), tab1, tab2,
    )

    down, w_conv2a = lax.optimization_barrier((down, w_conv2a))
    t2a = banded(w_conv2a, 2, CP, 3)
    y_below, y_above = shift_along(down[:HALO], down[Y2 - HALO :], "gy")
    wide = jnp.concatenate([y_below, down, y_above], axis=0)
    feat, wide, w_conv2b = lax.optimization_barrier((feat, wide, w_conv2b))
    t2b = banded(w_conv2b, 2, CP, 3)
    one = pl.pallas_call(
        one_kernel, out_shape=shaped(lanes1, Y1 * X1), compiler_params=params(), cost_estimate=cost(2e-6)
    )(feat)
    z_below, z_above = shift_along(wide[:, :, : 2 * CP], wide[:, :, 2 * CP :], "gz")
    bias2a = pad_lanes(b_conv2a[None])
    moved = [shaped(Y2 + 2, X2, 2 * CP)] * 3
    middle = pl.pallas_call(
        level_two_middle_kernel,
        out_shape=[shaped(ROWS2, PITCH2, Z2 * CP)] * 3 + moved,
        compiler_params=params(),
        cost_estimate=cost(3e-6),
    )(wide, t2a, bias2a, tab2)
    two = pl.pallas_call(
        level_two_kernel,
        out_shape=shaped(C2 * Z2, Y2 * X2),
        scratch_shapes=[pltpu.VMEM((ROWS2, PITCH2, 2 * CP), BF)] * 6 + [pltpu.VMEM((Y2 + 2, X2, 2 * CP), BF)] * 6,
        compiler_params=params(),
        cost_estimate=cost(5e-6),
    )(*middle, z_below, z_above, t2a, t2b, bias2a, pad_lanes(b_conv2b[None]), tab2)
    return one.reshape(C1, Z1, Y1 * X1), two.reshape(C2, Z2, Y2 * X2)


def solution(mesh):
    block = P(None, "gz", ("gx", "gy"))
    return jax.shard_map(
        local,
        mesh=mesh,
        in_specs=(block,) + (P(),) * 13,
        out_specs=(block, block),
        check_vma=False,
    )
```

```python
import itertools

import jax
import jax.numpy as jnp
from jax import lax
from jax.experimental import pallas as pl
from jax.experimental.pallas import tpu as pltpu
from jax.sharding import PartitionSpec as P

CX = 64
CY = 32
X1 = CX // 2
Y1 = CY // 2
X2 = X1 // 2
Y2 = Y1 // 2
Z1 = 8
Z2 = 4
C0 = 48
C1 = 64
C2 = 96
CP = 128
HALO = 2
HALO_X = 6
HALO_X2 = 2
XB = 12
XB_BELOW = 2
XB_PITCH = 16
YB = 6
ROWS1 = Y1 + 2 * HALO
ROWS2 = Y2 + 2 * HALO
EDGE = 16
PITCH2 = 32
BF = jnp.bfloat16
F32 = jnp.float32
NN = (((1,), (0,)), ((), ()))
NT = (((1,), (1,)), ((), ()))
VMEM_BYTES = 20 * 1024 * 1024


def mm(a, b, dims=NN):
    return lax.dot_general(a, b, dims, preferred_element_type=F32)


def iota(shape, dim):
    return lax.broadcasted_iota(jnp.int32, shape, dim)


def one_hot(flag):
    return jnp.where(flag, 1.0, 0.0).astype(BF)


def one_hot_rows(key, lanes):
    lane = iota(key.shape, 1)
    return jnp.concatenate([one_hot(key == lane + q) for q in range(0, lanes, 128)], axis=1)


def mask_rows(tab, y_start, rows, pitch, x_of, cell):
    bits = cell.bit_length() - 1
    shape = (rows, pitch, 128)
    y_block = (iota(shape, 0) + (y_start + cell)) >> bits
    x_block = jnp.minimum((x_of(iota(shape, 1)) + XB_BELOW * cell) >> bits, XB - 1)
    hit = one_hot(y_block * XB_PITCH + x_block == iota(shape, 2)).reshape(rows * pitch, 128)
    return mm(hit, tab)


def tissue_tables(t_ref):
    n_y, n_z, n_x = t_ref.shape
    here = lax.axis_index("gz")
    layers = []
    for k in (-1, 0, 1):
        z = here + k
        inside = jnp.where((z >= 0) & (z < n_z), 1.0, 0.0)
        layers.append(t_ref[:, jnp.clip(z, 0, n_z - 1), :].astype(F32) * inside)
    block = iota((128, n_y), 0)
    bits = XB_PITCH.bit_length() - 1
    hot_y = one_hot(lax.axis_index("gy") * 4 - 1 + (block >> bits) == iota((128, n_y), 1))
    block = iota((128, 3 * n_x), 0)
    layer = sum((iota((128, 3 * n_x), 1) >= k * n_x).astype(jnp.int32) for k in (1, 2))
    hot_x = lax.axis_index("gx") * 8 - XB_BELOW + (block & (XB_PITCH - 1)) == iota((128, 3 * n_x), 1) - layer * n_x
    rows = jnp.where(hot_x, mm(hot_y, jnp.concatenate(layers, axis=1).astype(BF)), 0.0).astype(BF)
    shape = (3 * n_x, 384)
    layer = sum((iota(shape, 0) >= k * n_x).astype(jnp.int32) for k in (1, 2))
    lane = iota(shape, 1)

    def spread(first, last):
        place = jnp.where(lane < first, 0, jnp.where(lane < last, 1, 2))
        return mm(rows, one_hot(layer == place)).astype(BF)

    return spread(64, 320), spread(128, 256)


def down1_kernel(
    v_hbm, wd_hbm, b_hbm, t_hbm, out_ref, tab_ref, tab2_ref, v_ref, w_ref, b_ref, t_ref, wd_ref, cells_ref, sems
):
    half = v_ref.shape[2]
    kz = C0 * half
    part = 16 * half
    lanes = Z1 // 2 * C1
    small = ((t_hbm, t_ref), (wd_hbm, w_ref), (b_hbm, b_ref))
    copies = [pltpu.make_async_copy(src, dst, sems.at[n]) for n, (src, dst) in enumerate(small)]
    for n in range(C0 // 4):
        cut = slice(n * 4, n * 4 + 4)
        copies.append(pltpu.make_async_copy(v_hbm.at[cut], v_ref.at[cut], sems.at[len(small) + n]))
    for copy in copies:
        copy.start()

    copies[0].wait()
    tab, tab2 = tissue_tables(t_ref)
    tab_ref[...] = tab
    tab2_ref[...] = tab2
    copies[1].wait()
    copies[2].wait()
    r = iota((kz, 2 * C0), 0)
    l = iota((kz, 2 * C0), 1)
    odd = l >= C0
    spread = one_hot(((r >> 3) == jnp.where(odd, l - C0, l)) & ((r & 1) == odd.astype(jnp.int32)))
    keep = (iota((kz, lanes), 0) & 7) >> 1 == iota((kz, lanes), 1) >> 6
    for ab in range(4):
        pair = w_ref[2 * ab : 2 * ab + 2].reshape(2 * C0, C1)
        wide = jnp.concatenate([pair] * (Z1 // 2), axis=1)
        block = jnp.where(keep, mm(spread, wide), 0.0).astype(BF)
        for n in range(C0 // 16):
            wd_ref[n, ab * part : ab * part + part, :] = block[n * part : n * part + part]

    r = iota((4 * CX, 128), 0)
    select = one_hot_rows(((r & 32) << 2) | (r & 64) | ((r & 31) << 1) | (r >> 7), 4 * CX)
    part = 16 * half
    acc = [0.0, 0.0]
    for n in range(C0 // 16):
        for copy in copies[3 + 4 * n : 7 + 4 * n]:
            copy.wait()
        for m in range(v_ref.shape[3] // 256):
            v = [v_ref[n * 16 : n * 16 + 16, h, :, m * 256 : m * 256 + 256].reshape(part, 256) for h in range(2)]
            cells = mm(select, jnp.concatenate(v, axis=0), NT).astype(BF)
            for ab in range(4):
                for h in range(2):
                    piece = cells[64 * ab : 64 * ab + 64, h * part : h * part + part]
                    cells_ref[n, h, m * 64 : m * 64 + 64, ab * part : ab * part + part] = piece
        acc = [acc[h] + mm(cells_ref[n, h], wd_ref[n]) for h in range(2)]
    mask = mask_rows(tab[:, 128:256], 0, Y1, X1, lambda x: x, 4)
    bias = twice(b_ref)
    for h in range(2):
        for q in range(2):
            value = finish(acc[h][:, q * 128 : q * 128 + 128], bias, mask, Y1)
            out_ref[:, :, (2 * h + q) * 128 : (2 * h + q + 1) * 128] = value


def twice(b_ref):
    return jnp.concatenate([b_ref[...]] * 2, axis=1)


def fill_banded(w_ref, t_ref, group, pad):
    chan = w_ref.shape[1]
    t_ref[...] = jnp.zeros_like(t_ref)
    for j in range(3):
        for i in range(3):
            for zo in range(group):
                for k in range(3):
                    lane = (3 * j + i) * (group + 2) * pad + (zo + k) * pad
                    cut, lane = divmod(lane, t_ref.shape[2])
                    t_ref[cut, zo * pad : zo * pad + chan, lane : lane + chan] = w_ref[9 * i + 3 * j + k]


def banded_shape(group, pad, cuts):
    return shaped(cuts, group * pad, 9 * (group + 2) * pad // cuts)


def banded(weights, group, pad, cuts):
    def kernel(w_ref, t_ref):
        fill_banded(w_ref, t_ref, group, pad)

    return pl.pallas_call(
        kernel, out_shape=banded_shape(group, pad, cuts), compiler_params=params(), cost_estimate=cost(1e-6)
    )(weights)


def conv_group(taps, t_ref, rows, group_out, group_full):
    pitch = taps[0][0][0].shape[1]
    width = sum(piece[2] for piece in taps[0])
    cuts = t_ref.shape[0]
    total = None
    for cut in range(cuts):
        js = range(3 * cut // cuts, 3 * (cut + 1) // cuts)
        parts = [ref[j : j + rows, :, lane : lane + n] for j in js for tap in taps for ref, lane, n in tap]
        left = jnp.concatenate([p.reshape(rows * pitch, p.shape[2]) for p in parts], axis=1)
        if width == group_full:
            right = t_ref[cut, 0:group_out, :]
        else:
            starts = range(0, t_ref.shape[2], group_full)
            right = jnp.concatenate([t_ref[cut, 0:group_out, lane : lane + width] for lane in starts], axis=1)
        term = mm(left, right, NT)
        total = term if total is None else total + term
    return total


def finish(acc, bias, mask, rows):
    value = jnp.maximum(acc + bias, 0.0) * mask
    return value.astype(BF).reshape(rows, value.shape[0] // rows, value.shape[1])


def fill_sides(left, right, lane, inner):
    cut = slice(lane, lane + inner.shape[2])
    none = jnp.zeros_like(inner[:, :1])
    left[:, :, cut] = jnp.concatenate([none, inner[:, :-1]], axis=1)
    right[:, :, cut] = jnp.concatenate([inner[:, 1:], none], axis=1)


def middle_kernel(win_ref, t_ref, b_ref, tab_ref, w_ref, left_ref, right_ref, out_ref, next_ref):
    fill_banded(w_ref, next_ref, 4, C1)
    for q in range(4):
        fill_sides(left_ref, right_ref, q * 128, win_ref[:, :, q * 128 : q * 128 + 128])
    rows = Y1 + 2
    mask = mask_rows(tab_ref[:, 128:256], -1, rows, X1, lambda x: x, 4)
    acc = conv_group([[(ref, 128, 384)] for ref in (left_ref, win_ref, right_ref)], t_ref, rows, 256, 384)
    for q in range(2):
        cut = slice(q * 128, q * 128 + 128)
        out_ref[:, :, cut] = finish(acc[:, cut], twice(b_ref), mask, rows)


def outer_kernel(win_ref, left_ref, right_ref, zl_ref, zr_ref, t_ref, b_ref, tab_ref, low_ref, high_ref, ll, lr, hl, hr):
    fill_sides(ll, lr, 0, zl_ref[...])
    fill_sides(hl, hr, 0, zr_ref[...])
    own = (left_ref, win_ref, right_ref)
    rows = Y1 + 2
    mask = mask_rows(tab_ref[...], -1, rows, X1, lambda x: x, 4)
    taps = [[(z, 0, 128), (ref, 0, 256)] for z, ref in zip((ll, zl_ref, lr), own)]
    acc = conv_group(taps, t_ref, rows, 256, 384)
    for q in range(2):
        cut = slice(q * 128, q * 128 + 128)
        low_ref[:, :, cut] = finish(acc[:, cut], twice(b_ref), mask[:, cut], rows)
    taps = [[(ref, 384, 128), (z, 0, 128)] for z, ref in zip((hl, zr_ref, hr), own)]
    acc = conv_group(taps, t_ref, rows, 128, 384)
    high_ref[...] = finish(acc, twice(b_ref), mask[:, 256:384], rows)


def fill_edges(copies, pieces):
    line = jnp.concatenate(pieces, axis=1)
    copies[0][...] = line
    for i in (1, 2):
        copies[i][...] = jnp.concatenate([line[:, i:], jnp.zeros_like(line[:, :i])], axis=1)


def edge_masks(tab_ref):
    mask = mask_rows(tab_ref[...], -1, Y1 + 2, EDGE, lambda r: jnp.where(r < 8, r - 5, r + X1 - 9), 4)
    return [mask[:, q * 128 : q * 128 + 128] for q in range(3)]


def edge_group(taps, t_ref, b_ref, masks, inner_ref, moved):
    rows = Y1 + 2
    acc = conv_group(taps, t_ref, rows, 128 * len(masks), 384)
    i0, i1, i2 = moved
    for q, mask in enumerate(masks):
        cut = slice(q * 128, q * 128 + 128)
        edge = finish(acc[:, cut], twice(b_ref), mask, rows)
        inner = inner_ref[:, :, cut][:, 1:-1]
        i0[:, :X1, cut] = jnp.concatenate([edge[:, 4:6], inner], axis=1)
        i1[:, :X1, cut] = jnp.concatenate([edge[:, 5:6], inner, edge[:, 8:9]], axis=1)
        i2[:, :X1, cut] = jnp.concatenate([inner, edge[:, 8:10]], axis=1)
        i0[:, X1:, cut] = edge
        for i, copy in ((1, i1), (2, i2)):
            copy[:, X1:, cut] = jnp.concatenate([edge[:, i:], jnp.zeros((rows, i, 128), BF)], axis=1)


def column_lanes(field, lane, stride=Z1 * C1):
    return [field[:, :, first : first + 128] for first in range(lane, field.shape[2], stride)]


def edge_middle_kernel(xl_ref, win_ref, xr_ref, g_ref, t_ref, b_ref, tab_ref, e0, e1, e2, m0, m1, m2):
    for lane in range(0, Z1 * C1, 128):
        cut = slice(lane, lane + 128)
        inner = win_ref[:, :, cut]
        left, right = (column_lanes(ref, lane) for ref in (xl_ref, xr_ref))
        pieces = left + [inner[:, :2], inner[:, X1 - 2 :]] + right
        fill_edges([e.at[:, :, cut] for e in (e0, e1, e2)], pieces)
    here = edge_masks(tab_ref)[1]
    edge_group([[(e, 128, 384)] for e in (e0, e1, e2)], t_ref, b_ref, (here, here), g_ref, (m0, m1, m2))


def level_one_kernel(
    zl_ref, zr_ref, cl_ref, cr_ref, e0, e1, e2, m0, m1, m2, g1_ref, g3_ref, ta_ref, tb_ref, ba_ref, bb_ref, wd_ref, bd_ref, tab_ref,
    tab2_ref, feat_ref, down_ref, l0, l1, l2, h0, h1, h2, i0, i1, i2, j0, j1, j2, side_ref, d_ref,
):
    own, mid, low, high = (e0, e1, e2), (m0, m1, m2), (i0, i1, i2), (j0, j1, j2)
    for z_ref, c_ref, copies in ((zl_ref, cl_ref, (l0, l1, l2)), (zr_ref, cr_ref, (h0, h1, h2))):
        inner = z_ref[...]
        corner = column_lanes(c_ref, 0, 128)
        fill_edges(copies, corner[:3] + [inner[:, :2], inner[:, X1 - 2 :]] + corner[3:])
    below, here, above = edge_masks(tab_ref)
    taps = [[(z, 0, 128), (e, 0, 256)] for z, e in zip((l0, l1, l2), own)]
    edge_group(taps, ta_ref, ba_ref, (below, here), g1_ref, low)
    taps = [[(e, 384, 128), (z, 0, 128)] for z, e in zip((h0, h1, h2), own)]
    edge_group(taps, ta_ref, ba_ref, (above,), g3_ref, high)

    def cell_of(r):
        return jnp.where(r < X1, r, jnp.where(r < X1 + 8, r - X1 - 4, r - 8))

    mask = mask_rows(tab_ref[:, 128:256], 0, Y1, X1 + EDGE, cell_of, 4)
    first = [[(a, 0, 256), (b, 0, 128)] for a, b in zip(low, mid)]
    second = [[(a, 0, 256), (b, 0, 128)] for a, b in zip(mid, high)]
    for g, taps in enumerate((first, second)):
        acc = conv_group(taps, tb_ref, Y1, 256, 384)
        for q in range(2):
            value = finish(acc[:, q * 128 : q * 128 + 128], twice(bb_ref), mask, Y1)
            cut = slice((2 * g + q) * 128, (2 * g + q + 1) * 128)
            feat_ref[:, cut] = value[:, :X1].reshape(Y1 * X1, 128)
            side_ref[:, cut] = value[:, X1:].reshape(Y1 * EDGE, 128)

    size = 8 * X1
    quarter = size // 4
    r = iota((size, 128), 0)
    select = one_hot_rows(((r & 48) << 2) | ((r & 64) >> 1) | ((r & 15) << 1) | (r >> 7), size)
    for n in range(Y1 // 8):
        cells = mm(select, feat_ref[n * size : n * size + size, :]).astype(BF)
        for q in range(4):
            d_ref[q, n * quarter : n * quarter + quarter, :] = cells[q * quarter : (q + 1) * quarter]
    select = one_hot_rows(((r & 56) << 2) | ((r & 64) >> 2) | ((r & 7) << 1) | (r >> 7), size)
    cells = mm(select, side_ref[...]).astype(BF)
    for q in range(4):
        d_ref[q, Y2 * X2 :, :] = cells[q * quarter : (q + 1) * quarter]
    inner_mask = mask_rows(tab2_ref[:, 128:256], 0, Y2, X2, lambda x: x, 2)
    side_mask = mask_rows(tab2_ref[:, 128:256], 0, Y2, EDGE // 2, lambda r: jnp.where(r < 4, r - 2, r + X2 - 4), 2)
    for z in range(Z2):
        left = jnp.concatenate([d_ref[q, :, z * 128 : z * 128 + 128] for q in range(4)], axis=1)
        acc = mm(left, wd_ref[...])
        inner = finish(acc[: Y2 * X2], bd_ref[...], inner_mask, Y2)
        side = finish(acc[Y2 * X2 :], bd_ref[...], side_mask, Y2)
        down_ref[:, :, z * CP : z * CP + CP] = jnp.concatenate([side[:, 0:2], inner, side[:, 4:6]], axis=1)


def one_kernel(feat_ref, out_ref):
    lanes = feat_ref.shape[1]
    r = iota((lanes, 128), 0)
    order = one_hot_rows(((r & 7) << 6) | (r >> 3), lanes)
    out_ref[...] = mm(order, feat_ref[...], NT).astype(BF)


def fill_pitch(copies, wide):
    pitch = copies[0].shape[1]
    for lane in range(0, wide.shape[2], 128):
        line = wide[:, :, lane : lane + 128]
        for i, copy in enumerate(copies):
            spare = jnp.zeros((line.shape[0], pitch - line.shape[1] + i, 128), BF)
            copy[:, :, lane : lane + 128] = jnp.concatenate([line[:, i:], spare], axis=1)


def level_two_group(taps, t_ref, b_ref, masks, moved):
    rows = Y2 + 2
    acc = conv_group(taps, t_ref, rows, 256, 512)
    for q in range(2):
        cut = slice(q * 128, q * 128 + 128)
        value = finish(acc[:, cut], b_ref[...], masks[q], rows)
        for i, ref in enumerate(moved):
            ref[:, :, cut] = value[:, i : i + X2]


def level_two_masks(tab_ref):
    mask = mask_rows(tab_ref[...], -1, Y2 + 2, PITCH2, lambda x: x - 1, 2)
    return [mask[:, q * 128 : q * 128 + 128] for q in range(3)]


def level_two_middle_kernel(wide_ref, t_ref, b_ref, tab_ref, a0, a1, a2, m0, m1, m2):
    fill_pitch((a0, a1, a2), wide_ref[...])
    here = level_two_masks(tab_ref)[1]
    level_two_group([[(a, 0, 512)] for a in (a0, a1, a2)], t_ref, b_ref, (here, here), (m0, m1, m2))


def level_two_kernel(
    a0, a1, a2, m0, m1, m2, zl_ref, zr_ref, ta_ref, tb_ref, ba_ref, bb_ref, tab_ref, out_ref,
    l0, l1, l2, h0, h1, h2, i0, i1, i2, j0, j1, j2,
):
    fill_pitch((l0, l1, l2), zl_ref[...])
    fill_pitch((h0, h1, h2), zr_ref[...])
    below, here, above = level_two_masks(tab_ref)
    own, mid, low, high = (a0, a1, a2), (m0, m1, m2), (i0, i1, i2), (j0, j1, j2)
    taps = [[(z, 0, 256), (a, 0, 256)] for z, a in zip((l0, l1, l2), own)]
    level_two_group(taps, ta_ref, ba_ref, (below, here), low)
    taps = [[(a, 256, 256), (z, 0, 256)] for z, a in zip((h0, h1, h2), own)]
    level_two_group(taps, ta_ref, ba_ref, (here, above), high)
    mask = mask_rows(tab_ref[:, 128:256], 0, Y2, X2, lambda x: x, 2)
    feat = []
    for pair in ((low, mid), (mid, high)):
        acc = conv_group([[(a, 0, 256), (b, 0, 256)] for a, b in zip(*pair)], tb_ref, Y2, 256, 512)
        for q in range(2):
            feat.append((jnp.maximum(acc[:, q * 128 : q * 128 + 128] + bb_ref[...], 0.0) * mask).astype(BF))
    r = iota((C2 * Z2, 128), 0)
    order = one_hot_rows(((r & 3) << 7) | (r >> 2), Z2 * CP)
    out_ref[...] = mm(order, jnp.concatenate(feat, axis=1), NT).astype(BF)


def partner(index, second, count):
    other = index + 1 if index % 2 == second else index - 1
    return other if 0 <= other < count else None


def swap(value, moves):
    axes = ("gx", "gy", "gz")
    sizes = [lax.axis_size(axis) for axis in axes]
    pairs = []
    for source in itertools.product(*(range(size) for size in sizes)):
        target = [partner(i, moves[axis], size) if axis in moves else i for i, axis, size in zip(source, axes, sizes)]
        if None in target:
            other = sizes[1] - 1 - source[1] if "gy" in moves else source[1] ^ 1
            target = [source[0], other, source[2]]
        pairs.append(tuple((x * sizes[1] + y) * sizes[2] + z for x, y, z in (source, target)))
    return lax.ppermute(value, axes, pairs)


def parity(axis):
    return lax.axis_index(axis) % 2 == 0


def sides(first, second, axis):
    index = lax.axis_index(axis)
    even = parity(axis)
    below = jnp.where(index > 0, jnp.where(even, second, first), jnp.zeros_like(first))
    above = jnp.where(index < lax.axis_size(axis) - 1, jnp.where(even, first, second), jnp.zeros_like(first))
    return below, above


def swaps(low_edge, high_edge, axis):
    even = parity(axis)
    first = swap(jnp.where(even, high_edge, low_edge), {axis: 0})
    second = swap(jnp.where(even, low_edge, high_edge), {axis: 1}) if lax.axis_size(axis) > 2 else first
    return first, second


def shift_along(low_edge, high_edge, axis):
    return sides(*swaps(low_edge, high_edge, axis), axis)


def column_pairs(field):
    return jnp.concatenate([field[:, i : i + 2] for i in range(0, field.shape[1], 2)], axis=2)


def params():
    return pltpu.CompilerParams(vmem_limit_bytes=VMEM_BYTES)


def cost(seconds):
    return pl.CostEstimate(flops=int(1e15 * seconds), bytes_accessed=0, transcendentals=0)


def shaped(*shape):
    return jax.ShapeDtypeStruct(shape, BF)


def pad_lanes(value):
    return jnp.pad(value, [(0, 0)] * (value.ndim - 1) + [(0, CP - value.shape[-1])])


def local(
    volume, tissue, w_down1, b_down1, w_conv1a, b_conv1a, w_conv1b, b_conv1b,
    w_down2, b_down2, w_conv2a, b_conv2a, w_conv2b, b_conv2b,
):
    depth = volume.shape[1]
    lanes1 = Z1 * C1
    half = depth // 2
    operands = [volume.reshape(C0, 2, half, -1), jnp.swapaxes(w_down1, 1, 2), b_down1[None], tissue.transpose(1, 2, 0)]
    operands = [pltpu.with_memory_space_constraint(x, pltpu.HBM) for x in operands]
    own, tab1, tab2 = pl.pallas_call(
        down1_kernel,
        in_specs=[pl.BlockSpec(memory_space=pltpu.HBM)] * 4,
        out_shape=[shaped(Y1, X1, lanes1), shaped(128, 384), shaped(128, 384)],
        scratch_shapes=[pltpu.VMEM(x.shape, x.dtype) for x in operands]
        + [
            pltpu.VMEM((C0 // 16, 64 * half, lanes1 // 2), BF),
            pltpu.VMEM((C0 // 16, 2, Y1 * X1, 64 * half), BF),
            pltpu.SemaphoreType.DMA((3 + C0 // 4,)),
        ],
        compiler_params=params(),
        cost_estimate=cost(4e-6),
    )(*operands)

    t1a = banded(w_conv1a, 4, C1, 1)
    bias1a = b_conv1a[None]

    y_below, y_above = shift_along(own[:HALO], own[Y1 - HALO :], "gy")
    win = jnp.concatenate([y_below, own, y_above], axis=0)
    z_below, z_above = shift_along(win[:, :, :128], win[:, :, lanes1 - 128 :], "gz")
    low, high = win[:, :HALO_X], win[:, X1 - HALO_X :]
    x_got = lax.optimization_barrier(swaps(column_pairs(low), column_pairs(high), "gx"))
    rows = Y1 + 2
    left, right, g2, t1b = pl.pallas_call(
        middle_kernel,
        out_shape=[shaped(ROWS1, X1, lanes1), shaped(ROWS1, X1, lanes1), shaped(rows, X1, 256), banded_shape(4, C1, 1)],
        compiler_params=params(),
        cost_estimate=cost(1e-7),
    )(win, t1a, bias1a, tab1, w_conv1b)

    corner = []
    for lane in (0, lanes1 - 128):
        cut = [jnp.concatenate(column_lanes(got, lane), axis=2) for got in x_got]
        corner.append(jnp.concatenate(sides(*cut, "gx"), axis=2))
    low, high = corner
    low, high, g2, *x_got = lax.optimization_barrier((low, high, g2, *x_got))
    x_below, x_above = sides(*x_got, "gx")
    corner_below, corner_above = shift_along(low, high, "gz")
    g1, g3 = pl.pallas_call(
        outer_kernel,
        out_shape=[shaped(rows, X1, 256), shaped(rows, X1, 128)],
        scratch_shapes=[pltpu.VMEM((ROWS1, X1, 128), BF)] * 4,
        compiler_params=params(),
        cost_estimate=cost(4e-6),
    )(win, left, right, z_below, z_above, t1a, bias1a, tab1)

    wide_x = X1 + EDGE
    edges = pl.pallas_call(
        edge_middle_kernel,
        out_shape=[shaped(ROWS1, EDGE, lanes1)] * 3 + [shaped(rows, wide_x, 256)] * 3,
        compiler_params=params(),
        cost_estimate=cost(3e-6),
    )(x_below, win, x_above, g2, t1a, bias1a, tab1)
    feat, down = pl.pallas_call(
        level_one_kernel,
        out_shape=[shaped(Y1 * X1, lanes1), shaped(Y2, X2 + 2 * HALO_X2, Z2 * CP)],
        scratch_shapes=[pltpu.VMEM((ROWS1, EDGE, 128), BF)] * 6
        + [pltpu.VMEM((rows, wide_x, 256), BF)] * 3
        + [pltpu.VMEM((rows, wide_x, 128), BF)] * 3
        + [pltpu.VMEM((Y1 * EDGE, lanes1), BF), pltpu.VMEM((4, Y2 * (X2 + EDGE // 2), lanes1), BF)],
        compiler_params=params(),
        cost_estimate=cost(6e-6),
    )(
        z_below, z_above, corner_below, corner_above, *edges, g1, g3, t1a, t1b, bias1a, b_conv1b[None],
        pad_lanes(jnp.swapaxes(w_down2, 1, 2).reshape(8 * C1, C2)), pad_lanes(b_down2[None]), tab1, tab2,
    )

    down, w_conv2a = lax.optimization_barrier((down, w_conv2a))
    t2a = banded(w_conv2a, 2, CP, 3)
    y_below, y_above = shift_along(down[:HALO], down[Y2 - HALO :], "gy")
    wide = jnp.concatenate([y_below, down, y_above], axis=0)
    feat, wide, w_conv2b = lax.optimization_barrier((feat, wide, w_conv2b))
    t2b = banded(w_conv2b, 2, CP, 3)
    one = pl.pallas_call(
        one_kernel, out_shape=shaped(lanes1, Y1 * X1), compiler_params=params(), cost_estimate=cost(2e-6)
    )(feat)
    z_below, z_above = shift_along(wide[:, :, : 2 * CP], wide[:, :, 2 * CP :], "gz")
    bias2a = pad_lanes(b_conv2a[None])
    moved = [shaped(Y2 + 2, X2, 2 * CP)] * 3
    middle = pl.pallas_call(
        level_two_middle_kernel,
        out_shape=[shaped(ROWS2, PITCH2, Z2 * CP)] * 3 + moved,
        compiler_params=params(),
        cost_estimate=cost(3e-6),
    )(wide, t2a, bias2a, tab2)
    two = pl.pallas_call(
        level_two_kernel,
        out_shape=shaped(C2 * Z2, Y2 * X2),
        scratch_shapes=[pltpu.VMEM((ROWS2, PITCH2, 2 * CP), BF)] * 6 + [pltpu.VMEM((Y2 + 2, X2, 2 * CP), BF)] * 6,
        compiler_params=params(),
        cost_estimate=cost(5e-6),
    )(*middle, z_below, z_above, t2a, t2b, bias2a, pad_lanes(b_conv2b[None]), tab2)
    return one.reshape(C1, Z1, Y1 * X1), two.reshape(C2, Z2, Y2 * X2)


def solution(mesh):
    block = P(None, "gz", ("gx", "gy"))
    return jax.shard_map(
        local,
        mesh=mesh,
        in_specs=(block,) + (P(),) * 13,
        out_specs=(block, block),
        check_vma=False,
    )
```

```python
import itertools

import jax
import jax.numpy as jnp
from jax import lax
from jax.experimental import pallas as pl
from jax.experimental.pallas import tpu as pltpu
from jax.sharding import PartitionSpec as P

CX = 64
CY = 32
X1 = CX // 2
Y1 = CY // 2
X2 = X1 // 2
Y2 = Y1 // 2
Z1 = 8
Z2 = 4
C0 = 48
C1 = 64
C2 = 96
CP = 128
HALO = 2
HALO_X = 6
HALO_X2 = 2
XB = 12
XB_BELOW = 2
XB_PITCH = 16
YB = 6
ROWS1 = Y1 + 2 * HALO
ROWS2 = Y2 + 2 * HALO
EDGE = 16
PITCH2 = 32
BF = jnp.bfloat16
F32 = jnp.float32
NN = (((1,), (0,)), ((), ()))
NT = (((1,), (1,)), ((), ()))
VMEM_BYTES = 20 * 1024 * 1024


def mm(a, b, dims=NN):
    return lax.dot_general(a, b, dims, preferred_element_type=F32)


def iota(shape, dim):
    return lax.broadcasted_iota(jnp.int32, shape, dim)


def one_hot(flag):
    return jnp.where(flag, 1.0, 0.0).astype(BF)


def one_hot_rows(key, lanes):
    lane = iota(key.shape, 1)
    return jnp.concatenate([one_hot(key == lane + q) for q in range(0, lanes, 128)], axis=1)


def mask_rows(tab, y_start, rows, pitch, x_of, cell):
    bits = cell.bit_length() - 1
    shape = (rows, pitch, 128)
    y_block = (iota(shape, 0) + (y_start + cell)) >> bits
    x_block = jnp.minimum((x_of(iota(shape, 1)) + XB_BELOW * cell) >> bits, XB - 1)
    hit = one_hot(y_block * XB_PITCH + x_block == iota(shape, 2)).reshape(rows * pitch, 128)
    return mm(hit, tab)


def tissue_tables(t_ref):
    n_y, n_z, n_x = t_ref.shape
    here = lax.axis_index("gz")
    layers = []
    for k in (-1, 0, 1):
        z = here + k
        inside = jnp.where((z >= 0) & (z < n_z), 1.0, 0.0)
        layers.append(t_ref[:, jnp.clip(z, 0, n_z - 1), :].astype(F32) * inside)
    block = iota((128, n_y), 0)
    bits = XB_PITCH.bit_length() - 1
    hot_y = one_hot(lax.axis_index("gy") * 4 - 1 + (block >> bits) == iota((128, n_y), 1))
    block = iota((128, 3 * n_x), 0)
    layer = sum((iota((128, 3 * n_x), 1) >= k * n_x).astype(jnp.int32) for k in (1, 2))
    hot_x = lax.axis_index("gx") * 8 - XB_BELOW + (block & (XB_PITCH - 1)) == iota((128, 3 * n_x), 1) - layer * n_x
    rows = jnp.where(hot_x, mm(hot_y, jnp.concatenate(layers, axis=1).astype(BF)), 0.0).astype(BF)
    shape = (3 * n_x, 384)
    layer = sum((iota(shape, 0) >= k * n_x).astype(jnp.int32) for k in (1, 2))
    lane = iota(shape, 1)

    def spread(first, last):
        place = jnp.where(lane < first, 0, jnp.where(lane < last, 1, 2))
        return mm(rows, one_hot(layer == place)).astype(BF)

    return spread(64, 320), spread(128, 256)


def down1_kernel(
    v_hbm, wd_hbm, b_hbm, t_hbm, out_ref, tab_ref, tab2_ref, v_ref, w_ref, b_ref, t_ref, wd_ref, cells_ref, sems
):
    half = v_ref.shape[2]
    kz = C0 * half
    part = 16 * half
    lanes = Z1 // 2 * C1
    small = ((t_hbm, t_ref), (wd_hbm, w_ref), (b_hbm, b_ref))
    copies = [pltpu.make_async_copy(src, dst, sems.at[n]) for n, (src, dst) in enumerate(small)]
    for n in range(C0 // 16):
        cut = slice(n * 16, n * 16 + 16)
        copies.append(pltpu.make_async_copy(v_hbm.at[cut], v_ref.at[cut], sems.at[len(small) + n]))
    for copy in copies:
        copy.start()

    copies[0].wait()
    tab, tab2 = tissue_tables(t_ref)
    tab_ref[...] = tab
    tab2_ref[...] = tab2
    copies[1].wait()
    copies[2].wait()
    r = iota((kz, 2 * C0), 0)
    l = iota((kz, 2 * C0), 1)
    odd = l >= C0
    spread = one_hot(((r >> 3) == jnp.where(odd, l - C0, l)) & ((r & 1) == odd.astype(jnp.int32)))
    keep = (iota((kz, lanes), 0) & 7) >> 1 == iota((kz, lanes), 1) >> 6
    for ab in range(4):
        pair = w_ref[2 * ab : 2 * ab + 2].reshape(2 * C0, C1)
        wide = jnp.concatenate([pair] * (Z1 // 2), axis=1)
        block = jnp.where(keep, mm(spread, wide), 0.0).astype(BF)
        for n in range(C0 // 16):
            wd_ref[n, ab * part : ab * part + part, :] = block[n * part : n * part + part]

    r = iota((4 * CX, 128), 0)
    select = one_hot_rows(((r & 32) << 2) | (r & 64) | ((r & 31) << 1) | (r >> 7), 4 * CX)
    part = 16 * half
    acc = [0.0, 0.0]
    for n, copy in enumerate(copies[3:]):
        copy.wait()
        for m in range(v_ref.shape[3] // 256):
            v = [v_ref[n * 16 : n * 16 + 16, h, :, m * 256 : m * 256 + 256].reshape(part, 256) for h in range(2)]
            cells = mm(select, jnp.concatenate(v, axis=0), NT).astype(BF)
            for ab in range(4):
                for h in range(2):
                    piece = cells[64 * ab : 64 * ab + 64, h * part : h * part + part]
                    cells_ref[n, h, m * 64 : m * 64 + 64, ab * part : ab * part + part] = piece
        acc = [acc[h] + mm(cells_ref[n, h], wd_ref[n]) for h in range(2)]
    mask = mask_rows(tab[:, 128:256], 0, Y1, X1, lambda x: x, 4)
    bias = twice(b_ref)
    for h in range(2):
        for q in range(2):
            value = finish(acc[h][:, q * 128 : q * 128 + 128], bias, mask, Y1)
            out_ref[:, :, (2 * h + q) * 128 : (2 * h + q + 1) * 128] = value


def twice(b_ref):
    return jnp.concatenate([b_ref[...]] * 2, axis=1)


def fill_banded(w_ref, t_ref, group, pad):
    chan = w_ref.shape[1]
    t_ref[...] = jnp.zeros_like(t_ref)
    for j in range(3):
        for i in range(3):
            for zo in range(group):
                for k in range(3):
                    lane = (3 * j + i) * (group + 2) * pad + (zo + k) * pad
                    cut, lane = divmod(lane, t_ref.shape[2])
                    t_ref[cut, zo * pad : zo * pad + chan, lane : lane + chan] = w_ref[9 * i + 3 * j + k]


def banded_shape(group, pad, cuts):
    return shaped(cuts, group * pad, 9 * (group + 2) * pad // cuts)


def banded(weights, group, pad, cuts):
    def kernel(w_ref, t_ref):
        fill_banded(w_ref, t_ref, group, pad)

    return pl.pallas_call(
        kernel, out_shape=banded_shape(group, pad, cuts), compiler_params=params(), cost_estimate=cost(1e-6)
    )(weights)


def conv_group(taps, t_ref, rows, group_out, group_full):
    pitch = taps[0][0][0].shape[1]
    width = sum(piece[2] for piece in taps[0])
    cuts = t_ref.shape[0]
    total = None
    for cut in range(cuts):
        js = range(3 * cut // cuts, 3 * (cut + 1) // cuts)
        parts = [ref[j : j + rows, :, lane : lane + n] for j in js for tap in taps for ref, lane, n in tap]
        left = jnp.concatenate([p.reshape(rows * pitch, p.shape[2]) for p in parts], axis=1)
        if width == group_full:
            right = t_ref[cut, 0:group_out, :]
        else:
            starts = range(0, t_ref.shape[2], group_full)
            right = jnp.concatenate([t_ref[cut, 0:group_out, lane : lane + width] for lane in starts], axis=1)
        term = mm(left, right, NT)
        total = term if total is None else total + term
    return total


def finish(acc, bias, mask, rows):
    value = jnp.maximum(acc + bias, 0.0) * mask
    return value.astype(BF).reshape(rows, value.shape[0] // rows, value.shape[1])


def fill_sides(left, right, lane, inner):
    cut = slice(lane, lane + inner.shape[2])
    none = jnp.zeros_like(inner[:, :1])
    left[:, :, cut] = jnp.concatenate([none, inner[:, :-1]], axis=1)
    right[:, :, cut] = jnp.concatenate([inner[:, 1:], none], axis=1)


def middle_kernel(win_ref, t_ref, b_ref, tab_ref, w_ref, left_ref, right_ref, out_ref, next_ref):
    fill_banded(w_ref, next_ref, 4, C1)
    for q in range(4):
        fill_sides(left_ref, right_ref, q * 128, win_ref[:, :, q * 128 : q * 128 + 128])
    rows = Y1 + 2
    mask = mask_rows(tab_ref[:, 128:256], -1, rows, X1, lambda x: x, 4)
    acc = conv_group([[(ref, 128, 384)] for ref in (left_ref, win_ref, right_ref)], t_ref, rows, 256, 384)
    for q in range(2):
        cut = slice(q * 128, q * 128 + 128)
        out_ref[:, :, cut] = finish(acc[:, cut], twice(b_ref), mask, rows)


def outer_kernel(win_ref, left_ref, right_ref, zl_ref, zr_ref, t_ref, b_ref, tab_ref, low_ref, high_ref, ll, lr, hl, hr):
    fill_sides(ll, lr, 0, zl_ref[...])
    fill_sides(hl, hr, 0, zr_ref[...])
    own = (left_ref, win_ref, right_ref)
    rows = Y1 + 2
    mask = mask_rows(tab_ref[...], -1, rows, X1, lambda x: x, 4)
    taps = [[(z, 0, 128), (ref, 0, 256)] for z, ref in zip((ll, zl_ref, lr), own)]
    acc = conv_group(taps, t_ref, rows, 256, 384)
    for q in range(2):
        cut = slice(q * 128, q * 128 + 128)
        low_ref[:, :, cut] = finish(acc[:, cut], twice(b_ref), mask[:, cut], rows)
    taps = [[(ref, 384, 128), (z, 0, 128)] for z, ref in zip((hl, zr_ref, hr), own)]
    acc = conv_group(taps, t_ref, rows, 128, 384)
    high_ref[...] = finish(acc, twice(b_ref), mask[:, 256:384], rows)


def fill_edges(copies, pieces):
    line = jnp.concatenate(pieces, axis=1)
    copies[0][...] = line
    for i in (1, 2):
        copies[i][...] = jnp.concatenate([line[:, i:], jnp.zeros_like(line[:, :i])], axis=1)


def edge_masks(tab_ref):
    mask = mask_rows(tab_ref[...], -1, Y1 + 2, EDGE, lambda r: jnp.where(r < 8, r - 5, r + X1 - 9), 4)
    return [mask[:, q * 128 : q * 128 + 128] for q in range(3)]


def edge_group(taps, t_ref, b_ref, masks, inner_ref, moved):
    rows = Y1 + 2
    acc = conv_group(taps, t_ref, rows, 128 * len(masks), 384)
    i0, i1, i2 = moved
    for q, mask in enumerate(masks):
        cut = slice(q * 128, q * 128 + 128)
        edge = finish(acc[:, cut], twice(b_ref), mask, rows)
        inner = inner_ref[:, :, cut][:, 1:-1]
        i0[:, :X1, cut] = jnp.concatenate([edge[:, 4:6], inner], axis=1)
        i1[:, :X1, cut] = jnp.concatenate([edge[:, 5:6], inner, edge[:, 8:9]], axis=1)
        i2[:, :X1, cut] = jnp.concatenate([inner, edge[:, 8:10]], axis=1)
        i0[:, X1:, cut] = edge
        for i, copy in ((1, i1), (2, i2)):
            copy[:, X1:, cut] = jnp.concatenate([edge[:, i:], jnp.zeros((rows, i, 128), BF)], axis=1)


def column_lanes(field, lane, stride=Z1 * C1):
    return [field[:, :, first : first + 128] for first in range(lane, field.shape[2], stride)]


def edge_middle_kernel(xl_ref, win_ref, xr_ref, g_ref, t_ref, b_ref, tab_ref, e0, e1, e2, m0, m1, m2):
    for lane in range(0, Z1 * C1, 128):
        cut = slice(lane, lane + 128)
        inner = win_ref[:, :, cut]
        left, right = (column_lanes(ref, lane) for ref in (xl_ref, xr_ref))
        pieces = left + [inner[:, :2], inner[:, X1 - 2 :]] + right
        fill_edges([e.at[:, :, cut] for e in (e0, e1, e2)], pieces)
    here = edge_masks(tab_ref)[1]
    edge_group([[(e, 128, 384)] for e in (e0, e1, e2)], t_ref, b_ref, (here, here), g_ref, (m0, m1, m2))


def level_one_kernel(
    zl_ref, zr_ref, cl_ref, cr_ref, e0, e1, e2, m0, m1, m2, g1_ref, g3_ref, ta_ref, tb_ref, ba_ref, bb_ref, wd_ref, bd_ref, tab_ref,
    tab2_ref, feat_ref, down_ref, l0, l1, l2, h0, h1, h2, i0, i1, i2, j0, j1, j2, side_ref, d_ref,
):
    own, mid, low, high = (e0, e1, e2), (m0, m1, m2), (i0, i1, i2), (j0, j1, j2)
    for z_ref, c_ref, copies in ((zl_ref, cl_ref, (l0, l1, l2)), (zr_ref, cr_ref, (h0, h1, h2))):
        inner = z_ref[...]
        corner = column_lanes(c_ref, 0, 128)
        fill_edges(copies, corner[:3] + [inner[:, :2], inner[:, X1 - 2 :]] + corner[3:])
    below, here, above = edge_masks(tab_ref)
    taps = [[(z, 0, 128), (e, 0, 256)] for z, e in zip((l0, l1, l2), own)]
    edge_group(taps, ta_ref, ba_ref, (below, here), g1_ref, low)
    taps = [[(e, 384, 128), (z, 0, 128)] for z, e in zip((h0, h1, h2), own)]
    edge_group(taps, ta_ref, ba_ref, (above,), g3_ref, high)

    def cell_of(r):
        return jnp.where(r < X1, r, jnp.where(r < X1 + 8, r - X1 - 4, r - 8))

    mask = mask_rows(tab_ref[:, 128:256], 0, Y1, X1 + EDGE, cell_of, 4)
    first = [[(a, 0, 256), (b, 0, 128)] for a, b in zip(low, mid)]
    second = [[(a, 0, 256), (b, 0, 128)] for a, b in zip(mid, high)]
    for g, taps in enumerate((first, second)):
        acc = conv_group(taps, tb_ref, Y1, 256, 384)
        for q in range(2):
            value = finish(acc[:, q * 128 : q * 128 + 128], twice(bb_ref), mask, Y1)
            cut = slice((2 * g + q) * 128, (2 * g + q + 1) * 128)
            feat_ref[:, cut] = value[:, :X1].reshape(Y1 * X1, 128)
            side_ref[:, cut] = value[:, X1:].reshape(Y1 * EDGE, 128)

    size = 8 * X1
    quarter = size // 4
    r = iota((size, 128), 0)
    select = one_hot_rows(((r & 48) << 2) | ((r & 64) >> 1) | ((r & 15) << 1) | (r >> 7), size)
    for n in range(Y1 // 8):
        cells = mm(select, feat_ref[n * size : n * size + size, :]).astype(BF)
        for q in range(4):
            d_ref[q, n * quarter : n * quarter + quarter, :] = cells[q * quarter : (q + 1) * quarter]
    select = one_hot_rows(((r & 56) << 2) | ((r & 64) >> 2) | ((r & 7) << 1) | (r >> 7), size)
    cells = mm(select, side_ref[...]).astype(BF)
    for q in range(4):
        d_ref[q, Y2 * X2 :, :] = cells[q * quarter : (q + 1) * quarter]
    inner_mask = mask_rows(tab2_ref[:, 128:256], 0, Y2, X2, lambda x: x, 2)
    side_mask = mask_rows(tab2_ref[:, 128:256], 0, Y2, EDGE // 2, lambda r: jnp.where(r < 4, r - 2, r + X2 - 4), 2)
    for z in range(Z2):
        left = jnp.concatenate([d_ref[q, :, z * 128 : z * 128 + 128] for q in range(4)], axis=1)
        acc = mm(left, wd_ref[...])
        inner = finish(acc[: Y2 * X2], bd_ref[...], inner_mask, Y2)
        side = finish(acc[Y2 * X2 :], bd_ref[...], side_mask, Y2)
        down_ref[:, :, z * CP : z * CP + CP] = jnp.concatenate([side[:, 0:2], inner, side[:, 4:6]], axis=1)


def one_kernel(feat_ref, out_ref):
    lanes = feat_ref.shape[1]
    r = iota((lanes, 128), 0)
    order = one_hot_rows(((r & 7) << 6) | (r >> 3), lanes)
    out_ref[...] = mm(order, feat_ref[...], NT).astype(BF)


def fill_pitch(copies, wide):
    pitch = copies[0].shape[1]
    for lane in range(0, wide.shape[2], 128):
        line = wide[:, :, lane : lane + 128]
        for i, copy in enumerate(copies):
            spare = jnp.zeros((line.shape[0], pitch - line.shape[1] + i, 128), BF)
            copy[:, :, lane : lane + 128] = jnp.concatenate([line[:, i:], spare], axis=1)


def level_two_group(taps, t_ref, b_ref, masks, moved):
    rows = Y2 + 2
    acc = conv_group(taps, t_ref, rows, 256, 512)
    for q in range(2):
        cut = slice(q * 128, q * 128 + 128)
        value = finish(acc[:, cut], b_ref[...], masks[q], rows)
        for i, ref in enumerate(moved):
            ref[:, :, cut] = value[:, i : i + X2]


def level_two_masks(tab_ref):
    mask = mask_rows(tab_ref[...], -1, Y2 + 2, PITCH2, lambda x: x - 1, 2)
    return [mask[:, q * 128 : q * 128 + 128] for q in range(3)]


def level_two_middle_kernel(wide_ref, t_ref, b_ref, tab_ref, a0, a1, a2, m0, m1, m2):
    fill_pitch((a0, a1, a2), wide_ref[...])
    here = level_two_masks(tab_ref)[1]
    level_two_group([[(a, 0, 512)] for a in (a0, a1, a2)], t_ref, b_ref, (here, here), (m0, m1, m2))


def level_two_kernel(
    a0, a1, a2, m0, m1, m2, zl_ref, zr_ref, ta_ref, tb_ref, ba_ref, bb_ref, tab_ref, out_ref,
    l0, l1, l2, h0, h1, h2, i0, i1, i2, j0, j1, j2,
):
    fill_pitch((l0, l1, l2), zl_ref[...])
    fill_pitch((h0, h1, h2), zr_ref[...])
    below, here, above = level_two_masks(tab_ref)
    own, mid, low, high = (a0, a1, a2), (m0, m1, m2), (i0, i1, i2), (j0, j1, j2)
    taps = [[(z, 0, 256), (a, 0, 256)] for z, a in zip((l0, l1, l2), own)]
    level_two_group(taps, ta_ref, ba_ref, (below, here), low)
    taps = [[(a, 256, 256), (z, 0, 256)] for z, a in zip((h0, h1, h2), own)]
    level_two_group(taps, ta_ref, ba_ref, (here, above), high)
    mask = mask_rows(tab_ref[:, 128:256], 0, Y2, X2, lambda x: x, 2)
    feat = []
    for pair in ((low, mid), (mid, high)):
        acc = conv_group([[(a, 0, 256), (b, 0, 256)] for a, b in zip(*pair)], tb_ref, Y2, 256, 512)
        for q in range(2):
            feat.append((jnp.maximum(acc[:, q * 128 : q * 128 + 128] + bb_ref[...], 0.0) * mask).astype(BF))
    r = iota((C2 * Z2, 128), 0)
    order = one_hot_rows(((r & 3) << 7) | (r >> 2), Z2 * CP)
    out_ref[...] = mm(order, jnp.concatenate(feat, axis=1), NT).astype(BF)


def partner(index, second, count):
    other = index + 1 if index % 2 == second else index - 1
    return other if 0 <= other < count else None


def swap(value, moves):
    axes = ("gx", "gy", "gz")
    sizes = [lax.axis_size(axis) for axis in axes]
    pairs = []
    for source in itertools.product(*(range(size) for size in sizes)):
        target = [partner(i, moves[axis], size) if axis in moves else i for i, axis, size in zip(source, axes, sizes)]
        if None in target:
            other = sizes[1] - 1 - source[1] if "gy" in moves else source[1] ^ 1
            target = [source[0], other, source[2]]
        pairs.append(tuple((x * sizes[1] + y) * sizes[2] + z for x, y, z in (source, target)))
    return lax.ppermute(value, axes, pairs)


def parity(axis):
    return lax.axis_index(axis) % 2 == 0


def sides(first, second, axis):
    index = lax.axis_index(axis)
    even = parity(axis)
    below = jnp.where(index > 0, jnp.where(even, second, first), jnp.zeros_like(first))
    above = jnp.where(index < lax.axis_size(axis) - 1, jnp.where(even, first, second), jnp.zeros_like(first))
    return below, above


def swaps(low_edge, high_edge, axis):
    even = parity(axis)
    first = swap(jnp.where(even, high_edge, low_edge), {axis: 0})
    second = swap(jnp.where(even, low_edge, high_edge), {axis: 1}) if lax.axis_size(axis) > 2 else first
    return first, second


def shift_along(low_edge, high_edge, axis):
    return sides(*swaps(low_edge, high_edge, axis), axis)


def column_pairs(field):
    return jnp.concatenate([field[:, i : i + 2] for i in range(0, field.shape[1], 2)], axis=2)


def params():
    return pltpu.CompilerParams(vmem_limit_bytes=VMEM_BYTES)


def cost(seconds):
    return pl.CostEstimate(flops=int(1e15 * seconds), bytes_accessed=0, transcendentals=0)


def shaped(*shape):
    return jax.ShapeDtypeStruct(shape, BF)


def pad_lanes(value):
    return jnp.pad(value, [(0, 0)] * (value.ndim - 1) + [(0, CP - value.shape[-1])])


def local(
    volume, tissue, w_down1, b_down1, w_conv1a, b_conv1a, w_conv1b, b_conv1b,
    w_down2, b_down2, w_conv2a, b_conv2a, w_conv2b, b_conv2b,
):
    depth = volume.shape[1]
    lanes1 = Z1 * C1
    half = depth // 2
    operands = [volume.reshape(C0, 2, half, -1), jnp.swapaxes(w_down1, 1, 2), b_down1[None], tissue.transpose(1, 2, 0)]
    operands = [pltpu.with_memory_space_constraint(x, pltpu.HBM) for x in operands]
    own, tab1, tab2 = pl.pallas_call(
        down1_kernel,
        in_specs=[pl.BlockSpec(memory_space=pltpu.HBM)] * 4,
        out_shape=[shaped(Y1, X1, lanes1), shaped(128, 384), shaped(128, 384)],
        scratch_shapes=[pltpu.VMEM(x.shape, x.dtype) for x in operands]
        + [
            pltpu.VMEM((C0 // 16, 64 * half, lanes1 // 2), BF),
            pltpu.VMEM((C0 // 16, 2, Y1 * X1, 64 * half), BF),
            pltpu.SemaphoreType.DMA((3 + C0 // 16,)),
        ],
        compiler_params=params(),
        cost_estimate=cost(4e-6),
    )(*operands)

    t1a = banded(w_conv1a, 4, C1, 1)
    bias1a = b_conv1a[None]

    y_below, y_above = shift_along(own[:HALO], own[Y1 - HALO :], "gy")
    win = jnp.concatenate([y_below, own, y_above], axis=0)
    z_below, z_above = shift_along(win[:, :, :128], win[:, :, lanes1 - 128 :], "gz")
    low, high = win[:, :HALO_X], win[:, X1 - HALO_X :]
    even = parity("gx")
    faces = lax.optimization_barrier((jnp.where(even, high, low), jnp.where(even, low, high)))
    x_got = tuple(swap(column_pairs(face), {"gx": n}) for n, face in enumerate(faces))
    x_got = lax.optimization_barrier(x_got[::-1])[::-1]
    rows = Y1 + 2
    left, right, g2, t1b = pl.pallas_call(
        middle_kernel,
        out_shape=[shaped(ROWS1, X1, lanes1), shaped(ROWS1, X1, lanes1), shaped(rows, X1, 256), banded_shape(4, C1, 1)],
        compiler_params=params(),
        cost_estimate=cost(1e-7),
    )(win, t1a, bias1a, tab1, w_conv1b)

    corner = []
    for lane in (0, lanes1 - 128):
        cut = [jnp.concatenate(column_lanes(got, lane), axis=2) for got in x_got]
        corner.append(jnp.concatenate(sides(*cut, "gx"), axis=2))
    low, high = corner
    low, high, g2, *x_got = lax.optimization_barrier((low, high, g2, *x_got))
    x_below, x_above = sides(*x_got, "gx")
    corner_below, corner_above = shift_along(low, high, "gz")
    g1, g3 = pl.pallas_call(
        outer_kernel,
        out_shape=[shaped(rows, X1, 256), shaped(rows, X1, 128)],
        scratch_shapes=[pltpu.VMEM((ROWS1, X1, 128), BF)] * 4,
        compiler_params=params(),
        cost_estimate=cost(4e-6),
    )(win, left, right, z_below, z_above, t1a, bias1a, tab1)

    wide_x = X1 + EDGE
    edges = pl.pallas_call(
        edge_middle_kernel,
        out_shape=[shaped(ROWS1, EDGE, lanes1)] * 3 + [shaped(rows, wide_x, 256)] * 3,
        compiler_params=params(),
        cost_estimate=cost(3e-6),
    )(x_below, win, x_above, g2, t1a, bias1a, tab1)
    feat, down = pl.pallas_call(
        level_one_kernel,
        out_shape=[shaped(Y1 * X1, lanes1), shaped(Y2, X2 + 2 * HALO_X2, Z2 * CP)],
        scratch_shapes=[pltpu.VMEM((ROWS1, EDGE, 128), BF)] * 6
        + [pltpu.VMEM((rows, wide_x, 256), BF)] * 3
        + [pltpu.VMEM((rows, wide_x, 128), BF)] * 3
        + [pltpu.VMEM((Y1 * EDGE, lanes1), BF), pltpu.VMEM((4, Y2 * (X2 + EDGE // 2), lanes1), BF)],
        compiler_params=params(),
        cost_estimate=cost(6e-6),
    )(
        z_below, z_above, corner_below, corner_above, *edges, g1, g3, t1a, t1b, bias1a, b_conv1b[None],
        pad_lanes(jnp.swapaxes(w_down2, 1, 2).reshape(8 * C1, C2)), pad_lanes(b_down2[None]), tab1, tab2,
    )

    down, w_conv2a = lax.optimization_barrier((down, w_conv2a))
    t2a = banded(w_conv2a, 2, CP, 3)
    y_below, y_above = shift_along(down[:HALO], down[Y2 - HALO :], "gy")
    wide = jnp.concatenate([y_below, down, y_above], axis=0)
    feat, wide, w_conv2b = lax.optimization_barrier((feat, wide, w_conv2b))
    t2b = banded(w_conv2b, 2, CP, 3)
    one = pl.pallas_call(
        one_kernel, out_shape=shaped(lanes1, Y1 * X1), compiler_params=params(), cost_estimate=cost(2e-6)
    )(feat)
    z_below, z_above = shift_along(wide[:, :, : 2 * CP], wide[:, :, 2 * CP :], "gz")
    bias2a = pad_lanes(b_conv2a[None])
    moved = [shaped(Y2 + 2, X2, 2 * CP)] * 3
    middle = pl.pallas_call(
        level_two_middle_kernel,
        out_shape=[shaped(ROWS2, PITCH2, Z2 * CP)] * 3 + moved,
        compiler_params=params(),
        cost_estimate=cost(3e-6),
    )(wide, t2a, bias2a, tab2)
    two = pl.pallas_call(
        level_two_kernel,
        out_shape=shaped(C2 * Z2, Y2 * X2),
        scratch_shapes=[pltpu.VMEM((ROWS2, PITCH2, 2 * CP), BF)] * 6 + [pltpu.VMEM((Y2 + 2, X2, 2 * CP), BF)] * 6,
        compiler_params=params(),
        cost_estimate=cost(5e-6),
    )(*middle, z_below, z_above, t2a, t2b, bias2a, pad_lanes(b_conv2b[None]), tab2)
    return one.reshape(C1, Z1, Y1 * X1), two.reshape(C2, Z2, Y2 * X2)


def solution(mesh):
    block = P(None, "gz", ("gx", "gy"))
    return jax.shard_map(
        local,
        mesh=mesh,
        in_specs=(block,) + (P(),) * 13,
        out_specs=(block, block),
        check_vma=False,
    )
```

```python
import itertools

import jax
import jax.numpy as jnp
from jax import lax
from jax.experimental import pallas as pl
from jax.experimental.pallas import tpu as pltpu
from jax.sharding import PartitionSpec as P

CX = 64
CY = 32
X1 = CX // 2
Y1 = CY // 2
X2 = X1 // 2
Y2 = Y1 // 2
Z1 = 8
Z2 = 4
C0 = 48
C1 = 64
C2 = 96
CP = 128
HALO = 2
HALO_X = 6
HALO_X2 = 2
XB = 12
XB_BELOW = 2
XB_PITCH = 16
YB = 6
ROWS1 = Y1 + 2 * HALO
ROWS2 = Y2 + 2 * HALO
EDGE = 16
PITCH2 = 32
BF = jnp.bfloat16
F32 = jnp.float32
NN = (((1,), (0,)), ((), ()))
NT = (((1,), (1,)), ((), ()))
VMEM_BYTES = 20 * 1024 * 1024


def mm(a, b, dims=NN):
    return lax.dot_general(a, b, dims, preferred_element_type=F32)


def iota(shape, dim):
    return lax.broadcasted_iota(jnp.int32, shape, dim)


def one_hot(flag):
    return jnp.where(flag, 1.0, 0.0).astype(BF)


def one_hot_rows(key, lanes):
    lane = iota(key.shape, 1)
    return jnp.concatenate([one_hot(key == lane + q) for q in range(0, lanes, 128)], axis=1)


def mask_rows(tab, y_start, rows, pitch, x_of, cell):
    bits = cell.bit_length() - 1
    shape = (rows, pitch, 128)
    y_block = (iota(shape, 0) + (y_start + cell)) >> bits
    x_block = jnp.minimum((x_of(iota(shape, 1)) + XB_BELOW * cell) >> bits, XB - 1)
    hit = one_hot(y_block * XB_PITCH + x_block == iota(shape, 2)).reshape(rows * pitch, 128)
    return mm(hit, tab)


def tissue_tables(t_ref):
    n_y, n_z, n_x = t_ref.shape
    here = lax.axis_index("gz")
    layers = []
    for k in (-1, 0, 1):
        z = here + k
        inside = jnp.where((z >= 0) & (z < n_z), 1.0, 0.0)
        layers.append(t_ref[:, jnp.clip(z, 0, n_z - 1), :].astype(F32) * inside)
    block = iota((128, n_y), 0)
    bits = XB_PITCH.bit_length() - 1
    hot_y = one_hot(lax.axis_index("gy") * 4 - 1 + (block >> bits) == iota((128, n_y), 1))
    block = iota((128, 3 * n_x), 0)
    layer = sum((iota((128, 3 * n_x), 1) >= k * n_x).astype(jnp.int32) for k in (1, 2))
    hot_x = lax.axis_index("gx") * 8 - XB_BELOW + (block & (XB_PITCH - 1)) == iota((128, 3 * n_x), 1) - layer * n_x
    rows = jnp.where(hot_x, mm(hot_y, jnp.concatenate(layers, axis=1).astype(BF)), 0.0).astype(BF)
    shape = (3 * n_x, 384)
    layer = sum((iota(shape, 0) >= k * n_x).astype(jnp.int32) for k in (1, 2))
    lane = iota(shape, 1)

    def spread(first, last):
        place = jnp.where(lane < first, 0, jnp.where(lane < last, 1, 2))
        return mm(rows, one_hot(layer == place)).astype(BF)

    return spread(64, 320), spread(128, 256)


def down1_kernel(
    v_hbm, wd_hbm, b_hbm, t_hbm, out_ref, tab_ref, tab2_ref, v_ref, w_ref, b_ref, t_ref, wd_ref, cells_ref, sems
):
    half = v_ref.shape[2]
    kz = C0 * half
    part = 16 * half
    lanes = Z1 // 2 * C1
    small = ((t_hbm, t_ref), (wd_hbm, w_ref), (b_hbm, b_ref))
    copies = [pltpu.make_async_copy(src, dst, sems.at[n]) for n, (src, dst) in enumerate(small)]
    for n in range(C0 // 16):
        cut = slice(n * 16, n * 16 + 16)
        copies.append(pltpu.make_async_copy(v_hbm.at[cut], v_ref.at[cut], sems.at[len(small) + n]))
    for copy in copies:
        copy.start()

    copies[0].wait()
    tab, tab2 = tissue_tables(t_ref)
    tab_ref[...] = tab
    tab2_ref[...] = tab2
    copies[1].wait()
    copies[2].wait()
    r = iota((kz, 2 * C0), 0)
    l = iota((kz, 2 * C0), 1)
    odd = l >= C0
    spread = one_hot(((r >> 3) == jnp.where(odd, l - C0, l)) & ((r & 1) == odd.astype(jnp.int32)))
    keep = (iota((kz, lanes), 0) & 7) >> 1 == iota((kz, lanes), 1) >> 6
    for ab in range(4):
        pair = w_ref[2 * ab : 2 * ab + 2].reshape(2 * C0, C1)
        wide = jnp.concatenate([pair] * (Z1 // 2), axis=1)
        block = jnp.where(keep, mm(spread, wide), 0.0).astype(BF)
        for n in range(C0 // 16):
            wd_ref[n, ab * part : ab * part + part, :] = block[n * part : n * part + part]

    r = iota((4 * CX, 128), 0)
    select = one_hot_rows(((r & 32) << 2) | (r & 64) | ((r & 31) << 1) | (r >> 7), 4 * CX)
    part = 16 * half
    acc = [0.0, 0.0]
    for n, copy in enumerate(copies[3:]):
        copy.wait()
        for m in range(v_ref.shape[3] // 256):
            v = [v_ref[n * 16 : n * 16 + 16, h, :, m * 256 : m * 256 + 256].reshape(part, 256) for h in range(2)]
            cells = mm(select, jnp.concatenate(v, axis=0), NT).astype(BF)
            for ab in range(4):
                for h in range(2):
                    piece = cells[64 * ab : 64 * ab + 64, h * part : h * part + part]
                    cells_ref[n, h, m * 64 : m * 64 + 64, ab * part : ab * part + part] = piece
        acc = [acc[h] + mm(cells_ref[n, h], wd_ref[n]) for h in range(2)]
    mask = mask_rows(tab[:, 128:256], 0, Y1, X1, lambda x: x, 4)
    bias = twice(b_ref)
    for h in range(2):
        for q in range(2):
            value = finish(acc[h][:, q * 128 : q * 128 + 128], bias, mask, Y1)
            out_ref[:, :, (2 * h + q) * 128 : (2 * h + q + 1) * 128] = value


def twice(b_ref):
    return jnp.concatenate([b_ref[...]] * 2, axis=1)


def fill_banded(w_ref, t_ref, group, pad):
    chan = w_ref.shape[1]
    t_ref[...] = jnp.zeros_like(t_ref)
    for j in range(3):
        for i in range(3):
            for zo in range(group):
                for k in range(3):
                    lane = (3 * j + i) * (group + 2) * pad + (zo + k) * pad
                    cut, lane = divmod(lane, t_ref.shape[2])
                    t_ref[cut, zo * pad : zo * pad + chan, lane : lane + chan] = w_ref[9 * i + 3 * j + k]


def banded_shape(group, pad, cuts):
    return shaped(cuts, group * pad, 9 * (group + 2) * pad // cuts)


def banded(weights, group, pad, cuts):
    def kernel(w_ref, t_ref):
        fill_banded(w_ref, t_ref, group, pad)

    return pl.pallas_call(
        kernel, out_shape=banded_shape(group, pad, cuts), compiler_params=params(), cost_estimate=cost(1e-6)
    )(weights)


def conv_group(taps, t_ref, rows, group_out, group_full):
    pitch = taps[0][0][0].shape[1]
    width = sum(piece[2] for piece in taps[0])
    cuts = t_ref.shape[0]
    total = None
    for cut in range(cuts):
        js = range(3 * cut // cuts, 3 * (cut + 1) // cuts)
        parts = [ref[j : j + rows, :, lane : lane + n] for j in js for tap in taps for ref, lane, n in tap]
        left = jnp.concatenate([p.reshape(rows * pitch, p.shape[2]) for p in parts], axis=1)
        if width == group_full:
            right = t_ref[cut, 0:group_out, :]
        else:
            starts = range(0, t_ref.shape[2], group_full)
            right = jnp.concatenate([t_ref[cut, 0:group_out, lane : lane + width] for lane in starts], axis=1)
        term = mm(left, right, NT)
        total = term if total is None else total + term
    return total


def finish(acc, bias, mask, rows):
    value = jnp.maximum(acc + bias, 0.0) * mask
    return value.astype(BF).reshape(rows, value.shape[0] // rows, value.shape[1])


def fill_sides(left, right, lane, inner):
    cut = slice(lane, lane + inner.shape[2])
    none = jnp.zeros_like(inner[:, :1])
    left[:, :, cut] = jnp.concatenate([none, inner[:, :-1]], axis=1)
    right[:, :, cut] = jnp.concatenate([inner[:, 1:], none], axis=1)


def middle_kernel(win_ref, t_ref, b_ref, tab_ref, w_ref, left_ref, right_ref, out_ref, next_ref):
    fill_banded(w_ref, next_ref, 4, C1)
    for q in range(4):
        fill_sides(left_ref, right_ref, q * 128, win_ref[:, :, q * 128 : q * 128 + 128])
    rows = Y1 + 2
    mask = mask_rows(tab_ref[:, 128:256], -1, rows, X1, lambda x: x, 4)
    acc = conv_group([[(ref, 128, 384)] for ref in (left_ref, win_ref, right_ref)], t_ref, rows, 256, 384)
    for q in range(2):
        cut = slice(q * 128, q * 128 + 128)
        out_ref[:, :, cut] = finish(acc[:, cut], twice(b_ref), mask, rows)


def outer_kernel(win_ref, left_ref, right_ref, zl_ref, zr_ref, t_ref, b_ref, tab_ref, low_ref, high_ref, ll, lr, hl, hr):
    fill_sides(ll, lr, 0, zl_ref[...])
    fill_sides(hl, hr, 0, zr_ref[...])
    own = (left_ref, win_ref, right_ref)
    rows = Y1 + 2
    mask = mask_rows(tab_ref[...], -1, rows, X1, lambda x: x, 4)
    taps = [[(z, 0, 128), (ref, 0, 256)] for z, ref in zip((ll, zl_ref, lr), own)]
    acc = conv_group(taps, t_ref, rows, 256, 384)
    for q in range(2):
        cut = slice(q * 128, q * 128 + 128)
        low_ref[:, :, cut] = finish(acc[:, cut], twice(b_ref), mask[:, cut], rows)
    taps = [[(ref, 384, 128), (z, 0, 128)] for z, ref in zip((hl, zr_ref, hr), own)]
    acc = conv_group(taps, t_ref, rows, 128, 384)
    high_ref[...] = finish(acc, twice(b_ref), mask[:, 256:384], rows)


def fill_edges(copies, pieces):
    line = jnp.concatenate(pieces, axis=1)
    copies[0][...] = line
    for i in (1, 2):
        copies[i][...] = jnp.concatenate([line[:, i:], jnp.zeros_like(line[:, :i])], axis=1)


def edge_masks(tab_ref):
    mask = mask_rows(tab_ref[...], -1, Y1 + 2, EDGE, lambda r: jnp.where(r < 8, r - 5, r + X1 - 9), 4)
    return [mask[:, q * 128 : q * 128 + 128] for q in range(3)]


def edge_group(taps, t_ref, b_ref, masks, inner_ref, moved):
    rows = Y1 + 2
    acc = conv_group(taps, t_ref, rows, 128 * len(masks), 384)
    i0, i1, i2 = moved
    for q, mask in enumerate(masks):
        cut = slice(q * 128, q * 128 + 128)
        edge = finish(acc[:, cut], twice(b_ref), mask, rows)
        inner = inner_ref[:, :, cut][:, 1:-1]
        i0[:, :X1, cut] = jnp.concatenate([edge[:, 4:6], inner], axis=1)
        i1[:, :X1, cut] = jnp.concatenate([edge[:, 5:6], inner, edge[:, 8:9]], axis=1)
        i2[:, :X1, cut] = jnp.concatenate([inner, edge[:, 8:10]], axis=1)
        i0[:, X1:, cut] = edge
        for i, copy in ((1, i1), (2, i2)):
            copy[:, X1:, cut] = jnp.concatenate([edge[:, i:], jnp.zeros((rows, i, 128), BF)], axis=1)


def column_lanes(field, lane, stride=Z1 * C1):
    return [field[:, :, first : first + 128] for first in range(lane, field.shape[2], stride)]


def edge_middle_kernel(xl_ref, win_ref, xr_ref, g_ref, t_ref, b_ref, tab_ref, e0, e1, e2, m0, m1, m2):
    for lane in range(0, Z1 * C1, 128):
        cut = slice(lane, lane + 128)
        inner = win_ref[:, :, cut]
        left, right = (column_lanes(ref, lane) for ref in (xl_ref, xr_ref))
        pieces = left + [inner[:, :2], inner[:, X1 - 2 :]] + right
        fill_edges([e.at[:, :, cut] for e in (e0, e1, e2)], pieces)
    here = edge_masks(tab_ref)[1]
    edge_group([[(e, 128, 384)] for e in (e0, e1, e2)], t_ref, b_ref, (here, here), g_ref, (m0, m1, m2))


def level_one_kernel(
    zl_ref, zr_ref, cl_ref, cr_ref, e0, e1, e2, m0, m1, m2, g1_ref, g3_ref, ta_ref, tb_ref, ba_ref, bb_ref, wd_ref, bd_ref, tab_ref,
    tab2_ref, feat_ref, down_ref, l0, l1, l2, h0, h1, h2, i0, i1, i2, j0, j1, j2, side_ref, d_ref,
):
    own, mid, low, high = (e0, e1, e2), (m0, m1, m2), (i0, i1, i2), (j0, j1, j2)
    for z_ref, c_ref, copies in ((zl_ref, cl_ref, (l0, l1, l2)), (zr_ref, cr_ref, (h0, h1, h2))):
        inner = z_ref[...]
        corner = column_lanes(c_ref, 0, 128)
        fill_edges(copies, corner[:3] + [inner[:, :2], inner[:, X1 - 2 :]] + corner[3:])
    below, here, above = edge_masks(tab_ref)
    taps = [[(z, 0, 128), (e, 0, 256)] for z, e in zip((l0, l1, l2), own)]
    edge_group(taps, ta_ref, ba_ref, (below, here), g1_ref, low)
    taps = [[(e, 384, 128), (z, 0, 128)] for z, e in zip((h0, h1, h2), own)]
    edge_group(taps, ta_ref, ba_ref, (above,), g3_ref, high)

    def cell_of(r):
        return jnp.where(r < X1, r, jnp.where(r < X1 + 8, r - X1 - 4, r - 8))

    mask = mask_rows(tab_ref[:, 128:256], 0, Y1, X1 + EDGE, cell_of, 4)
    first = [[(a, 0, 256), (b, 0, 128)] for a, b in zip(low, mid)]
    second = [[(a, 0, 256), (b, 0, 128)] for a, b in zip(mid, high)]
    for g, taps in enumerate((first, second)):
        acc = conv_group(taps, tb_ref, Y1, 256, 384)
        for q in range(2):
            value = finish(acc[:, q * 128 : q * 128 + 128], twice(bb_ref), mask, Y1)
            cut = slice((2 * g + q) * 128, (2 * g + q + 1) * 128)
            feat_ref[:, cut] = value[:, :X1].reshape(Y1 * X1, 128)
            side_ref[:, cut] = value[:, X1:].reshape(Y1 * EDGE, 128)

    size = 8 * X1
    quarter = size // 4
    r = iota((size, 128), 0)
    select = one_hot_rows(((r & 48) << 2) | ((r & 64) >> 1) | ((r & 15) << 1) | (r >> 7), size)
    for n in range(Y1 // 8):
        cells = mm(select, feat_ref[n * size : n * size + size, :]).astype(BF)
        for q in range(4):
            d_ref[q, n * quarter : n * quarter + quarter, :] = cells[q * quarter : (q + 1) * quarter]
    select = one_hot_rows(((r & 56) << 2) | ((r & 64) >> 2) | ((r & 7) << 1) | (r >> 7), size)
    cells = mm(select, side_ref[...]).astype(BF)
    for q in range(4):
        d_ref[q, Y2 * X2 :, :] = cells[q * quarter : (q + 1) * quarter]
    inner_mask = mask_rows(tab2_ref[:, 128:256], 0, Y2, X2, lambda x: x, 2)
    side_mask = mask_rows(tab2_ref[:, 128:256], 0, Y2, EDGE // 2, lambda r: jnp.where(r < 4, r - 2, r + X2 - 4), 2)
    for z in range(Z2):
        left = jnp.concatenate([d_ref[q, :, z * 128 : z * 128 + 128] for q in range(4)], axis=1)
        acc = mm(left, wd_ref[...])
        inner = finish(acc[: Y2 * X2], bd_ref[...], inner_mask, Y2)
        side = finish(acc[Y2 * X2 :], bd_ref[...], side_mask, Y2)
        down_ref[:, :, z * CP : z * CP + CP] = jnp.concatenate([side[:, 0:2], inner, side[:, 4:6]], axis=1)


def one_kernel(feat_ref, out_ref):
    lanes = feat_ref.shape[1]
    r = iota((lanes, 128), 0)
    order = one_hot_rows(((r & 7) << 6) | (r >> 3), lanes)
    out_ref[...] = mm(order, feat_ref[...], NT).astype(BF)


def fill_pitch(copies, wide):
    pitch = copies[0].shape[1]
    for lane in range(0, wide.shape[2], 128):
        line = wide[:, :, lane : lane + 128]
        for i, copy in enumerate(copies):
            spare = jnp.zeros((line.shape[0], pitch - line.shape[1] + i, 128), BF)
            copy[:, :, lane : lane + 128] = jnp.concatenate([line[:, i:], spare], axis=1)


def level_two_group(taps, t_ref, b_ref, masks, moved):
    rows = Y2 + 2
    acc = conv_group(taps, t_ref, rows, 256, 512)
    for q in range(2):
        cut = slice(q * 128, q * 128 + 128)
        value = finish(acc[:, cut], b_ref[...], masks[q], rows)
        for i, ref in enumerate(moved):
            ref[:, :, cut] = value[:, i : i + X2]


def level_two_masks(tab_ref):
    mask = mask_rows(tab_ref[...], -1, Y2 + 2, PITCH2, lambda x: x - 1, 2)
    return [mask[:, q * 128 : q * 128 + 128] for q in range(3)]


def level_two_middle_kernel(wide_ref, t_ref, b_ref, tab_ref, a0, a1, a2, m0, m1, m2):
    fill_pitch((a0, a1, a2), wide_ref[...])
    here = level_two_masks(tab_ref)[1]
    level_two_group([[(a, 0, 512)] for a in (a0, a1, a2)], t_ref, b_ref, (here, here), (m0, m1, m2))


def level_two_kernel(
    a0, a1, a2, m0, m1, m2, zl_ref, zr_ref, ta_ref, tb_ref, ba_ref, bb_ref, tab_ref, out_ref,
    l0, l1, l2, h0, h1, h2, i0, i1, i2, j0, j1, j2,
):
    fill_pitch((l0, l1, l2), zl_ref[...])
    fill_pitch((h0, h1, h2), zr_ref[...])
    below, here, above = level_two_masks(tab_ref)
    own, mid, low, high = (a0, a1, a2), (m0, m1, m2), (i0, i1, i2), (j0, j1, j2)
    taps = [[(z, 0, 256), (a, 0, 256)] for z, a in zip((l0, l1, l2), own)]
    level_two_group(taps, ta_ref, ba_ref, (below, here), low)
    taps = [[(a, 256, 256), (z, 0, 256)] for z, a in zip((h0, h1, h2), own)]
    level_two_group(taps, ta_ref, ba_ref, (here, above), high)
    mask = mask_rows(tab_ref[:, 128:256], 0, Y2, X2, lambda x: x, 2)
    feat = []
    for pair in ((low, mid), (mid, high)):
        acc = conv_group([[(a, 0, 256), (b, 0, 256)] for a, b in zip(*pair)], tb_ref, Y2, 256, 512)
        for q in range(2):
            feat.append((jnp.maximum(acc[:, q * 128 : q * 128 + 128] + bb_ref[...], 0.0) * mask).astype(BF))
    r = iota((C2 * Z2, 128), 0)
    order = one_hot_rows(((r & 3) << 7) | (r >> 2), Z2 * CP)
    out_ref[...] = mm(order, jnp.concatenate(feat, axis=1), NT).astype(BF)


def partner(index, second, count):
    other = index + 1 if index % 2 == second else index - 1
    return other if 0 <= other < count else None


def swap(value, moves):
    axes = ("gx", "gy", "gz")
    sizes = [lax.axis_size(axis) for axis in axes]
    pairs = []
    for source in itertools.product(*(range(size) for size in sizes)):
        target = [partner(i, moves[axis], size) if axis in moves else i for i, axis, size in zip(source, axes, sizes)]
        if None in target:
            other = sizes[1] - 1 - source[1] if "gy" in moves else source[1] ^ 1
            target = [source[0], other, source[2]]
        pairs.append(tuple((x * sizes[1] + y) * sizes[2] + z for x, y, z in (source, target)))
    return lax.ppermute(value, axes, pairs)


def parity(axis):
    return lax.axis_index(axis) % 2 == 0


def sides(first, second, axis):
    index = lax.axis_index(axis)
    even = parity(axis)
    below = jnp.where(index > 0, jnp.where(even, second, first), jnp.zeros_like(first))
    above = jnp.where(index < lax.axis_size(axis) - 1, jnp.where(even, first, second), jnp.zeros_like(first))
    return below, above


def swaps(low_edge, high_edge, axis):
    even = parity(axis)
    first = swap(jnp.where(even, high_edge, low_edge), {axis: 0})
    second = swap(jnp.where(even, low_edge, high_edge), {axis: 1}) if lax.axis_size(axis) > 2 else first
    return first, second


def shift_along(low_edge, high_edge, axis):
    return sides(*swaps(low_edge, high_edge, axis), axis)


def column_pairs(field):
    return jnp.concatenate([field[:, i : i + 2] for i in range(0, field.shape[1], 2)], axis=2)


def params():
    return pltpu.CompilerParams(vmem_limit_bytes=VMEM_BYTES)


def cost(seconds):
    return pl.CostEstimate(flops=int(1e15 * seconds), bytes_accessed=0, transcendentals=0)


def shaped(*shape):
    return jax.ShapeDtypeStruct(shape, BF)


def pad_lanes(value):
    return jnp.pad(value, [(0, 0)] * (value.ndim - 1) + [(0, CP - value.shape[-1])])


def local(
    volume, tissue, w_down1, b_down1, w_conv1a, b_conv1a, w_conv1b, b_conv1b,
    w_down2, b_down2, w_conv2a, b_conv2a, w_conv2b, b_conv2b,
):
    depth = volume.shape[1]
    lanes1 = Z1 * C1
    half = depth // 2
    operands = [volume.reshape(C0, 2, half, -1), jnp.swapaxes(w_down1, 1, 2), b_down1[None], tissue.transpose(1, 2, 0)]
    operands = [pltpu.with_memory_space_constraint(x, pltpu.HBM) for x in operands]
    own, tab1, tab2 = pl.pallas_call(
        down1_kernel,
        in_specs=[pl.BlockSpec(memory_space=pltpu.HBM)] * 4,
        out_shape=[shaped(Y1, X1, lanes1), shaped(128, 384), shaped(128, 384)],
        scratch_shapes=[pltpu.VMEM(x.shape, x.dtype) for x in operands]
        + [
            pltpu.VMEM((C0 // 16, 64 * half, lanes1 // 2), BF),
            pltpu.VMEM((C0 // 16, 2, Y1 * X1, 64 * half), BF),
            pltpu.SemaphoreType.DMA((3 + C0 // 16,)),
        ],
        compiler_params=params(),
        cost_estimate=cost(4e-6),
    )(*operands)

    t1a = banded(w_conv1a, 4, C1, 1)
    bias1a = b_conv1a[None]

    y_below, y_above = shift_along(own[:HALO], own[Y1 - HALO :], "gy")
    win = jnp.concatenate([y_below, own, y_above], axis=0)
    z_below, z_above = shift_along(win[:, :, :128], win[:, :, lanes1 - 128 :], "gz")
    low, high = win[:, :HALO_X], win[:, X1 - HALO_X :]
    even = parity("gx")
    trim = lax.axis_size("gy") == 2
    first_row = lax.axis_index("gy") == 0
    if trim:
        low, high = (jnp.where(first_row, e[HALO:], e[:-HALO]) for e in (low, high))
    faces = lax.optimization_barrier((jnp.where(even, high, low), jnp.where(even, low, high)))
    x_got = tuple(swap(column_pairs(face), {"gx": n}) for n, face in enumerate(faces))
    x_got = lax.optimization_barrier(x_got[::-1])[::-1]
    if trim:
        rim = jnp.zeros_like(x_got[0][:HALO])
        x_got = [
            jnp.where(first_row, jnp.concatenate([rim, got], axis=0), jnp.concatenate([got, rim], axis=0)) for got in x_got
        ]
    rows = Y1 + 2
    left, right, g2, t1b = pl.pallas_call(
        middle_kernel,
        out_shape=[shaped(ROWS1, X1, lanes1), shaped(ROWS1, X1, lanes1), shaped(rows, X1, 256), banded_shape(4, C1, 1)],
        compiler_params=params(),
        cost_estimate=cost(1e-7),
    )(win, t1a, bias1a, tab1, w_conv1b)

    corner = []
    for lane in (0, lanes1 - 128):
        cut = [jnp.concatenate(column_lanes(got, lane), axis=2) for got in x_got]
        corner.append(jnp.concatenate(sides(*cut, "gx"), axis=2))
    low, high = corner
    low, high, g2, *x_got = lax.optimization_barrier((low, high, g2, *x_got))
    x_below, x_above = sides(*x_got, "gx")
    corner_below, corner_above = shift_along(low, high, "gz")
    g1, g3 = pl.pallas_call(
        outer_kernel,
        out_shape=[shaped(rows, X1, 256), shaped(rows, X1, 128)],
        scratch_shapes=[pltpu.VMEM((ROWS1, X1, 128), BF)] * 4,
        compiler_params=params(),
        cost_estimate=cost(4e-6),
    )(win, left, right, z_below, z_above, t1a, bias1a, tab1)

    wide_x = X1 + EDGE
    edges = pl.pallas_call(
        edge_middle_kernel,
        out_shape=[shaped(ROWS1, EDGE, lanes1)] * 3 + [shaped(rows, wide_x, 256)] * 3,
        compiler_params=params(),
        cost_estimate=cost(3e-6),
    )(x_below, win, x_above, g2, t1a, bias1a, tab1)
    feat, down = pl.pallas_call(
        level_one_kernel,
        out_shape=[shaped(Y1 * X1, lanes1), shaped(Y2, X2 + 2 * HALO_X2, Z2 * CP)],
        scratch_shapes=[pltpu.VMEM((ROWS1, EDGE, 128), BF)] * 6
        + [pltpu.VMEM((rows, wide_x, 256), BF)] * 3
        + [pltpu.VMEM((rows, wide_x, 128), BF)] * 3
        + [pltpu.VMEM((Y1 * EDGE, lanes1), BF), pltpu.VMEM((4, Y2 * (X2 + EDGE // 2), lanes1), BF)],
        compiler_params=params(),
        cost_estimate=cost(6e-6),
    )(
        z_below, z_above, corner_below, corner_above, *edges, g1, g3, t1a, t1b, bias1a, b_conv1b[None],
        pad_lanes(jnp.swapaxes(w_down2, 1, 2).reshape(8 * C1, C2)), pad_lanes(b_down2[None]), tab1, tab2,
    )

    down, w_conv2a = lax.optimization_barrier((down, w_conv2a))
    t2a = banded(w_conv2a, 2, CP, 3)
    y_below, y_above = shift_along(down[:HALO], down[Y2 - HALO :], "gy")
    wide = jnp.concatenate([y_below, down, y_above], axis=0)
    feat, wide, w_conv2b = lax.optimization_barrier((feat, wide, w_conv2b))
    t2b = banded(w_conv2b, 2, CP, 3)
    one = pl.pallas_call(
        one_kernel, out_shape=shaped(lanes1, Y1 * X1), compiler_params=params(), cost_estimate=cost(2e-6)
    )(feat)
    z_below, z_above = shift_along(wide[:, :, : 2 * CP], wide[:, :, 2 * CP :], "gz")
    bias2a = pad_lanes(b_conv2a[None])
    moved = [shaped(Y2 + 2, X2, 2 * CP)] * 3
    middle = pl.pallas_call(
        level_two_middle_kernel,
        out_shape=[shaped(ROWS2, PITCH2, Z2 * CP)] * 3 + moved,
        compiler_params=params(),
        cost_estimate=cost(3e-6),
    )(wide, t2a, bias2a, tab2)
    two = pl.pallas_call(
        level_two_kernel,
        out_shape=shaped(C2 * Z2, Y2 * X2),
        scratch_shapes=[pltpu.VMEM((ROWS2, PITCH2, 2 * CP), BF)] * 6 + [pltpu.VMEM((Y2 + 2, X2, 2 * CP), BF)] * 6,
        compiler_params=params(),
        cost_estimate=cost(5e-6),
    )(*middle, z_below, z_above, t2a, t2b, bias2a, pad_lanes(b_conv2b[None]), tab2)
    return one.reshape(C1, Z1, Y1 * X1), two.reshape(C2, Z2, Y2 * X2)


def solution(mesh):
    block = P(None, "gz", ("gx", "gy"))
    return jax.shard_map(
        local,
        mesh=mesh,
        in_specs=(block,) + (P(),) * 13,
        out_specs=(block, block),
        check_vma=False,
    )
```
